128 devices in a mesh: fsdp: 8 (over x_hi, z), context: 8 (over x_lo, y), tensor: 2 (over core).
Axes of the slice: x: 4 (x_hi: 2, x_lo: 2; x = x_hi * 2 + x_lo), y: 4, z: 4, core: 2. Of those that a mesh axis runs over, the one named last changes fastest.
Arguments:
- stream: bfloat16 [1024, 16, 1024], P('context', 'fsdp'), may hold values from -6 to 6
- lengths: int32 [16], P('fsdp'), may hold values from 256 to 1024, as said below
- query_weight: bfloat16 [1024, 1024], P(('fsdp', 'context'), 'tensor'), may hold values from -0.1875 to 0.1875
- query_bias: bfloat16 [1024], P('tensor'), may hold values from -1.75 to 1.75
- key_weight: bfloat16 [1024, 1024], P(('fsdp', 'context'), 'tensor'), may hold values from -0.1875 to 0.1875
- value_weight: bfloat16 [1024, 1024], P(('fsdp', 'context'), 'tensor'), may hold values from -0.1875 to 0.1875
- value_bias: bfloat16 [1024], P('tensor'), may hold values from -0.1875 to 0.1875
- output_weight: bfloat16 [1024, 1024], P('tensor', ('fsdp', 'context')), may hold values from -3 to 3
- output_bias: bfloat16 [1024], P(('fsdp', 'context')), may hold values from -1.75 to 1.75
- first_gain: bfloat16 [1024], P(('fsdp', 'context')), may hold values from 0.5 to 1.5
- first_shift: bfloat16 [1024], P(('fsdp', 'context')), may hold values from -1.75 to 1.75
- inner_weight: bfloat16 [1024, 4096], P(('fsdp', 'context'), 'tensor'), may hold values from -0.1875 to 0.1875
- inner_bias: bfloat16 [4096], P('tensor'), may hold values from -1.75 to 1.75
- outer_weight: bfloat16 [4096, 1024], P('tensor', ('fsdp', 'context')), may hold values from -0.09375 to 0.09375
- outer_bias: bfloat16 [1024], P(('fsdp', 'context')), may hold values from -1.75 to 1.75
- second_gain: bfloat16 [1024], P(('fsdp', 'context')), may hold values from 0.5 to 1.5
- second_shift: bfloat16 [1024], P(('fsdp', 'context')), may hold values from -1.75 to 1.75
- cotangent: bfloat16 [1024, 16, 1024], P('context', 'fsdp'), may hold values from -6 to 6
Outputs:
- result: bfloat16 [1024, 16, 1024], P('context', 'fsdp')
- stream_grad: float32 [1024, 16, 1024], P('context', 'fsdp')
- grad_query_weight: float32 [1024, 1024], P(('fsdp', 'context'), 'tensor')
- grad_query_bias: float32 [1024], P('tensor')
- grad_key_weight: float32 [1024, 1024], P(('fsdp', 'context'), 'tensor')
- grad_value_weight: float32 [1024, 1024], P(('fsdp', 'context'), 'tensor')
- grad_value_bias: float32 [1024], P('tensor')
- grad_output_weight: float32 [1024, 1024], P('tensor', ('fsdp', 'context'))
- grad_output_bias: float32 [1024], P(('fsdp', 'context'))
- grad_first_gain: float32 [1024], P(('fsdp', 'context'))
- grad_first_shift: float32 [1024], P(('fsdp', 'context'))
- grad_inner_weight: float32 [1024, 4096], P(('fsdp', 'context'), 'tensor')
- grad_inner_bias: float32 [4096], P('tensor')
- grad_outer_weight: float32 [4096, 1024], P('tensor', ('fsdp', 'context'))
- grad_outer_bias: float32 [1024], P(('fsdp', 'context'))
- grad_second_gain: float32 [1024], P(('fsdp', 'context'))
- grad_second_shift: float32 [1024], P(('fsdp', 'context'))
- root_squares: float32 [2, 3], replicated
The draws below stay inside these ranges and needn't reach their ends.
Inputs may be any that keep to these rules, and one draw needn't show every extreme that they name: `lengths`: among the 2 sequences of each index of fsdp, one, drawn from the seed, has more than 896 valid slots.
All inputs are finite; a program needn't handle non-finite values.
Results may differ from the reference program's by a relative error of at most 0.03.
Values may be sent and summed in bfloat16 or wider, within the bound.
A program may use at most 192 MiB of HBM per device.

```python
import math
import jax
import jax.numpy as jnp
from jax import lax

D = 1024
HEADS = 16
HEAD = 64
FF = 4096
LENGTH = 1024
LAYERS = 2
SEQS_DEV = 2
SEQS = 16
SLOTS = 128


def draw_lengths(key, part):
    key = jax.random.fold_in(key, 7)
    first_key, second_key, third_key = jax.random.split(key, 3)
    groups = SEQS // SEQS_DEV
    common = jax.random.randint(first_key, (groups, SEQS_DEV), LENGTH // 4, LENGTH + 1)
    reaching = jax.random.randint(second_key, (groups, SEQS_DEV), LENGTH - SLOTS + 1, LENGTH + 1)
    picked = jax.random.randint(third_key, (groups, 1), 0, SEQS_DEV)
    chosen = jnp.arange(SEQS_DEV, dtype=jnp.int32)[None, :] == picked
    return jnp.where(chosen, reaching, common).reshape(SEQS).astype(jnp.int32)


def block_levels(own_key, extent, pieces, smallest, high):
    factor_of, own = 1.0, jax.random.fold_in(own_key, 6)
    for position, parts in pieces:
        draws = jnp.exp(jax.random.uniform(jax.random.fold_in(own, position), (parts,), jnp.float32, smallest / len(pieces), high / len(pieces)))
        factor_of = factor_of * jnp.repeat(draws, extent[position] // parts).reshape([-1 if axis == position else 1 for axis in range(len(extent))])
    return factor_of


def normal_values(stream_key, dims, scale, bound, cuts=(), kind=jnp.bfloat16):
    gain = block_levels(stream_key, dims, cuts, -0.22, 0.18) if cuts else 1.0
    entries = jax.random.normal(stream_key, dims, jnp.float32) * scale * gain
    return jnp.minimum(jnp.maximum(entries, -bound), bound).astype(kind)


def setup_inputs(seed: int = 0) -> dict:
    splits = jax.random.split(jax.random.key(seed), 19)
    return {
        "stream": normal_values(splits[0], (LENGTH, SEQS, D), 1.0, 6.0, ((0, 8), (1, 8))),
        "lengths": draw_lengths(jax.random.fold_in(splits[18], 71), 0),
        "query_weight": normal_values(splits[2], (D, D), D ** -0.5, 0.1875, ((0, 64), (1, 2))),
        "query_bias": normal_values(splits[3], (D,), 0.3, 1.75, ((0, 2),)),
        "key_weight": normal_values(splits[4], (D, D), D ** -0.5, 0.1875, ((0, 64), (1, 2))),
        "value_weight": normal_values(splits[5], (D, D), D ** -0.5, 0.1875, ((0, 64), (1, 2))),
        "value_bias": normal_values(splits[6], (D,), 0.03, 0.1875, ((0, 2),)),
        "output_weight": normal_values(splits[7], (D, D), (max(D // 256, 4)) ** -0.5, 3.0, ((0, 2), (1, 64))),
        "output_bias": normal_values(splits[8], (D,), 0.3, 1.75, ((0, 64),)),
        "first_gain": jnp.clip(1.0 + 0.1 * jax.random.normal(splits[9], (D,), jnp.float32), 0.5, 1.5).astype(jnp.bfloat16),
        "first_shift": normal_values(splits[10], (D,), 0.3, 1.75, ((0, 64),)),
        "inner_weight": normal_values(splits[11], (D, FF), D ** -0.5, 0.1875, ((0, 64), (1, 2))),
        "inner_bias": normal_values(splits[12], (FF,), 0.3, 1.75, ((0, 2),)),
        "outer_weight": normal_values(splits[13], (FF, D), FF ** -0.5, 0.09375, ((0, 2), (1, 64))),
        "outer_bias": normal_values(splits[14], (D,), 0.3, 1.75, ((0, 64),)),
        "second_gain": jnp.clip(1.0 + 0.1 * jax.random.normal(splits[15], (D,), jnp.float32), 0.5, 1.5).astype(jnp.bfloat16),
        "second_shift": normal_values(splits[16], (D,), 0.3, 1.75, ((0, 64),)),
        "cotangent": normal_values(splits[17], (LENGTH, SEQS, D), 1.0, 6.0, ((0, 8), (1, 8))),
    }


@jax.custom_vjp
def low(v):
    return lax.optimization_barrier(v.astype(jnp.bfloat16)).astype(jnp.float32)

@jax.custom_vjp
def low_back(v):
    return v

def low_keep(v):
    return (low(v), None)

def low_pass(kept, grad):
    return (grad,)

def back_keep(v):
    return (v, None)

def back_low(kept, grad):
    return (low(grad),)
low.defvjp(low_keep, low_pass)
low_back.defvjp(back_keep, back_low)

def round_both(value_in):
    return low(low_back(value_in))

def product(left, right):
    return jnp.dot(left, right, precision=lax.Precision.HIGHEST, preferred_element_type=jnp.float32)

def gelu_tanh(argument):
    return 0.5 * argument * (1.0 + jnp.tanh(0.7978845608028654 * (argument + 0.044715 * argument * argument * argument)))

def normalize(hidden, gain_vector, shift_term):
    centre = hidden - lax.optimization_barrier(jnp.mean(hidden, -1, keepdims=True))
    inverse = lax.rsqrt(lax.optimization_barrier(jnp.mean(centre * centre, -1, keepdims=True)) + 1e-05)
    return centre * inverse * gain_vector + shift_term

def attend(inputs):
    queries, keys, values, length = inputs
    scale_factor = 1.0 / math.sqrt(HEAD)
    raw = jnp.einsum('qhd,khd->hqk', queries, keys, precision=lax.Precision.HIGHEST)
    key_live = jnp.arange(LENGTH) < length
    scores = low_back(jnp.where(key_live[None, None, :], raw * scale_factor, -1e+30))
    row_top = lax.optimization_barrier(jnp.max(scores, -1, keepdims=True))
    exponent = jnp.exp(scores - row_top)
    attend_soft = exponent / lax.optimization_barrier(jnp.sum(exponent, -1, keepdims=True))
    return jnp.einsum('hqk,khd->qhd', low(attend_soft), values, precision=lax.Precision.HIGHEST)

def split_heads(matrix):
    return matrix.reshape(LENGTH, SEQS, HEADS, HEAD).transpose(1, 0, 2, 3)

def encoder_layer(current, lengths, row_live, query_weight, query_bias, key_weight, value_weight, value_bias, output_weight, output_bias, first_gain, first_shift, inner_weight, inner_bias, outer_weight, outer_bias, second_gain, second_shift):
    flat_in = low(current)
    queries = round_both(product(flat_in, query_weight) + query_bias)
    keys = round_both(product(flat_in, key_weight))
    values = round_both(product(flat_in, value_weight) + value_bias)
    mixed = lax.map(jax.checkpoint(attend), (split_heads(queries), split_heads(keys), split_heads(values), lengths))
    mixed = round_both(mixed.transpose(1, 0, 2, 3).reshape(LENGTH * SEQS, D))
    attn_out = low_back(product(mixed, output_weight) + output_bias)
    middle = normalize(current + attn_out, first_gain, first_shift)
    inner_pre = low_back(product(low(middle), inner_weight) + inner_bias)
    outer_out = low_back(product(low(gelu_tanh(inner_pre)), outer_weight) + outer_bias)
    produced = normalize(middle + outer_out, second_gain, second_shift)
    squares = jnp.stack([jnp.sum(row_live * current * current), jnp.sum(row_live * attn_out * attn_out), jnp.sum(row_live * outer_out * outer_out)])
    return (produced, squares)

def reference(stream, lengths, query_weight, query_bias, key_weight, value_weight, value_bias, output_weight, output_bias, first_gain, first_shift, inner_weight, inner_bias, outer_weight, outer_bias, second_gain, second_shift, cotangent):
    params = (query_weight, query_bias, key_weight, value_weight, value_bias, output_weight, output_bias, first_gain, first_shift, inner_weight, inner_bias, outer_weight, outer_bias, second_gain, second_shift)
    params = tuple((member.astype(jnp.float32) for member in params))
    row_live = (jnp.arange(LENGTH)[:, None] < lengths[None, :]).astype(jnp.float32).reshape(LENGTH * SEQS, 1)

    def forward(start, *weights):
        current = start.reshape(LENGTH * SEQS, D)
        squares_all = []
        for repeat in range(LAYERS):
            current, squares = encoder_layer(current, lengths, row_live, *weights)
            squares_all.append(squares)
        return ((current * row_live).reshape(LENGTH, SEQS, D), jnp.stack(squares_all))
    result, pullback, squares_all = jax.vjp(forward, stream.astype(jnp.float32), *params, has_aux=True)
    grads = pullback(cotangent.astype(jnp.float32))
    count_total = jnp.sum(lengths.astype(jnp.float32))
    root_values = jnp.sqrt(squares_all / (count_total * D) + 1e-06)
    return (result.astype(jnp.bfloat16), grads[0], grads[1], grads[2], grads[3], grads[4], grads[5], grads[6], grads[7], grads[8], grads[9], grads[10], grads[11], grads[12], grads[13], grads[14], grads[15], root_values)
```

```python
import functools
import math

import jax
import jax.numpy as jnp
from jax import lax
from jax.experimental import pallas as pl
from jax.experimental.pallas import tpu as pltpu
from jax.sharding import PartitionSpec as P

HEAD = 64
LAYERS = 2
MESH = pl.DeviceIdType.MESH
LANES = 128


def place():
    f = lax.axis_index("fsdp"); c = lax.axis_index("context"); t = lax.axis_index("tensor")
    return {"x": 2*(f//4)+c//4, "y": c%4, "z": f%4, "t": t}

def device(at):
    x = at["x"]
    return ((x//2)*4+at["z"], (x%2)*4+at["y"], at["t"])

def shifted(at, axis, step):
    moved = dict(at); moved[axis] = lax.rem(at[axis]+step+4, 4)
    return moved

def greet(at, steps):
    barrier = pltpu.get_barrier_semaphore()
    for axis in "xyz":
        for step in steps:
            pl.semaphore_signal(barrier, inc=1, device_id=device(shifted(at,axis,step)), device_id_type=MESH)
    pl.semaphore_wait(barrier, 3*len(steps))

ORDERS = ("zyx","yxz","xzy")

def view(ref, at, whole, cols):
    x = at["x"]
    xh = slice(None) if "x" in whole else x//2
    xl = slice(None) if "x" in whole else x%2
    z = slice(None) if "z" in whole else at["z"]
    y = slice(None) if "y" in whole else at["y"]
    return ref.at[xh, z, xl, y, :, pl.ds(cols[0], cols[1])]

def parts_of(width):
    tiles = width//LANES
    cuts = [tiles*i//6*LANES for i in range(7)]
    return [((cuts[2*i], cuts[2*i+1]-cuts[2*i]), (cuts[2*i+1], cuts[2*i+2]-cuts[2*i+1])) for i in range(3)]

def gather_kernel(own_ref, all_ref, own_sem, send_sem, recv_sem):
    at = place()
    width = own_ref.shape[-1]
    parts = parts_of(width)
    x=at["x"]
    mine = pltpu.make_async_copy(own_ref, all_ref.at[x//2, at["z"], x%2, at["y"]], own_sem)
    mine.start()
    greet(at, (1,-1))
    mine.wait()

    def send(part, phase, kind, whole, origin, cols, axis, step):
        block = view(all_ref, origin, whole, cols)
        return pltpu.make_async_remote_copy(src_ref=block, dst_ref=block, send_sem=send_sem.at[part,phase,kind], recv_sem=recv_sem.at[part,phase,kind], device_id=device(shifted(at,axis,step)), device_id_type=MESH)

    for phase in range(3):
        first=[]; second=[]
        for part,(order) in enumerate(ORDERS):
            axis=order[phase]; whole=order[:phase]
            lo,hi=parts[part]; both=(lo[0],lo[1]+hi[1])
            r=send(part,phase,0,whole,at,both,axis,1); l=send(part,phase,1,whole,at,both,axis,-1)
            r.start(); l.start(); first.append((r,l))
        for part,(order) in enumerate(ORDERS):
            axis=order[phase]; whole=order[:phase]
            lo,hi=parts[part]
            r,l=first[part]
            r.wait_recv()
            fr=send(part,phase,2,whole,shifted(at,axis,-1),lo,axis,1); fr.start()
            l.wait_recv()
            fl=send(part,phase,3,whole,shifted(at,axis,1),hi,axis,-1); fl.start()
            second.append((fr,fl))
        for part in range(3):
            for c in second[part]: c.wait_recv()
        for part in range(3):
            for c in first[part]+second[part]: c.wait_send()

def gather_all(own):
    rows,width=own.shape
    out=pl.pallas_call(gather_kernel,
        out_shape=jax.ShapeDtypeStruct((2,4,2,4,rows,width), own.dtype),
        in_specs=[pl.BlockSpec(memory_space=pl.ANY)], out_specs=pl.BlockSpec(memory_space=pl.ANY),
        scratch_shapes=[pltpu.SemaphoreType.DMA, pltpu.SemaphoreType.DMA((3,3,4)), pltpu.SemaphoreType.DMA((3,3,4))],
        compiler_params=pltpu.CompilerParams(collective_id=1, has_side_effects=True),
        name="gather_weights")(own)
    return out

def scatter_kernel(all_ref, small_ref, own_ref, total_ref, work, small_land, load_sem, send_sem, recv_sem, small_send, small_recv, *landings):
    at = place()
    parts = parts_of(all_ref.shape[-1])
    loads=[]
    for part in range(3):
        lo,hi=parts[part]; both=pl.ds(lo[0],lo[1]+hi[1])
        cp=pltpu.make_async_copy(all_ref.at[:,:,:,:,:,both], work.at[:,:,:,:,:,both], load_sem.at[part]); cp.start(); loads.append(cp)
    greet(at, (1,2,3))
    for cp in loads: cp.wait()

    def push(part,phase,kind,origin,whole,cols,axis,step):
        land=landings[phase*3+part]
        src=view(work,origin,whole,cols)
        return pltpu.make_async_remote_copy(src_ref=src,dst_ref=land.at[kind] if cols[1]==land.shape[-1] else land.at[kind,...,pl.ds(0,cols[1])],send_sem=send_sem.at[part,phase,kind],recv_sem=recv_sem.at[part,phase,kind],device_id=device(shifted(at,axis,step)),device_id_type=MESH)

    def add(origin,whole,cols,land_list):
        x=origin["x"]
        xs=[(a,b) for a in range(2) for b in range(2)] if "x" in whole else [(x//2,x%2)]
        zs=list(range(4)) if "z" in whole else [origin["z"]]
        ys=list(range(4)) if "y" in whole else [origin["y"]]
        sx="x" in whole; sz="z" in whole; sy="y" in whole
        def one(ix,iz,iy):
            xh,xl=(ix//2,ix%2) if sx else (x//2,x%2)
            z=iz if sz else origin["z"]; y=iy if sy else origin["y"]
            index=(xh,z,xl,y,slice(None),pl.ds(cols[0],cols[1]))
            total=work[index].astype(jnp.float32)
            for land,kind in land_list:
                li=(kind,)
                if sx: li+=(xh,)
                if sz: li+=(z,)
                if sx: li+=(xl,)
                if sy: li+=(y,)
                li+=(slice(None),pl.ds(0,cols[1]))
                total=total+land[li].astype(jnp.float32)
            work[index]=total.astype(work.dtype)
        nx=4 if sx else 1; nz=4 if sz else 1; ny=4 if sy else 1
        n=nx*nz*ny
        def body(i,_):
            one(i//(nz*ny), (i//ny)%nz, i%ny); return 0
        if n==1: one(0,0,0)
        else: lax.fori_loop(0,n,body,0)

    total_ref[...]=small_ref[...]
    for phase in range(3):
        early=[]
        small=[]
        for step in (1,2,3):
            cp=pltpu.make_async_remote_copy(src_ref=total_ref,dst_ref=small_land.at[phase,step-1],send_sem=small_send.at[phase,step-1],recv_sem=small_recv.at[phase,step-1],device_id=device(shifted(at,"xyz"[phase],step)),device_id_type=MESH)
            cp.start(); small.append(cp)
        for part in range(3):
            order=ORDERS[part][::-1]; axis=order[phase]; whole=order[phase+1:]
            lo,hi=parts[part]
            far=shifted(at,axis,2); up=shifted(at,axis,1); down=shifted(at,axis,-1)
            a=push(part,phase,0,far,whole,lo,axis,1); a.start()
            b=push(part,phase,1,far,whole,hi,axis,-1); b.start()
            c=push(part,phase,2,up,whole,hi,axis,1); c.start()
            d=push(part,phase,3,down,whole,lo,axis,-1); d.start()
            early.append((a,b,c,d))
        late=[]
        for part in range(3):
            order=ORDERS[part][::-1]; axis=order[phase]; whole=order[phase+1:]
            lo,hi=parts[part]; land=landings[phase*3+part]
            up=shifted(at,axis,1); down=shifted(at,axis,-1)
            a,b,c,d=early[part]
            a.wait_recv(); add(up,whole,lo,[(land,0)])
            e=push(part,phase,4,up,whole,lo,axis,1); e.start()
            b.wait_recv(); add(down,whole,hi,[(land,1)])
            f=push(part,phase,5,down,whole,hi,axis,-1); f.start()
            late.append((e,f))
        for part in range(3):
            order=ORDERS[part][::-1]; axis=order[phase]; whole=order[phase+1:]
            lo,hi=parts[part]; land=landings[phase*3+part]
            a,b,c,d=early[part]; e,f=late[part]
            c.wait_recv(); f.wait_recv()
            add(at,whole,hi,[(land,2),(land,5)])
            d.wait_recv(); e.wait_recv()
            add(at,whole,lo,[(land,3),(land,4)])
        for part in range(3):
            for cp in early[part]+late[part]: cp.wait_send()
        for cp in small: cp.wait_recv()
        for cp in small: cp.wait_send()
        total_ref[...]=total_ref[...]+small_land[phase,0]+small_land[phase,1]+small_land[phase,2]
    x=at["x"]
    own_ref[...]=work[x//2,at["z"],x%2,at["y"]].astype(jnp.float32)

def scatter_all(whole, small):
    rows,width=whole.shape[-2:]
    parts=parts_of(width)
    landings=[]
    for phase in range(3):
        for part in range(3):
            order=ORDERS[part][::-1]; w=order[phase+1:]
            shape=[6]
            if "x" in w: shape.append(2)
            if "z" in w: shape.append(4)
            if "x" in w: shape.append(2)
            if "y" in w: shape.append(4)
            shape+= [rows, max(parts[part][0][1],parts[part][1][1])]
            landings.append(pltpu.VMEM(tuple(shape), whole.dtype))
    return pl.pallas_call(scatter_kernel,
        out_shape=(jax.ShapeDtypeStruct((rows,width), jnp.float32),jax.ShapeDtypeStruct(small.shape, jnp.float32)),
        in_specs=[pl.BlockSpec(memory_space=pl.ANY),pl.BlockSpec(memory_space=pltpu.VMEM)], out_specs=(pl.BlockSpec(memory_space=pltpu.VMEM),pl.BlockSpec(memory_space=pltpu.VMEM)),
        scratch_shapes=[pltpu.VMEM(whole.shape, whole.dtype), pltpu.VMEM((3,3)+small.shape,jnp.float32), pltpu.SemaphoreType.DMA((3,)), pltpu.SemaphoreType.DMA((3,3,6)), pltpu.SemaphoreType.DMA((3,3,6)), pltpu.SemaphoreType.DMA((3,3)), pltpu.SemaphoreType.DMA((3,3))]+landings,
        compiler_params=pltpu.CompilerParams(collective_id=2, has_side_effects=True, vmem_limit_bytes=60*2**20),
        name="scatter_grads")(whole, small)


def gelu_tanh(argument):
    return (
        0.5
        * argument
        * (
            1.0
            + jnp.tanh(0.7978845608028654 * (argument + 0.044715 * argument * argument * argument))
        )
    )


def normalize(hidden, gain_vector, shift_term):
    centre = hidden - jnp.mean(hidden, -1, keepdims=True)
    inverse = lax.rsqrt(jnp.mean(centre * centre, -1, keepdims=True) + 1e-05)
    normed = centre * inverse
    return (normed * gain_vector + shift_term, normed, inverse)


def normalize_back(grad_out, normed, inverse, gain_vector):
    scaled = grad_out * gain_vector
    return inverse * (
        scaled
        - jnp.mean(scaled, -1, keepdims=True)
        - normed * jnp.mean(scaled * normed, -1, keepdims=True)
    )


def body(
    stream,
    lengths,
    query_weight,
    query_bias,
    key_weight,
    value_weight,
    value_bias,
    output_weight,
    output_bias,
    first_gain,
    first_shift,
    inner_weight,
    inner_bias,
    outer_weight,
    outer_bias,
    second_gain,
    second_shift,
    cotangent,
):
    slot_count, seq_count, model_width = stream.shape
    row_count = slot_count * seq_count
    heads_here = query_weight.shape[1] // HEAD
    scale_factor = 1.0 / math.sqrt(HEAD)
    position = lax.axis_index("context") * slot_count + jnp.arange(slot_count, dtype=jnp.int32)
    row_live = (position[:, None] < lengths[None, :]).astype(jnp.float32).reshape(row_count, 1)

    extras = jnp.stack(
        [output_bias, outer_bias, first_gain, first_shift, second_gain, second_shift], 1
    )
    packed = jnp.concatenate(
        [
            query_weight,
            key_weight,
            value_weight,
            output_weight.T,
            inner_weight,
            outer_weight.T,
            jnp.pad(extras, ((0, 0), (0, LANES - 6))),
        ],
        1,
    )
    gathered = gather_all(packed).reshape(model_width, packed.shape[1])
    vectors = gathered[:, 6144:6150].T

    def fetch_weights():
        return (
            gathered[:, 0:512],
            gathered[:, 512:1024],
            gathered[:, 1024:1536],
            gathered[:, 1536:2048].T,
            gathered[:, 2048:4096],
            gathered[:, 4096:6144].T,
            vectors[0],
            vectors[1],
            vectors[2],
            vectors[3],
            vectors[4],
            vectors[5],
        )

    def join_partial(partial_value):
        return lax.psum(partial_value.astype(jnp.bfloat16), "tensor").astype(jnp.float32)

    def join_back(partial_value):
        return lax.psum(partial_value.astype(jnp.bfloat16), "tensor").astype(jnp.float32)

    def score_block(queries, keys_all):
        key_live = jnp.arange(keys_all.shape[0], dtype=jnp.int32)[None, :] < lengths[:, None]
        raw = jnp.einsum("rshd,kshd->shrk", queries, keys_all, preferred_element_type=jnp.float32)
        return jnp.where(key_live[:, None, None, :], raw * scale_factor, -1e30)

    def head_split(matrix):
        return matrix.reshape(slot_count, seq_count, heads_here, HEAD)

    def backward_attn(grad_middle, stored, weights, grad_sums):
        (
            query_full,
            key_full,
            value_full,
            output_full,
            inner_full,
            outer_full,
            bias_output,
            bias_outer,
            gain_first,
            shift_first,
            gain_second,
            shift_second,
        ) = weights
        (
            flat_in,
            queries,
            keys_all,
            values_all,
            log_total,
            mixed,
            normed_first,
            inverse_first,
            middle_low,
            inner_pre,
            normed_second,
            inverse_second,
        ) = stored
        grad_sums = list(grad_sums)
        grad_sums[8] = grad_sums[8] + jnp.sum(grad_middle * normed_first, 0)
        grad_sums[9] = grad_sums[9] + jnp.sum(grad_middle, 0)
        grad_first = normalize_back(grad_middle, normed_first, inverse_first, gain_first)
        grad_attn = grad_first.astype(jnp.bfloat16)
        grad_sums[6] = grad_sums[6] + jnp.sum(grad_attn.astype(jnp.float32), 0)
        grad_sums[3] = grad_sums[3] + jnp.einsum(
            "nc,nd->cd", mixed, grad_attn, preferred_element_type=jnp.float32
        )
        grad_mixed = head_split(
            jnp.einsum(
                "nd,cd->nc", grad_attn, output_full, preferred_element_type=jnp.float32
            ).astype(jnp.bfloat16)
        )
        attend_soft = jnp.exp(score_block(queries, keys_all) - log_total)
        grad_soft = jnp.einsum(
            "rshd,kshd->shrk", grad_mixed, values_all, preferred_element_type=jnp.float32
        )
        grad_values_all = jnp.einsum(
            "shrk,rshd->kshd",
            attend_soft.astype(jnp.bfloat16),
            grad_mixed,
            preferred_element_type=jnp.float32,
        )
        inner_prod = jnp.sum(grad_soft * attend_soft, -1, keepdims=True)
        grad_scores = (attend_soft * (grad_soft - inner_prod)).astype(jnp.bfloat16)
        grad_queries = (
            jnp.einsum("shrk,kshd->rshd", grad_scores, keys_all, preferred_element_type=jnp.float32)
            * scale_factor
        )
        grad_queries = grad_queries.astype(jnp.bfloat16).reshape(row_count, heads_here * HEAD)
        grad_keys_all = (
            jnp.einsum("shrk,rshd->kshd", grad_scores, queries, preferred_element_type=jnp.float32)
            * scale_factor
        )
        grad_keys, grad_values = (
            lax.psum_scatter(
                grad_keys_all.astype(jnp.bfloat16), "context", scatter_dimension=0, tiled=True
            ).astype(jnp.float32),
            lax.psum_scatter(
                grad_values_all.astype(jnp.bfloat16), "context", scatter_dimension=0, tiled=True
            ).astype(jnp.float32),
        )
        grad_keys = grad_keys.astype(jnp.bfloat16).reshape(row_count, heads_here * HEAD)
        grad_values = grad_values.astype(jnp.bfloat16).reshape(row_count, heads_here * HEAD)
        grad_sums[12] = grad_sums[12] + jnp.sum(grad_queries.astype(jnp.float32), 0)
        grad_sums[13] = grad_sums[13] + jnp.sum(grad_values.astype(jnp.float32), 0)
        grad_sums[0] = grad_sums[0] + jnp.einsum(
            "nd,nc->dc", flat_in, grad_queries, preferred_element_type=jnp.float32
        )
        grad_sums[1] = grad_sums[1] + jnp.einsum(
            "nd,nc->dc", flat_in, grad_keys, preferred_element_type=jnp.float32
        )
        grad_sums[2] = grad_sums[2] + jnp.einsum(
            "nd,nc->dc", flat_in, grad_values, preferred_element_type=jnp.float32
        )
        partial_value = jnp.einsum(
            "nc,dc->nd", grad_queries, query_full, preferred_element_type=jnp.float32
        )
        partial_value = partial_value + jnp.einsum(
            "nc,dc->nd", grad_keys, key_full, preferred_element_type=jnp.float32
        )
        partial_value = partial_value + jnp.einsum(
            "nc,dc->nd", grad_values, value_full, preferred_element_type=jnp.float32
        )
        return (grad_first + join_back(partial_value), grad_sums)

    current = stream.reshape(row_count, model_width).astype(jnp.float32)
    stored_all = []
    squares_all = []
    for repeat in range(LAYERS):
        weights = fetch_weights()
        (
            forward_query_full,
            forward_key_full,
            forward_value_full,
            forward_output_full,
            forward_inner_full,
            forward_outer_full,
            forward_bias_output,
            forward_bias_outer,
            forward_gain_first,
            forward_shift_first,
            forward_gain_second,
            forward_shift_second,
        ) = weights
        forward_flat_in = current.astype(jnp.bfloat16)
        forward_queries = head_split(
            (
                jnp.dot(forward_flat_in, forward_query_full, preferred_element_type=jnp.float32)
                + query_bias
            ).astype(jnp.bfloat16)
        )
        keys_here = head_split(
            jnp.dot(forward_flat_in, forward_key_full, preferred_element_type=jnp.float32).astype(
                jnp.bfloat16
            )
        )
        values_here = head_split(
            (
                jnp.dot(forward_flat_in, forward_value_full, preferred_element_type=jnp.float32)
                + value_bias
            ).astype(jnp.bfloat16)
        )
        forward_keys_all = lax.all_gather(keys_here, "context", axis=0, tiled=True)
        forward_values_all = lax.all_gather(values_here, "context", axis=0, tiled=True)
        scores = score_block(forward_queries, forward_keys_all)
        row_top = jnp.max(scores, -1, keepdims=True)
        exponent = jnp.exp(scores - row_top)
        row_total = jnp.sum(exponent, -1, keepdims=True)
        forward_attend_soft = (exponent / row_total).astype(jnp.bfloat16)
        forward_log_total = row_top + jnp.log(row_total)
        forward_mixed = jnp.einsum(
            "shrk,kshd->rshd",
            forward_attend_soft,
            forward_values_all,
            preferred_element_type=jnp.float32,
        )
        forward_mixed = forward_mixed.astype(jnp.bfloat16).reshape(row_count, heads_here * HEAD)
        attn_out = (
            join_partial(
                jnp.dot(forward_mixed, forward_output_full, preferred_element_type=jnp.float32)
            )
            + forward_bias_output
        )
        middle, forward_normed_first, forward_inverse_first = normalize(
            current + attn_out, forward_gain_first, forward_shift_first
        )
        forward_middle_low = middle.astype(jnp.bfloat16)
        forward_inner_pre = (
            jnp.dot(forward_middle_low, forward_inner_full, preferred_element_type=jnp.float32)
            + inner_bias
        )
        forward_inner_act = gelu_tanh(forward_inner_pre).astype(jnp.bfloat16)
        outer_out = (
            join_partial(
                jnp.dot(forward_inner_act, forward_outer_full, preferred_element_type=jnp.float32)
            )
            + forward_bias_outer
        )
        produced, forward_normed_second, forward_inverse_second = normalize(
            middle + outer_out, forward_gain_second, forward_shift_second
        )
        squares = jnp.stack(
            [
                jnp.sum(row_live * current * current),
                jnp.sum(row_live * attn_out * attn_out),
                jnp.sum(row_live * outer_out * outer_out),
            ]
        )
        forward_stored = (
            forward_flat_in,
            forward_queries,
            forward_keys_all,
            forward_values_all,
            forward_log_total,
            forward_mixed,
            forward_normed_first,
            forward_inverse_first,
            forward_middle_low,
            forward_inner_pre,
            forward_normed_second,
            forward_inverse_second,
        )
        current, stored, squares = (produced, forward_stored, squares)
        stored_all.append(stored)
        squares_all.append(squares)
    result = (current * row_live).astype(jnp.bfloat16).reshape(slot_count, seq_count, model_width)
    grad_next = cotangent.reshape(row_count, model_width).astype(jnp.float32) * row_live
    grad_sums = [jnp.zeros(member.shape, jnp.float32) for member in weights]
    grad_sums = grad_sums + [
        jnp.zeros(query_bias.shape, jnp.float32),
        jnp.zeros(value_bias.shape, jnp.float32),
        jnp.zeros(inner_bias.shape, jnp.float32),
    ]
    shared = [None] * 12
    for repeat in reversed(range(LAYERS)):
        weights = fetch_weights()
        backward_grad_sums = grad_sums
        (
            backward_query_full,
            backward_key_full,
            backward_value_full,
            backward_output_full,
            backward_inner_full,
            backward_outer_full,
            backward_bias_output,
            backward_bias_outer,
            backward_gain_first,
            backward_shift_first,
            backward_gain_second,
            backward_shift_second,
        ) = weights
        (
            backward_flat_in,
            backward_queries,
            backward_keys_all,
            backward_values_all,
            backward_log_total,
            backward_mixed,
            backward_normed_first,
            backward_inverse_first,
            backward_middle_low,
            backward_inner_pre,
            backward_normed_second,
            backward_inverse_second,
        ) = stored_all[repeat]
        backward_grad_sums = list(backward_grad_sums)
        backward_grad_sums[10] = backward_grad_sums[10] + jnp.sum(
            grad_next * backward_normed_second, 0
        )
        backward_grad_sums[11] = backward_grad_sums[11] + jnp.sum(grad_next, 0)
        grad_second = normalize_back(
            grad_next, backward_normed_second, backward_inverse_second, backward_gain_second
        )
        grad_outer = grad_second.astype(jnp.bfloat16)
        backward_grad_sums[7] = backward_grad_sums[7] + jnp.sum(grad_outer.astype(jnp.float32), 0)
        inner_act = gelu_tanh(backward_inner_pre).astype(jnp.bfloat16)
        backward_grad_sums[5] = backward_grad_sums[5] + jnp.einsum(
            "nf,nd->fd", inner_act, grad_outer, preferred_element_type=jnp.float32
        )
        grad_act = jnp.einsum(
            "nd,fd->nf", grad_outer, backward_outer_full, preferred_element_type=jnp.float32
        )
        unused_value, gelu_pull = jax.vjp(gelu_tanh, backward_inner_pre)
        grad_inner = gelu_pull(grad_act)[0].astype(jnp.bfloat16)
        backward_grad_sums[14] = backward_grad_sums[14] + jnp.sum(grad_inner.astype(jnp.float32), 0)
        backward_grad_sums[4] = backward_grad_sums[4] + jnp.einsum(
            "nd,nf->df", backward_middle_low, grad_inner, preferred_element_type=jnp.float32
        )
        backward_grad_middle = grad_second + join_back(
            jnp.einsum(
                "nf,df->nd", grad_inner, backward_inner_full, preferred_element_type=jnp.float32
            )
        )
        grad_middle = backward_grad_middle
        grad_sums = backward_grad_sums
        grad_next, grad_sums = backward_attn(grad_middle, stored_all[repeat], weights, grad_sums)
    grad_extras = jnp.stack(grad_sums[6:12], 1)
    grads = jnp.concatenate(
        [
            grad_sums[0],
            grad_sums[1],
            grad_sums[2],
            grad_sums[3].T,
            grad_sums[4],
            grad_sums[5].T,
            jnp.pad(grad_extras, ((0, 0), (0, LANES - 6))),
        ],
        1,
    ).astype(jnp.bfloat16)
    counted = jnp.sum(row_live)
    small = jnp.concatenate(
        [
            grad_sums[12],
            grad_sums[13],
            grad_sums[14],
            jnp.stack(squares_all).reshape(-1),
            counted[None],
            jnp.zeros((1024 - 7,), jnp.float32),
        ]
    ).reshape(32, LANES)
    summed, total = scatter_all(grads.reshape(2, 4, 2, 4, 16, grads.shape[1]), small)
    total = total.reshape(-1)
    bias_query, bias_value, bias_inner = total[0:512], total[512:1024], total[1024:3072]
    square_total, count_total = total[3072:3078].reshape(LAYERS, 3), total[3078]
    shared = (
        summed[:, 0:512],
        summed[:, 512:1024],
        summed[:, 1024:1536],
        summed[:, 1536:2048].T,
        summed[:, 2048:4096],
        summed[:, 4096:6144].T,
    ) + tuple(summed[:, 6144 + place_at] for place_at in range(6))
    root_values = jnp.sqrt(square_total / (count_total * model_width) + 1e-06)
    stream_grad = grad_next.reshape(slot_count, seq_count, model_width)
    return (
        result,
        stream_grad,
        shared[0],
        bias_query,
        shared[1],
        shared[2],
        bias_value,
        shared[3],
        shared[6],
        shared[8],
        shared[9],
        shared[4],
        bias_inner,
        shared[5],
        shared[7],
        shared[10],
        shared[11],
        root_values,
    )


def solution(mesh):
    in_specs = (
        P("context", "fsdp", None),
        P("fsdp"),
        P(("fsdp", "context"), "tensor"),
        P("tensor"),
        P(("fsdp", "context"), "tensor"),
        P(("fsdp", "context"), "tensor"),
        P("tensor"),
        P("tensor", ("fsdp", "context")),
        P(("fsdp", "context")),
        P(("fsdp", "context")),
        P(("fsdp", "context")),
        P(("fsdp", "context"), "tensor"),
        P("tensor"),
        P("tensor", ("fsdp", "context")),
        P(("fsdp", "context")),
        P(("fsdp", "context")),
        P(("fsdp", "context")),
        P("context", "fsdp", None),
    )
    out_specs = (
        P("context", "fsdp", None),
        P("context", "fsdp", None),
        P(("fsdp", "context"), "tensor"),
        P("tensor"),
        P(("fsdp", "context"), "tensor"),
        P(("fsdp", "context"), "tensor"),
        P("tensor"),
        P("tensor", ("fsdp", "context")),
        P(("fsdp", "context")),
        P(("fsdp", "context")),
        P(("fsdp", "context")),
        P(("fsdp", "context"), "tensor"),
        P("tensor"),
        P("tensor", ("fsdp", "context")),
        P(("fsdp", "context")),
        P(("fsdp", "context")),
        P(("fsdp", "context")),
        P(),
    )
    return jax.shard_map(body, mesh=mesh, in_specs=in_specs, out_specs=out_specs, check_vma=False)
```

```python
import jax
import jax.numpy as jnp
from jax import lax
from jax.experimental import pallas as pl
from jax.experimental.pallas import tpu as pltpu
from jax.sharding import PartitionSpec as P

HEAD = 64
LAYERS = 2
LANES = 128
MESH = pl.DeviceIdType.MESH


def place():
    f = lax.axis_index("fsdp"); c = lax.axis_index("context"); t = lax.axis_index("tensor")
    return {"x": 2*(f//4)+c//4, "y": c%4, "z": f%4, "t": t}

def device(at):
    x = at["x"]
    return ((x//2)*4+at["z"], (x%2)*4+at["y"], at["t"])

def shifted(at, axis, step):
    moved = dict(at); moved[axis] = lax.rem(at[axis]+step+4, 4)
    return moved

def greet(at, steps):
    barrier = pltpu.get_barrier_semaphore()
    for axis in "xyz":
        for step in steps:
            pl.semaphore_signal(barrier, inc=1, device_id=device(shifted(at,axis,step)), device_id_type=MESH)
    pl.semaphore_wait(barrier, 3*len(steps))

ORDERS = ("zyx","yxz","xzy")

def view(ref, at, whole, cols):
    x = at["x"]
    xh = slice(None) if "x" in whole else x//2
    xl = slice(None) if "x" in whole else x%2
    z = slice(None) if "z" in whole else at["z"]
    y = slice(None) if "y" in whole else at["y"]
    return ref.at[xh, z, xl, y, :, pl.ds(cols[0], cols[1])]

def parts_of(width):
    tiles = width//LANES
    cuts = [tiles*i//6*LANES for i in range(7)]
    return [((cuts[2*i], cuts[2*i+1]-cuts[2*i]), (cuts[2*i+1], cuts[2*i+2]-cuts[2*i+1])) for i in range(3)]

def gather_kernel(own_ref, all_ref, own_sem, send_sem, recv_sem):
    at = place()
    width = own_ref.shape[-1]
    parts = parts_of(width)
    x=at["x"]
    mine = pltpu.make_async_copy(own_ref, all_ref.at[x//2, at["z"], x%2, at["y"]], own_sem)
    mine.start()
    greet(at, (1,-1))
    mine.wait()

    def send(part, phase, kind, whole, origin, cols, axis, step):
        block = view(all_ref, origin, whole, cols)
        return pltpu.make_async_remote_copy(src_ref=block, dst_ref=block, send_sem=send_sem.at[part,phase,kind], recv_sem=recv_sem.at[part,phase,kind], device_id=device(shifted(at,axis,step)), device_id_type=MESH)

    for phase in range(3):
        first=[]; second=[]
        for part,(order) in enumerate(ORDERS):
            axis=order[phase]; whole=order[:phase]
            lo,hi=parts[part]; both=(lo[0],lo[1]+hi[1])
            r=send(part,phase,0,whole,at,both,axis,1); l=send(part,phase,1,whole,at,both,axis,-1)
            r.start(); l.start(); first.append((r,l))
        for part,(order) in enumerate(ORDERS):
            axis=order[phase]; whole=order[:phase]
            lo,hi=parts[part]
            r,l=first[part]
            r.wait_recv()
            fr=send(part,phase,2,whole,shifted(at,axis,-1),lo,axis,1); fr.start()
            l.wait_recv()
            fl=send(part,phase,3,whole,shifted(at,axis,1),hi,axis,-1); fl.start()
            second.append((fr,fl))
        for part in range(3):
            for c in second[part]: c.wait_recv()
        for part in range(3):
            for c in first[part]+second[part]: c.wait_send()

def gather_all(own):
    rows,width=own.shape
    out=pl.pallas_call(gather_kernel,
        out_shape=jax.ShapeDtypeStruct((2,4,2,4,rows,width), own.dtype),
        in_specs=[pl.BlockSpec(memory_space=pl.ANY)], out_specs=pl.BlockSpec(memory_space=pl.ANY),
        scratch_shapes=[pltpu.SemaphoreType.DMA, pltpu.SemaphoreType.DMA((3,3,4)), pltpu.SemaphoreType.DMA((3,3,4))],
        compiler_params=pltpu.CompilerParams(collective_id=1, has_side_effects=True),
        name="gather_weights")(own)
    return out

def scatter_kernel(all_ref, small_ref, own_ref, total_ref, work, small_land, load_sem, send_sem, recv_sem, small_send, small_recv, *landings):
    at = place()
    parts = parts_of(all_ref.shape[-1])
    loads=[]
    for part in range(3):
        lo,hi=parts[part]; both=pl.ds(lo[0],lo[1]+hi[1])
        cp=pltpu.make_async_copy(all_ref.at[:,:,:,:,:,both], work.at[:,:,:,:,:,both], load_sem.at[part]); cp.start(); loads.append(cp)
    greet(at, (1,2,3))
    for cp in loads: cp.wait()

    def push(part,phase,kind,origin,whole,cols,axis,step):
        land=landings[phase*3+part]
        src=view(work,origin,whole,cols)
        return pltpu.make_async_remote_copy(src_ref=src,dst_ref=land.at[kind] if cols[1]==land.shape[-1] else land.at[kind,...,pl.ds(0,cols[1])],send_sem=send_sem.at[part,phase,kind],recv_sem=recv_sem.at[part,phase,kind],device_id=device(shifted(at,axis,step)),device_id_type=MESH)

    def add(origin,whole,cols,land_list):
        x=origin["x"]
        xs=[(a,b) for a in range(2) for b in range(2)] if "x" in whole else [(x//2,x%2)]
        zs=list(range(4)) if "z" in whole else [origin["z"]]
        ys=list(range(4)) if "y" in whole else [origin["y"]]
        sx="x" in whole; sz="z" in whole; sy="y" in whole
        def one(ix,iz,iy):
            xh,xl=(ix//2,ix%2) if sx else (x//2,x%2)
            z=iz if sz else origin["z"]; y=iy if sy else origin["y"]
            index=(xh,z,xl,y,slice(None),pl.ds(cols[0],cols[1]))
            total=work[index].astype(jnp.float32)
            for land,kind in land_list:
                li=(kind,)
                if sx: li+=(xh,)
                if sz: li+=(z,)
                if sx: li+=(xl,)
                if sy: li+=(y,)
                li+=(slice(None),pl.ds(0,cols[1]))
                total=total+land[li].astype(jnp.float32)
            work[index]=total.astype(work.dtype)
        nx=4 if sx else 1; nz=4 if sz else 1; ny=4 if sy else 1
        n=nx*nz*ny
        def body(i,_):
            one(i//(nz*ny), (i//ny)%nz, i%ny); return 0
        if n==1: one(0,0,0)
        else: lax.fori_loop(0,n,body,0)

    total_ref[...]=small_ref[...]
    for phase in range(3):
        early=[]
        small=[]
        for step in (1,2,3):
            cp=pltpu.make_async_remote_copy(src_ref=total_ref,dst_ref=small_land.at[phase,step-1],send_sem=small_send.at[phase,step-1],recv_sem=small_recv.at[phase,step-1],device_id=device(shifted(at,"xyz"[phase],step)),device_id_type=MESH)
            cp.start(); small.append(cp)
        for part in range(3):
            order=ORDERS[part][::-1]; axis=order[phase]; whole=order[phase+1:]
            lo,hi=parts[part]
            far=shifted(at,axis,2); up=shifted(at,axis,1); down=shifted(at,axis,-1)
            a=push(part,phase,0,far,whole,lo,axis,1); a.start()
            b=push(part,phase,1,far,whole,hi,axis,-1); b.start()
            c=push(part,phase,2,up,whole,hi,axis,1); c.start()
            d=push(part,phase,3,down,whole,lo,axis,-1); d.start()
            early.append((a,b,c,d))
        late=[]
        for part in range(3):
            order=ORDERS[part][::-1]; axis=order[phase]; whole=order[phase+1:]
            lo,hi=parts[part]; land=landings[phase*3+part]
            up=shifted(at,axis,1); down=shifted(at,axis,-1)
            a,b,c,d=early[part]
            a.wait_recv(); add(up,whole,lo,[(land,0)])
            e=push(part,phase,4,up,whole,lo,axis,1); e.start()
            b.wait_recv(); add(down,whole,hi,[(land,1)])
            f=push(part,phase,5,down,whole,hi,axis,-1); f.start()
            late.append((e,f))
        for part in range(3):
            order=ORDERS[part][::-1]; axis=order[phase]; whole=order[phase+1:]
            lo,hi=parts[part]; land=landings[phase*3+part]
            a,b,c,d=early[part]; e,f=late[part]
            c.wait_recv(); f.wait_recv()
            add(at,whole,hi,[(land,2),(land,5)])
            d.wait_recv(); e.wait_recv()
            add(at,whole,lo,[(land,3),(land,4)])
        for part in range(3):
            for cp in early[part]+late[part]: cp.wait_send()
        for cp in small: cp.wait_recv()
        for cp in small: cp.wait_send()
        total_ref[...]=total_ref[...]+small_land[phase,0]+small_land[phase,1]+small_land[phase,2]
    x=at["x"]
    own_ref[...]=work[x//2,at["z"],x%2,at["y"]].astype(jnp.float32)

def scatter_all(whole, small):
    rows,width=whole.shape[-2:]
    parts=parts_of(width)
    landings=[]
    for phase in range(3):
        for part in range(3):
            order=ORDERS[part][::-1]; w=order[phase+1:]
            shape=[6]
            if "x" in w: shape.append(2)
            if "z" in w: shape.append(4)
            if "x" in w: shape.append(2)
            if "y" in w: shape.append(4)
            shape+= [rows, max(parts[part][0][1],parts[part][1][1])]
            landings.append(pltpu.VMEM(tuple(shape), whole.dtype))
    return pl.pallas_call(scatter_kernel,
        out_shape=(jax.ShapeDtypeStruct((rows,width), jnp.float32),jax.ShapeDtypeStruct(small.shape, jnp.float32)),
        in_specs=[pl.BlockSpec(memory_space=pl.ANY),pl.BlockSpec(memory_space=pltpu.VMEM)], out_specs=(pl.BlockSpec(memory_space=pltpu.VMEM),pl.BlockSpec(memory_space=pltpu.VMEM)),
        scratch_shapes=[pltpu.VMEM(whole.shape, whole.dtype), pltpu.VMEM((3,3)+small.shape,jnp.float32), pltpu.SemaphoreType.DMA((3,)), pltpu.SemaphoreType.DMA((3,3,6)), pltpu.SemaphoreType.DMA((3,3,6)), pltpu.SemaphoreType.DMA((3,3)), pltpu.SemaphoreType.DMA((3,3))]+landings,
        compiler_params=pltpu.CompilerParams(collective_id=2, has_side_effects=True, vmem_limit_bytes=60*2**20),
        name="scatter_grads")(whole, small)


F32 = jnp.float32
BF16 = jnp.bfloat16
ROWS = 128
LIMIT = 60 * 2**20


def spec(space):
    return pl.BlockSpec(memory_space=space)


def greet_group(devices):
    barrier = pltpu.get_barrier_semaphore()
    for device_id in devices:
        pl.semaphore_signal(barrier, inc=1, device_id=device_id, device_id_type=MESH)
    pl.semaphore_wait(barrier, len(devices))


def remote(src, dst, send_sem, recv_sem, device_id):
    return pltpu.make_async_remote_copy(
        src_ref=src,
        dst_ref=dst,
        send_sem=send_sem,
        recv_sem=recv_sem,
        device_id=device_id,
        device_id_type=MESH,
    )


def across(left, right):
    return lax.dot_general(left, right, (((1,), (1,)), ((), ())), preferred_element_type=F32)


def straight(left, right):
    return jnp.dot(left, right, preferred_element_type=F32)


def rows_of(block):
    return pl.ds(pl.multiple_of(block * ROWS, ROWS), ROWS)


def by_head(block):
    first = lax.broadcasted_iota(jnp.int32, block.shape, 1) < HEAD
    zero = jnp.zeros_like(block)
    return jnp.concatenate([jnp.where(first, block, zero), jnp.where(first, zero, block)], 0)


def key_mask(length, first, count):
    position = first + lax.broadcasted_iota(jnp.int32, (count, 1), 0)
    return jnp.where(position < length, 0.0, -1e30)


def attend_kernel(
    x_ref, w_ref, query_bias, value_bias, lengths,
    mixed_ref, unit_ref, exact_ref, logs_ref,
    w_buf, own_buf, outcome_ref, w_sem, local_sem, send_sem, recv_sem, back_send, back_recv,
):
    f = lax.axis_index("fsdp")
    c = lax.axis_index("context")
    t = lax.axis_index("tensor")
    loads = []
    for j, column in enumerate((512, 1024, 0)):
        load = pltpu.make_async_copy(w_ref.at[:, pl.ds(column, 512)], w_buf.at[j], w_sem.at[j])
        load.start()
        loads.append(load)
    greet_group([(f, lax.rem(c + d, 8), t) for d in range(1, 8)])

    def part(ref, peer):
        return ref.at[rows_of(peer // 4), rows_of(peer % 4)]

    def push(j, d):
        peer = lax.rem(c + d, 8)
        return remote(
            part(own_buf.at[j], peer), unit_ref.at[j, rows_of(c)],
            send_sem.at[j, d - 1], recv_sem.at[j, d - 1], (f, peer, t),
        )

    locals_here = []
    for j in range(3):
        loads[j].wait()
        product = straight(x_ref[...], w_buf[j])
        if j == 1:
            product = product + value_bias[...]
        if j == 2:
            product = product + query_bias[...]
        own_buf[j] = product.astype(BF16)
        for d in range(1, 8):
            push(j, d).start()
        keep = pltpu.make_async_copy(part(own_buf.at[j], c), unit_ref.at[j, rows_of(c)], local_sem.at[j])
        keep.start()
        locals_here.append(keep)
    for j in range(3):
        locals_here[j].wait()
    for j in range(2):
        for d in range(1, 8):
            push(j, d).wait_recv()
    length = lengths[c // 4]
    mask = key_mask(length, 0, 8 * ROWS)
    keys = unit_ref[0]
    values_across = unit_ref[1].T

    def answer(d):
        peer = lax.rem(c + d, 8)
        return remote(
            outcome_ref.at[rows_of(peer)], part(mixed_ref, c),
            back_send.at[d - 1], back_recv.at[d - 1], (f, peer, t),
        )

    def step(d, carry):
        block = lax.rem(c + d, 8)

        @pl.when(d < 8)
        def _():
            push(2, 8 - d).wait_recv()

        queries = unit_ref[2, rows_of(block), :] * jnp.asarray(0.125, BF16)
        scores = across(keys, by_head(queries)) + mask
        top = jnp.max(scores, 0, keepdims=True)
        exponent = jnp.exp(scores - top)
        total = jnp.sum(exponent, 0, keepdims=True)
        outcome = straight(values_across, exponent.astype(BF16)) / total
        both = jnp.concatenate([outcome[:HEAD, :ROWS], outcome[HEAD:, ROWS:]], 0)
        both = both.T
        exact_ref[rows_of(block), :] = both
        outcome_ref[rows_of(block), :] = both.astype(BF16)
        logs_ref[pl.ds(block, 1), :] = top + jnp.log(total)

        @pl.when(d < 8)
        def _():
            answer(d).start()

        return carry

    lax.fori_loop(1, 9, step, 0)
    keep = pltpu.make_async_copy(outcome_ref.at[rows_of(c)], part(mixed_ref, c), local_sem.at[0])
    keep.start()
    keep.wait()
    for d in range(1, 8):
        answer(d).wait_recv()
    for d in range(1, 8):
        answer(d).wait_send()
        for j in range(3):
            push(j, d).wait_send()


def attend(x_low, gathered, query_bias, value_bias, lengths):
    return pl.pallas_call(
        attend_kernel,
        out_shape=(
            jax.ShapeDtypeStruct((256, 512), BF16),
            jax.ShapeDtypeStruct((3, 1024, LANES), BF16),
            jax.ShapeDtypeStruct((1024, LANES), F32),
            jax.ShapeDtypeStruct((8, 256), F32),
        ),
        in_specs=[spec(pltpu.VMEM), spec(pl.ANY), spec(pltpu.VMEM), spec(pltpu.VMEM), spec(pltpu.SMEM)],
        out_specs=(spec(pltpu.VMEM),) * 4,
        scratch_shapes=[
            pltpu.VMEM((3, 1024, 512), BF16),
            pltpu.VMEM((3, 256, 512), BF16),
            pltpu.VMEM((1024, LANES), BF16),
            pltpu.SemaphoreType.DMA((3,)),
            pltpu.SemaphoreType.DMA((3,)),
            pltpu.SemaphoreType.DMA((3, 7)),
            pltpu.SemaphoreType.DMA((3, 7)),
            pltpu.SemaphoreType.DMA((7,)),
            pltpu.SemaphoreType.DMA((7,)),
        ],
        compiler_params=pltpu.CompilerParams(
            collective_id=3, has_side_effects=True, vmem_limit_bytes=LIMIT
        ),
        name="attend",
    )(x_low, gathered, query_bias, value_bias, lengths)


def gelu_parts(argument):
    square = argument * argument
    inner = 0.7978845608028654 * argument * (1.0 + 0.044715 * square)
    bend = jnp.tanh(inner)
    half = 0.5 * (1.0 + bend)
    slope = half + 0.5 * argument * (1.0 - bend * bend) * 0.7978845608028654 * (
        1.0 + 3.0 * 0.044715 * square
    )
    return argument * half, slope


def norm_parts(hidden):
    centre = hidden - jnp.mean(hidden, -1, keepdims=True)
    inverse = lax.rsqrt(jnp.mean(centre * centre, -1, keepdims=True) + 1e-05)
    return centre * inverse, inverse


def norm_back(grad_out, normed, inverse, gain):
    scaled = grad_out * gain
    return inverse * (
        scaled
        - jnp.mean(scaled, -1, keepdims=True)
        - normed * jnp.mean(scaled * normed, -1, keepdims=True)
    )


def live_rows(lengths):
    c = lax.axis_index("context")
    position = c * ROWS + lax.broadcasted_iota(jnp.int32, (ROWS, 1), 0)
    return [jnp.where(position < lengths[s], 1.0, 0.0) for s in range(2)]


def forward_kernel(
    mixed_ref, x_ref, w_ref, vectors_ref, inner_bias, lengths,
    next_ref, low_ref, normed1_ref, inverse1_ref, middle_ref, act_ref, slope_ref,
    normed2_ref, inverse2_ref, squares_ref,
    out_w, inner_w, outer_w, sent, landed, middle_buf, w_sem, send_sem, recv_sem,
):
    f = lax.axis_index("fsdp")
    c = lax.axis_index("context")
    t = lax.axis_index("tensor")
    partner = (f, c, 1 - t)
    loads = []
    for j, (column, buffer) in enumerate(((1536, out_w), (2048, inner_w), (4096, outer_w))):
        load = pltpu.make_async_copy(
            w_ref.at[:, pl.ds(column, buffer.shape[1])], buffer, w_sem.at[j]
        )
        load.start()
        loads.append(load)
    greet_group([partner])
    live = live_rows(lengths)

    def join(stage, half):
        return remote(
            sent.at[stage, half], landed.at[stage, half],
            send_sem.at[stage, half], recv_sem.at[stage, half], partner,
        )

    def rows(half):
        return pl.ds(half * ROWS, ROWS)

    loads[0].wait()
    for half in range(2):
        sent[0, half] = across(mixed_ref[rows(half), :], out_w[...]).astype(BF16)
        join(0, half).start()
    squares = [0.0, 0.0, 0.0]
    for half in range(2):
        join(0, half).wait_recv()
        x = x_ref[rows(half), :]
        branch = sent[0, half].astype(F32) + landed[0, half].astype(F32) + vectors_ref[0:1, :]
        normed, inverse = norm_parts(x + branch)
        middle = normed * vectors_ref[2:3, :] + vectors_ref[3:4, :]
        normed1_ref[rows(half), :] = normed
        inverse1_ref[rows(half), :] = inverse
        middle_buf[rows(half), :] = middle
        middle_ref[rows(half), :] = middle.astype(BF16)
        squares[0] += jnp.sum(live[half] * x * x, 0, keepdims=True)
        squares[1] += jnp.sum(live[half] * branch * branch, 0, keepdims=True)
    loads[1].wait()

    def inner(tile, carry):
        columns = pl.ds(pl.multiple_of(tile * 512, 512), 512)
        pre = straight(middle_ref[...], inner_w[:, columns]) + inner_bias[:, columns]
        act, slope = gelu_parts(pre)
        act_ref[:, columns] = act.astype(BF16)
        slope_ref[:, columns] = slope.astype(BF16)
        return carry

    lax.fori_loop(0, 4, inner, 0)
    loads[2].wait()
    for half in range(2):
        sent[1, half] = across(act_ref[rows(half), :], outer_w[...]).astype(BF16)
        join(1, half).start()
    for half in range(2):
        join(1, half).wait_recv()
        branch = sent[1, half].astype(F32) + landed[1, half].astype(F32) + vectors_ref[1:2, :]
        normed, inverse = norm_parts(middle_buf[rows(half), :] + branch)
        produced = normed * vectors_ref[4:5, :] + vectors_ref[5:6, :]
        normed2_ref[rows(half), :] = normed
        inverse2_ref[rows(half), :] = inverse
        next_ref[rows(half), :] = produced
        low_ref[rows(half), :] = produced.astype(BF16)
        squares[2] += jnp.sum(live[half] * branch * branch, 0, keepdims=True)
    squares_ref[...] = jnp.zeros_like(squares_ref)
    for j in range(3):
        squares_ref[j : j + 1, :] = squares[j]
    for stage in range(2):
        for half in range(2):
            join(stage, half).wait_send()


def forward(mixed, x, gathered, vectors, inner_bias, lengths):
    return pl.pallas_call(
        forward_kernel,
        out_shape=(
            jax.ShapeDtypeStruct((256, 1024), F32),
            jax.ShapeDtypeStruct((256, 1024), BF16),
            jax.ShapeDtypeStruct((256, 1024), F32),
            jax.ShapeDtypeStruct((256, 1), F32),
            jax.ShapeDtypeStruct((256, 1024), BF16),
            jax.ShapeDtypeStruct((256, 2048), BF16),
            jax.ShapeDtypeStruct((256, 2048), BF16),
            jax.ShapeDtypeStruct((256, 1024), F32),
            jax.ShapeDtypeStruct((256, 1), F32),
            jax.ShapeDtypeStruct((8, 1024), F32),
        ),
        in_specs=[
            spec(pltpu.VMEM), spec(pltpu.VMEM), spec(pl.ANY), spec(pltpu.VMEM), spec(pltpu.VMEM),
            spec(pltpu.SMEM),
        ],
        out_specs=(spec(pltpu.VMEM),) * 10,
        scratch_shapes=[
            pltpu.VMEM((1024, 512), BF16),
            pltpu.VMEM((1024, 2048), BF16),
            pltpu.VMEM((1024, 2048), BF16),
            pltpu.VMEM((2, 2, ROWS, 1024), BF16),
            pltpu.VMEM((2, 2, ROWS, 1024), BF16),
            pltpu.VMEM((256, 1024), F32),
            pltpu.SemaphoreType.DMA((3,)),
            pltpu.SemaphoreType.DMA((2, 2)),
            pltpu.SemaphoreType.DMA((2, 2)),
        ],
        compiler_params=pltpu.CompilerParams(
            collective_id=4, has_side_effects=True, vmem_limit_bytes=LIMIT
        ),
        name="forward",
    )(mixed, x, gathered, vectors, inner_bias, lengths)


def backward_kernel(
    grad_ref, normed2_ref, inverse2_ref, slope_ref, normed1_ref, inverse1_ref, w_ref, vectors_ref,
    outer_grad_ref, inner_grad_ref, first_ref, attn_ref, mixed_grad_ref, sums_ref, bias_ref,
    out_w, inner_w, outer_w, second_buf, sent, landed, w_sem, send_sem, recv_sem,
):
    f = lax.axis_index("fsdp")
    c = lax.axis_index("context")
    t = lax.axis_index("tensor")
    partner = (f, c, 1 - t)
    loads = []
    for j, (column, buffer) in enumerate(((4096, outer_w), (2048, inner_w), (1536, out_w))):
        load = pltpu.make_async_copy(
            w_ref.at[:, pl.ds(column, buffer.shape[1])], buffer, w_sem.at[j]
        )
        load.start()
        loads.append(load)
    greet_group([partner])

    def join(half):
        return remote(
            sent.at[half], landed.at[half], send_sem.at[half], recv_sem.at[half], partner
        )

    def rows(half):
        return pl.ds(half * ROWS, ROWS)

    sums = [0.0] * 6
    for half in range(2):
        grad = grad_ref[rows(half), :]
        normed = normed2_ref[rows(half), :]
        second = norm_back(grad, normed, inverse2_ref[rows(half), :], vectors_ref[4:5, :])
        low = second.astype(BF16)
        second_buf[rows(half), :] = second
        outer_grad_ref[rows(half), :] = low
        sums[4] += jnp.sum(grad * normed, 0, keepdims=True)
        sums[5] += jnp.sum(grad, 0, keepdims=True)
        sums[1] += jnp.sum(low.astype(F32), 0, keepdims=True)
    loads[0].wait()

    def inner(tile, carry):
        columns = pl.ds(pl.multiple_of(tile * 512, 512), 512)
        act = straight(outer_grad_ref[...], outer_w[:, columns])
        low = (act * slope_ref[:, columns].astype(F32)).astype(BF16)
        inner_grad_ref[:, columns] = low
        bias_ref[:, columns] = jnp.sum(low.astype(F32), 0, keepdims=True)
        return carry

    lax.fori_loop(0, 4, inner, 0)
    loads[1].wait()
    for half in range(2):
        sent[half] = across(inner_grad_ref[rows(half), :], inner_w[...]).astype(BF16)
        join(half).start()
    loads[2].wait()
    for half in range(2):
        join(half).wait_recv()
        middle = second_buf[rows(half), :] + (sent[half].astype(F32) + landed[half].astype(F32))
        normed = normed1_ref[rows(half), :]
        sums[2] += jnp.sum(middle * normed, 0, keepdims=True)
        sums[3] += jnp.sum(middle, 0, keepdims=True)
        first = norm_back(middle, normed, inverse1_ref[rows(half), :], vectors_ref[2:3, :])
        low = first.astype(BF16)
        first_ref[rows(half), :] = first
        attn_ref[rows(half), :] = low
        sums[0] += jnp.sum(low.astype(F32), 0, keepdims=True)
        mixed_grad_ref[rows(half), :] = straight(low, out_w[...]).astype(BF16)
    sums_ref[...] = jnp.zeros_like(sums_ref)
    for j in range(6):
        sums_ref[j : j + 1, :] = sums[j]
    for half in range(2):
        join(half).wait_send()


def backward(grad, saved, gathered, vectors):
    normed1, inverse1, slope, normed2, inverse2 = saved
    return pl.pallas_call(
        backward_kernel,
        out_shape=(
            jax.ShapeDtypeStruct((256, 1024), BF16),
            jax.ShapeDtypeStruct((256, 2048), BF16),
            jax.ShapeDtypeStruct((256, 1024), F32),
            jax.ShapeDtypeStruct((256, 1024), BF16),
            jax.ShapeDtypeStruct((256, 512), BF16),
            jax.ShapeDtypeStruct((8, 1024), F32),
            jax.ShapeDtypeStruct((1, 2048), F32),
        ),
        in_specs=[spec(pltpu.VMEM)] * 6 + [spec(pl.ANY), spec(pltpu.VMEM)],
        out_specs=(spec(pltpu.VMEM),) * 7,
        scratch_shapes=[
            pltpu.VMEM((1024, 512), BF16),
            pltpu.VMEM((1024, 2048), BF16),
            pltpu.VMEM((1024, 2048), BF16),
            pltpu.VMEM((256, 1024), F32),
            pltpu.VMEM((2, ROWS, 1024), BF16),
            pltpu.VMEM((2, ROWS, 1024), BF16),
            pltpu.SemaphoreType.DMA((3,)),
            pltpu.SemaphoreType.DMA((2,)),
            pltpu.SemaphoreType.DMA((2,)),
        ],
        compiler_params=pltpu.CompilerParams(
            collective_id=5, has_side_effects=True, vmem_limit_bytes=LIMIT
        ),
        name="backward",
    )(grad, normed2, inverse2, slope, normed1, inverse1, gathered, vectors)


def attend_back_kernel(
    mixed_grad_ref, unit_ref, outcome_ref, logs_ref, first_ref, w_ref, lengths,
    grads_ref, next_ref, sums_ref,
    w_buf, taken, grad_buf, query_sum, key_value_buf, query_buf, sent, landed,
    w_sem, local_sem, send_sem, recv_sem, back_send, back_recv, pair_send, pair_recv,
):
    f = lax.axis_index("fsdp")
    c = lax.axis_index("context")
    t = lax.axis_index("tensor")
    partner = (f, c, 1 - t)
    loads = []
    for j, column in enumerate((512, 1024, 0)):
        load = pltpu.make_async_copy(w_ref.at[:, pl.ds(column, 512)], w_buf.at[j], w_sem.at[j])
        load.start()
        loads.append(load)
    greet_group([(f, lax.rem(c + d, 8), t) for d in range(1, 8)] + [partner])

    def part(ref, peer):
        return ref.at[rows_of(peer // 4), rows_of(peer % 4)]

    def push(d):
        peer = lax.rem(c + d, 8)
        return remote(
            part(mixed_grad_ref, peer), taken.at[rows_of(c)],
            send_sem.at[d - 1], recv_sem.at[d - 1], (f, peer, t),
        )

    for d in range(1, 8):
        push(d).start()
    keep = pltpu.make_async_copy(part(mixed_grad_ref, c), taken.at[rows_of(c)], local_sem.at[0])
    keep.start()
    scale = jnp.asarray(0.125, BF16)
    queries = jnp.concatenate(
        [by_head(unit_ref[2, pl.ds(block * ROWS, ROWS), :] * scale) for block in range(8)], 0
    )
    logs = jnp.concatenate([logs_ref[block : block + 1, :] for block in range(8)], 1)
    query_sum[...] = jnp.zeros_like(query_sum)
    keep.wait()
    for d in range(1, 8):
        push(d).wait_recv()
    for block in range(8):
        grad_buf[pl.ds(block * 256, 256), :] = by_head(taken[pl.ds(block * ROWS, ROWS), :])
    head_row = lax.broadcasted_iota(jnp.int32, (8, LANES), 0)
    head_lane = lax.broadcasted_iota(jnp.int32, (8, LANES), 1) // HEAD
    chosen = jnp.where(head_row == head_lane, 1.0, 0.0)
    weighted = lax.dot_general(
        chosen, taken[...].astype(F32) * outcome_ref[...],
        (((1,), (1,)), ((), ())), precision=lax.Precision.HIGHEST, preferred_element_type=F32,
    )
    delta = jnp.concatenate(
        [
            weighted[head : head + 1, block * ROWS : (block + 1) * ROWS]
            for block in range(8)
            for head in range(2)
        ],
        1,
    )
    length = lengths[c // 4]

    def answer(j, d):
        peer = lax.rem(c + d, 8)
        source = query_buf if j == 2 else key_value_buf.at[j]
        return remote(
            source.at[rows_of(peer)], part(grads_ref.at[j], c),
            back_send.at[j, d - 1], back_recv.at[j, d - 1], (f, peer, t),
        )

    def step(turn, carry):
        pair = lax.rem(c // 2 + turn, 4)
        spot = pl.ds(pl.multiple_of(pair * 256, 256), 256)
        keys = unit_ref[0, spot, :]
        values = unit_ref[1, spot, :]
        scores = across(keys, queries) + key_mask(length, pair * 256, 256)
        soft = jnp.exp(scores - logs)
        key_value_buf[1, spot, :] = straight(soft.astype(BF16), grad_buf[...]).astype(BF16)
        soft_grad = across(values, grad_buf[...])
        score_grad = (soft * (soft_grad - delta)).astype(BF16)
        key_value_buf[0, spot, :] = straight(score_grad, queries).astype(BF16)
        query_sum[...] += lax.dot_general(
            score_grad, keys, (((0,), (0,)), ((), ())), preferred_element_type=F32
        )

        for side in range(2):
            block = pair * 2 + side
            d = lax.rem(block - c + 8, 8)

            @pl.when(d > 0)
            def _():
                for j in range(2):
                    answer(j, d).start()

        return carry

    lax.fori_loop(1, 5, step, 0)
    first_lane = lax.broadcasted_iota(jnp.int32, (ROWS, LANES), 1) < HEAD
    for block in range(8):
        start = block * 256
        total = jnp.where(
            first_lane,
            query_sum[pl.ds(start, ROWS), :],
            query_sum[pl.ds(start + ROWS, ROWS), :],
        )
        query_buf[pl.ds(block * ROWS, ROWS), :] = (total * 0.125).astype(BF16)
    for d in range(1, 8):
        answer(2, d).start()
    kept = []
    for j in range(3):
        source = query_buf if j == 2 else key_value_buf.at[j]
        keep = pltpu.make_async_copy(source.at[rows_of(c)], part(grads_ref.at[j], c), local_sem.at[j])
        keep.start()
        kept.append(keep)
    for j in range(3):
        kept[j].wait()
        loads[j].wait()
    for j in range(2):
        for d in range(1, 8):
            answer(j, d).wait_recv()
    sums_ref[...] = jnp.zeros_like(sums_ref)
    sums_ref[1:2, :] = jnp.sum(grads_ref[1].astype(F32), 0, keepdims=True)
    early = across(grads_ref[0], w_buf[0]) + across(grads_ref[1], w_buf[1])
    for d in range(1, 8):
        answer(2, d).wait_recv()
    sums_ref[0:1, :] = jnp.sum(grads_ref[2].astype(F32), 0, keepdims=True)
    sent[...] = (early + across(grads_ref[2], w_buf[2])).astype(BF16)
    swap = remote(sent, landed, pair_send, pair_recv, partner)
    swap.start()
    swap.wait()
    next_ref[...] = first_ref[...] + (sent[...].astype(F32) + landed[...].astype(F32))
    for d in range(1, 8):
        push(d).wait_send()
        for j in range(3):
            answer(j, d).wait_send()


def attend_back(mixed_grad, unit, outcome, logs, first, gathered, lengths):
    return pl.pallas_call(
        attend_back_kernel,
        out_shape=(
            jax.ShapeDtypeStruct((3, 256, 512), BF16),
            jax.ShapeDtypeStruct((256, 1024), F32),
            jax.ShapeDtypeStruct((8, 512), F32),
        ),
        in_specs=[spec(pltpu.VMEM)] * 5 + [spec(pl.ANY), spec(pltpu.SMEM)],
        out_specs=(spec(pltpu.VMEM),) * 3,
        scratch_shapes=[
            pltpu.VMEM((3, 1024, 512), BF16),
            pltpu.VMEM((1024, LANES), BF16),
            pltpu.VMEM((2048, LANES), BF16),
            pltpu.VMEM((2048, LANES), F32),
            pltpu.VMEM((2, 1024, LANES), BF16),
            pltpu.VMEM((1024, LANES), BF16),
            pltpu.VMEM((256, 1024), BF16),
            pltpu.VMEM((256, 1024), BF16),
            pltpu.SemaphoreType.DMA((3,)),
            pltpu.SemaphoreType.DMA((3,)),
            pltpu.SemaphoreType.DMA((7,)),
            pltpu.SemaphoreType.DMA((7,)),
            pltpu.SemaphoreType.DMA((3, 7)),
            pltpu.SemaphoreType.DMA((3, 7)),
            pltpu.SemaphoreType.DMA,
            pltpu.SemaphoreType.DMA,
        ],
        compiler_params=pltpu.CompilerParams(
            collective_id=6, has_side_effects=True, vmem_limit_bytes=LIMIT
        ),
        name="attend_back",
    )(mixed_grad, unit, outcome, logs, first, gathered, lengths)


def body(
    stream,
    lengths,
    query_weight,
    query_bias,
    key_weight,
    value_weight,
    value_bias,
    output_weight,
    output_bias,
    first_gain,
    first_shift,
    inner_weight,
    inner_bias,
    outer_weight,
    outer_bias,
    second_gain,
    second_shift,
    cotangent,
):
    slot_count, seq_count, model_width = stream.shape
    row_count = slot_count * seq_count
    position = lax.axis_index("context") * slot_count + jnp.arange(slot_count, dtype=jnp.int32)
    row_live = (position[None, :] < lengths[:, None]).astype(F32).reshape(row_count, 1)
    extras = jnp.stack(
        [output_bias, outer_bias, first_gain, first_shift, second_gain, second_shift], 1
    )
    packed = jnp.concatenate(
        [
            query_weight,
            key_weight,
            value_weight,
            output_weight.T,
            inner_weight,
            outer_weight.T,
            jnp.pad(extras, ((0, 0), (0, LANES - 6))),
        ],
        1,
    )
    gathered = gather_all(packed).reshape(model_width, packed.shape[1])
    vectors = jnp.pad(gathered[:, 6144:6150].T.astype(F32), ((0, 2), (0, 0)))
    query_row = query_bias.astype(F32)[None]
    value_row = value_bias.astype(F32)[None]
    inner_row = inner_bias.astype(F32)[None]

    low = stream.transpose(1, 0, 2).reshape(row_count, model_width)
    current = low.astype(F32)
    stored = []
    squares_all = []
    for repeat in range(LAYERS):
        mixed, unit, outcome, logs = attend(low, gathered, query_row, value_row, lengths)
        current, low_next, normed1, inverse1, middle, act, slope, normed2, inverse2, squares = forward(
            mixed, current, gathered, vectors, inner_row, lengths
        )
        stored.append((low, mixed, unit, outcome, logs, middle, act, (normed1, inverse1, slope, normed2, inverse2)))
        squares_all.append(jnp.sum(squares[:3], 1))
        low = low_next
    result = (current * row_live).astype(BF16).reshape(seq_count, slot_count, model_width).transpose(1, 0, 2)
    grad = cotangent.transpose(1, 0, 2).reshape(row_count, model_width).astype(F32) * row_live
    taken = []
    for repeat in reversed(range(LAYERS)):
        low, mixed, unit, outcome, logs, middle, act, saved = stored[repeat]
        outer_grad, inner_grad, first, attn, mixed_grad, sums, bias = backward(
            grad, saved, gathered, vectors
        )
        qkv, grad, head_sums = attend_back(mixed_grad, unit, outcome, logs, first, gathered, lengths)
        taken.append((low, qkv, attn, mixed, middle, inner_grad, outer_grad, act, sums, bias, head_sums))

    def twice(left, right):
        return sum(
            lax.dot_general(left(t), right(t), (((0,), (0,)), ((), ())), preferred_element_type=F32)
            for t in taken
        )

    sums = taken[0][8] + taken[1][8]
    bias = taken[0][9] + taken[1][9]
    head_sums = taken[0][10] + taken[1][10]
    grads = jnp.concatenate(
        [
            twice(lambda t: t[0], lambda t: t[1][2]),
            twice(lambda t: t[0], lambda t: t[1][0]),
            twice(lambda t: t[0], lambda t: t[1][1]),
            twice(lambda t: t[2], lambda t: t[3]),
            twice(lambda t: t[4], lambda t: t[5]),
            twice(lambda t: t[6], lambda t: t[7]),
            jnp.pad(sums[:6].T, ((0, 0), (0, LANES - 6))),
        ],
        1,
    ).astype(BF16)
    small = jnp.concatenate(
        [
            head_sums[0],
            head_sums[1],
            bias[0],
            jnp.stack(squares_all).reshape(-1),
            jnp.sum(row_live)[None],
            jnp.zeros((1024 - 7,), F32),
        ]
    ).reshape(32, LANES)
    summed, total = scatter_all(grads.reshape(2, 4, 2, 4, 16, grads.shape[1]), small)
    total = total.reshape(-1)
    square_total, count_total = total[3072:3078].reshape(LAYERS, 3), total[3078]
    root_values = jnp.sqrt(square_total / (count_total * model_width) + 1e-06)
    stream_grad = grad.reshape(seq_count, slot_count, model_width).transpose(1, 0, 2)
    return (
        result,
        stream_grad,
        summed[:, 0:512],
        total[0:512],
        summed[:, 512:1024],
        summed[:, 1024:1536],
        total[512:1024],
        summed[:, 1536:2048].T,
        summed[:, 6144],
        summed[:, 6146],
        summed[:, 6147],
        summed[:, 2048:4096],
        total[1024:3072],
        summed[:, 4096:6144].T,
        summed[:, 6145],
        summed[:, 6148],
        summed[:, 6149],
        root_values,
    )


def solution(mesh):
    in_specs = (
        P("context", "fsdp", None),
        P("fsdp"),
        P(("fsdp", "context"), "tensor"),
        P("tensor"),
        P(("fsdp", "context"), "tensor"),
        P(("fsdp", "context"), "tensor"),
        P("tensor"),
        P("tensor", ("fsdp", "context")),
        P(("fsdp", "context")),
        P(("fsdp", "context")),
        P(("fsdp", "context")),
        P(("fsdp", "context"), "tensor"),
        P("tensor"),
        P("tensor", ("fsdp", "context")),
        P(("fsdp", "context")),
        P(("fsdp", "context")),
        P(("fsdp", "context")),
        P("context", "fsdp", None),
    )
    out_specs = (
        P("context", "fsdp", None),
        P("context", "fsdp", None),
        P(("fsdp", "context"), "tensor"),
        P("tensor"),
        P(("fsdp", "context"), "tensor"),
        P(("fsdp", "context"), "tensor"),
        P("tensor"),
        P("tensor", ("fsdp", "context")),
        P(("fsdp", "context")),
        P(("fsdp", "context")),
        P(("fsdp", "context")),
        P(("fsdp", "context"), "tensor"),
        P("tensor"),
        P("tensor", ("fsdp", "context")),
        P(("fsdp", "context")),
        P(("fsdp", "context")),
        P(("fsdp", "context")),
        P(),
    )
    return jax.shard_map(body, mesh=mesh, in_specs=in_specs, out_specs=out_specs, check_vma=False)
```

```python
import jax
import jax.numpy as jnp
from jax import lax
from jax.experimental import pallas as pl
from jax.experimental.pallas import tpu as pltpu
from jax.sharding import PartitionSpec as P

HEAD = 64
LAYERS = 2
LANES = 128
MESH = pl.DeviceIdType.MESH

F32 = jnp.float32
BF16 = jnp.bfloat16
ROWS = 128
LIMIT = 60 * 2**20
WIDTH = 6272
QUERY, KEY, VALUE, OUT, INNER, OUTER, EXTRA = 0, 512, 1024, 1536, 2048, 4096, 6144
GROUPS = ((QUERY, OUT), (OUT, WIDTH))
ORDERS = ("zyx", "yxz", "xzy")
SHARDS = (2, 4, 2, 4)


def spec(space):
    return pl.BlockSpec(memory_space=space)


def place():
    f = lax.axis_index("fsdp")
    c = lax.axis_index("context")
    t = lax.axis_index("tensor")
    return {"x": 2 * (f // 4) + c // 4, "y": c % 4, "z": f % 4, "t": t}


def device(at):
    x = at["x"]
    return ((x // 2) * 4 + at["z"], (x % 2) * 4 + at["y"], at["t"])


def shifted(at, axis, step):
    moved = dict(at)
    moved[axis] = lax.rem(at[axis] + step + 4, 4)
    return moved


def greet(devices):
    barrier = pltpu.get_barrier_semaphore()
    for device_id in devices:
        pl.semaphore_signal(barrier, inc=1, device_id=device_id, device_id_type=MESH)
    pl.semaphore_wait(barrier, len(devices))


def neighbours(at, steps):
    return [device(shifted(at, axis, step)) for axis in "xyz" for step in steps]


def context_peers():
    f = lax.axis_index("fsdp")
    c = lax.axis_index("context")
    t = lax.axis_index("tensor")
    return [(f, lax.rem(c + d, 8), t) for d in range(1, 8)]


def remote(src, dst, send_sem, recv_sem, device_id):
    return pltpu.make_async_remote_copy(
        src_ref=src,
        dst_ref=dst,
        send_sem=send_sem,
        recv_sem=recv_sem,
        device_id=device_id,
        device_id_type=MESH,
    )


def shards(ref, at, whole, cols):
    x = at["x"]
    xh = slice(None) if "x" in whole else x // 2
    xl = slice(None) if "x" in whole else x % 2
    z = slice(None) if "z" in whole else at["z"]
    y = slice(None) if "y" in whole else at["y"]
    return ref.at[xh, z, xl, y, :, pl.ds(cols[0], cols[1])]


def thirds(group):
    start, end = GROUPS[group]
    tiles = (end - start) // LANES
    cuts = [start + tiles * i // 6 * LANES for i in range(7)]
    return [
        ((cuts[2 * i], cuts[2 * i + 1] - cuts[2 * i]), (cuts[2 * i + 1], cuts[2 * i + 2] - cuts[2 * i + 1]))
        for i in range(3)
    ]


def across(left, right):
    return lax.dot_general(left, right, (((1,), (1,)), ((), ())), preferred_element_type=F32)


def straight(left, right):
    return jnp.dot(left, right, preferred_element_type=F32)


def rows_of(block):
    return pl.ds(pl.multiple_of(block * ROWS, ROWS), ROWS)


def by_head(block):
    first = lax.broadcasted_iota(jnp.int32, block.shape, 1) < HEAD
    zero = jnp.zeros_like(block)
    return jnp.concatenate([jnp.where(first, block, zero), jnp.where(first, zero, block)], 0)


def key_mask(length, first, count):
    position = first + lax.broadcasted_iota(jnp.int32, (count, 1), 0)
    return jnp.where(position < length, 0.0, -1e30)


def columns_of(weights, start, width):
    return weights[:, :, :, :, :, pl.ds(start, width)].reshape(1024, width)


def quarter_of(weights, quarter, start, width):
    z = 2 * (quarter % 2)
    return weights[quarter // 2, z : z + 2, :, :, :, start : start + width].reshape(256, width)


def part(ref, peer):
    return ref.at[rows_of(peer // 4), rows_of(peer % 4)]


def parts_of(width):
    tiles = width//LANES
    cuts = [tiles*i//6*LANES for i in range(7)]
    return [((cuts[2*i], cuts[2*i+1]-cuts[2*i]), (cuts[2*i+1], cuts[2*i+2]-cuts[2*i+1])) for i in range(3)]

def scatter_kernel(all_ref, small_ref, own_ref, total_ref, work, small_land, load_sem, send_sem, recv_sem, small_send, small_recv, *landings):
    at = place()
    parts = parts_of(all_ref.shape[-1])
    loads=[]
    for part in range(3):
        lo,hi=parts[part]; both=pl.ds(lo[0],lo[1]+hi[1])
        cp=pltpu.make_async_copy(all_ref.at[:,:,:,:,:,both], work.at[:,:,:,:,:,both], load_sem.at[part]); cp.start(); loads.append(cp)
    greet(neighbours(at, (1, 2, 3)))
    for cp in loads: cp.wait()

    def push(part,phase,kind,origin,whole,cols,axis,step):
        land=landings[phase*3+part]
        src=shards(work,origin,whole,cols)
        return pltpu.make_async_remote_copy(src_ref=src,dst_ref=land.at[kind] if cols[1]==land.shape[-1] else land.at[kind,...,pl.ds(0,cols[1])],send_sem=send_sem.at[part,phase,kind],recv_sem=recv_sem.at[part,phase,kind],device_id=device(shifted(at,axis,step)),device_id_type=MESH)

    def add(origin,whole,cols,land_list):
        x=origin["x"]
        xs=[(a,b) for a in range(2) for b in range(2)] if "x" in whole else [(x//2,x%2)]
        zs=list(range(4)) if "z" in whole else [origin["z"]]
        ys=list(range(4)) if "y" in whole else [origin["y"]]
        sx="x" in whole; sz="z" in whole; sy="y" in whole
        def one(ix,iz,iy):
            xh,xl=(ix//2,ix%2) if sx else (x//2,x%2)
            z=iz if sz else origin["z"]; y=iy if sy else origin["y"]
            index=(xh,z,xl,y,slice(None),pl.ds(cols[0],cols[1]))
            total=work[index].astype(jnp.float32)
            for land,kind in land_list:
                li=(kind,)
                if sx: li+=(xh,)
                if sz: li+=(z,)
                if sx: li+=(xl,)
                if sy: li+=(y,)
                li+=(slice(None),pl.ds(0,cols[1]))
                total=total+land[li].astype(jnp.float32)
            work[index]=total.astype(work.dtype)
        nx=4 if sx else 1; nz=4 if sz else 1; ny=4 if sy else 1
        n=nx*nz*ny
        def body(i,_):
            one(i//(nz*ny), (i//ny)%nz, i%ny); return 0
        if n==1: one(0,0,0)
        else: lax.fori_loop(0,n,body,0)

    total_ref[...]=small_ref[...]
    for phase in range(3):
        early=[]
        small=[]
        for step in (1,2,3):
            cp=pltpu.make_async_remote_copy(src_ref=total_ref,dst_ref=small_land.at[phase,step-1],send_sem=small_send.at[phase,step-1],recv_sem=small_recv.at[phase,step-1],device_id=device(shifted(at,"xyz"[phase],step)),device_id_type=MESH)
            cp.start(); small.append(cp)
        for part in range(3):
            order=ORDERS[part][::-1]; axis=order[phase]; whole=order[phase+1:]
            lo,hi=parts[part]
            far=shifted(at,axis,2); up=shifted(at,axis,1); down=shifted(at,axis,-1)
            a=push(part,phase,0,far,whole,lo,axis,1); a.start()
            b=push(part,phase,1,far,whole,hi,axis,-1); b.start()
            c=push(part,phase,2,up,whole,hi,axis,1); c.start()
            d=push(part,phase,3,down,whole,lo,axis,-1); d.start()
            early.append((a,b,c,d))
        late=[]
        for part in range(3):
            order=ORDERS[part][::-1]; axis=order[phase]; whole=order[phase+1:]
            lo,hi=parts[part]; land=landings[phase*3+part]
            up=shifted(at,axis,1); down=shifted(at,axis,-1)
            a,b,c,d=early[part]
            a.wait_recv(); add(up,whole,lo,[(land,0)])
            e=push(part,phase,4,up,whole,lo,axis,1); e.start()
            b.wait_recv(); add(down,whole,hi,[(land,1)])
            f=push(part,phase,5,down,whole,hi,axis,-1); f.start()
            late.append((e,f))
        for part in range(3):
            order=ORDERS[part][::-1]; axis=order[phase]; whole=order[phase+1:]
            lo,hi=parts[part]; land=landings[phase*3+part]
            a,b,c,d=early[part]; e,f=late[part]
            c.wait_recv(); f.wait_recv()
            add(at,whole,hi,[(land,2),(land,5)])
            d.wait_recv(); e.wait_recv()
            add(at,whole,lo,[(land,3),(land,4)])
        for part in range(3):
            for cp in early[part]+late[part]: cp.wait_send()
        for cp in small: cp.wait_recv()
        for cp in small: cp.wait_send()
        total_ref[...]=total_ref[...]+small_land[phase,0]+small_land[phase,1]+small_land[phase,2]
    x=at["x"]
    own_ref[...]=work[x//2,at["z"],x%2,at["y"]].astype(jnp.float32)

def scatter_all(whole, small):
    rows,width=whole.shape[-2:]
    parts=parts_of(width)
    landings=[]
    for phase in range(3):
        for part in range(3):
            order=ORDERS[part][::-1]; w=order[phase+1:]
            shape=[6]
            if "x" in w: shape.append(2)
            if "z" in w: shape.append(4)
            if "x" in w: shape.append(2)
            if "y" in w: shape.append(4)
            shape+= [rows, max(parts[part][0][1],parts[part][1][1])]
            landings.append(pltpu.VMEM(tuple(shape), whole.dtype))
    return pl.pallas_call(scatter_kernel,
        out_shape=(jax.ShapeDtypeStruct((rows,width), jnp.float32),jax.ShapeDtypeStruct(small.shape, jnp.float32)),
        in_specs=[pl.BlockSpec(memory_space=pl.ANY),pl.BlockSpec(memory_space=pltpu.VMEM)], out_specs=(pl.BlockSpec(memory_space=pltpu.VMEM),pl.BlockSpec(memory_space=pltpu.VMEM)),
        scratch_shapes=[pltpu.VMEM(whole.shape, whole.dtype), pltpu.VMEM((3,3)+small.shape,jnp.float32), pltpu.SemaphoreType.DMA((3,)), pltpu.SemaphoreType.DMA((3,3,6)), pltpu.SemaphoreType.DMA((3,3,6)), pltpu.SemaphoreType.DMA((3,3)), pltpu.SemaphoreType.DMA((3,3))]+landings,
        compiler_params=pltpu.CompilerParams(collective_id=2, has_side_effects=True, vmem_limit_bytes=60*2**20),
        name="scatter_grads")(whole, small)


class Gather:
    def __init__(self, weights, group, send_sem, recv_sem):
        self.at = place()
        self.weights, self.group = weights, group
        self.send_sem, self.recv_sem = send_sem, recv_sem
        self.parts = thirds(group)
        self.sent = {}

    def send(self, third, phase, kind, origin, cols, step):
        order = ORDERS[third]
        block = shards(self.weights, origin, order[:phase], cols)
        index = (self.group, third, phase, kind)
        copy = remote(
            block, block, self.send_sem.at[index], self.recv_sem.at[index],
            device(shifted(self.at, order[phase], step)),
        )
        copy.start()
        self.sent[third, phase, kind] = copy

    def first(self, phase):
        for third in range(3):
            low, high = self.parts[third]
            both = (low[0], low[1] + high[1])
            self.send(third, phase, 0, self.at, both, 1)
            self.send(third, phase, 1, self.at, both, -1)

    def onward(self, phase):
        for third in range(3):
            axis = ORDERS[third][phase]
            low, high = self.parts[third]
            self.sent[third, phase, 0].wait_recv()
            self.send(third, phase, 2, shifted(self.at, axis, -1), low, 1)
            self.sent[third, phase, 1].wait_recv()
            self.send(third, phase, 3, shifted(self.at, axis, 1), high, -1)

    def settle(self, phase):
        for third in range(3):
            self.sent[third, phase, 2].wait_recv()
            self.sent[third, phase, 3].wait_recv()

    def close(self):
        for copy in self.sent.values():
            copy.wait_send()


class Heads:
    def __init__(self, own, unit, outcome, mixed, local_sem, send_sem, recv_sem, back_send, back_recv):
        self.f = lax.axis_index("fsdp")
        self.c = lax.axis_index("context")
        self.t = lax.axis_index("tensor")
        self.own, self.unit, self.outcome, self.mixed = own, unit, outcome, mixed
        self.local_sem, self.send_sem, self.recv_sem = local_sem, send_sem, recv_sem
        self.back_send, self.back_recv = back_send, back_recv

    def push(self, j, d):
        peer = lax.rem(self.c + d, 8)
        return remote(
            part(self.own.at[j], peer), self.unit.at[j, rows_of(self.c)],
            self.send_sem.at[j, d - 1], self.recv_sem.at[j, d - 1], (self.f, peer, self.t),
        )

    def keep(self, j):
        return pltpu.make_async_copy(
            part(self.own.at[j], self.c), self.unit.at[j, rows_of(self.c)], self.local_sem.at[j]
        )

    def answer(self, d):
        peer = lax.rem(self.c + d, 8)
        return remote(
            self.outcome.at[rows_of(peer)], part(self.mixed, self.c),
            self.back_send.at[d - 1], self.back_recv.at[d - 1], (self.f, peer, self.t),
        )

    def keep_back(self):
        return pltpu.make_async_copy(
            self.outcome.at[rows_of(self.c)], part(self.mixed, self.c), self.local_sem.at[3]
        )

    def project(self, x, weights, bias):
        for j, column in enumerate((KEY, VALUE, QUERY)):
            product = straight(x, columns_of(weights, column, 512))
            if j == 1:
                product = product + bias[:, 512:1024]
            if j == 2:
                product = product + bias[:, 0:512]
            self.own[j] = product.astype(BF16)
            for d in (4, 1, 7, 5, 3, 2, 6):
                self.push(j, d).start()
            self.keep(j).start()

    def attend(self, length, exact, logs):
        c = self.c
        for j in range(2):
            self.keep(j).wait()
            for d in range(1, 8):
                self.push(j, d).wait_recv()
        mask = key_mask(length, 0, 8 * ROWS)
        keys = self.unit[0]
        values_across = self.unit[1].T
        self.keep(2).wait()

        def step(d, carry):
            block = lax.rem(c + d, 8)

            @pl.when(d > 0)
            def _():
                self.push(2, 8 - d).wait_recv()

            queries = self.unit[2, rows_of(block), :] * jnp.asarray(0.125, BF16)
            scores = across(keys, by_head(queries)) + mask
            top = jnp.max(scores, 0, keepdims=True)
            exponent = jnp.exp(scores - top)
            total = jnp.sum(exponent, 0, keepdims=True)
            outcome = straight(values_across, exponent.astype(BF16)) / total
            both = jnp.concatenate([outcome[:HEAD, :ROWS], outcome[HEAD:, ROWS:]], 0).T
            exact[rows_of(block), :] = both
            self.outcome[rows_of(block), :] = both.astype(BF16)
            logs[pl.ds(block, 1), :] = top + jnp.log(total)

            @pl.when(d > 0)
            def _():
                self.answer(d).start()

            return carry

        lax.fori_loop(0, 8, step, 0)
        self.keep_back().start()

    def collect(self):
        self.keep_back().wait()
        for d in range(1, 8):
            self.answer(d).wait_recv()

    def close(self):
        for d in range(1, 8):
            self.answer(d).wait_send()
            for j in range(3):
                self.push(j, d).wait_send()


class Joins:
    def __init__(self, sent, landed, send_sem, recv_sem):
        t = lax.axis_index("tensor")
        self.partner = (lax.axis_index("fsdp"), lax.axis_index("context"), 1 - t)
        self.sent, self.landed, self.send_sem, self.recv_sem = sent, landed, send_sem, recv_sem

    def copy(self, half):
        return remote(
            self.sent.at[half], self.landed.at[half], self.send_sem.at[half], self.recv_sem.at[half],
            self.partner,
        )

    def offer(self, quarter, term):
        half, side = quarter // 2, quarter % 2
        self.sent[half, :, side * 256 : side * 256 + 256] = term.astype(BF16)
        if side == 1:
            self.copy(half).start()

    def wait(self):
        for half in range(2):
            self.copy(half).wait_recv()

    def total(self, rows):
        return jnp.concatenate(
            [self.sent[half, rows, :].astype(F32) + self.landed[half, rows, :].astype(F32) for half in range(2)],
            1,
        )

    def close(self):
        for half in range(2):
            self.copy(half).wait_send()


def gelu_parts(argument):
    square = argument * argument
    inner = 0.7978845608028654 * argument * (1.0 + 0.044715 * square)
    bend = jnp.tanh(inner)
    half = 0.5 * (1.0 + bend)
    slope = half + 0.5 * argument * (1.0 - bend * bend) * 0.7978845608028654 * (
        1.0 + 3.0 * 0.044715 * square
    )
    return argument * half, slope


def norm_parts(hidden):
    centre = hidden - jnp.mean(hidden, -1, keepdims=True)
    inverse = lax.rsqrt(jnp.mean(centre * centre, -1, keepdims=True) + 1e-05)
    return centre * inverse, inverse


def live_rows(lengths, block, count):
    c = lax.axis_index("context")
    row = block * count + lax.broadcasted_iota(jnp.int32, (count, 1), 0)
    slot = c * ROWS + lax.rem(row, ROWS)
    return jnp.where(slot < jnp.where(row < ROWS, lengths[0], lengths[1]), 1.0, 0.0)


SLAB = 64


def slab_of(block):
    return pl.ds(pl.multiple_of(block * SLAB, SLAB), SLAB)


def pack(weights, own, query, key, value, output, inner, outer, vectors):
    xh, z, xl, y = own
    eye = jnp.where(
        lax.broadcasted_iota(jnp.int32, (16, 16), 0) == lax.broadcasted_iota(jnp.int32, (16, 16), 1), 1.0, 0.0
    ).astype(BF16)

    def put(start, block):
        weights[xh, z, xl, y, :, start : start + block.shape[1]] = block

    put(QUERY, query[...])
    put(KEY, key[...])
    put(VALUE, value[...])
    put(OUT, across(eye, output[...]).astype(BF16))
    put(INNER, inner[...])
    put(OUTER, across(eye, outer[...]).astype(BF16))
    put(EXTRA, across(eye, vectors[...]).astype(BF16))


def forward_kernel(
    x_ref, query, key, value, output, inner, outer, vectors, bias, lengths,
    result_ref, rows_ref, squares_ref, w_out, unit_out, exact_out, logs_out, mixed_out, normed_out, inverse_out,
    middle_out, act_out, slope_out, low_out,
    weights, own, unit, exact, logs, outcome, mixed, normed, inverse, middle, act, slope, low, current,
    sent, landed,
    local_sem, save_sem, gather_send, gather_recv, send_sem, recv_sem, back_send, back_recv, pair_send, pair_recv,
):
    at = place()
    c = lax.axis_index("context")
    t = lax.axis_index("tensor")
    partner = (lax.axis_index("fsdp"), c, 1 - t)
    x = at["x"]
    pack(weights, (x // 2, at["z"], x % 2, at["y"]), query, key, value, output, inner, outer, vectors)
    greet(neighbours(at, (1, -1)) + context_peers() + [partner])
    one, two = (Gather(weights, group, gather_send, gather_recv) for group in range(2))
    one.first(0)
    two.first(0)
    one.onward(0)
    two.onward(0)
    one.settle(0)
    one.first(1)
    two.settle(0)
    two.first(1)
    one.onward(1)
    two.onward(1)
    one.settle(1)
    one.first(2)
    two.settle(1)
    one.onward(2)
    two.first(2)
    current[...] = x_ref[...].astype(F32)
    one.settle(2)
    squares_ref[...] = jnp.zeros_like(squares_ref)
    length = lengths[c // 4]
    saves = []

    def save(source, target):
        copy = pltpu.make_async_copy(source, target, save_sem.at[len(saves)])
        copy.start()
        saves.append(copy)

    closing = [one, two]
    for layer in range(LAYERS):
        first = layer == 0
        heads = Heads(
            own.at[layer], unit.at[layer], outcome.at[layer], mixed.at[layer], local_sem.at[layer],
            send_sem.at[layer], recv_sem.at[layer], back_send.at[layer], back_recv.at[layer],
        )
        joins = [
            Joins(sent.at[layer, stage], landed.at[layer, stage], pair_send.at[layer, stage], pair_recv.at[layer, stage])
            for stage in range(2)
        ]
        heads.project(x_ref[...] if first else low[...], weights, bias)
        heads.attend(length, exact.at[layer], logs.at[layer])
        if first:
            two.onward(2)
        heads.collect()
        if first:
            two.settle(2)
            save(weights, w_out)
            pick = jnp.where(
                lax.broadcasted_iota(jnp.int32, (8, LANES), 0) == lax.broadcasted_iota(jnp.int32, (8, LANES), 1),
                1.0, 0.0,
            ).astype(BF16)
            rows_ref[...] = across(pick, columns_of(weights, EXTRA, LANES))
        for quarter in range(4):
            joins[0].offer(quarter, across(mixed[layer], quarter_of(weights, quarter, OUT, 512)))
        save(unit.at[layer], unit_out.at[layer])
        save(exact.at[layer], exact_out.at[layer])
        save(logs.at[layer], logs_out.at[layer])
        save(mixed.at[layer], mixed_out.at[layer])
        joins[0].wait()

        def after_attention(block, total):
            rows = slab_of(block)
            live = live_rows(lengths, block, SLAB)
            before = current[rows, :]
            branch = joins[0].total(rows) + rows_ref[0:1, :]
            scaled, root = norm_parts(before + branch)
            after = scaled * rows_ref[2:3, :] + rows_ref[3:4, :]
            normed[layer, 0, rows, :] = scaled
            inverse[layer, 0, rows, :] = root
            current[rows, :] = after
            middle[layer, rows, :] = after.astype(BF16)
            return (
                total[0] + jnp.sum(live * before * before, 0, keepdims=True),
                total[1] + jnp.sum(live * branch * branch, 0, keepdims=True),
            )

        zero = jnp.zeros((1, 1024), F32)
        total = lax.fori_loop(0, 256 // SLAB, after_attention, (zero, zero))
        squares_ref[3 * layer : 3 * layer + 1, :] = total[0]
        squares_ref[3 * layer + 1 : 3 * layer + 2, :] = total[1]
        save(middle.at[layer], middle_out.at[layer])

        def hidden(tile, carry):
            start = pl.multiple_of(tile * 512, 512)
            columns = pl.ds(start, 512)
            pre = straight(middle[layer], columns_of(weights, INNER + start, 512)) + bias[:, pl.ds(1024 + start, 512)]
            act_part, slope_part = gelu_parts(pre)
            act[layer, :, columns] = act_part.astype(BF16)
            slope[layer, :, columns] = slope_part.astype(BF16)
            return carry

        lax.fori_loop(0, 4, hidden, 0)
        for quarter in range(4):
            joins[1].offer(quarter, across(act[layer], quarter_of(weights, quarter, OUTER, 2048)))
        save(act.at[layer], act_out.at[layer])
        save(slope.at[layer], slope_out.at[layer])
        joins[1].wait()

        def after_hidden(block, total):
            rows = slab_of(block)
            live = live_rows(lengths, block, SLAB)
            branch = joins[1].total(rows) + rows_ref[1:2, :]
            scaled, root = norm_parts(current[rows, :] + branch)
            after = scaled * rows_ref[4:5, :] + rows_ref[5:6, :]
            normed[layer, 1, rows, :] = scaled
            inverse[layer, 1, rows, :] = root
            current[rows, :] = after
            if first:
                low[rows, :] = after.astype(BF16)
            else:
                result_ref[rows, :] = (after * live).astype(BF16)
            return total + jnp.sum(live * branch * branch, 0, keepdims=True)

        squares_ref[3 * layer + 2 : 3 * layer + 3, :] = lax.fori_loop(0, 256 // SLAB, after_hidden, zero)
        save(normed.at[layer], normed_out.at[layer])
        save(inverse.at[layer], inverse_out.at[layer])
        if first:
            save(low, low_out)
        closing += [heads] + joins
    for item in closing:
        item.close()
    for copy in saves:
        copy.wait()


def run_forward(x, query, key, value, output, inner, outer, vectors, bias, lengths):
    saved = (
        ((*SHARDS, 16, WIDTH), BF16),
        ((2, 3, 1024, LANES), BF16),
        ((2, 1024, LANES), F32),
        ((2, 8, 256), F32),
        ((2, 256, 512), BF16),
        ((2, 2, 256, 1024), F32),
        ((2, 2, 256, 1), F32),
        ((2, 256, 1024), BF16),
        ((2, 256, 2048), BF16),
        ((2, 256, 2048), BF16),
        ((256, 1024), BF16),
    )
    dma = pltpu.SemaphoreType.DMA
    return pl.pallas_call(
        forward_kernel,
        out_shape=(
            jax.ShapeDtypeStruct((256, 1024), BF16),
            jax.ShapeDtypeStruct((8, 1024), F32),
            jax.ShapeDtypeStruct((8, 1024), F32),
            *(jax.ShapeDtypeStruct(shape, kind) for shape, kind in saved),
        ),
        in_specs=[spec(pltpu.VMEM)] * 9 + [spec(pltpu.SMEM)],
        out_specs=(spec(pltpu.VMEM),) * 3 + (spec(pl.ANY),) * len(saved),
        scratch_shapes=[
            pltpu.VMEM((*SHARDS, 16, WIDTH), BF16),
            pltpu.VMEM((2, 3, 256, 512), BF16),
            pltpu.VMEM((2, 3, 1024, LANES), BF16),
            pltpu.VMEM((2, 1024, LANES), F32),
            pltpu.VMEM((2, 8, 256), F32),
            pltpu.VMEM((2, 1024, LANES), BF16),
            pltpu.VMEM((2, 256, 512), BF16),
            pltpu.VMEM((2, 2, 256, 1024), F32),
            pltpu.VMEM((2, 2, 256, 1), F32),
            pltpu.VMEM((2, 256, 1024), BF16),
            pltpu.VMEM((2, 256, 2048), BF16),
            pltpu.VMEM((2, 256, 2048), BF16),
            pltpu.VMEM((256, 1024), BF16),
            pltpu.VMEM((256, 1024), F32),
            pltpu.VMEM((2, 2, 2, 256, 512), BF16),
            pltpu.VMEM((2, 2, 2, 256, 512), BF16),
            dma((2, 4)),
            dma((24,)),
            dma((2, 3, 3, 4)),
            dma((2, 3, 3, 4)),
            dma((2, 3, 7)),
            dma((2, 3, 7)),
            dma((2, 7)),
            dma((2, 7)),
            dma((2, 2, 2)),
            dma((2, 2, 2)),
        ],
        compiler_params=pltpu.CompilerParams(
            collective_id=3, has_side_effects=True, vmem_limit_bytes=LIMIT
        ),
        name="forward_layers",
    )(x, query, key, value, output, inner, outer, vectors, bias, lengths)


def norm_back(grad_out, normed, inverse, gain):
    scaled = grad_out * gain
    return inverse * (
        scaled
        - jnp.mean(scaled, -1, keepdims=True)
        - normed * jnp.mean(scaled * normed, -1, keepdims=True)
    )


def backward_kernel(
    grad_ref, normed2_ref, inverse2_ref, slope_ref, normed1_ref, inverse1_ref, w_ref, vectors_ref,
    outer_grad_ref, inner_grad_ref, first_ref, attn_ref, mixed_grad_ref, sums_ref, bias_ref,
    out_w, inner_w, outer_w, second_buf, sent, landed, w_sem, send_sem, recv_sem,
):
    f = lax.axis_index("fsdp")
    c = lax.axis_index("context")
    t = lax.axis_index("tensor")
    partner = (f, c, 1 - t)
    loads = []
    for j, (column, buffer) in enumerate(((4096, outer_w), (2048, inner_w), (1536, out_w))):
        load = pltpu.make_async_copy(
            w_ref.at[:, pl.ds(column, buffer.shape[1])], buffer, w_sem.at[j]
        )
        load.start()
        loads.append(load)
    greet([partner])

    def join(half):
        return remote(
            sent.at[half], landed.at[half], send_sem.at[half], recv_sem.at[half], partner
        )

    def rows(half):
        return pl.ds(half * ROWS, ROWS)

    sums = [0.0] * 6
    for half in range(2):
        grad = grad_ref[rows(half), :]
        normed = normed2_ref[rows(half), :]
        second = norm_back(grad, normed, inverse2_ref[rows(half), :], vectors_ref[4:5, :])
        low = second.astype(BF16)
        second_buf[rows(half), :] = second
        outer_grad_ref[rows(half), :] = low
        sums[4] += jnp.sum(grad * normed, 0, keepdims=True)
        sums[5] += jnp.sum(grad, 0, keepdims=True)
        sums[1] += jnp.sum(low.astype(F32), 0, keepdims=True)
    loads[0].wait()

    def inner(tile, carry):
        columns = pl.ds(pl.multiple_of(tile * 512, 512), 512)
        act = straight(outer_grad_ref[...], outer_w[:, columns])
        low = (act * slope_ref[:, columns].astype(F32)).astype(BF16)
        inner_grad_ref[:, columns] = low
        bias_ref[:, columns] = jnp.sum(low.astype(F32), 0, keepdims=True)
        return carry

    lax.fori_loop(0, 4, inner, 0)
    loads[1].wait()
    for half in range(2):
        sent[half] = across(inner_grad_ref[rows(half), :], inner_w[...]).astype(BF16)
        join(half).start()
    loads[2].wait()
    for half in range(2):
        join(half).wait_recv()
        middle = second_buf[rows(half), :] + (sent[half].astype(F32) + landed[half].astype(F32))
        normed = normed1_ref[rows(half), :]
        sums[2] += jnp.sum(middle * normed, 0, keepdims=True)
        sums[3] += jnp.sum(middle, 0, keepdims=True)
        first = norm_back(middle, normed, inverse1_ref[rows(half), :], vectors_ref[2:3, :])
        low = first.astype(BF16)
        first_ref[rows(half), :] = first
        attn_ref[rows(half), :] = low
        sums[0] += jnp.sum(low.astype(F32), 0, keepdims=True)
        mixed_grad_ref[rows(half), :] = straight(low, out_w[...]).astype(BF16)
    sums_ref[...] = jnp.zeros_like(sums_ref)
    for j in range(6):
        sums_ref[j : j + 1, :] = sums[j]
    for half in range(2):
        join(half).wait_send()


def backward(grad, saved, gathered, vectors):
    normed1, inverse1, slope, normed2, inverse2 = saved
    return pl.pallas_call(
        backward_kernel,
        out_shape=(
            jax.ShapeDtypeStruct((256, 1024), BF16),
            jax.ShapeDtypeStruct((256, 2048), BF16),
            jax.ShapeDtypeStruct((256, 1024), F32),
            jax.ShapeDtypeStruct((256, 1024), BF16),
            jax.ShapeDtypeStruct((256, 512), BF16),
            jax.ShapeDtypeStruct((8, 1024), F32),
            jax.ShapeDtypeStruct((1, 2048), F32),
        ),
        in_specs=[spec(pltpu.VMEM)] * 6 + [spec(pl.ANY), spec(pltpu.VMEM)],
        out_specs=(spec(pltpu.VMEM),) * 7,
        scratch_shapes=[
            pltpu.VMEM((1024, 512), BF16),
            pltpu.VMEM((1024, 2048), BF16),
            pltpu.VMEM((1024, 2048), BF16),
            pltpu.VMEM((256, 1024), F32),
            pltpu.VMEM((2, ROWS, 1024), BF16),
            pltpu.VMEM((2, ROWS, 1024), BF16),
            pltpu.SemaphoreType.DMA((3,)),
            pltpu.SemaphoreType.DMA((2,)),
            pltpu.SemaphoreType.DMA((2,)),
        ],
        compiler_params=pltpu.CompilerParams(
            collective_id=5, has_side_effects=True, vmem_limit_bytes=LIMIT
        ),
        name="backward",
    )(grad, normed2, inverse2, slope, normed1, inverse1, gathered, vectors)


def attend_back_kernel(
    mixed_grad_ref, unit_ref, outcome_ref, logs_ref, first_ref, w_ref, lengths,
    grads_ref, next_ref, sums_ref,
    w_buf, taken, grad_buf, query_sum, key_value_buf, query_buf, sent, landed,
    w_sem, local_sem, send_sem, recv_sem, back_send, back_recv, pair_send, pair_recv,
):
    f = lax.axis_index("fsdp")
    c = lax.axis_index("context")
    t = lax.axis_index("tensor")
    partner = (f, c, 1 - t)
    loads = []
    for j, column in enumerate((512, 1024, 0)):
        load = pltpu.make_async_copy(w_ref.at[:, pl.ds(column, 512)], w_buf.at[j], w_sem.at[j])
        load.start()
        loads.append(load)
    greet([(f, lax.rem(c + d, 8), t) for d in range(1, 8)] + [partner])

    def push(d):
        peer = lax.rem(c + d, 8)
        return remote(
            part(mixed_grad_ref, peer), taken.at[rows_of(c)],
            send_sem.at[d - 1], recv_sem.at[d - 1], (f, peer, t),
        )

    for d in range(1, 8):
        push(d).start()
    keep = pltpu.make_async_copy(part(mixed_grad_ref, c), taken.at[rows_of(c)], local_sem.at[0])
    keep.start()
    scale = jnp.asarray(0.125, BF16)
    queries = jnp.concatenate(
        [by_head(unit_ref[2, pl.ds(block * ROWS, ROWS), :] * scale) for block in range(8)], 0
    )
    logs = jnp.concatenate([logs_ref[block : block + 1, :] for block in range(8)], 1)
    query_sum[...] = jnp.zeros_like(query_sum)
    keep.wait()
    for d in range(1, 8):
        push(d).wait_recv()
    for block in range(8):
        grad_buf[pl.ds(block * 256, 256), :] = by_head(taken[pl.ds(block * ROWS, ROWS), :])
    head_row = lax.broadcasted_iota(jnp.int32, (8, LANES), 0)
    head_lane = lax.broadcasted_iota(jnp.int32, (8, LANES), 1) // HEAD
    chosen = jnp.where(head_row == head_lane, 1.0, 0.0)
    weighted = lax.dot_general(
        chosen, taken[...].astype(F32) * outcome_ref[...],
        (((1,), (1,)), ((), ())), precision=lax.Precision.HIGHEST, preferred_element_type=F32,
    )
    delta = jnp.concatenate(
        [
            weighted[head : head + 1, block * ROWS : (block + 1) * ROWS]
            for block in range(8)
            for head in range(2)
        ],
        1,
    )
    length = lengths[c // 4]

    def answer(j, d):
        peer = lax.rem(c + d, 8)
        source = query_buf if j == 2 else key_value_buf.at[j]
        return remote(
            source.at[rows_of(peer)], part(grads_ref.at[j], c),
            back_send.at[j, d - 1], back_recv.at[j, d - 1], (f, peer, t),
        )

    def step(turn, carry):
        pair = lax.rem(c // 2 + turn, 4)
        spot = pl.ds(pl.multiple_of(pair * 256, 256), 256)
        keys = unit_ref[0, spot, :]
        values = unit_ref[1, spot, :]
        scores = across(keys, queries) + key_mask(length, pair * 256, 256)
        soft = jnp.exp(scores - logs)
        key_value_buf[1, spot, :] = straight(soft.astype(BF16), grad_buf[...]).astype(BF16)
        soft_grad = across(values, grad_buf[...])
        score_grad = (soft * (soft_grad - delta)).astype(BF16)
        key_value_buf[0, spot, :] = straight(score_grad, queries).astype(BF16)
        query_sum[...] += lax.dot_general(
            score_grad, keys, (((0,), (0,)), ((), ())), preferred_element_type=F32
        )

        for side in range(2):
            block = pair * 2 + side
            d = lax.rem(block - c + 8, 8)

            @pl.when(d > 0)
            def _():
                for j in range(2):
                    answer(j, d).start()

        return carry

    lax.fori_loop(1, 5, step, 0)
    first_lane = lax.broadcasted_iota(jnp.int32, (ROWS, LANES), 1) < HEAD
    for block in range(8):
        start = block * 256
        total = jnp.where(
            first_lane,
            query_sum[pl.ds(start, ROWS), :],
            query_sum[pl.ds(start + ROWS, ROWS), :],
        )
        query_buf[pl.ds(block * ROWS, ROWS), :] = (total * 0.125).astype(BF16)
    for d in range(1, 8):
        answer(2, d).start()
    kept = []
    for j in range(3):
        source = query_buf if j == 2 else key_value_buf.at[j]
        keep = pltpu.make_async_copy(source.at[rows_of(c)], part(grads_ref.at[j], c), local_sem.at[j])
        keep.start()
        kept.append(keep)
    for j in range(3):
        kept[j].wait()
        loads[j].wait()
    for j in range(2):
        for d in range(1, 8):
            answer(j, d).wait_recv()
    sums_ref[...] = jnp.zeros_like(sums_ref)
    sums_ref[1:2, :] = jnp.sum(grads_ref[1].astype(F32), 0, keepdims=True)
    early = across(grads_ref[0], w_buf[0]) + across(grads_ref[1], w_buf[1])
    for d in range(1, 8):
        answer(2, d).wait_recv()
    sums_ref[0:1, :] = jnp.sum(grads_ref[2].astype(F32), 0, keepdims=True)
    sent[...] = (early + across(grads_ref[2], w_buf[2])).astype(BF16)
    swap = remote(sent, landed, pair_send, pair_recv, partner)
    swap.start()
    swap.wait()
    next_ref[...] = first_ref[...] + (sent[...].astype(F32) + landed[...].astype(F32))
    for d in range(1, 8):
        push(d).wait_send()
        for j in range(3):
            answer(j, d).wait_send()


def attend_back(mixed_grad, unit, outcome, logs, first, gathered, lengths):
    return pl.pallas_call(
        attend_back_kernel,
        out_shape=(
            jax.ShapeDtypeStruct((3, 256, 512), BF16),
            jax.ShapeDtypeStruct((256, 1024), F32),
            jax.ShapeDtypeStruct((8, 512), F32),
        ),
        in_specs=[spec(pltpu.VMEM)] * 5 + [spec(pl.ANY), spec(pltpu.SMEM)],
        out_specs=(spec(pltpu.VMEM),) * 3,
        scratch_shapes=[
            pltpu.VMEM((3, 1024, 512), BF16),
            pltpu.VMEM((1024, LANES), BF16),
            pltpu.VMEM((2048, LANES), BF16),
            pltpu.VMEM((2048, LANES), F32),
            pltpu.VMEM((2, 1024, LANES), BF16),
            pltpu.VMEM((1024, LANES), BF16),
            pltpu.VMEM((256, 1024), BF16),
            pltpu.VMEM((256, 1024), BF16),
            pltpu.SemaphoreType.DMA((3,)),
            pltpu.SemaphoreType.DMA((3,)),
            pltpu.SemaphoreType.DMA((7,)),
            pltpu.SemaphoreType.DMA((7,)),
            pltpu.SemaphoreType.DMA((3, 7)),
            pltpu.SemaphoreType.DMA((3, 7)),
            pltpu.SemaphoreType.DMA,
            pltpu.SemaphoreType.DMA,
        ],
        compiler_params=pltpu.CompilerParams(
            collective_id=6, has_side_effects=True, vmem_limit_bytes=LIMIT
        ),
        name="attend_back",
    )(mixed_grad, unit, outcome, logs, first, gathered, lengths)


def body(
    stream,
    lengths,
    query_weight,
    query_bias,
    key_weight,
    value_weight,
    value_bias,
    output_weight,
    output_bias,
    first_gain,
    first_shift,
    inner_weight,
    inner_bias,
    outer_weight,
    outer_bias,
    second_gain,
    second_shift,
    cotangent,
):
    slot_count, seq_count, model_width = stream.shape
    row_count = slot_count * seq_count
    position = lax.axis_index("context") * slot_count + jnp.arange(slot_count, dtype=jnp.int32)
    row_live = (position[None, :] < lengths[:, None]).astype(F32).reshape(row_count, 1)
    vectors = jnp.pad(
        jnp.stack([output_bias, outer_bias, first_gain, first_shift, second_gain, second_shift]),
        ((0, LANES - 6), (0, 0)),
    )
    bias = jnp.concatenate([query_bias, value_bias, inner_bias]).astype(F32)[None]
    low = stream.transpose(1, 0, 2).reshape(row_count, model_width)
    (
        result, vectors, squares, gathered, unit, exact, logs, mixed, normed, inverse, middle, act, slope, low_next,
    ) = run_forward(
        low, query_weight, key_weight, value_weight, output_weight, inner_weight, outer_weight, vectors, bias, lengths
    )
    gathered = gathered.reshape(model_width, WIDTH)
    stored = []
    for repeat in range(LAYERS):
        stored.append(
            (
                low_next if repeat else low, mixed[repeat], unit[repeat], exact[repeat], logs[repeat],
                middle[repeat], act[repeat],
                (normed[repeat, 0], inverse[repeat, 0], slope[repeat], normed[repeat, 1], inverse[repeat, 1]),
            )
        )
    result = result.reshape(seq_count, slot_count, model_width).transpose(1, 0, 2)
    grad = cotangent.transpose(1, 0, 2).reshape(row_count, model_width).astype(F32) * row_live
    taken = []
    for repeat in reversed(range(LAYERS)):
        low, mixed, unit, outcome, logs, middle, act, saved = stored[repeat]
        outer_grad, inner_grad, first, attn, mixed_grad, sums, bias = backward(
            grad, saved, gathered, vectors
        )
        qkv, grad, head_sums = attend_back(mixed_grad, unit, outcome, logs, first, gathered, lengths)
        taken.append((low, qkv, attn, mixed, middle, inner_grad, outer_grad, act, sums, bias, head_sums))

    def twice(left, right):
        return sum(
            lax.dot_general(left(t), right(t), (((0,), (0,)), ((), ())), preferred_element_type=F32)
            for t in taken
        )

    sums = taken[0][8] + taken[1][8]
    bias = taken[0][9] + taken[1][9]
    head_sums = taken[0][10] + taken[1][10]
    grads = jnp.concatenate(
        [
            twice(lambda t: t[0], lambda t: t[1][2]),
            twice(lambda t: t[0], lambda t: t[1][0]),
            twice(lambda t: t[0], lambda t: t[1][1]),
            twice(lambda t: t[2], lambda t: t[3]),
            twice(lambda t: t[4], lambda t: t[5]),
            twice(lambda t: t[6], lambda t: t[7]),
            jnp.pad(sums[:6].T, ((0, 0), (0, LANES - 6))),
        ],
        1,
    ).astype(BF16)
    small = jnp.concatenate(
        [
            head_sums[0],
            head_sums[1],
            bias[0],
            jnp.sum(squares[:6], 1),
            jnp.sum(row_live)[None],
            jnp.zeros((1024 - 7,), F32),
        ]
    ).reshape(32, LANES)
    summed, total = scatter_all(grads.reshape(2, 4, 2, 4, 16, grads.shape[1]), small)
    total = total.reshape(-1)
    square_total, count_total = total[3072:3078].reshape(LAYERS, 3), total[3078]
    root_values = jnp.sqrt(square_total / (count_total * model_width) + 1e-06)
    stream_grad = grad.reshape(seq_count, slot_count, model_width).transpose(1, 0, 2)
    return (
        result,
        stream_grad,
        summed[:, 0:512],
        total[0:512],
        summed[:, 512:1024],
        summed[:, 1024:1536],
        total[512:1024],
        summed[:, 1536:2048].T,
        summed[:, 6144],
        summed[:, 6146],
        summed[:, 6147],
        summed[:, 2048:4096],
        total[1024:3072],
        summed[:, 4096:6144].T,
        summed[:, 6145],
        summed[:, 6148],
        summed[:, 6149],
        root_values,
    )


def solution(mesh):
    in_specs = (
        P("context", "fsdp", None),
        P("fsdp"),
        P(("fsdp", "context"), "tensor"),
        P("tensor"),
        P(("fsdp", "context"), "tensor"),
        P(("fsdp", "context"), "tensor"),
        P("tensor"),
        P("tensor", ("fsdp", "context")),
        P(("fsdp", "context")),
        P(("fsdp", "context")),
        P(("fsdp", "context")),
        P(("fsdp", "context"), "tensor"),
        P("tensor"),
        P("tensor", ("fsdp", "context")),
        P(("fsdp", "context")),
        P(("fsdp", "context")),
        P(("fsdp", "context")),
        P("context", "fsdp", None),
    )
    out_specs = (
        P("context", "fsdp", None),
        P("context", "fsdp", None),
        P(("fsdp", "context"), "tensor"),
        P("tensor"),
        P(("fsdp", "context"), "tensor"),
        P(("fsdp", "context"), "tensor"),
        P("tensor"),
        P("tensor", ("fsdp", "context")),
        P(("fsdp", "context")),
        P(("fsdp", "context")),
        P(("fsdp", "context")),
        P(("fsdp", "context"), "tensor"),
        P("tensor"),
        P("tensor", ("fsdp", "context")),
        P(("fsdp", "context")),
        P(("fsdp", "context")),
        P(("fsdp", "context")),
        P(),
    )
    return jax.shard_map(body, mesh=mesh, in_specs=in_specs, out_specs=out_specs, check_vma=False)
```

```python
import jax
import jax.numpy as jnp
from jax import lax
from jax.experimental import pallas as pl
from jax.experimental.pallas import tpu as pltpu
from jax.sharding import PartitionSpec as P

HEAD = 64
LAYERS = 2
LANES = 128
MESH = pl.DeviceIdType.MESH

F32 = jnp.float32
BF16 = jnp.bfloat16
ROWS = 128
LIMIT = 60 * 2**20
WIDTH = 6272
QUERY, KEY, VALUE, OUT, INNER, OUTER, EXTRA = 0, 512, 1024, 1536, 2048, 4096, 6144
GROUPS = ((QUERY, OUT), (OUT, WIDTH))
ORDERS = ("zyx", "yxz", "xzy")
SHARDS = (2, 4, 2, 4)


def spec(space):
    return pl.BlockSpec(memory_space=space)


def place():
    f = lax.axis_index("fsdp")
    c = lax.axis_index("context")
    t = lax.axis_index("tensor")
    return {"x": 2 * (f // 4) + c // 4, "y": c % 4, "z": f % 4, "t": t}


def device(at):
    x = at["x"]
    return ((x // 2) * 4 + at["z"], (x % 2) * 4 + at["y"], at["t"])


def shifted(at, axis, step):
    moved = dict(at)
    moved[axis] = lax.rem(at[axis] + step + 4, 4)
    return moved


def greet(devices):
    barrier = pltpu.get_barrier_semaphore()
    for device_id in devices:
        pl.semaphore_signal(barrier, inc=1, device_id=device_id, device_id_type=MESH)
    pl.semaphore_wait(barrier, len(devices))


def neighbours(at, steps):
    return [device(shifted(at, axis, step)) for axis in "xyz" for step in steps]


def context_peers():
    f = lax.axis_index("fsdp")
    c = lax.axis_index("context")
    t = lax.axis_index("tensor")
    return [(f, lax.rem(c + d, 8), t) for d in range(1, 8)]


def remote(src, dst, send_sem, recv_sem, device_id):
    return pltpu.make_async_remote_copy(
        src_ref=src,
        dst_ref=dst,
        send_sem=send_sem,
        recv_sem=recv_sem,
        device_id=device_id,
        device_id_type=MESH,
    )


def shards(ref, at, whole, cols):
    x = at["x"]
    xh = slice(None) if "x" in whole else x // 2
    xl = slice(None) if "x" in whole else x % 2
    z = slice(None) if "z" in whole else at["z"]
    y = slice(None) if "y" in whole else at["y"]
    return ref.at[xh, z, xl, y, :, pl.ds(cols[0], cols[1])]


def thirds(group):
    start, end = GROUPS[group]
    tiles = (end - start) // LANES
    cuts = [start + tiles * i // 6 * LANES for i in range(7)]
    return [
        ((cuts[2 * i], cuts[2 * i + 1] - cuts[2 * i]), (cuts[2 * i + 1], cuts[2 * i + 2] - cuts[2 * i + 1]))
        for i in range(3)
    ]


def across(left, right):
    return lax.dot_general(left, right, (((1,), (1,)), ((), ())), preferred_element_type=F32)


def straight(left, right):
    return jnp.dot(left, right, preferred_element_type=F32)


def rows_of(block):
    return pl.ds(pl.multiple_of(block * ROWS, ROWS), ROWS)


def by_head(block):
    first = lax.broadcasted_iota(jnp.int32, block.shape, 1) < HEAD
    zero = jnp.zeros_like(block)
    return jnp.concatenate([jnp.where(first, block, zero), jnp.where(first, zero, block)], 0)


def key_mask(length, first, count):
    position = first + lax.broadcasted_iota(jnp.int32, (count, 1), 0)
    return jnp.where(position < length, 0.0, -1e30)


def columns_of(weights, start, width):
    return weights[:, :, :, :, :, pl.ds(start, width)].reshape(1024, width)


def quarter_of(weights, quarter, start, width):
    z = 2 * (quarter % 2)
    return weights[quarter // 2, z : z + 2, :, :, :, start : start + width].reshape(256, width)


def part(ref, peer):
    return ref.at[rows_of(peer // 4), rows_of(peer % 4)]


class Gather:
    def __init__(self, weights, group, send_sem, recv_sem):
        self.at = place()
        self.weights, self.group = weights, group
        self.send_sem, self.recv_sem = send_sem, recv_sem
        self.parts = thirds(group)
        self.sent = {}

    def send(self, third, phase, kind, origin, cols, step):
        order = ORDERS[third]
        block = shards(self.weights, origin, order[:phase], cols)
        index = (self.group, third, phase, kind)
        copy = remote(
            block, block, self.send_sem.at[index], self.recv_sem.at[index],
            device(shifted(self.at, order[phase], step)),
        )
        copy.start()
        self.sent[third, phase, kind] = copy

    def first(self, phase):
        for third in range(3):
            low, high = self.parts[third]
            both = (low[0], low[1] + high[1])
            self.send(third, phase, 0, self.at, both, 1)
            self.send(third, phase, 1, self.at, both, -1)

    def onward(self, phase):
        for third in range(3):
            axis = ORDERS[third][phase]
            low, high = self.parts[third]
            self.sent[third, phase, 0].wait_recv()
            self.send(third, phase, 2, shifted(self.at, axis, -1), low, 1)
            self.sent[third, phase, 1].wait_recv()
            self.send(third, phase, 3, shifted(self.at, axis, 1), high, -1)

    def settle(self, phase):
        for third in range(3):
            self.sent[third, phase, 2].wait_recv()
            self.sent[third, phase, 3].wait_recv()

    def close(self):
        for copy in self.sent.values():
            copy.wait_send()


class Heads:
    def __init__(self, own, unit, outcome, mixed, local_sem, send_sem, recv_sem, back_send, back_recv):
        self.f = lax.axis_index("fsdp")
        self.c = lax.axis_index("context")
        self.t = lax.axis_index("tensor")
        self.own, self.unit, self.outcome, self.mixed = own, unit, outcome, mixed
        self.local_sem, self.send_sem, self.recv_sem = local_sem, send_sem, recv_sem
        self.back_send, self.back_recv = back_send, back_recv

    def push(self, j, d):
        peer = lax.rem(self.c + d, 8)
        return remote(
            part(self.own.at[j], peer), self.unit.at[j, rows_of(self.c)],
            self.send_sem.at[j, d - 1], self.recv_sem.at[j, d - 1], (self.f, peer, self.t),
        )

    def keep(self, j):
        return pltpu.make_async_copy(
            part(self.own.at[j], self.c), self.unit.at[j, rows_of(self.c)], self.local_sem.at[j]
        )

    def answer(self, d):
        peer = lax.rem(self.c + d, 8)
        return remote(
            self.outcome.at[rows_of(peer)], part(self.mixed, self.c),
            self.back_send.at[d - 1], self.back_recv.at[d - 1], (self.f, peer, self.t),
        )

    def keep_back(self):
        return pltpu.make_async_copy(
            self.outcome.at[rows_of(self.c)], part(self.mixed, self.c), self.local_sem.at[3]
        )

    def project(self, x, weights, bias):
        for j, column in enumerate((KEY, VALUE, QUERY)):
            product = straight(x, columns_of(weights, column, 512))
            if j == 1:
                product = product + bias[:, 512:1024]
            if j == 2:
                product = product + bias[:, 0:512]
            self.own[j] = product.astype(BF16)
            for d in (4, 1, 7, 5, 3, 2, 6):
                self.push(j, d).start()
            self.keep(j).start()

    def attend(self, length, exact, logs):
        c = self.c
        for j in range(2):
            self.keep(j).wait()
            for d in range(1, 8):
                self.push(j, d).wait_recv()
        mask = key_mask(length, 0, 8 * ROWS)
        keys = self.unit[0]
        values_across = self.unit[1].T
        self.keep(2).wait()

        def step(d, carry):
            block = lax.rem(c + d, 8)

            @pl.when(d > 0)
            def _():
                self.push(2, 8 - d).wait_recv()

            queries = self.unit[2, rows_of(block), :] * jnp.asarray(0.125, BF16)
            scores = across(keys, by_head(queries)) + mask
            top = jnp.max(scores, 0, keepdims=True)
            exponent = jnp.exp(scores - top)
            total = jnp.sum(exponent, 0, keepdims=True)
            outcome = straight(values_across, exponent.astype(BF16)) / total
            both = jnp.concatenate([outcome[:HEAD, :ROWS], outcome[HEAD:, ROWS:]], 0).T
            exact[rows_of(block), :] = both
            self.outcome[rows_of(block), :] = both.astype(BF16)
            logs[pl.ds(block, 1), :] = top + jnp.log(total)

            @pl.when(d > 0)
            def _():
                self.answer(d).start()

            return carry

        lax.fori_loop(0, 8, step, 0)
        self.keep_back().start()

    def collect(self):
        self.keep_back().wait()
        for d in range(1, 8):
            self.answer(d).wait_recv()

    def close(self):
        for d in range(1, 8):
            self.answer(d).wait_send()
            for j in range(3):
                self.push(j, d).wait_send()


class Joins:
    def __init__(self, sent, landed, send_sem, recv_sem):
        t = lax.axis_index("tensor")
        self.partner = (lax.axis_index("fsdp"), lax.axis_index("context"), 1 - t)
        self.sent, self.landed, self.send_sem, self.recv_sem = sent, landed, send_sem, recv_sem

    def copy(self, half):
        return remote(
            self.sent.at[half], self.landed.at[half], self.send_sem.at[half], self.recv_sem.at[half],
            self.partner,
        )

    def offer(self, quarter, term):
        half, side = quarter // 2, quarter % 2
        self.sent[half, :, side * 256 : side * 256 + 256] = term.astype(BF16)
        if side == 1:
            self.copy(half).start()

    def wait(self):
        for half in range(2):
            self.copy(half).wait_recv()

    def total(self, rows):
        return jnp.concatenate(
            [self.sent[half, rows, :].astype(F32) + self.landed[half, rows, :].astype(F32) for half in range(2)],
            1,
        )

    def close(self):
        for half in range(2):
            self.copy(half).wait_send()


def gelu_parts(argument):
    square = argument * argument
    inner = 0.7978845608028654 * argument * (1.0 + 0.044715 * square)
    bend = jnp.tanh(inner)
    half = 0.5 * (1.0 + bend)
    slope = half + 0.5 * argument * (1.0 - bend * bend) * 0.7978845608028654 * (
        1.0 + 3.0 * 0.044715 * square
    )
    return argument * half, slope


def norm_parts(hidden):
    centre = hidden - jnp.mean(hidden, -1, keepdims=True)
    inverse = lax.rsqrt(jnp.mean(centre * centre, -1, keepdims=True) + 1e-05)
    return centre * inverse, inverse


def live_rows(lengths, block, count):
    c = lax.axis_index("context")
    row = block * count + lax.broadcasted_iota(jnp.int32, (count, 1), 0)
    slot = c * ROWS + lax.rem(row, ROWS)
    return jnp.where(slot < jnp.where(row < ROWS, lengths[0], lengths[1]), 1.0, 0.0)


SLAB = 64


def slab_of(block):
    return pl.ds(pl.multiple_of(block * SLAB, SLAB), SLAB)


def pack(weights, own, query, key, value, output, inner, outer, vectors):
    xh, z, xl, y = own
    eye = jnp.where(
        lax.broadcasted_iota(jnp.int32, (16, 16), 0) == lax.broadcasted_iota(jnp.int32, (16, 16), 1), 1.0, 0.0
    ).astype(BF16)

    def put(start, block):
        weights[xh, z, xl, y, :, start : start + block.shape[1]] = block

    put(QUERY, query[...])
    put(KEY, key[...])
    put(VALUE, value[...])
    put(OUT, across(eye, output[...]).astype(BF16))
    put(INNER, inner[...])
    put(OUTER, across(eye, outer[...]).astype(BF16))
    put(EXTRA, across(eye, vectors[...]).astype(BF16))


def forward_kernel(
    x_ref, query, key, value, output, inner, outer, vectors, bias, lengths,
    result_ref, rows_ref, squares_ref, w_out, unit_out, exact_out, logs_out, mixed_out, normed_out, inverse_out,
    middle_out, act_out, slope_out, low_out,
    weights, own, unit, exact, logs, outcome, mixed, normed, inverse, middle, act, slope, low, current,
    sent, landed,
    local_sem, save_sem, gather_send, gather_recv, send_sem, recv_sem, back_send, back_recv, pair_send, pair_recv,
):
    at = place()
    c = lax.axis_index("context")
    t = lax.axis_index("tensor")
    partner = (lax.axis_index("fsdp"), c, 1 - t)
    x = at["x"]
    pack(weights, (x // 2, at["z"], x % 2, at["y"]), query, key, value, output, inner, outer, vectors)
    greet(neighbours(at, (1, -1)) + context_peers() + [partner])
    one, two = (Gather(weights, group, gather_send, gather_recv) for group in range(2))
    one.first(0)
    two.first(0)
    one.onward(0)
    two.onward(0)
    one.settle(0)
    one.first(1)
    two.settle(0)
    two.first(1)
    one.onward(1)
    two.onward(1)
    one.settle(1)
    one.first(2)
    two.settle(1)
    one.onward(2)
    two.first(2)
    current[...] = x_ref[...].astype(F32)
    one.settle(2)
    squares_ref[...] = jnp.zeros_like(squares_ref)
    length = lengths[c // 4]
    saves = []

    def save(source, target):
        copy = pltpu.make_async_copy(source, target, save_sem.at[len(saves)])
        copy.start()
        saves.append(copy)

    closing = [one, two]
    for layer in range(LAYERS):
        first = layer == 0
        heads = Heads(
            own.at[layer], unit.at[layer], outcome.at[layer], mixed.at[layer], local_sem.at[layer],
            send_sem.at[layer], recv_sem.at[layer], back_send.at[layer], back_recv.at[layer],
        )
        joins = [
            Joins(sent.at[layer, stage], landed.at[layer, stage], pair_send.at[layer, stage], pair_recv.at[layer, stage])
            for stage in range(2)
        ]
        heads.project(x_ref[...] if first else low[...], weights, bias)
        heads.attend(length, exact.at[layer], logs.at[layer])
        if first:
            two.onward(2)
        heads.collect()
        if first:
            two.settle(2)
            save(weights, w_out)
            pick = jnp.where(
                lax.broadcasted_iota(jnp.int32, (8, LANES), 0) == lax.broadcasted_iota(jnp.int32, (8, LANES), 1),
                1.0, 0.0,
            ).astype(BF16)
            rows_ref[...] = across(pick, columns_of(weights, EXTRA, LANES))
        for quarter in range(4):
            joins[0].offer(quarter, across(mixed[layer], quarter_of(weights, quarter, OUT, 512)))
        save(unit.at[layer], unit_out.at[layer])
        save(exact.at[layer], exact_out.at[layer])
        save(logs.at[layer], logs_out.at[layer])
        save(mixed.at[layer], mixed_out.at[layer])
        joins[0].wait()

        def after_attention(block, total):
            rows = slab_of(block)
            live = live_rows(lengths, block, SLAB)
            before = current[rows, :]
            branch = joins[0].total(rows) + rows_ref[0:1, :]
            scaled, root = norm_parts(before + branch)
            after = scaled * rows_ref[2:3, :] + rows_ref[3:4, :]
            normed[layer, 0, rows, :] = scaled
            inverse[layer, 0, rows, :] = root
            current[rows, :] = after
            middle[layer, rows, :] = after.astype(BF16)
            return (
                total[0] + jnp.sum(live * before * before, 0, keepdims=True),
                total[1] + jnp.sum(live * branch * branch, 0, keepdims=True),
            )

        zero = jnp.zeros((1, 1024), F32)
        total = lax.fori_loop(0, 256 // SLAB, after_attention, (zero, zero))
        squares_ref[3 * layer : 3 * layer + 1, :] = total[0]
        squares_ref[3 * layer + 1 : 3 * layer + 2, :] = total[1]
        save(middle.at[layer], middle_out.at[layer])

        def hidden(tile, carry):
            start = pl.multiple_of(tile * 512, 512)
            columns = pl.ds(start, 512)
            pre = straight(middle[layer], columns_of(weights, INNER + start, 512)) + bias[:, pl.ds(1024 + start, 512)]
            act_part, slope_part = gelu_parts(pre)
            act[layer, :, columns] = act_part.astype(BF16)
            slope[layer, :, columns] = slope_part.astype(BF16)
            return carry

        lax.fori_loop(0, 4, hidden, 0)
        for quarter in range(4):
            joins[1].offer(quarter, across(act[layer], quarter_of(weights, quarter, OUTER, 2048)))
        save(act.at[layer], act_out.at[layer])
        save(slope.at[layer], slope_out.at[layer])
        joins[1].wait()

        def after_hidden(block, total):
            rows = slab_of(block)
            live = live_rows(lengths, block, SLAB)
            branch = joins[1].total(rows) + rows_ref[1:2, :]
            scaled, root = norm_parts(current[rows, :] + branch)
            after = scaled * rows_ref[4:5, :] + rows_ref[5:6, :]
            normed[layer, 1, rows, :] = scaled
            inverse[layer, 1, rows, :] = root
            current[rows, :] = after
            if first:
                low[rows, :] = after.astype(BF16)
            else:
                result_ref[rows, :] = (after * live).astype(BF16)
            return total + jnp.sum(live * branch * branch, 0, keepdims=True)

        squares_ref[3 * layer + 2 : 3 * layer + 3, :] = lax.fori_loop(0, 256 // SLAB, after_hidden, zero)
        save(normed.at[layer], normed_out.at[layer])
        save(inverse.at[layer], inverse_out.at[layer])
        if first:
            save(low, low_out)
        closing += [heads] + joins
    for item in closing:
        item.close()
    for copy in saves:
        copy.wait()


def run_forward(x, query, key, value, output, inner, outer, vectors, bias, lengths):
    saved = (
        ((*SHARDS, 16, WIDTH), BF16),
        ((2, 3, 1024, LANES), BF16),
        ((2, 1024, LANES), F32),
        ((2, 8, 256), F32),
        ((2, 256, 512), BF16),
        ((2, 2, 256, 1024), F32),
        ((2, 2, 256, 1), F32),
        ((2, 256, 1024), BF16),
        ((2, 256, 2048), BF16),
        ((2, 256, 2048), BF16),
        ((256, 1024), BF16),
    )
    dma = pltpu.SemaphoreType.DMA
    return pl.pallas_call(
        forward_kernel,
        out_shape=(
            jax.ShapeDtypeStruct((256, 1024), BF16),
            jax.ShapeDtypeStruct((8, 1024), F32),
            jax.ShapeDtypeStruct((8, 1024), F32),
            *(jax.ShapeDtypeStruct(shape, kind) for shape, kind in saved),
        ),
        in_specs=[spec(pltpu.VMEM)] * 9 + [spec(pltpu.SMEM)],
        out_specs=(spec(pltpu.VMEM),) * 3 + (spec(pl.ANY),) * len(saved),
        scratch_shapes=[
            pltpu.VMEM((*SHARDS, 16, WIDTH), BF16),
            pltpu.VMEM((2, 3, 256, 512), BF16),
            pltpu.VMEM((2, 3, 1024, LANES), BF16),
            pltpu.VMEM((2, 1024, LANES), F32),
            pltpu.VMEM((2, 8, 256), F32),
            pltpu.VMEM((2, 1024, LANES), BF16),
            pltpu.VMEM((2, 256, 512), BF16),
            pltpu.VMEM((2, 2, 256, 1024), F32),
            pltpu.VMEM((2, 2, 256, 1), F32),
            pltpu.VMEM((2, 256, 1024), BF16),
            pltpu.VMEM((2, 256, 2048), BF16),
            pltpu.VMEM((2, 256, 2048), BF16),
            pltpu.VMEM((256, 1024), BF16),
            pltpu.VMEM((256, 1024), F32),
            pltpu.VMEM((2, 2, 2, 256, 512), BF16),
            pltpu.VMEM((2, 2, 2, 256, 512), BF16),
            dma((2, 4)),
            dma((24,)),
            dma((2, 3, 3, 4)),
            dma((2, 3, 3, 4)),
            dma((2, 3, 7)),
            dma((2, 3, 7)),
            dma((2, 7)),
            dma((2, 7)),
            dma((2, 2, 2)),
            dma((2, 2, 2)),
        ],
        compiler_params=pltpu.CompilerParams(
            collective_id=3, has_side_effects=True, vmem_limit_bytes=LIMIT
        ),
        name="forward_layers",
    )(x, query, key, value, output, inner, outer, vectors, bias, lengths)


def norm_back(grad_out, normed, inverse, gain):
    scaled = grad_out * gain
    return inverse * (
        scaled
        - jnp.mean(scaled, -1, keepdims=True)
        - normed * jnp.mean(scaled * normed, -1, keepdims=True)
    )


class Scatter:
    def __init__(self, work, group, landings, send_sem, recv_sem):
        self.at = place()
        self.work, self.group, self.landings = work, group, landings
        self.send_sem, self.recv_sem = send_sem, recv_sem
        self.parts = thirds(group)
        self.sent = {}

    def ring(self, third, phase):
        order = ORDERS[third][::-1]
        return order[phase], order[phase + 1 :]

    def send(self, third, phase, kind, away, cols, step):
        axis, whole = self.ring(third, phase)
        land = self.landings[third][phase].at[kind]
        if cols[1] != land.shape[-1]:
            land = land.at[..., pl.ds(0, cols[1])]
        index = (self.group, third, phase, kind)
        copy = remote(
            shards(self.work, shifted(self.at, axis, away), whole, cols), land,
            self.send_sem.at[index], self.recv_sem.at[index], device(shifted(self.at, axis, step)),
        )
        copy.start()
        self.sent[third, phase, kind] = copy

    def add(self, third, phase, away, cols, kinds):
        axis, whole = self.ring(third, phase)
        origin = shifted(self.at, axis, away)
        land = self.landings[third][phase]
        x = origin["x"]
        wide = {name: name in whole for name in "xyz"}
        columns = pl.ds(cols[0], cols[1])

        def one(ix, iz):
            xh, xl = (ix // 2, ix % 2) if wide["x"] else (x // 2, x % 2)
            z = iz if wide["z"] else origin["z"]
            y = slice(None) if wide["y"] else origin["y"]
            index = (xh, z, xl, y, slice(None), columns)
            total = self.work[index].astype(F32)
            for kind in kinds:
                at = (kind,)
                at += (xh,) if wide["x"] else ()
                at += (z,) if wide["z"] else ()
                at += (xl,) if wide["x"] else ()
                at += (slice(None),) if wide["y"] else ()
                total = total + land[at + (slice(None), pl.ds(0, cols[1]))].astype(F32)
            self.work[index] = total.astype(BF16)

        count_x = 4 if wide["x"] else 1
        count_z = 4 if wide["z"] else 1
        if count_x * count_z == 1:
            one(0, 0)
        else:
            def turn(i, carry):
                one(i // count_z, i % count_z)
                return carry

            lax.fori_loop(0, count_x * count_z, turn, 0)

    def first(self, phase, third):
        low, high = self.parts[third]
        self.send(third, phase, 0, 2, low, 1)
        self.send(third, phase, 1, 2, high, -1)
        self.send(third, phase, 2, 1, high, 1)
        self.send(third, phase, 3, -1, low, -1)

    def onward(self, phase, third):
        low, high = self.parts[third]
        self.sent[third, phase, 0].wait_recv()
        self.add(third, phase, 1, low, (0,))
        self.send(third, phase, 4, 1, low, 1)
        self.sent[third, phase, 1].wait_recv()
        self.add(third, phase, -1, high, (1,))
        self.send(third, phase, 5, -1, high, -1)

    def settle(self, phase, third):
        low, high = self.parts[third]
        self.sent[third, phase, 2].wait_recv()
        self.sent[third, phase, 5].wait_recv()
        self.add(third, phase, 0, high, (2, 5))
        self.sent[third, phase, 3].wait_recv()
        self.sent[third, phase, 4].wait_recv()
        self.add(third, phase, 0, low, (3, 4))

    def close(self):
        for copy in self.sent.values():
            copy.wait_send()


def landing_shapes(group):
    shapes = []
    for third in range(3):
        order = ORDERS[third][::-1]
        low, high = thirds(group)[third]
        for phase in range(3):
            whole = order[phase + 1 :]
            shape = [6]
            shape += [2] if "x" in whole else []
            shape += [4] if "z" in whole else []
            shape += [2] if "x" in whole else []
            shape += [4] if "y" in whole else []
            shapes.append(pltpu.VMEM((*shape, 16, max(low[1], high[1])), BF16))
    return shapes


class Totals:
    def __init__(self, total, landed, send_sem, recv_sem):
        self.at = place()
        self.total, self.landed, self.send_sem, self.recv_sem = total, landed, send_sem, recv_sem

    def copy(self, phase, step):
        return remote(
            self.total, self.landed.at[phase, step - 1], self.send_sem.at[phase, step - 1],
            self.recv_sem.at[phase, step - 1], device(shifted(self.at, "xyz"[phase], step)),
        )

    def first(self, phase):
        for step in (1, 2, 3):
            self.copy(phase, step).start()

    def settle(self, phase):
        for step in (1, 2, 3):
            self.copy(phase, step).wait()
        self.total[...] += self.landed[phase, 0] + self.landed[phase, 1] + self.landed[phase, 2]


class HeadsBack:
    def __init__(self, mixed_grad, taken, key_value, query, grads, local_sem, send_sem, recv_sem, back_send, back_recv):
        self.f = lax.axis_index("fsdp")
        self.c = lax.axis_index("context")
        self.t = lax.axis_index("tensor")
        self.mixed_grad, self.taken, self.grads = mixed_grad, taken, grads
        self.sources = (key_value.at[0], key_value.at[1], query)
        self.key_value, self.query = key_value, query
        self.local_sem, self.send_sem, self.recv_sem = local_sem, send_sem, recv_sem
        self.back_send, self.back_recv = back_send, back_recv

    def push(self, d):
        peer = lax.rem(self.c + d, 8)
        return remote(
            part(self.mixed_grad, peer), self.taken.at[rows_of(self.c)],
            self.send_sem.at[d - 1], self.recv_sem.at[d - 1], (self.f, peer, self.t),
        )

    def keep(self):
        return pltpu.make_async_copy(
            part(self.mixed_grad, self.c), self.taken.at[rows_of(self.c)], self.local_sem.at[3]
        )

    def answer(self, j, d):
        peer = lax.rem(self.c + d, 8)
        return remote(
            self.sources[j].at[rows_of(peer)], part(self.grads.at[j], self.c),
            self.back_send.at[j, d - 1], self.back_recv.at[j, d - 1], (self.f, peer, self.t),
        )

    def keep_back(self, j):
        return pltpu.make_async_copy(
            self.sources[j].at[rows_of(self.c)], part(self.grads.at[j], self.c), self.local_sem.at[j]
        )

    def start(self):
        for d in (4, 1, 7, 5, 3, 2, 6):
            self.push(d).start()
        self.keep().start()

    def attend(self, length, unit, exact, logs_ref, grad_buf, query_sum):
        c = self.c
        scale = jnp.asarray(0.125, BF16)
        queries = jnp.concatenate(
            [by_head(unit[2, pl.ds(block * ROWS, ROWS), :] * scale) for block in range(8)], 0
        )
        logs = jnp.concatenate([logs_ref[block : block + 1, :] for block in range(8)], 1)
        query_sum[...] = jnp.zeros_like(query_sum)
        self.keep().wait()
        for d in range(1, 8):
            self.push(d).wait_recv()
        for block in range(8):
            grad_buf[pl.ds(block * 256, 256), :] = by_head(self.taken[pl.ds(block * ROWS, ROWS), :])
        head_row = lax.broadcasted_iota(jnp.int32, (8, LANES), 0)
        head_lane = lax.broadcasted_iota(jnp.int32, (8, LANES), 1) // HEAD
        chosen = jnp.where(head_row == head_lane, 1.0, 0.0)
        weighted = lax.dot_general(
            chosen, self.taken[...].astype(F32) * exact[...],
            (((1,), (1,)), ((), ())), precision=lax.Precision.HIGHEST, preferred_element_type=F32,
        )
        delta = jnp.concatenate(
            [
                weighted[head : head + 1, block * ROWS : (block + 1) * ROWS]
                for block in range(8)
                for head in range(2)
            ],
            1,
        )

        def step(turn, carry):
            pair = lax.rem(c // 2 + turn, 4)
            spot = pl.ds(pl.multiple_of(pair * 256, 256), 256)
            keys = unit[0, spot, :]
            values = unit[1, spot, :]
            scores = across(keys, queries) + key_mask(length, pair * 256, 256)
            soft = jnp.exp(scores - logs)
            self.key_value[1, spot, :] = straight(soft.astype(BF16), grad_buf[...]).astype(BF16)
            soft_grad = across(values, grad_buf[...])
            score_grad = (soft * (soft_grad - delta)).astype(BF16)
            self.key_value[0, spot, :] = straight(score_grad, queries).astype(BF16)
            query_sum[...] += lax.dot_general(
                score_grad, keys, (((0,), (0,)), ((), ())), preferred_element_type=F32
            )

            for side in range(2):
                d = lax.rem(pair * 2 + side - c + 8, 8)

                @pl.when(d > 0)
                def _():
                    for j in range(2):
                        self.answer(j, d).start()

            return carry

        lax.fori_loop(1, 5, step, 0)
        first_lane = lax.broadcasted_iota(jnp.int32, (ROWS, LANES), 1) < HEAD
        for block in range(8):
            start = block * 256
            total = jnp.where(
                first_lane, query_sum[pl.ds(start, ROWS), :], query_sum[pl.ds(start + ROWS, ROWS), :]
            )
            self.query[pl.ds(block * ROWS, ROWS), :] = (total * 0.125).astype(BF16)
        for d in (4, 1, 7, 5, 3, 2, 6):
            self.answer(2, d).start()
        for j in range(3):
            self.keep_back(j).start()

    def collect(self, j):
        self.keep_back(j).wait()
        for d in range(1, 8):
            self.answer(j, d).wait_recv()

    def close(self):
        for d in range(1, 8):
            self.push(d).wait_send()
            for j in range(3):
                self.answer(j, d).wait_send()


def put_quarter(work, quarter, start, value):
    z = 2 * (quarter % 2)
    work[quarter // 2, z : z + 2, :, :, :, pl.ds(start, value.shape[1])] = value.astype(BF16).reshape(
        2, 2, 4, 16, value.shape[1]
    )


def weight_grad(work, start, left, right, width):
    turned = left.T
    tile = 512

    def turn(i, carry):
        offset = pl.multiple_of(i * tile, tile)
        term = right[:, :, pl.ds(offset, tile)].reshape(512, tile)
        for quarter in range(4):
            put_quarter(work, quarter, start + offset, straight(turned[quarter * 256 : quarter * 256 + 256], term))
        return carry

    lax.fori_loop(0, width // tile, turn, 0)


def backward_kernel(
    cotangent, low0, rows_ref, squares, lengths,
    w_in, unit_in, exact_in, logs_in, mixed_in, normed_in, inverse_in, middle_in, act_in, slope_in, low1_in,
    stream_grad, query_out, key_out, value_out, output_out, inner_out, outer_out, vector_out, total_ref, root_ref,
    weights, unit, exact, logs, mixed, normed, inverse, middle, act, slope, low,
    attn_grad, inner_grad, outer_grad, grads, mixed_grad, trunk,
    taken, grad_buf, query_sum, key_value, query_buf, sent, landed, total_land,
    load_sem, local_sem, send_sem, recv_sem, back_send, back_recv, pair_send, pair_recv,
    total_send, total_recv, scatter_send, scatter_recv, *landings,
):
    at = place()
    c = lax.axis_index("context")
    t = lax.axis_index("tensor")
    partner = (lax.axis_index("fsdp"), c, 1 - t)
    loads, started = {}, []

    def load(name, source, target):
        copy = pltpu.make_async_copy(source, target, load_sem.at[len(started)])
        copy.start()
        started.append(copy)
        loads[name] = copy

    def load_weights(name, start, width):
        columns = (slice(None),) * 5 + (pl.ds(start, width),)
        load(name, w_in.at[columns], weights.at[columns])

    load("normed", normed_in.at[1], normed)
    load("inverse", inverse_in.at[1], inverse)
    load_weights("outer", OUTER, 2048)
    load("slope", slope_in.at[1], slope)
    load_weights("inner", INNER, 2048)
    load_weights("out", OUT, 512)
    load("unit", unit_in.at[1], unit)
    load("exact", exact_in.at[1], exact)
    load("logs", logs_in.at[1], logs)
    load_weights("qkv", QUERY, 1536)
    load("act", act_in, act)
    load("mixed", mixed_in, mixed)
    load("middle", middle_in, middle)
    load("low1", low1_in, low.at[1])
    low[0] = low0[...]
    greet(neighbours(at, (1, 2, 3)) + context_peers() + [partner])

    three = [landings[9 * group : 9 * group + 9] for group in range(2)]
    one, two = (
        Scatter(weights, group, [three[group][3 * i : 3 * i + 3] for i in range(3)], scatter_send, scatter_recv)
        for group in range(2)
    )
    zero = jnp.zeros((1, 1024), F32)
    sums = [zero] * 6
    bias_sum = jnp.zeros((1, 2048), F32)
    head_sum = [jnp.zeros((1, 512), F32)] * 2
    length = lengths[c // 4]
    closing = [one, two]
    total_ref[...] = jnp.zeros_like(total_ref)

    for layer in (1, 0):
        last = layer == 0
        joins = [
            Joins(sent.at[layer, stage], landed.at[layer, stage], pair_send.at[layer, stage], pair_recv.at[layer, stage])
            for stage in range(2)
        ]
        heads = HeadsBack(
            mixed_grad.at[layer], taken.at[layer], key_value.at[layer], query_buf.at[layer], grads.at[layer],
            local_sem.at[layer], send_sem.at[layer], recv_sem.at[layer], back_send.at[layer], back_recv.at[layer],
        )
        for name in ("normed", "inverse"):
            loads[name].wait()

        def from_output(block, total):
            rows = slab_of(block)
            if last:
                grad = trunk[rows, :]
            else:
                grad = cotangent[rows, :].astype(F32) * live_rows(lengths, block, SLAB)
            scaled = normed[1, rows, :]
            second = norm_back(grad, scaled, inverse[1, rows, :], rows_ref[4:5, :])
            small = second.astype(BF16)
            trunk[rows, :] = second
            outer_grad[layer, rows, :] = small
            return (
                total[0] + jnp.sum(small.astype(F32), 0, keepdims=True),
                total[1] + jnp.sum(grad * scaled, 0, keepdims=True),
                total[2] + jnp.sum(grad, 0, keepdims=True),
            )

        sums[1], sums[4], sums[5] = lax.fori_loop(0, 256 // SLAB, from_output, (sums[1], sums[4], sums[5]))
        loads["slope"].wait()
        if not last:
            loads["outer"].wait()

        def hidden(tile, carry):
            start = pl.multiple_of(tile * 512, 512)
            columns = pl.ds(start, 512)
            grad = straight(outer_grad[layer], columns_of(weights, OUTER + start, 512))
            small = (grad * slope[:, columns].astype(F32)).astype(BF16)
            inner_grad[layer, :, columns] = small
            total_ref[0:1, columns] += jnp.sum(small.astype(F32), 0, keepdims=True)
            return carry

        lax.fori_loop(0, 4, hidden, 0)
        if not last:
            loads["inner"].wait()
        for quarter in range(4):
            joins[0].offer(quarter, across(inner_grad[layer], quarter_of(weights, quarter, INNER, 2048)))
        joins[0].wait()

        def from_middle(block, total):
            rows = slab_of(block)
            grad = trunk[rows, :] + joins[0].total(rows)
            scaled = normed[0, rows, :]
            first = norm_back(grad, scaled, inverse[0, rows, :], rows_ref[2:3, :])
            small = first.astype(BF16)
            trunk[rows, :] = first
            attn_grad[layer, rows, :] = small
            return (
                total[0] + jnp.sum(small.astype(F32), 0, keepdims=True),
                total[1] + jnp.sum(grad * scaled, 0, keepdims=True),
                total[2] + jnp.sum(grad, 0, keepdims=True),
            )

        sums[0], sums[2], sums[3] = lax.fori_loop(0, 256 // SLAB, from_middle, (sums[0], sums[2], sums[3]))
        if not last:
            loads["out"].wait()
        mixed_grad[layer] = straight(attn_grad[layer], columns_of(weights, OUT, 512)).astype(BF16)
        heads.start()
        if last:
            weight_grad(weights, OUT, attn_grad[...].reshape(512, 1024), mixed, 512)
            weight_grad(weights, INNER, middle[...].reshape(512, 1024), inner_grad, 2048)
            two.first(0, 0)
            weight_grad(weights, OUTER, outer_grad[...].reshape(512, 1024), act, 2048)
            two.first(0, 1)
            columns = jnp.concatenate(sums + [jnp.zeros((LANES - 6, 1024), F32)], 0).T
            weights[:, :, :, :, :, EXTRA:WIDTH] = columns.astype(BF16).reshape(*SHARDS, 16, LANES)
            two.first(0, 2)
        else:
            load("normed", normed_in.at[0], normed)
            load("inverse", inverse_in.at[0], inverse)
            load("slope", slope_in.at[0], slope)
        for name in ("unit", "exact", "logs"):
            loads[name].wait()
        heads.attend(length, unit, exact, logs, grad_buf, query_sum)
        if last:
            for third in range(3):
                two.onward(0, third)
        else:
            load("unit", unit_in.at[0], unit)
            load("exact", exact_in.at[0], exact)
            load("logs", logs_in.at[0], logs)
            loads["qkv"].wait()
        heads.collect(0)
        heads.collect(1)
        head_sum[1] = head_sum[1] + jnp.sum(grads[layer, 1].astype(F32), 0, keepdims=True)
        early = [
            across(grads[layer, 0], quarter_of(weights, quarter, KEY, 512))
            + across(grads[layer, 1], quarter_of(weights, quarter, VALUE, 512))
            for quarter in range(4)
        ]
        heads.collect(2)
        head_sum[0] = head_sum[0] + jnp.sum(grads[layer, 2].astype(F32), 0, keepdims=True)
        for quarter in range(4):
            joins[1].offer(
                quarter, early[quarter] + across(grads[layer, 2], quarter_of(weights, quarter, QUERY, 512))
            )
        if last:
            left = low[...].reshape(512, 1024)
            for start, j in ((KEY, 0), (VALUE, 1), (QUERY, 2)):
                weight_grad(weights, start, left, grads.at[:, j], 512)
            for third in range(3):
                one.first(0, third)
            total_ref[1:2, 0:512] = head_sum[0]
            total_ref[1:2, 512:1024] = head_sum[1]
            total_ref[2:8, 0:1024] = squares[0:6, :]
            count = sum(jnp.clip(lengths[s] - c * ROWS, 0, ROWS) for s in range(2)).astype(F32)
            total_ref[1:2, 1024:1152] = jnp.full((1, LANES), count, F32)
        else:
            for name in ("act", "mixed", "middle", "low1"):
                loads[name].wait()
        joins[1].wait()

        def to_input(block, carry):
            rows = slab_of(block)
            grad = trunk[rows, :] + joins[1].total(rows)
            if last:
                stream_grad[rows, :] = grad
            else:
                trunk[rows, :] = grad
            return carry

        lax.fori_loop(0, 256 // SLAB, to_input, 0)
        closing += [heads] + joins

    totals = Totals(total_ref, total_land, total_send, total_recv)
    thirds_all = range(3)
    totals.first(0)
    for third in thirds_all:
        two.settle(0, third)
        two.first(1, third)
    for third in thirds_all:
        one.onward(0, third)
    totals.settle(0)
    totals.first(1)
    for third in thirds_all:
        two.onward(1, third)
    for third in thirds_all:
        one.settle(0, third)
        one.first(1, third)
    for third in thirds_all:
        two.settle(1, third)
        two.first(2, third)
    totals.settle(1)
    totals.first(2)
    for third in thirds_all:
        one.onward(1, third)
    for third in thirds_all:
        two.onward(2, third)
    for third in thirds_all:
        one.settle(1, third)
        one.first(2, third)
    for third in thirds_all:
        two.settle(2, third)
    totals.settle(2)
    for third in thirds_all:
        one.onward(2, third)
    for third in thirds_all:
        one.settle(2, third)
    x = at["x"]

    def own(start, width):
        return weights[x // 2, at["z"], x % 2, at["y"], :, start : start + width].astype(F32)

    query_out[...] = own(QUERY, 512)
    key_out[...] = own(KEY, 512)
    value_out[...] = own(VALUE, 512)
    output_out[...] = own(OUT, 512).T
    inner_out[...] = own(INNER, 2048)
    outer_out[...] = own(OUTER, 2048).T
    vector_out[...] = own(EXTRA, LANES).T[0:8, :]
    for item in closing:
        item.close()
    scale = 1.0 / (total_ref[1:2, 1024:1025] * 1024.0)
    square = jnp.sum(total_ref[:, 0:1024], 1, keepdims=True)
    root_ref[...] = jnp.broadcast_to(jnp.sqrt(square * scale + 1e-06), root_ref.shape)


def run_backward(cotangent, low, rows, squares, lengths, saved):
    dma = pltpu.SemaphoreType.DMA
    out = lambda *shape: jax.ShapeDtypeStruct(shape, F32)
    return pl.pallas_call(
        backward_kernel,
        out_shape=(
            out(256, 1024), out(16, 512), out(16, 512), out(16, 512), out(512, 16), out(16, 2048), out(2048, 16),
            out(8, 16), out(8, 2048), out(8, LANES),
        ),
        in_specs=[spec(pltpu.VMEM)] * 4 + [spec(pltpu.SMEM)] + [spec(pl.ANY)] * len(saved),
        out_specs=(spec(pltpu.VMEM),) * 10,
        scratch_shapes=[
            pltpu.VMEM((*SHARDS, 16, WIDTH), BF16),
            pltpu.VMEM((3, 1024, LANES), BF16),
            pltpu.VMEM((1024, LANES), F32),
            pltpu.VMEM((8, 256), F32),
            pltpu.VMEM((2, 256, 512), BF16),
            pltpu.VMEM((2, 256, 1024), F32),
            pltpu.VMEM((2, 256, 1), F32),
            pltpu.VMEM((2, 256, 1024), BF16),
            pltpu.VMEM((2, 256, 2048), BF16),
            pltpu.VMEM((256, 2048), BF16),
            pltpu.VMEM((2, 256, 1024), BF16),
            pltpu.VMEM((2, 256, 1024), BF16),
            pltpu.VMEM((2, 256, 2048), BF16),
            pltpu.VMEM((2, 256, 1024), BF16),
            pltpu.VMEM((2, 3, 256, 512), BF16),
            pltpu.VMEM((2, 256, 512), BF16),
            pltpu.VMEM((256, 1024), F32),
            pltpu.VMEM((2, 1024, LANES), BF16),
            pltpu.VMEM((2048, LANES), BF16),
            pltpu.VMEM((2048, LANES), F32),
            pltpu.VMEM((2, 2, 1024, LANES), BF16),
            pltpu.VMEM((2, 1024, LANES), BF16),
            pltpu.VMEM((2, 2, 2, 256, 512), BF16),
            pltpu.VMEM((2, 2, 2, 256, 512), BF16),
            pltpu.VMEM((3, 3, 8, 2048), F32),
            dma((32,)),
            dma((2, 4)),
            dma((2, 7)),
            dma((2, 7)),
            dma((2, 3, 7)),
            dma((2, 3, 7)),
            dma((2, 2, 2)),
            dma((2, 2, 2)),
            dma((3, 3)),
            dma((3, 3)),
            dma((2, 3, 3, 6)),
            dma((2, 3, 3, 6)),
            *landing_shapes(0),
            *landing_shapes(1),
        ],
        compiler_params=pltpu.CompilerParams(
            collective_id=4, has_side_effects=True, vmem_limit_bytes=LIMIT
        ),
        name="backward_layers",
    )(cotangent, low, rows, squares, lengths, *saved)


def body(
    stream,
    lengths,
    query_weight,
    query_bias,
    key_weight,
    value_weight,
    value_bias,
    output_weight,
    output_bias,
    first_gain,
    first_shift,
    inner_weight,
    inner_bias,
    outer_weight,
    outer_bias,
    second_gain,
    second_shift,
    cotangent,
):
    slot_count, seq_count, model_width = stream.shape
    row_count = slot_count * seq_count
    vectors = jnp.pad(
        jnp.stack([output_bias, outer_bias, first_gain, first_shift, second_gain, second_shift]),
        ((0, LANES - 6), (0, 0)),
    )
    bias = jnp.concatenate([query_bias, value_bias, inner_bias]).astype(F32)[None]
    low = stream.transpose(1, 0, 2).reshape(row_count, model_width)
    result, rows, squares, *saved = run_forward(
        low, query_weight, key_weight, value_weight, output_weight, inner_weight, outer_weight, vectors, bias, lengths
    )
    grad = cotangent.transpose(1, 0, 2).reshape(row_count, model_width)
    (
        stream_grad, grad_query, grad_key, grad_value, grad_output, grad_inner, grad_outer, grad_vectors, totals, roots,
    ) = run_backward(grad, low, rows, squares, lengths, saved)

    def slots_first(matrix):
        return matrix.reshape(seq_count, slot_count, model_width).transpose(1, 0, 2)

    return (
        slots_first(result),
        slots_first(stream_grad),
        grad_query,
        totals[1, 0:512],
        grad_key,
        grad_value,
        totals[1, 512:1024],
        grad_output,
        grad_vectors[0],
        grad_vectors[2],
        grad_vectors[3],
        grad_inner,
        totals[0],
        grad_outer,
        grad_vectors[1],
        grad_vectors[4],
        grad_vectors[5],
        roots[2:8, 0].reshape(LAYERS, 3),
    )


def solution(mesh):
    in_specs = (
        P("context", "fsdp", None),
        P("fsdp"),
        P(("fsdp", "context"), "tensor"),
        P("tensor"),
        P(("fsdp", "context"), "tensor"),
        P(("fsdp", "context"), "tensor"),
        P("tensor"),
        P("tensor", ("fsdp", "context")),
        P(("fsdp", "context")),
        P(("fsdp", "context")),
        P(("fsdp", "context")),
        P(("fsdp", "context"), "tensor"),
        P("tensor"),
        P("tensor", ("fsdp", "context")),
        P(("fsdp", "context")),
        P(("fsdp", "context")),
        P(("fsdp", "context")),
        P("context", "fsdp", None),
    )
    out_specs = (
        P("context", "fsdp", None),
        P("context", "fsdp", None),
        P(("fsdp", "context"), "tensor"),
        P("tensor"),
        P(("fsdp", "context"), "tensor"),
        P(("fsdp", "context"), "tensor"),
        P("tensor"),
        P("tensor", ("fsdp", "context")),
        P(("fsdp", "context")),
        P(("fsdp", "context")),
        P(("fsdp", "context")),
        P(("fsdp", "context"), "tensor"),
        P("tensor"),
        P("tensor", ("fsdp", "context")),
        P(("fsdp", "context")),
        P(("fsdp", "context")),
        P(("fsdp", "context")),
        P(),
    )
    return jax.shard_map(body, mesh=mesh, in_specs=in_specs, out_specs=out_specs, check_vma=False)
```

```python
import jax
import jax.numpy as jnp
from jax import lax
from jax.experimental import pallas as pl
from jax.experimental.pallas import tpu as pltpu
from jax.sharding import PartitionSpec as P

HEAD = 64
LAYERS = 2
LANES = 128
MESH = pl.DeviceIdType.MESH

F32 = jnp.float32
BF16 = jnp.bfloat16
ROWS = 128
LIMIT = 60 * 2**20
WIDTH = 6272
QUERY, KEY, VALUE, OUT, EXTRA, INNER, OUTER = 0, 512, 1024, 1536, 2048, 2176, 4224
GROUPS = ((QUERY, OUT), (OUT, WIDTH))
ORDERS = ("zyx", "yxz", "xzy")
SHARDS = (2, 4, 2, 4)


def spec(space):
    return pl.BlockSpec(memory_space=space)


def place():
    f = lax.axis_index("fsdp")
    c = lax.axis_index("context")
    t = lax.axis_index("tensor")
    return {"x": 2 * (f // 4) + c // 4, "y": c % 4, "z": f % 4, "t": t}


def device(at):
    x = at["x"]
    return ((x // 2) * 4 + at["z"], (x % 2) * 4 + at["y"], at["t"])


def shifted(at, axis, step):
    moved = dict(at)
    moved[axis] = lax.rem(at[axis] + step + 4, 4)
    return moved


def greet(devices):
    barrier = pltpu.get_barrier_semaphore()
    for device_id in devices:
        pl.semaphore_signal(barrier, inc=1, device_id=device_id, device_id_type=MESH)
    pl.semaphore_wait(barrier, len(devices))


def neighbours(at, steps):
    return [device(shifted(at, axis, step)) for axis in "xyz" for step in steps]


def context_peers():
    f = lax.axis_index("fsdp")
    c = lax.axis_index("context")
    t = lax.axis_index("tensor")
    return [(f, lax.rem(c + d, 8), t) for d in range(1, 8)]


def remote(src, dst, send_sem, recv_sem, device_id):
    return pltpu.make_async_remote_copy(
        src_ref=src,
        dst_ref=dst,
        send_sem=send_sem,
        recv_sem=recv_sem,
        device_id=device_id,
        device_id_type=MESH,
    )


def shards(ref, at, whole, cols):
    x = at["x"]
    xh = slice(None) if "x" in whole else x // 2
    xl = slice(None) if "x" in whole else x % 2
    z = slice(None) if "z" in whole else at["z"]
    y = slice(None) if "y" in whole else at["y"]
    return ref.at[xh, z, xl, y, :, pl.ds(cols[0], cols[1])]


def thirds(group):
    start, end = GROUPS[group]
    tiles = (end - start) // LANES
    cuts = [start + tiles * i // 6 * LANES for i in range(7)]
    return [
        ((cuts[2 * i], cuts[2 * i + 1] - cuts[2 * i]), (cuts[2 * i + 1], cuts[2 * i + 2] - cuts[2 * i + 1]))
        for i in range(3)
    ]


def across(left, right):
    return lax.dot_general(left, right, (((1,), (1,)), ((), ())), preferred_element_type=F32)


def straight(left, right):
    return jnp.dot(left, right, preferred_element_type=F32)


def rows_of(block):
    return pl.ds(pl.multiple_of(block * ROWS, ROWS), ROWS)


def by_head(block):
    first = lax.broadcasted_iota(jnp.int32, block.shape, 1) < HEAD
    zero = jnp.zeros_like(block)
    return jnp.concatenate([jnp.where(first, block, zero), jnp.where(first, zero, block)], 0)


def key_mask(length, first, count):
    position = first + lax.broadcasted_iota(jnp.int32, (count, 1), 0)
    return jnp.where(position < length, 0.0, -1e30)


def columns_of(weights, start, width):
    return weights[:, :, :, :, :, pl.ds(start, width)].reshape(1024, width)


def quarter_of(weights, quarter, start, width):
    z = 2 * (quarter % 2)
    return weights[quarter // 2, z : z + 2, :, :, :, start : start + width].reshape(256, width)


def part(ref, peer):
    return ref.at[rows_of(peer // 4), rows_of(peer % 4)]


class Gather:
    def __init__(self, weights, group, send_sem, recv_sem):
        self.at = place()
        self.weights, self.group = weights, group
        self.send_sem, self.recv_sem = send_sem, recv_sem
        self.parts = thirds(group)
        self.sent = {}

    def send(self, third, phase, kind, origin, cols, step):
        order = ORDERS[third]
        block = shards(self.weights, origin, order[:phase], cols)
        index = (self.group, third, phase, kind)
        copy = remote(
            block, block, self.send_sem.at[index], self.recv_sem.at[index],
            device(shifted(self.at, order[phase], step)),
        )
        copy.start()
        self.sent[third, phase, kind] = copy

    def first(self, phase):
        for third in range(3):
            low, high = self.parts[third]
            both = (low[0], low[1] + high[1])
            self.send(third, phase, 0, self.at, both, 1)
            self.send(third, phase, 1, self.at, both, -1)

    def direct(self, phase):
        for third in range(3):
            low, high = self.parts[third]
            for step in (1, 2, 3):
                self.send(third, phase, step - 1, self.at, (low[0], low[1] + high[1]), step)

    def arrive(self, phase):
        for third in range(3):
            for kind in range(3):
                self.sent[third, phase, kind].wait_recv()

    def onward(self, phase):
        for third in range(3):
            axis = ORDERS[third][phase]
            low, high = self.parts[third]
            self.sent[third, phase, 0].wait_recv()
            self.send(third, phase, 2, shifted(self.at, axis, -1), low, 1)
            self.sent[third, phase, 1].wait_recv()
            self.send(third, phase, 3, shifted(self.at, axis, 1), high, -1)

    def settle(self, phase):
        for third in range(3):
            self.sent[third, phase, 2].wait_recv()
            self.sent[third, phase, 3].wait_recv()

    def close(self):
        for copy in self.sent.values():
            copy.wait_send()


class Heads:
    def __init__(self, own, unit, outcome, mixed, local_sem, send_sem, recv_sem, back_send, back_recv):
        self.f = lax.axis_index("fsdp")
        self.c = lax.axis_index("context")
        self.t = lax.axis_index("tensor")
        self.own, self.unit, self.outcome, self.mixed = own, unit, outcome, mixed
        self.local_sem, self.send_sem, self.recv_sem = local_sem, send_sem, recv_sem
        self.back_send, self.back_recv = back_send, back_recv

    def push(self, j, d):
        peer = lax.rem(self.c + d, 8)
        return remote(
            part(self.own.at[j], peer), self.unit.at[j, rows_of(self.c)],
            self.send_sem.at[j, d - 1], self.recv_sem.at[j, d - 1], (self.f, peer, self.t),
        )

    def keep(self, j):
        return pltpu.make_async_copy(
            part(self.own.at[j], self.c), self.unit.at[j, rows_of(self.c)], self.local_sem.at[j]
        )

    def answer(self, d):
        peer = lax.rem(self.c + d, 8)
        return remote(
            self.outcome.at[rows_of(peer)], part(self.mixed, self.c),
            self.back_send.at[d - 1], self.back_recv.at[d - 1], (self.f, peer, self.t),
        )

    def keep_back(self):
        return pltpu.make_async_copy(
            self.outcome.at[rows_of(self.c)], part(self.mixed, self.c), self.local_sem.at[3]
        )

    def project(self, x, weights, bias):
        for j, column in enumerate((KEY, VALUE, QUERY)):
            product = straight(x, columns_of(weights, column, 512))
            if j == 1:
                product = product + bias[:, 512:1024]
            if j == 2:
                product = product + bias[:, 0:512]
            self.own[j] = product.astype(BF16)
            for d in (4, 1, 7, 5, 3, 2, 6):
                self.push(j, d).start()
            self.keep(j).start()

    def attend(self, length, exact, logs, midway):
        c = self.c
        for j in range(2):
            self.keep(j).wait()
            for d in range(1, 8):
                self.push(j, d).wait_recv()
        mask = key_mask(length, 0, 8 * ROWS)
        keys = self.unit[0]
        values_across = self.unit[1].T
        self.keep(2).wait()

        def step(d, carry):
            block = lax.rem(c + d, 8)

            @pl.when(d > 0)
            def _():
                self.push(2, 8 - d).wait_recv()

            queries = self.unit[2, rows_of(block), :] * jnp.asarray(0.125, BF16)
            scores = across(keys, by_head(queries)) + mask
            top = jnp.max(scores, 0, keepdims=True)
            exponent = jnp.exp(scores - top)
            total = jnp.sum(exponent, 0, keepdims=True)
            outcome = straight(values_across, exponent.astype(BF16)) / total
            both = jnp.concatenate([outcome[:HEAD, :ROWS], outcome[HEAD:, ROWS:]], 0).T
            exact[rows_of(block), :] = both
            self.outcome[rows_of(block), :] = both.astype(BF16)
            logs[pl.ds(block, 1), :] = top + jnp.log(total)

            @pl.when(d > 0)
            def _():
                self.answer(d).start()

            return carry

        lax.fori_loop(0, 4, step, 0)
        midway()
        lax.fori_loop(4, 8, step, 0)
        self.keep_back().start()

    def collect(self):
        self.keep_back().wait()
        for d in range(1, 8):
            self.answer(d).wait_recv()

    def close(self):
        for d in range(1, 8):
            self.answer(d).wait_send()
            for j in range(3):
                self.push(j, d).wait_send()


class Joins:
    def __init__(self, sent, landed, send_sem, recv_sem):
        t = lax.axis_index("tensor")
        self.partner = (lax.axis_index("fsdp"), lax.axis_index("context"), 1 - t)
        self.sent, self.landed, self.send_sem, self.recv_sem = sent, landed, send_sem, recv_sem

    def copy(self, half):
        return remote(
            self.sent.at[half], self.landed.at[half], self.send_sem.at[half], self.recv_sem.at[half],
            self.partner,
        )

    def offer(self, quarter, term):
        half, side = quarter // 2, quarter % 2
        self.sent[half, :, side * 256 : side * 256 + 256] = term.astype(BF16)
        if side == 1:
            self.copy(half).start()

    def wait(self):
        for half in range(2):
            self.copy(half).wait_recv()

    def total(self, rows):
        return jnp.concatenate(
            [self.sent[half, rows, :].astype(F32) + self.landed[half, rows, :].astype(F32) for half in range(2)],
            1,
        )

    def close(self):
        for half in range(2):
            self.copy(half).wait_send()


def gelu_parts(argument):
    square = argument * argument
    inner = 0.7978845608028654 * argument * (1.0 + 0.044715 * square)
    bend = jnp.tanh(inner)
    half = 0.5 * (1.0 + bend)
    slope = half + 0.5 * argument * (1.0 - bend * bend) * 0.7978845608028654 * (
        1.0 + 3.0 * 0.044715 * square
    )
    return argument * half, slope


def norm_parts(hidden):
    centre = hidden - jnp.mean(hidden, -1, keepdims=True)
    inverse = lax.rsqrt(jnp.mean(centre * centre, -1, keepdims=True) + 1e-05)
    return centre * inverse, inverse


def live_rows(lengths, block, count):
    c = lax.axis_index("context")
    row = block * count + lax.broadcasted_iota(jnp.int32, (count, 1), 0)
    slot = c * ROWS + lax.rem(row, ROWS)
    return jnp.where(slot < jnp.where(row < ROWS, lengths[0], lengths[1]), 1.0, 0.0)


SLAB = 64


def slab_of(block):
    return pl.ds(pl.multiple_of(block * SLAB, SLAB), SLAB)


def pack(weights, own, query, key, value, output, inner, outer, vectors):
    xh, z, xl, y = own

    def put(start, block):
        weights[xh, z, xl, y, :, start : start + block.shape[1]] = block

    put(QUERY, query[...])
    put(KEY, key[...])
    put(VALUE, value[...])
    put(OUT, output[...])
    put(INNER, inner[...])
    put(OUTER, outer[...])
    eye = jnp.where(
        lax.broadcasted_iota(jnp.int32, (16, 16), 0) == lax.broadcasted_iota(jnp.int32, (16, 16), 1), 1.0, 0.0
    ).astype(BF16)
    rows = [vector[...].astype(F32).reshape(1, 16) for vector in vectors]
    table = jnp.concatenate(rows + [jnp.zeros((LANES - 6, 16), F32)], 0).astype(BF16)
    put(EXTRA, across(eye, table).astype(BF16))


def rows_by_sequence(source, target, keep):
    whole = source[...].astype(F32)
    for s in range(2):
        target[s * ROWS : s * ROWS + ROWS, :] = (whole[:, s, :] * keep(s)).astype(target.dtype)


def forward_kernel(
    stream, cotangent, query, key, value, output, inner, outer, bias0, bias1, gain1, shift1, gain2, shift2,
    query_bias, value_bias, inner_bias, lengths,
    x_ref, grad_ref, result_ref, rows_ref, squares_ref, w_out, unit_out, exact_out, logs_out, mixed_out, normed_out, inverse_out,
    middle_out, act_out, slope_out, low_out,
    weights, bias, own, unit, exact, logs, outcome, mixed, normed, inverse, middle, act, slope, low, current,
    sent, landed,
    local_sem, save_sem, gather_send, gather_recv, send_sem, recv_sem, back_send, back_recv, pair_send, pair_recv,
):
    at = place()
    c = lax.axis_index("context")
    t = lax.axis_index("tensor")
    partner = (lax.axis_index("fsdp"), c, 1 - t)
    x = at["x"]
    pack(
        weights, (x // 2, at["z"], x % 2, at["y"]), query, key, value, output, inner, outer,
        (bias0, bias1, gain1, shift1, gain2, shift2),
    )
    greet(neighbours(at, (1, 2, 3)) + context_peers() + [partner])
    one, two = (Gather(weights, group, gather_send, gather_recv) for group in range(2))
    one.direct(0)
    two.direct(0)
    rows_by_sequence(stream, x_ref, lambda s: 1.0)
    one.arrive(0)
    one.direct(1)
    two.arrive(0)
    two.first(1)
    bias[:, 0:512] = query_bias[...].astype(F32).reshape(1, 512)
    bias[:, 512:1024] = value_bias[...].astype(F32).reshape(1, 512)
    bias[:, 1024:3072] = inner_bias[...].astype(F32).reshape(1, 2048)
    one.arrive(1)
    one.first(2)
    two.onward(1)
    position = c * ROWS + lax.broadcasted_iota(jnp.int32, (ROWS, 1), 0)
    rows_by_sequence(cotangent, grad_ref, lambda s: jnp.where(position < lengths[s], 1.0, 0.0))
    current[...] = x_ref[...].astype(F32)
    one.onward(2)
    two.settle(1)
    two.first(2)
    one.settle(2)
    squares_ref[...] = jnp.zeros_like(squares_ref)
    length = lengths[c // 4]
    saves = []

    def save(source, target):
        copy = pltpu.make_async_copy(source, target, save_sem.at[len(saves)])
        copy.start()
        saves.append(copy)

    closing = [one, two]
    for layer in range(LAYERS):
        first = layer == 0
        heads = Heads(
            own.at[layer], unit.at[layer], outcome.at[layer], mixed.at[layer], local_sem.at[layer],
            send_sem.at[layer], recv_sem.at[layer], back_send.at[layer], back_recv.at[layer],
        )
        joins = [
            Joins(sent.at[layer, stage], landed.at[layer, stage], pair_send.at[layer, stage], pair_recv.at[layer, stage])
            for stage in range(2)
        ]
        heads.project(x_ref[...] if first else low[...], weights, bias)
        heads.attend(length, exact.at[layer], logs.at[layer], (lambda: two.onward(2)) if first else (lambda: None))
        heads.collect()
        if first:
            two.settle(2)
            save(weights, w_out)
            pick = jnp.where(
                lax.broadcasted_iota(jnp.int32, (8, LANES), 0) == lax.broadcasted_iota(jnp.int32, (8, LANES), 1),
                1.0, 0.0,
            ).astype(BF16)
            rows_ref[...] = across(pick, columns_of(weights, EXTRA, LANES))
        for quarter in range(4):
            joins[0].offer(quarter, across(mixed[layer], quarter_of(weights, quarter, OUT, 512)))
        save(unit.at[layer], unit_out.at[layer])
        save(exact.at[layer], exact_out.at[layer])
        save(logs.at[layer], logs_out.at[layer])
        save(mixed.at[layer], mixed_out.at[layer])
        joins[0].wait()

        def after_attention(block, total):
            rows = slab_of(block)
            live = live_rows(lengths, block, SLAB)
            before = current[rows, :]
            branch = joins[0].total(rows) + rows_ref[0:1, :]
            scaled, root = norm_parts(before + branch)
            after = scaled * rows_ref[2:3, :] + rows_ref[3:4, :]
            normed[layer, 0, rows, :] = scaled
            inverse[layer, 0, rows, :] = root
            current[rows, :] = after
            middle[layer, rows, :] = after.astype(BF16)
            return (
                total[0] + jnp.sum(live * before * before, 0, keepdims=True),
                total[1] + jnp.sum(live * branch * branch, 0, keepdims=True),
            )

        zero = jnp.zeros((1, 1024), F32)
        total = lax.fori_loop(0, 256 // SLAB, after_attention, (zero, zero))
        squares_ref[3 * layer : 3 * layer + 1, :] = total[0]
        squares_ref[3 * layer + 1 : 3 * layer + 2, :] = total[1]
        save(middle.at[layer], middle_out.at[layer])

        def hidden(tile, carry):
            start = pl.multiple_of(tile * 512, 512)
            columns = pl.ds(start, 512)
            pre = straight(middle[layer], columns_of(weights, INNER + start, 512)) + bias[:, pl.ds(1024 + start, 512)]
            act_part, slope_part = gelu_parts(pre)
            act[layer, :, columns] = act_part.astype(BF16)
            slope[layer, :, columns] = slope_part.astype(BF16)
            return carry

        lax.fori_loop(0, 4, hidden, 0)
        for quarter in range(4):
            joins[1].offer(quarter, across(act[layer], quarter_of(weights, quarter, OUTER, 2048)))
        save(act.at[layer], act_out.at[layer])
        save(slope.at[layer], slope_out.at[layer])
        joins[1].wait()

        def after_hidden(block, total):
            rows = slab_of(block)
            live = live_rows(lengths, block, SLAB)
            branch = joins[1].total(rows) + rows_ref[1:2, :]
            scaled, root = norm_parts(current[rows, :] + branch)
            after = scaled * rows_ref[4:5, :] + rows_ref[5:6, :]
            normed[layer, 1, rows, :] = scaled
            inverse[layer, 1, rows, :] = root
            current[rows, :] = after
            if first:
                low[rows, :] = after.astype(BF16)
            else:
                result_ref[rows, :] = (after * live).astype(BF16)
            return total + jnp.sum(live * branch * branch, 0, keepdims=True)

        squares_ref[3 * layer + 2 : 3 * layer + 3, :] = lax.fori_loop(0, 256 // SLAB, after_hidden, zero)
        save(normed.at[layer], normed_out.at[layer])
        save(inverse.at[layer], inverse_out.at[layer])
        if first:
            save(low, low_out)
        closing += [heads] + joins
    for item in closing:
        item.close()
    for copy in saves:
        copy.wait()


def run_forward(*arguments):
    saved = (
        ((*SHARDS, 16, WIDTH), BF16),
        ((2, 3, 1024, LANES), BF16),
        ((2, 1024, LANES), F32),
        ((2, 8, 256), F32),
        ((2, 256, 512), BF16),
        ((2, 2, 256, 1024), F32),
        ((2, 2, 256, 1), F32),
        ((2, 256, 1024), BF16),
        ((2, 256, 2048), BF16),
        ((2, 256, 2048), BF16),
        ((256, 1024), BF16),
    )
    dma = pltpu.SemaphoreType.DMA
    return pl.pallas_call(
        forward_kernel,
        out_shape=(
            jax.ShapeDtypeStruct((256, 1024), BF16),
            jax.ShapeDtypeStruct((256, 1024), BF16),
            jax.ShapeDtypeStruct((256, 1024), BF16),
            jax.ShapeDtypeStruct((8, 1024), F32),
            jax.ShapeDtypeStruct((8, 1024), F32),
            *(jax.ShapeDtypeStruct(shape, kind) for shape, kind in saved),
        ),
        in_specs=[spec(pltpu.VMEM)] * 17 + [spec(pltpu.SMEM)],
        out_specs=(spec(pltpu.VMEM),) * 5 + (spec(pl.ANY),) * len(saved),
        scratch_shapes=[
            pltpu.VMEM((*SHARDS, 16, WIDTH), BF16),
            pltpu.VMEM((1, 3072), F32),
            pltpu.VMEM((2, 3, 256, 512), BF16),
            pltpu.VMEM((2, 3, 1024, LANES), BF16),
            pltpu.VMEM((2, 1024, LANES), F32),
            pltpu.VMEM((2, 8, 256), F32),
            pltpu.VMEM((2, 1024, LANES), BF16),
            pltpu.VMEM((2, 256, 512), BF16),
            pltpu.VMEM((2, 2, 256, 1024), F32),
            pltpu.VMEM((2, 2, 256, 1), F32),
            pltpu.VMEM((2, 256, 1024), BF16),
            pltpu.VMEM((2, 256, 2048), BF16),
            pltpu.VMEM((2, 256, 2048), BF16),
            pltpu.VMEM((256, 1024), BF16),
            pltpu.VMEM((256, 1024), F32),
            pltpu.VMEM((2, 2, 2, 256, 512), BF16),
            pltpu.VMEM((2, 2, 2, 256, 512), BF16),
            dma((2, 4)),
            dma((24,)),
            dma((2, 3, 3, 4)),
            dma((2, 3, 3, 4)),
            dma((2, 3, 7)),
            dma((2, 3, 7)),
            dma((2, 7)),
            dma((2, 7)),
            dma((2, 2, 2)),
            dma((2, 2, 2)),
        ],
        compiler_params=pltpu.CompilerParams(
            collective_id=3, has_side_effects=True, vmem_limit_bytes=LIMIT
        ),
        name="forward_layers",
    )(*arguments)


def norm_back(grad_out, normed, inverse, gain):
    scaled = grad_out * gain
    return inverse * (
        scaled
        - jnp.mean(scaled, -1, keepdims=True)
        - normed * jnp.mean(scaled * normed, -1, keepdims=True)
    )


class Scatter:
    def __init__(self, work, group, landings, send_sem, recv_sem):
        self.at = place()
        self.work, self.group, self.landings = work, group, landings
        self.send_sem, self.recv_sem = send_sem, recv_sem
        self.parts = thirds(group)
        self.sent = {}

    def ring(self, third, phase):
        order = ORDERS[third][::-1]
        return order[phase], order[phase + 1 :]

    def send(self, third, phase, kind, away, cols, step):
        axis, whole = self.ring(third, phase)
        land = self.landings[third][phase].at[kind]
        if cols[1] != land.shape[-1]:
            land = land.at[..., pl.ds(0, cols[1])]
        index = (self.group, third, phase, kind)
        copy = remote(
            shards(self.work, shifted(self.at, axis, away), whole, cols), land,
            self.send_sem.at[index], self.recv_sem.at[index], device(shifted(self.at, axis, step)),
        )
        copy.start()
        self.sent[third, phase, kind] = copy

    def add(self, third, phase, away, cols, kinds):
        axis, whole = self.ring(third, phase)
        origin = shifted(self.at, axis, away)
        land = self.landings[third][phase]
        x = origin["x"]
        wide = {name: name in whole for name in "xyz"}
        columns = pl.ds(cols[0], cols[1])

        def one(ix, iz):
            xh, xl = (ix // 2, ix % 2) if wide["x"] else (x // 2, x % 2)
            z = iz if wide["z"] else origin["z"]
            y = slice(None) if wide["y"] else origin["y"]
            index = (xh, z, xl, y, slice(None), columns)
            total = self.work[index].astype(F32)
            for kind in kinds:
                at = (kind,)
                at += (xh,) if wide["x"] else ()
                at += (z,) if wide["z"] else ()
                at += (xl,) if wide["x"] else ()
                at += (slice(None),) if wide["y"] else ()
                total = total + land[at + (slice(None), pl.ds(0, cols[1]))].astype(F32)
            self.work[index] = total.astype(BF16)

        count_x = 4 if wide["x"] else 1
        count_z = 4 if wide["z"] else 1
        if count_x * count_z == 1:
            one(0, 0)
        else:
            def turn(i, carry):
                one(i // count_z, i % count_z)
                return carry

            lax.fori_loop(0, count_x * count_z, turn, 0)

    def first(self, phase, third):
        low, high = self.parts[third]
        self.send(third, phase, 0, 2, low, 1)
        self.send(third, phase, 1, 2, high, -1)
        self.send(third, phase, 2, 1, high, 1)
        self.send(third, phase, 3, -1, low, -1)

    def direct(self, phase, third):
        low, high = self.parts[third]
        for step in (1, 2, 3):
            self.send(third, phase, step - 1, step, (low[0], low[1] + high[1]), step)

    def arrive(self, phase, third):
        low, high = self.parts[third]
        for kind in range(3):
            self.sent[third, phase, kind].wait_recv()
        self.add(third, phase, 0, (low[0], low[1] + high[1]), (0, 1, 2))

    def onward(self, phase, third):
        low, high = self.parts[third]
        self.sent[third, phase, 0].wait_recv()
        self.add(third, phase, 1, low, (0,))
        self.send(third, phase, 4, 1, low, 1)
        self.sent[third, phase, 1].wait_recv()
        self.add(third, phase, -1, high, (1,))
        self.send(third, phase, 5, -1, high, -1)

    def settle(self, phase, third):
        low, high = self.parts[third]
        self.sent[third, phase, 2].wait_recv()
        self.sent[third, phase, 5].wait_recv()
        self.add(third, phase, 0, high, (2, 5))
        self.sent[third, phase, 3].wait_recv()
        self.sent[third, phase, 4].wait_recv()
        self.add(third, phase, 0, low, (3, 4))

    def close(self):
        for copy in self.sent.values():
            copy.wait_send()


DIRECT = ((1, 2), (2,))


def landing_shapes(group):
    shapes = []
    for third in range(3):
        order = ORDERS[third][::-1]
        low, high = thirds(group)[third]
        for phase in range(3):
            whole = order[phase + 1 :]
            direct = phase in DIRECT[group]
            shape = [3 if direct else 6]
            shape += [2] if "x" in whole else []
            shape += [4] if "z" in whole else []
            shape += [2] if "x" in whole else []
            shape += [4] if "y" in whole else []
            width = low[1] + high[1] if direct else max(low[1], high[1])
            shapes.append(pltpu.VMEM((*shape, 16, width), BF16))
    return shapes


class Totals:
    def __init__(self, total, landed, send_sem, recv_sem):
        self.at = place()
        self.total, self.landed, self.send_sem, self.recv_sem = total, landed, send_sem, recv_sem

    def copy(self, phase, step):
        return remote(
            self.total, self.landed.at[phase, step - 1], self.send_sem.at[phase, step - 1],
            self.recv_sem.at[phase, step - 1], device(shifted(self.at, "xyz"[phase], step)),
        )

    def first(self, phase):
        for step in (1, 2, 3):
            self.copy(phase, step).start()

    def settle(self, phase):
        for step in (1, 2, 3):
            self.copy(phase, step).wait()
        self.total[...] += self.landed[phase, 0] + self.landed[phase, 1] + self.landed[phase, 2]


class HeadsBack:
    def __init__(self, mixed_grad, taken, key_value, query, grads, local_sem, send_sem, recv_sem, back_send, back_recv):
        self.f = lax.axis_index("fsdp")
        self.c = lax.axis_index("context")
        self.t = lax.axis_index("tensor")
        self.mixed_grad, self.taken, self.grads = mixed_grad, taken, grads
        self.sources = (key_value.at[0], key_value.at[1], query)
        self.key_value, self.query = key_value, query
        self.local_sem, self.send_sem, self.recv_sem = local_sem, send_sem, recv_sem
        self.back_send, self.back_recv = back_send, back_recv

    def push(self, d):
        peer = lax.rem(self.c + d, 8)
        return remote(
            part(self.mixed_grad, peer), self.taken.at[rows_of(self.c)],
            self.send_sem.at[d - 1], self.recv_sem.at[d - 1], (self.f, peer, self.t),
        )

    def keep(self):
        return pltpu.make_async_copy(
            part(self.mixed_grad, self.c), self.taken.at[rows_of(self.c)], self.local_sem.at[3]
        )

    def answer(self, j, d):
        peer = lax.rem(self.c + d, 8)
        return remote(
            self.sources[j].at[rows_of(peer)], part(self.grads.at[j], self.c),
            self.back_send.at[j, d - 1], self.back_recv.at[j, d - 1], (self.f, peer, self.t),
        )

    def keep_back(self, j):
        return pltpu.make_async_copy(
            self.sources[j].at[rows_of(self.c)], part(self.grads.at[j], self.c), self.local_sem.at[j]
        )

    def start(self):
        for d in (4, 1, 7, 5, 3, 2, 6):
            self.push(d).start()
        self.keep().start()

    def attend(self, length, unit, exact, logs_ref, grad_buf, query_sum):
        c = self.c
        scale = jnp.asarray(0.125, BF16)
        queries = jnp.concatenate(
            [by_head(unit[2, pl.ds(block * ROWS, ROWS), :] * scale) for block in range(8)], 0
        )
        logs = jnp.concatenate([logs_ref[block : block + 1, :] for block in range(8)], 1)
        query_sum[...] = jnp.zeros_like(query_sum)
        self.keep().wait()
        for d in range(1, 8):
            self.push(d).wait_recv()
        for block in range(8):
            grad_buf[pl.ds(block * 256, 256), :] = by_head(self.taken[pl.ds(block * ROWS, ROWS), :])
        head_row = lax.broadcasted_iota(jnp.int32, (8, LANES), 0)
        head_lane = lax.broadcasted_iota(jnp.int32, (8, LANES), 1) // HEAD
        chosen = jnp.where(head_row == head_lane, 1.0, 0.0)
        weighted = lax.dot_general(
            chosen, self.taken[...].astype(F32) * exact[...],
            (((1,), (1,)), ((), ())), precision=lax.Precision.HIGHEST, preferred_element_type=F32,
        )
        delta = jnp.concatenate(
            [
                weighted[head : head + 1, block * ROWS : (block + 1) * ROWS]
                for block in range(8)
                for head in range(2)
            ],
            1,
        )

        def step(turn, carry):
            pair = lax.rem(c // 2 + turn, 4)
            spot = pl.ds(pl.multiple_of(pair * 256, 256), 256)
            keys = unit[0, spot, :]
            values = unit[1, spot, :]
            scores = across(keys, queries) + key_mask(length, pair * 256, 256)
            soft = jnp.exp(scores - logs)
            self.key_value[1, spot, :] = straight(soft.astype(BF16), grad_buf[...]).astype(BF16)
            soft_grad = across(values, grad_buf[...])
            score_grad = (soft * (soft_grad - delta)).astype(BF16)
            self.key_value[0, spot, :] = straight(score_grad, queries).astype(BF16)
            query_sum[...] += lax.dot_general(
                score_grad, keys, (((0,), (0,)), ((), ())), preferred_element_type=F32
            )

            for side in range(2):
                d = lax.rem(pair * 2 + side - c + 8, 8)

                @pl.when(d > 0)
                def _():
                    for j in range(2):
                        self.answer(j, d).start()

            return carry

        lax.fori_loop(1, 5, step, 0)
        first_lane = lax.broadcasted_iota(jnp.int32, (ROWS, LANES), 1) < HEAD
        for block in range(8):
            start = block * 256
            total = jnp.where(
                first_lane, query_sum[pl.ds(start, ROWS), :], query_sum[pl.ds(start + ROWS, ROWS), :]
            )
            self.query[pl.ds(block * ROWS, ROWS), :] = (total * 0.125).astype(BF16)
        for d in (4, 1, 7, 5, 3, 2, 6):
            self.answer(2, d).start()
        for j in range(3):
            self.keep_back(j).start()

    def collect(self, j):
        self.keep_back(j).wait()
        for d in range(1, 8):
            self.answer(j, d).wait_recv()

    def close(self):
        for d in range(1, 8):
            self.push(d).wait_send()
            for j in range(3):
                self.answer(j, d).wait_send()


def put_quarter(work, quarter, start, value):
    z = 2 * (quarter % 2)
    work[quarter // 2, z : z + 2, :, :, :, pl.ds(start, value.shape[1])] = value.astype(BF16).reshape(
        2, 2, 4, 16, value.shape[1]
    )


def weight_grad(work, start, left, right, width):
    turned = left.T
    tile = 512

    def turn(i, carry):
        offset = pl.multiple_of(i * tile, tile)
        term = right[:, :, pl.ds(offset, tile)].reshape(512, tile)
        for quarter in range(4):
            put_quarter(work, quarter, start + offset, straight(turned[quarter * 256 : quarter * 256 + 256], term))
        return carry

    lax.fori_loop(0, width // tile, turn, 0)


def backward_kernel(
    cotangent, rows_ref, squares, lengths,
    low0, result_in, w_in, unit_in, exact_in, logs_in, mixed_in, normed_in, inverse_in, middle_in, act_in, slope_in, low1_in,
    stream_grad, result_ref, query_out, key_out, value_out, output_out, inner_out, outer_out, vector_out, total_ref, root_ref,
    weights, unit, exact, logs, mixed, normed, inverse, middle, act, slope, low,
    attn_grad, inner_grad, outer_grad, grads, mixed_grad, trunk, result,
    taken, grad_buf, query_sum, key_value, query_buf, sent, landed, total_land,
    load_sem, local_sem, send_sem, recv_sem, back_send, back_recv, pair_send, pair_recv,
    total_send, total_recv, scatter_send, scatter_recv, *landings,
):
    at = place()
    c = lax.axis_index("context")
    t = lax.axis_index("tensor")
    partner = (lax.axis_index("fsdp"), c, 1 - t)
    loads, started = {}, []

    def load(name, source, target):
        copy = pltpu.make_async_copy(source, target, load_sem.at[len(started)])
        copy.start()
        started.append(copy)
        loads[name] = copy

    def load_weights(name, start, width):
        columns = (slice(None),) * 5 + (pl.ds(start, width),)
        load(name, w_in.at[columns], weights.at[columns])

    load("normed", normed_in.at[1], normed)
    load("inverse", inverse_in.at[1], inverse)
    load_weights("outer", OUTER, 2048)
    load("slope", slope_in.at[1], slope)
    load_weights("inner", INNER, 2048)
    load_weights("out", OUT, 512)
    load("unit", unit_in.at[1], unit)
    load("exact", exact_in.at[1], exact)
    load("logs", logs_in.at[1], logs)
    load_weights("qkv", QUERY, 1536)
    load("act", act_in, act)
    load("mixed", mixed_in, mixed)
    load("middle", middle_in, middle)
    load("low1", low1_in, low.at[1])
    load("result", result_in, result)
    load("low0", low0, low.at[0])
    greet(neighbours(at, (1, 2, 3)) + context_peers() + [partner])

    three = [landings[9 * group : 9 * group + 9] for group in range(2)]
    one, two = (
        Scatter(weights, group, [three[group][3 * i : 3 * i + 3] for i in range(3)], scatter_send, scatter_recv)
        for group in range(2)
    )
    zero = jnp.zeros((1, 1024), F32)
    sums = [zero] * 6
    bias_sum = jnp.zeros((1, 2048), F32)
    head_sum = [jnp.zeros((1, 512), F32)] * 2
    length = lengths[c // 4]
    closing = [one, two]
    total_ref[...] = jnp.zeros_like(total_ref)

    for layer in (1, 0):
        last = layer == 0
        joins = [
            Joins(sent.at[layer, stage], landed.at[layer, stage], pair_send.at[layer, stage], pair_recv.at[layer, stage])
            for stage in range(2)
        ]
        heads = HeadsBack(
            mixed_grad.at[layer], taken.at[layer], key_value.at[layer], query_buf.at[layer], grads.at[layer],
            local_sem.at[layer], send_sem.at[layer], recv_sem.at[layer], back_send.at[layer], back_recv.at[layer],
        )
        for name in ("normed", "inverse"):
            loads[name].wait()

        def from_output(block, total):
            rows = slab_of(block)
            if last:
                grad = trunk[rows, :]
            else:
                grad = cotangent[rows, :].astype(F32)
            scaled = normed[1, rows, :]
            second = norm_back(grad, scaled, inverse[1, rows, :], rows_ref[4:5, :])
            small = second.astype(BF16)
            trunk[rows, :] = second
            outer_grad[layer, rows, :] = small
            return (
                total[0] + jnp.sum(small.astype(F32), 0, keepdims=True),
                total[1] + jnp.sum(grad * scaled, 0, keepdims=True),
                total[2] + jnp.sum(grad, 0, keepdims=True),
            )

        sums[1], sums[4], sums[5] = lax.fori_loop(0, 256 // SLAB, from_output, (sums[1], sums[4], sums[5]))
        loads["slope"].wait()
        if not last:
            loads["outer"].wait()

        def hidden(tile, carry):
            start = pl.multiple_of(tile * 512, 512)
            columns = pl.ds(start, 512)
            grad = straight(outer_grad[layer], columns_of(weights, OUTER + start, 512))
            small = (grad * slope[:, columns].astype(F32)).astype(BF16)
            inner_grad[layer, :, columns] = small
            total_ref[0:1, columns] += jnp.sum(small.astype(F32), 0, keepdims=True)
            return carry

        lax.fori_loop(0, 4, hidden, 0)
        if not last:
            loads["inner"].wait()
        for quarter in range(4):
            joins[0].offer(quarter, across(inner_grad[layer], quarter_of(weights, quarter, INNER, 2048)))
        if last:
            weight_grad(weights, OUTER, outer_grad[...].reshape(512, 1024), act, 2048)
            two.first(0, 2)
            weight_grad(weights, INNER, middle[...].reshape(512, 1024), inner_grad, 2048)
            two.first(0, 1)
        joins[0].wait()

        def from_middle(block, total):
            rows = slab_of(block)
            grad = trunk[rows, :] + joins[0].total(rows)
            scaled = normed[0, rows, :]
            first = norm_back(grad, scaled, inverse[0, rows, :], rows_ref[2:3, :])
            small = first.astype(BF16)
            trunk[rows, :] = first
            attn_grad[layer, rows, :] = small
            return (
                total[0] + jnp.sum(small.astype(F32), 0, keepdims=True),
                total[1] + jnp.sum(grad * scaled, 0, keepdims=True),
                total[2] + jnp.sum(grad, 0, keepdims=True),
            )

        sums[0], sums[2], sums[3] = lax.fori_loop(0, 256 // SLAB, from_middle, (sums[0], sums[2], sums[3]))
        if not last:
            loads["out"].wait()
        mixed_grad[layer] = straight(attn_grad[layer], columns_of(weights, OUT, 512)).astype(BF16)
        heads.start()
        if last:
            weight_grad(weights, OUT, attn_grad[...].reshape(512, 1024), mixed, 512)
            columns = jnp.concatenate(sums + [jnp.zeros((LANES - 6, 1024), F32)], 0).T
            weights[:, :, :, :, :, EXTRA : EXTRA + LANES] = columns.astype(BF16).reshape(*SHARDS, 16, LANES)
            two.first(0, 0)
        else:
            load("normed", normed_in.at[0], normed)
            load("inverse", inverse_in.at[0], inverse)
            load("slope", slope_in.at[0], slope)
        for name in ("unit", "exact", "logs"):
            loads[name].wait()
        heads.attend(length, unit, exact, logs, grad_buf, query_sum)
        if last:
            for third in (2, 1, 0):
                two.onward(0, third)
        else:
            load("unit", unit_in.at[0], unit)
            load("exact", exact_in.at[0], exact)
            load("logs", logs_in.at[0], logs)
            loads["qkv"].wait()
        heads.collect(0)
        heads.collect(1)
        head_sum[1] = head_sum[1] + jnp.sum(grads[layer, 1].astype(F32), 0, keepdims=True)
        early = [
            across(grads[layer, 0], quarter_of(weights, quarter, KEY, 512))
            + across(grads[layer, 1], quarter_of(weights, quarter, VALUE, 512))
            for quarter in range(4)
        ]
        heads.collect(2)
        head_sum[0] = head_sum[0] + jnp.sum(grads[layer, 2].astype(F32), 0, keepdims=True)
        for quarter in range(4):
            joins[1].offer(
                quarter, early[quarter] + across(grads[layer, 2], quarter_of(weights, quarter, QUERY, 512))
            )
        if last:
            left = low[...].reshape(512, 1024)
            for start, j in ((KEY, 0), (VALUE, 1), (QUERY, 2)):
                weight_grad(weights, start, left, grads.at[:, j], 512)
            for third in range(3):
                one.first(0, third)
            total_ref[1:2, 0:512] = head_sum[0]
            total_ref[1:2, 512:1024] = head_sum[1]
            total_ref[2:8, 0:1024] = squares[0:6, :]
            count = sum(jnp.clip(lengths[s] - c * ROWS, 0, ROWS) for s in range(2)).astype(F32)
            total_ref[1:2, 1024:1152] = jnp.full((1, LANES), count, F32)
        else:
            for name in ("act", "mixed", "middle", "low0", "low1", "result"):
                loads[name].wait()
        joins[1].wait()

        def to_input(block, carry):
            rows = slab_of(block)
            trunk[rows, :] += joins[1].total(rows)
            return carry

        lax.fori_loop(0, 256 // SLAB, to_input, 0)
        closing += [heads] + joins

    totals = Totals(total_ref, total_land, total_send, total_recv)
    totals.first(0)
    for third in (2, 1, 0):
        two.settle(0, third)
        two.first(1, third)
    for s in range(2):
        stream_grad[:, s, :] = trunk[s * ROWS : s * ROWS + ROWS, :]
    for third in range(3):
        one.onward(0, third)
    totals.settle(0)
    totals.first(1)
    for third in (2, 1, 0):
        two.onward(1, third)
    pairs = [result[s * ROWS : s * ROWS + ROWS, :].astype(F32) for s in range(2)]
    result_ref[...] = jnp.stack(pairs, 1).astype(BF16)
    for third in range(3):
        one.settle(0, third)
        one.direct(1, third)
    for third in (2, 1, 0):
        two.settle(1, third)
        two.direct(2, third)
    totals.settle(1)
    totals.first(2)
    for third in range(3):
        one.arrive(1, third)
        one.direct(2, third)
    for third in (2, 1, 0):
        two.arrive(2, third)
    totals.settle(2)
    for third in range(3):
        one.arrive(2, third)
    x = at["x"]

    def own(start, width):
        return weights[x // 2, at["z"], x % 2, at["y"], :, start : start + width].astype(F32)

    query_out[...] = own(QUERY, 512)
    key_out[...] = own(KEY, 512)
    value_out[...] = own(VALUE, 512)
    output_out[...] = own(OUT, 512)
    inner_out[...] = own(INNER, 2048)
    outer_out[...] = own(OUTER, 2048)
    vector_out[...] = own(EXTRA, LANES).T[0:8, :]
    for item in closing:
        item.close()
    scale = 1.0 / (total_ref[1:2, 1024:1025] * 1024.0)
    square = jnp.sum(total_ref[:, 0:1024], 1, keepdims=True)
    root_ref[...] = jnp.broadcast_to(jnp.sqrt(square * scale + 1e-06), root_ref.shape)


def run_backward(grad, rows, squares, lengths, saved):
    dma = pltpu.SemaphoreType.DMA
    out = lambda *shape: jax.ShapeDtypeStruct(shape, F32)
    return pl.pallas_call(
        backward_kernel,
        out_shape=(
            out(ROWS, 2, 1024), jax.ShapeDtypeStruct((ROWS, 2, 1024), BF16),
            out(16, 512), out(16, 512), out(16, 512), out(16, 512), out(16, 2048), out(16, 2048),
            out(8, 16), out(8, 2048), out(8, LANES),
        ),
        in_specs=[spec(pltpu.VMEM)] * 3 + [spec(pltpu.SMEM)] + [spec(pl.ANY)] * len(saved),
        out_specs=(spec(pltpu.VMEM),) * 11,
        scratch_shapes=[
            pltpu.VMEM((*SHARDS, 16, WIDTH), BF16),
            pltpu.VMEM((3, 1024, LANES), BF16),
            pltpu.VMEM((1024, LANES), F32),
            pltpu.VMEM((8, 256), F32),
            pltpu.VMEM((2, 256, 512), BF16),
            pltpu.VMEM((2, 256, 1024), F32),
            pltpu.VMEM((2, 256, 1), F32),
            pltpu.VMEM((2, 256, 1024), BF16),
            pltpu.VMEM((2, 256, 2048), BF16),
            pltpu.VMEM((256, 2048), BF16),
            pltpu.VMEM((2, 256, 1024), BF16),
            pltpu.VMEM((2, 256, 1024), BF16),
            pltpu.VMEM((2, 256, 2048), BF16),
            pltpu.VMEM((2, 256, 1024), BF16),
            pltpu.VMEM((2, 3, 256, 512), BF16),
            pltpu.VMEM((2, 256, 512), BF16),
            pltpu.VMEM((256, 1024), F32),
            pltpu.VMEM((256, 1024), BF16),
            pltpu.VMEM((2, 1024, LANES), BF16),
            pltpu.VMEM((2048, LANES), BF16),
            pltpu.VMEM((2048, LANES), F32),
            pltpu.VMEM((2, 2, 1024, LANES), BF16),
            pltpu.VMEM((2, 1024, LANES), BF16),
            pltpu.VMEM((2, 2, 2, 256, 512), BF16),
            pltpu.VMEM((2, 2, 2, 256, 512), BF16),
            pltpu.VMEM((3, 3, 8, 2048), F32),
            dma((32,)),
            dma((2, 4)),
            dma((2, 7)),
            dma((2, 7)),
            dma((2, 3, 7)),
            dma((2, 3, 7)),
            dma((2, 2, 2)),
            dma((2, 2, 2)),
            dma((3, 3)),
            dma((3, 3)),
            dma((2, 3, 3, 6)),
            dma((2, 3, 3, 6)),
            *landing_shapes(0),
            *landing_shapes(1),
        ],
        compiler_params=pltpu.CompilerParams(
            collective_id=4, has_side_effects=True, vmem_limit_bytes=LIMIT
        ),
        name="backward_layers",
    )(grad, rows, squares, lengths, *saved)


def finish_kernel(
    stream_in, result_in, query_in, key_in, value_in, output_in, inner_in, outer_in, vectors, totals, roots,
    result, stream_grad, query, key, value, output, inner, outer, query_sum, value_sum, inner_sum, *rest,
):
    for source, target in (
        (result_in, result), (stream_in, stream_grad), (query_in, query), (key_in, key), (value_in, value),
        (output_in, output), (inner_in, inner), (outer_in, outer),
    ):
        target[...] = source[...]
    query_sum[...] = totals[1:2, 0:512].reshape(512)
    value_sum[...] = totals[1:2, 512:1024].reshape(512)
    inner_sum[...] = totals[0:1, :].reshape(2048)
    for j in range(6):
        rest[j][...] = vectors[j : j + 1, :].reshape(16)
    rest[6][...] = jnp.concatenate(
        [
            jnp.concatenate([roots[2 + 3 * layer + j : 3 + 3 * layer + j, 0:1] for j in range(3)], 1)
            for layer in range(LAYERS)
        ],
        0,
    )


def finish(partial):
    out = lambda *shape: jax.ShapeDtypeStruct(shape, F32)
    return pl.pallas_call(
        finish_kernel,
        out_shape=(
            jax.ShapeDtypeStruct((ROWS, 2, 1024), BF16), out(ROWS, 2, 1024),
            out(16, 512), out(16, 512), out(16, 512), out(16, 512), out(16, 2048), out(16, 2048),
            out(512), out(512), out(2048), *(out(16) for _ in range(6)), out(LAYERS, 3),
        ),
        in_specs=[spec(pltpu.VMEM)] * 11,
        out_specs=(spec(pltpu.VMEM),) * 18,
        name="finish",
    )(*partial)


def body(
    stream,
    lengths,
    query_weight,
    query_bias,
    key_weight,
    value_weight,
    value_bias,
    output_weight,
    output_bias,
    first_gain,
    first_shift,
    inner_weight,
    inner_bias,
    outer_weight,
    outer_bias,
    second_gain,
    second_shift,
    cotangent,
):
    grad_in = cotangent
    low, grad, result, rows, squares, *saved = run_forward(
        stream, grad_in, query_weight, key_weight, value_weight, output_weight.T, inner_weight, outer_weight.T,
        output_bias, outer_bias, first_gain, first_shift, second_gain, second_shift,
        query_bias, value_bias, inner_bias, lengths,
    )
    partial = run_backward(grad, rows, squares, lengths, [low, result, *saved])
    (
        result, stream_grad, grad_query, grad_key, grad_value, grad_output, grad_inner, grad_outer,
        query_sum, value_sum, inner_sum, *vectors, roots,
    ) = finish(partial)
    return (
        result,
        stream_grad,
        grad_query,
        query_sum,
        grad_key,
        grad_value,
        value_sum,
        grad_output.T,
        vectors[0],
        vectors[2],
        vectors[3],
        grad_inner,
        inner_sum,
        grad_outer.T,
        vectors[1],
        vectors[4],
        vectors[5],
        roots,
    )


def solution(mesh):
    in_specs = (
        P("context", "fsdp", None),
        P("fsdp"),
        P(("fsdp", "context"), "tensor"),
        P("tensor"),
        P(("fsdp", "context"), "tensor"),
        P(("fsdp", "context"), "tensor"),
        P("tensor"),
        P("tensor", ("fsdp", "context")),
        P(("fsdp", "context")),
        P(("fsdp", "context")),
        P(("fsdp", "context")),
        P(("fsdp", "context"), "tensor"),
        P("tensor"),
        P("tensor", ("fsdp", "context")),
        P(("fsdp", "context")),
        P(("fsdp", "context")),
        P(("fsdp", "context")),
        P("context", "fsdp", None),
    )
    out_specs = (
        P("context", "fsdp", None),
        P("context", "fsdp", None),
        P(("fsdp", "context"), "tensor"),
        P("tensor"),
        P(("fsdp", "context"), "tensor"),
        P(("fsdp", "context"), "tensor"),
        P("tensor"),
        P("tensor", ("fsdp", "context")),
        P(("fsdp", "context")),
        P(("fsdp", "context")),
        P(("fsdp", "context")),
        P(("fsdp", "context"), "tensor"),
        P("tensor"),
        P("tensor", ("fsdp", "context")),
        P(("fsdp", "context")),
        P(("fsdp", "context")),
        P(("fsdp", "context")),
        P(),
    )
    return jax.shard_map(body, mesh=mesh, in_specs=in_specs, out_specs=out_specs, check_vma=False)
```

```python
import jax
import jax.numpy as jnp
from jax import lax
from jax.experimental import pallas as pl
from jax.experimental.pallas import tpu as pltpu
from jax.sharding import PartitionSpec as P

HEAD = 64
LAYERS = 2
LANES = 128
MESH = pl.DeviceIdType.MESH

F32 = jnp.float32
BF16 = jnp.bfloat16
ROWS = 128
LIMIT = 60 * 2**20
WIDTH = 6272
QUERY, KEY, VALUE, OUT, EXTRA, INNER, OUTER = 0, 512, 1024, 1536, 2048, 2176, 4224
GROUPS = ((QUERY, OUT), (OUT, OUTER), (OUTER, WIDTH))
TILES = (((2, 2), (2, 2), (2, 2)), ((3, 3), (4, 5), (3, 3)), ((2, 3), (3, 3), (2, 3)))
ORDERS = ("zyx", "yxz", "xzy")
SHARDS = (2, 4, 2, 4)


def spec(space):
    return pl.BlockSpec(memory_space=space)


def place():
    f = lax.axis_index("fsdp")
    c = lax.axis_index("context")
    t = lax.axis_index("tensor")
    return {"x": 2 * (f // 4) + c // 4, "y": c % 4, "z": f % 4, "t": t}


def device(at):
    x = at["x"]
    return ((x // 2) * 4 + at["z"], (x % 2) * 4 + at["y"], at["t"])


def shifted(at, axis, step):
    moved = dict(at)
    moved[axis] = lax.rem(at[axis] + step + 4, 4)
    return moved


def greet(devices):
    barrier = pltpu.get_barrier_semaphore()
    for device_id in devices:
        pl.semaphore_signal(barrier, inc=1, device_id=device_id, device_id_type=MESH)
    pl.semaphore_wait(barrier, len(devices))


def neighbours(at, steps):
    return [device(shifted(at, axis, step)) for axis in "xyz" for step in steps]


def context_peers():
    f = lax.axis_index("fsdp")
    c = lax.axis_index("context")
    t = lax.axis_index("tensor")
    return [(f, lax.rem(c + d, 8), t) for d in range(1, 8)]


def remote(src, dst, send_sem, recv_sem, device_id):
    return pltpu.make_async_remote_copy(
        src_ref=src,
        dst_ref=dst,
        send_sem=send_sem,
        recv_sem=recv_sem,
        device_id=device_id,
        device_id_type=MESH,
    )


def shards(ref, at, whole, cols):
    x = at["x"]
    xh = slice(None) if "x" in whole else x // 2
    xl = slice(None) if "x" in whole else x % 2
    z = slice(None) if "z" in whole else at["z"]
    y = slice(None) if "y" in whole else at["y"]
    return ref.at[xh, z, xl, y, :, pl.ds(cols[0], cols[1])]


def thirds(group):
    start = GROUPS[group][0]
    parts = []
    for pair in TILES[group]:
        halves = []
        for tiles in pair:
            halves.append((start, tiles * LANES))
            start += tiles * LANES
        parts.append(tuple(halves))
    return parts


def across(left, right):
    return lax.dot_general(left, right, (((1,), (1,)), ((), ())), preferred_element_type=F32)


def straight(left, right):
    return jnp.dot(left, right, preferred_element_type=F32)


def rows_of(block):
    return pl.ds(pl.multiple_of(block * ROWS, ROWS), ROWS)


def by_head(block):
    first = lax.broadcasted_iota(jnp.int32, block.shape, 1) < HEAD
    zero = jnp.zeros_like(block)
    return jnp.concatenate([jnp.where(first, block, zero), jnp.where(first, zero, block)], 0)


def key_mask(length, first, count):
    position = first + lax.broadcasted_iota(jnp.int32, (count, 1), 0)
    return jnp.where(position < length, 0.0, -1e30)


def columns_of(weights, start, width):
    return weights[:, :, :, :, :, pl.ds(start, width)].reshape(1024, width)


def quarter_of(weights, quarter, start, width):
    z = 2 * (quarter % 2)
    return weights[quarter // 2, z : z + 2, :, :, :, start : start + width].reshape(256, width)


def part(ref, peer):
    return ref.at[rows_of(peer // 4), rows_of(peer % 4)]


class Gather:
    def __init__(self, weights, group, send_sem, recv_sem):
        self.at = place()
        self.weights, self.group = weights, group
        self.send_sem, self.recv_sem = send_sem, recv_sem
        self.parts = thirds(group)
        self.sent = {}

    def send(self, third, phase, kind, origin, cols, step):
        order = ORDERS[third]
        block = shards(self.weights, origin, order[:phase], cols)
        index = (self.group, third, phase, kind)
        copy = remote(
            block, block, self.send_sem.at[index], self.recv_sem.at[index],
            device(shifted(self.at, order[phase], step)),
        )
        copy.start()
        self.sent[third, phase, kind] = copy

    def first(self, phase):
        for third in range(3):
            low, high = self.parts[third]
            both = (low[0], low[1] + high[1])
            self.send(third, phase, 0, self.at, both, 1)
            self.send(third, phase, 1, self.at, both, -1)

    def direct(self, phase):
        for third in range(3):
            low, high = self.parts[third]
            for step in (1, 2, 3):
                self.send(third, phase, step - 1, self.at, (low[0], low[1] + high[1]), step)

    def arrive(self, phase):
        for third in range(3):
            for kind in range(3):
                self.sent[third, phase, kind].wait_recv()

    def onward(self, phase):
        for third in range(3):
            axis = ORDERS[third][phase]
            low, high = self.parts[third]
            self.sent[third, phase, 0].wait_recv()
            self.send(third, phase, 2, shifted(self.at, axis, -1), low, 1)
            self.sent[third, phase, 1].wait_recv()
            self.send(third, phase, 3, shifted(self.at, axis, 1), high, -1)

    def settle(self, phase):
        for third in range(3):
            self.sent[third, phase, 2].wait_recv()
            self.sent[third, phase, 3].wait_recv()

    def close(self):
        for copy in self.sent.values():
            copy.wait_send()


class Heads:
    def __init__(self, own, unit, outcome, mixed, local_sem, send_sem, recv_sem, back_send, back_recv):
        self.f = lax.axis_index("fsdp")
        self.c = lax.axis_index("context")
        self.t = lax.axis_index("tensor")
        self.own, self.unit, self.outcome, self.mixed = own, unit, outcome, mixed
        self.local_sem, self.send_sem, self.recv_sem = local_sem, send_sem, recv_sem
        self.back_send, self.back_recv = back_send, back_recv

    def push(self, j, d):
        peer = lax.rem(self.c + d, 8)
        return remote(
            part(self.own.at[j], peer), self.unit.at[j, rows_of(self.c)],
            self.send_sem.at[j, d - 1], self.recv_sem.at[j, d - 1], (self.f, peer, self.t),
        )

    def keep(self, j):
        return pltpu.make_async_copy(
            part(self.own.at[j], self.c), self.unit.at[j, rows_of(self.c)], self.local_sem.at[j]
        )

    def answer(self, d):
        peer = lax.rem(self.c + d, 8)
        return remote(
            self.outcome.at[rows_of(peer)], part(self.mixed, self.c),
            self.back_send.at[d - 1], self.back_recv.at[d - 1], (self.f, peer, self.t),
        )

    def keep_back(self):
        return pltpu.make_async_copy(
            self.outcome.at[rows_of(self.c)], part(self.mixed, self.c), self.local_sem.at[3]
        )

    def project(self, x, weights, bias):
        for j, column in enumerate((KEY, VALUE, QUERY)):
            product = straight(x, columns_of(weights, column, 512))
            if j == 1:
                product = product + bias[:, 512:1024]
            if j == 2:
                product = product + bias[:, 0:512]
            self.own[j] = product.astype(BF16)
            for d in (4, 1, 7, 5, 3, 2, 6):
                self.push(j, d).start()
            self.keep(j).start()

    def attend(self, length, exact, logs, midway):
        c = self.c
        for j in range(2):
            self.keep(j).wait()
            for d in range(1, 8):
                self.push(j, d).wait_recv()
        mask = key_mask(length, 0, 8 * ROWS)
        keys = self.unit[0]
        values_across = self.unit[1].T
        self.keep(2).wait()

        def step(d, carry):
            block = lax.rem(c + d, 8)

            @pl.when(d > 0)
            def _():
                self.push(2, 8 - d).wait_recv()

            queries = self.unit[2, rows_of(block), :] * jnp.asarray(0.125, BF16)
            scores = across(keys, by_head(queries)) + mask
            top = jnp.max(scores, 0, keepdims=True)
            exponent = jnp.exp(scores - top)
            total = jnp.sum(exponent, 0, keepdims=True)
            outcome = straight(values_across, exponent.astype(BF16)) / total
            both = jnp.concatenate([outcome[:HEAD, :ROWS], outcome[HEAD:, ROWS:]], 0).T
            exact[rows_of(block), :] = both
            self.outcome[rows_of(block), :] = both.astype(BF16)
            logs[pl.ds(block, 1), :] = top + jnp.log(total)

            @pl.when(d > 0)
            def _():
                self.answer(d).start()

            return carry

        lax.fori_loop(0, 4, step, 0)
        midway()
        lax.fori_loop(4, 8, step, 0)
        self.keep_back().start()

    def collect(self):
        self.keep_back().wait()
        for d in range(1, 8):
            self.answer(d).wait_recv()

    def close(self):
        for d in range(1, 8):
            self.answer(d).wait_send()
            for j in range(3):
                self.push(j, d).wait_send()


class Join:
    def __init__(self, number, before, sent, landed, send_sem, recv_sem):
        t = lax.axis_index("tensor")
        self.partner = (lax.axis_index("fsdp"), lax.axis_index("context"), 1 - t)
        self.sent, self.landed = sent.at[number % 2], landed.at[number % 2]
        self.send_sem, self.recv_sem = send_sem.at[number], recv_sem.at[number]
        self.before = before

    def copy(self, half):
        return remote(
            self.sent.at[half], self.landed.at[half], self.send_sem.at[half], self.recv_sem.at[half],
            self.partner,
        )

    def offer(self, quarter, term):
        half, side = quarter // 2, quarter % 2
        if side == 0 and self.before is not None:
            self.before.copy(half).wait_send()
        self.sent[half, :, side * 256 : side * 256 + 256] = term.astype(BF16)
        if side == 1:
            self.copy(half).start()

    def wait(self):
        for half in range(2):
            self.copy(half).wait_recv()

    def total(self, rows):
        return jnp.concatenate(
            [self.sent[half, rows, :].astype(F32) + self.landed[half, rows, :].astype(F32) for half in range(2)],
            1,
        )

    def close(self):
        for half in range(2):
            self.copy(half).wait_send()


def gelu_parts(argument):
    square = argument * argument
    inner = 0.7978845608028654 * argument * (1.0 + 0.044715 * square)
    bend = jnp.tanh(inner)
    half = 0.5 * (1.0 + bend)
    slope = half + 0.5 * argument * (1.0 - bend * bend) * 0.7978845608028654 * (
        1.0 + 3.0 * 0.044715 * square
    )
    return argument * half, slope


def norm_parts(hidden):
    centre = hidden - jnp.mean(hidden, -1, keepdims=True)
    inverse = lax.rsqrt(jnp.mean(centre * centre, -1, keepdims=True) + 1e-05)
    return centre * inverse, inverse


def live_rows(lengths, block, count):
    c = lax.axis_index("context")
    row = block * count + lax.broadcasted_iota(jnp.int32, (count, 1), 0)
    slot = c * ROWS + lax.rem(row, ROWS)
    return jnp.where(slot < jnp.where(row < ROWS, lengths[0], lengths[1]), 1.0, 0.0)


SLAB = 64


def slab_of(block):
    return pl.ds(pl.multiple_of(block * SLAB, SLAB), SLAB)


def pack(weights, own, query, key, value, output, inner, outer, vectors):
    xh, z, xl, y = own

    def put(start, block):
        weights[xh, z, xl, y, :, start : start + block.shape[1]] = block

    put(QUERY, query[...])
    put(KEY, key[...])
    put(VALUE, value[...])
    put(OUT, output[...])
    put(INNER, inner[...])
    put(OUTER, outer[...])
    eye = jnp.where(
        lax.broadcasted_iota(jnp.int32, (16, 16), 0) == lax.broadcasted_iota(jnp.int32, (16, 16), 1), 1.0, 0.0
    ).astype(BF16)
    rows = [vector[...].astype(F32).reshape(1, 16) for vector in vectors]
    table = jnp.concatenate(rows + [jnp.zeros((LANES - 6, 16), F32)], 0).astype(BF16)
    put(EXTRA, across(eye, table).astype(BF16))


def rows_by_sequence(source, target, keep):
    whole = source[...].astype(F32)
    for s in range(2):
        target[s * ROWS : s * ROWS + ROWS, :] = (whole[:, s, :] * keep(s)).astype(target.dtype)


def norm_back(grad_out, normed, inverse, gain):
    scaled = grad_out * gain
    return inverse * (
        scaled
        - jnp.mean(scaled, -1, keepdims=True)
        - normed * jnp.mean(scaled * normed, -1, keepdims=True)
    )


class Scatter:
    def __init__(self, work, group, landings, send_sem, recv_sem):
        self.at = place()
        self.work, self.group, self.landings = work, group, landings
        self.send_sem, self.recv_sem = send_sem, recv_sem
        self.parts = thirds(group)
        self.sent = {}

    def ring(self, third, phase):
        order = ORDERS[third][::-1]
        return order[phase], order[phase + 1 :]

    def send(self, third, phase, kind, away, cols, step):
        axis, whole = self.ring(third, phase)
        land = self.landings[third][phase].at[kind]
        if cols[1] != land.shape[-1]:
            land = land.at[..., pl.ds(0, cols[1])]
        index = (self.group, third, phase, kind)
        copy = remote(
            shards(self.work, shifted(self.at, axis, away), whole, cols), land,
            self.send_sem.at[index], self.recv_sem.at[index], device(shifted(self.at, axis, step)),
        )
        copy.start()
        self.sent[third, phase, kind] = copy

    def add(self, third, phase, away, cols, kinds):
        axis, whole = self.ring(third, phase)
        origin = shifted(self.at, axis, away)
        land = self.landings[third][phase]
        x = origin["x"]
        wide = {name: name in whole for name in "xyz"}
        columns = pl.ds(cols[0], cols[1])

        def one(ix, iz):
            xh, xl = (ix // 2, ix % 2) if wide["x"] else (x // 2, x % 2)
            z = iz if wide["z"] else origin["z"]
            y = slice(None) if wide["y"] else origin["y"]
            index = (xh, z, xl, y, slice(None), columns)
            total = self.work[index].astype(F32)
            for kind in kinds:
                at = (kind,)
                at += (xh,) if wide["x"] else ()
                at += (z,) if wide["z"] else ()
                at += (xl,) if wide["x"] else ()
                at += (slice(None),) if wide["y"] else ()
                total = total + land[at + (slice(None), pl.ds(0, cols[1]))].astype(F32)
            self.work[index] = total.astype(BF16)

        count_x = 4 if wide["x"] else 1
        count_z = 4 if wide["z"] else 1
        if count_x * count_z == 1:
            one(0, 0)
        else:
            def turn(i, carry):
                one(i // count_z, i % count_z)
                return carry

            lax.fori_loop(0, count_x * count_z, turn, 0)

    def first(self, phase, third):
        low, high = self.parts[third]
        self.send(third, phase, 0, 2, low, 1)
        self.send(third, phase, 1, 2, high, -1)
        self.send(third, phase, 2, 1, high, 1)
        self.send(third, phase, 3, -1, low, -1)

    def direct(self, phase, third):
        low, high = self.parts[third]
        for step in (1, 2, 3):
            self.send(third, phase, step - 1, step, (low[0], low[1] + high[1]), step)

    def arrive(self, phase, third):
        low, high = self.parts[third]
        for kind in range(3):
            self.sent[third, phase, kind].wait_recv()
        self.add(third, phase, 0, (low[0], low[1] + high[1]), (0, 1, 2))

    def onward(self, phase, third):
        low, high = self.parts[third]
        self.sent[third, phase, 0].wait_recv()
        self.add(third, phase, 1, low, (0,))
        self.send(third, phase, 4, 1, low, 1)
        self.sent[third, phase, 1].wait_recv()
        self.add(third, phase, -1, high, (1,))
        self.send(third, phase, 5, -1, high, -1)

    def settle(self, phase, third):
        low, high = self.parts[third]
        self.sent[third, phase, 2].wait_recv()
        self.sent[third, phase, 5].wait_recv()
        self.add(third, phase, 0, high, (2, 5))
        self.sent[third, phase, 3].wait_recv()
        self.sent[third, phase, 4].wait_recv()
        self.add(third, phase, 0, low, (3, 4))

    def close(self):
        for copy in self.sent.values():
            copy.wait_send()


DIRECT = ((1, 2), (2,), (2,))


def landing_shapes(group):
    shapes = []
    for third in range(3):
        order = ORDERS[third][::-1]
        low, high = thirds(group)[third]
        for phase in range(3):
            whole = order[phase + 1 :]
            direct = phase in DIRECT[group]
            shape = [3 if direct else 6]
            shape += [2] if "x" in whole else []
            shape += [4] if "z" in whole else []
            shape += [2] if "x" in whole else []
            shape += [4] if "y" in whole else []
            width = low[1] + high[1] if direct else max(low[1], high[1])
            shapes.append(pltpu.VMEM((*shape, 16, width), BF16))
    return shapes


class Totals:
    def __init__(self, total, landed, send_sem, recv_sem):
        self.at = place()
        self.total, self.landed, self.send_sem, self.recv_sem = total, landed, send_sem, recv_sem

    def copy(self, phase, step):
        return remote(
            self.total, self.landed.at[phase, step - 1], self.send_sem.at[phase, step - 1],
            self.recv_sem.at[phase, step - 1], device(shifted(self.at, "xyz"[phase], step)),
        )

    def first(self, phase):
        for step in (1, 2, 3):
            self.copy(phase, step).start()

    def settle(self, phase):
        for step in (1, 2, 3):
            self.copy(phase, step).wait()
        self.total[...] += self.landed[phase, 0] + self.landed[phase, 1] + self.landed[phase, 2]


class HeadsBack:
    def __init__(self, mixed_grad, taken, key_value, query, grads, local_sem, send_sem, recv_sem, back_send, back_recv):
        self.f = lax.axis_index("fsdp")
        self.c = lax.axis_index("context")
        self.t = lax.axis_index("tensor")
        self.mixed_grad, self.taken, self.grads = mixed_grad, taken, grads
        self.sources = (key_value.at[0], key_value.at[1], query)
        self.key_value, self.query = key_value, query
        self.local_sem, self.send_sem, self.recv_sem = local_sem, send_sem, recv_sem
        self.back_send, self.back_recv = back_send, back_recv

    def push(self, d):
        peer = lax.rem(self.c + d, 8)
        return remote(
            part(self.mixed_grad, peer), self.taken.at[rows_of(self.c)],
            self.send_sem.at[d - 1], self.recv_sem.at[d - 1], (self.f, peer, self.t),
        )

    def keep(self):
        return pltpu.make_async_copy(
            part(self.mixed_grad, self.c), self.taken.at[rows_of(self.c)], self.local_sem.at[3]
        )

    def answer(self, j, d):
        peer = lax.rem(self.c + d, 8)
        return remote(
            self.sources[j].at[rows_of(peer)], part(self.grads.at[j], self.c),
            self.back_send.at[j, d - 1], self.back_recv.at[j, d - 1], (self.f, peer, self.t),
        )

    def keep_back(self, j):
        return pltpu.make_async_copy(
            self.sources[j].at[rows_of(self.c)], part(self.grads.at[j], self.c), self.local_sem.at[j]
        )

    def start(self):
        for d in (4, 1, 7, 5, 3, 2, 6):
            self.push(d).start()
        self.keep().start()

    def attend(self, length, unit, exact, logs_ref, grad_buf, query_sum, ahead, midway):
        c = self.c
        scale = jnp.asarray(0.125, BF16)
        queries = jnp.concatenate(
            [by_head(unit[2, pl.ds(block * ROWS, ROWS), :] * scale) for block in range(8)], 0
        )
        logs = jnp.concatenate([logs_ref[block : block + 1, :] for block in range(8)], 1)
        query_sum[...] = jnp.zeros_like(query_sum)
        ahead()
        self.keep().wait()
        for d in range(1, 8):
            self.push(d).wait_recv()
        for block in range(8):
            grad_buf[pl.ds(block * 256, 256), :] = by_head(self.taken[pl.ds(block * ROWS, ROWS), :])
        head_row = lax.broadcasted_iota(jnp.int32, (8, LANES), 0)
        head_lane = lax.broadcasted_iota(jnp.int32, (8, LANES), 1) // HEAD
        chosen = jnp.where(head_row == head_lane, 1.0, 0.0)
        weighted = lax.dot_general(
            chosen, self.taken[...].astype(F32) * exact[...],
            (((1,), (1,)), ((), ())), precision=lax.Precision.HIGHEST, preferred_element_type=F32,
        )
        delta = jnp.concatenate(
            [
                weighted[head : head + 1, block * ROWS : (block + 1) * ROWS]
                for block in range(8)
                for head in range(2)
            ],
            1,
        )

        def step(turn, carry):
            pair = lax.rem(c // 2 + turn, 4)
            spot = pl.ds(pl.multiple_of(pair * 256, 256), 256)
            keys = unit[0, spot, :]
            values = unit[1, spot, :]
            scores = across(keys, queries) + key_mask(length, pair * 256, 256)
            soft = jnp.exp(scores - logs)
            self.key_value[1, spot, :] = straight(soft.astype(BF16), grad_buf[...]).astype(BF16)
            soft_grad = across(values, grad_buf[...])
            score_grad = (soft * (soft_grad - delta)).astype(BF16)
            self.key_value[0, spot, :] = straight(score_grad, queries).astype(BF16)
            query_sum[...] += lax.dot_general(
                score_grad, keys, (((0,), (0,)), ((), ())), preferred_element_type=F32
            )

            for side in range(2):
                d = lax.rem(pair * 2 + side - c + 8, 8)

                @pl.when(d > 0)
                def _():
                    for j in range(2):
                        self.answer(j, d).start()

            return carry

        lax.fori_loop(1, 3, step, 0)
        midway()
        lax.fori_loop(3, 5, step, 0)
        first_lane = lax.broadcasted_iota(jnp.int32, (ROWS, LANES), 1) < HEAD
        for block in range(8):
            start = block * 256
            total = jnp.where(
                first_lane, query_sum[pl.ds(start, ROWS), :], query_sum[pl.ds(start + ROWS, ROWS), :]
            )
            self.query[pl.ds(block * ROWS, ROWS), :] = (total * 0.125).astype(BF16)
        for d in (4, 1, 7, 5, 3, 2, 6):
            self.answer(2, d).start()
        for j in range(3):
            self.keep_back(j).start()

    def collect(self, j):
        self.keep_back(j).wait()
        for d in range(1, 8):
            self.answer(j, d).wait_recv()

    def close(self):
        for d in range(1, 8):
            self.push(d).wait_send()
            for j in range(3):
                self.answer(j, d).wait_send()


def put_quarter(work, quarter, start, value):
    z = 2 * (quarter % 2)
    work[quarter // 2, z : z + 2, :, :, :, pl.ds(start, value.shape[1])] = value.astype(BF16).reshape(
        2, 2, 4, 16, value.shape[1]
    )


def weight_grad(work, start, left, right, width):
    turned = left.T
    tile = 512

    def turn(i, carry):
        offset = pl.multiple_of(i * tile, tile)
        term = right[:, :, pl.ds(offset, tile)].reshape(512, tile)
        for quarter in range(4):
            put_quarter(work, quarter, start + offset, straight(turned[quarter * 256 : quarter * 256 + 256], term))
        return carry

    lax.fori_loop(0, width // tile, turn, 0)


def layers_kernel(
    stream, cotangent, query, key, value, output, inner, outer, bias0, bias1, gain1, shift1, gain2, shift2,
    query_bias, value_bias, inner_bias, lengths,
    stream_grad, result_ref, query_out, key_out, value_out, output_out, inner_out, outer_out, vector_out, total_ref,
    root_ref,
    weights, bias, rows_ref, low, grad_in, result, trunk,
    own, unit, exact, logs, outcome, mixed, normed, inverse, middle, act, slope,
    attn_grad, inner_grad, outer_grad, grads, mixed_grad, taken, grad_buf, query_sum, key_value, query_buf,
    sent, landed, total_land,
    local_sem, gather_send, gather_recv, send_sem, recv_sem, back_send, back_recv, pair_send, pair_recv,
    turn_local, turn_send, turn_recv, turn_back_send, turn_back_recv, total_send, total_recv,
    scatter_send, scatter_recv, *landings,
):
    at = place()
    c = lax.axis_index("context")
    t = lax.axis_index("tensor")
    partner = (lax.axis_index("fsdp"), c, 1 - t)
    x = at["x"]
    closing = []
    joined = []

    def new_join():
        before = joined[-2] if len(joined) > 1 else None
        joined.append(Join(len(joined), before, sent, landed, pair_send, pair_recv))
        return joined[-1]

    pack(
        weights, (x // 2, at["z"], x % 2, at["y"]), query, key, value, output, inner, outer,
        (bias0, bias1, gain1, shift1, gain2, shift2),
    )
    greet(neighbours(at, (1, 2, 3)) + context_peers() + [partner])
    one, two, three = (Gather(weights, group, gather_send, gather_recv) for group in range(3))
    gathers = (one, two, three)
    for group in gathers:
        group.direct(0)
    rows_by_sequence(stream, low.at[0], lambda s: 1.0)
    one.arrive(0)
    one.direct(1)
    two.arrive(0)
    two.first(1)
    three.arrive(0)
    three.first(1)
    bias[:, 0:512] = query_bias[...].astype(F32).reshape(1, 512)
    bias[:, 512:1024] = value_bias[...].astype(F32).reshape(1, 512)
    bias[:, 1024:3072] = inner_bias[...].astype(F32).reshape(1, 2048)
    one.arrive(1)
    one.first(2)
    two.onward(1)
    three.onward(1)
    position = c * ROWS + lax.broadcasted_iota(jnp.int32, (ROWS, 1), 0)
    rows_by_sequence(cotangent, grad_in, lambda s: jnp.where(position < lengths[s], 1.0, 0.0))
    trunk[...] = low[0].astype(F32)
    total_ref[...] = jnp.zeros_like(total_ref)
    one.onward(2)
    two.settle(1)
    two.first(2)
    one.settle(2)
    length = lengths[c // 4]
    zero = jnp.zeros((1, 1024), F32)
    sums = [zero] * 6

    for layer in range(LAYERS):
        first = layer == 0
        heads = Heads(
            own, unit.at[layer], outcome.at[layer], mixed.at[layer], local_sem.at[layer],
            send_sem.at[layer], recv_sem.at[layer], back_send.at[layer], back_recv.at[layer],
        )
        if not first:
            closing.pop().close()
        closing.append(heads)
        heads.project(low[layer], weights, bias)
        if first:
            three.settle(1)
            three.first(2)
            two.onward(2)
        heads.attend(length, exact.at[layer], logs.at[layer], (lambda: three.onward(2)) if first else (lambda: None))
        heads.collect()
        if first:
            two.settle(2)
            pick = jnp.where(
                lax.broadcasted_iota(jnp.int32, (8, LANES), 0) == lax.broadcasted_iota(jnp.int32, (8, LANES), 1),
                1.0, 0.0,
            ).astype(BF16)
            rows_ref[...] = across(pick, columns_of(weights, EXTRA, LANES))
        join = new_join()
        for quarter in range(4):
            join.offer(quarter, across(mixed[layer], quarter_of(weights, quarter, OUT, 512)))
        join.wait()

        def after_attention(block, total):
            rows = slab_of(block)
            live = live_rows(lengths, block, SLAB)
            before = trunk[rows, :]
            branch = join.total(rows) + rows_ref[0:1, :]
            scaled, root = norm_parts(before + branch)
            after = scaled * rows_ref[2:3, :] + rows_ref[3:4, :]
            normed[2 * layer, rows, :] = scaled
            inverse[2 * layer, rows, :] = root
            trunk[rows, :] = after
            middle[layer, rows, :] = after.astype(BF16)
            return (
                total[0] + jnp.sum(live * before * before, 0, keepdims=True),
                total[1] + jnp.sum(live * branch * branch, 0, keepdims=True),
            )

        squares = lax.fori_loop(0, 256 // SLAB, after_attention, (zero, zero))
        total_ref[2 + 3 * layer : 3 + 3 * layer, 0:1024] = squares[0]
        total_ref[3 + 3 * layer : 4 + 3 * layer, 0:1024] = squares[1]

        def hidden(tile, carry):
            start = pl.multiple_of(tile * 512, 512)
            columns = pl.ds(start, 512)
            pre = straight(middle[layer], columns_of(weights, INNER + start, 512)) + bias[:, pl.ds(1024 + start, 512)]
            act_part, slope_part = gelu_parts(pre)
            act[layer, :, columns] = act_part.astype(BF16)
            slope[layer, :, columns] = slope_part.astype(BF16)
            return carry

        lax.fori_loop(0, 4, hidden, 0)
        if first:
            three.settle(2)
        join = new_join()
        for quarter in range(4):
            join.offer(quarter, across(act[layer], quarter_of(weights, quarter, OUTER, 2048)))
        join.wait()

        def after_hidden(block, total):
            rows = slab_of(block)
            live = live_rows(lengths, block, SLAB)
            branch = join.total(rows) + rows_ref[1:2, :]
            scaled, root = norm_parts(trunk[rows, :] + branch)
            after = scaled * rows_ref[4:5, :] + rows_ref[5:6, :]
            square = total[0] + jnp.sum(live * branch * branch, 0, keepdims=True)
            if first:
                normed[1, rows, :] = scaled
                inverse[1, rows, :] = root
                trunk[rows, :] = after
                low[1, rows, :] = after.astype(BF16)
                return (square,)
            result[rows, :] = (after * live).astype(BF16)
            grad = grad_in[rows, :].astype(F32)
            return (square, *from_output(rows, grad, scaled, root, total[1:]))

        def from_output(rows, grad, scaled, root, total, layer=layer):
            second = norm_back(grad, scaled, root, rows_ref[4:5, :])
            small = second.astype(BF16)
            trunk[rows, :] = second
            outer_grad[layer, rows, :] = small
            return (
                total[0] + jnp.sum(small.astype(F32), 0, keepdims=True),
                total[1] + jnp.sum(grad * scaled, 0, keepdims=True),
                total[2] + jnp.sum(grad, 0, keepdims=True),
            )

        initial = (zero,) if first else (zero,) * 4
        square, *back = lax.fori_loop(0, 256 // SLAB, after_hidden, initial)
        total_ref[4 + 3 * layer : 5 + 3 * layer, 0:1024] = square
        if not first:
            sums[1], sums[4], sums[5] = back

    for item in gathers:
        item.close()
    grouped = [landings[9 * group : 9 * group + 9] for group in range(3)]
    one, two, three = (
        Scatter(weights, group, [grouped[group][3 * i : 3 * i + 3] for i in range(3)], scatter_send, scatter_recv)
        for group in range(3)
    )
    closing += [one, two, three]
    head_sum = [jnp.zeros((1, 512), F32)] * 2
    each = range(3)
    idle = lambda: None

    def onward(group, phase):
        for third in each:
            group.onward(phase, third)

    for layer in (1, 0):
        last = layer == 0
        heads = HeadsBack(
            mixed_grad.at[layer], taken.at[layer], key_value.at[layer], query_buf.at[layer], grads.at[layer],
            turn_local.at[layer], turn_send.at[layer], turn_recv.at[layer], turn_back_send.at[layer],
            turn_back_recv.at[layer],
        )
        closing.append(heads)
        if last:

            def from_above(block, total):
                rows = slab_of(block)
                grad = trunk[rows, :] + join.total(rows)
                return from_output(rows, grad, normed[1, rows, :], inverse[1, rows, :], total, 0)

            sums[1], sums[4], sums[5] = lax.fori_loop(0, 256 // SLAB, from_above, (sums[1], sums[4], sums[5]))

        def hidden_back(tile, carry):
            start = pl.multiple_of(tile * 512, 512)
            columns = pl.ds(start, 512)
            grad = straight(outer_grad[layer], columns_of(weights, OUTER + start, 512))
            small = (grad * slope[layer, :, columns].astype(F32)).astype(BF16)
            inner_grad[layer, :, columns] = small
            total_ref[0:1, columns] += jnp.sum(small.astype(F32), 0, keepdims=True)
            return carry

        lax.fori_loop(0, 4, hidden_back, 0)
        join = new_join()
        for quarter in range(4):
            join.offer(quarter, across(inner_grad[layer], quarter_of(weights, quarter, INNER, 2048)))
        if last:
            weight_grad(weights, OUTER, outer_grad[...].reshape(512, 1024), act, 2048)
            for third in each:
                three.first(0, third)
            weight_grad(weights, INNER, middle[...].reshape(512, 1024), inner_grad, 2048)
        join.wait()

        def from_middle(block, total):
            rows = slab_of(block)
            grad = trunk[rows, :] + join.total(rows)
            scaled = normed[2 * layer, rows, :]
            before = norm_back(grad, scaled, inverse[2 * layer, rows, :], rows_ref[2:3, :])
            small = before.astype(BF16)
            trunk[rows, :] = before
            attn_grad[layer, rows, :] = small
            return (
                total[0] + jnp.sum(small.astype(F32), 0, keepdims=True),
                total[1] + jnp.sum(grad * scaled, 0, keepdims=True),
                total[2] + jnp.sum(grad, 0, keepdims=True),
            )

        sums[0], sums[2], sums[3] = lax.fori_loop(0, 256 // SLAB, from_middle, (sums[0], sums[2], sums[3]))
        mixed_grad[layer] = straight(attn_grad[layer], columns_of(weights, OUT, 512)).astype(BF16)
        heads.start()
        if last:
            weight_grad(weights, OUT, attn_grad[...].reshape(512, 1024), mixed, 512)
            columns = jnp.concatenate(sums + [jnp.zeros((LANES - 6, 1024), F32)], 0).T
            weights[:, :, :, :, :, EXTRA : EXTRA + LANES] = columns.astype(BF16).reshape(*SHARDS, 16, LANES)
            for third in each:
                two.first(0, third)
        heads.attend(
            length, unit.at[layer], exact.at[layer], logs.at[layer], grad_buf, query_sum,
            (lambda: onward(three, 0)) if last else idle, (lambda: onward(two, 0)) if last else idle,
        )
        if last:
            for third in each:
                three.settle(0, third)
                three.first(1, third)
        heads.collect(0)
        heads.collect(1)
        head_sum[1] = head_sum[1] + jnp.sum(grads[layer, 1].astype(F32), 0, keepdims=True)
        early = [
            across(grads[layer, 0], quarter_of(weights, quarter, KEY, 512))
            + across(grads[layer, 1], quarter_of(weights, quarter, VALUE, 512))
            for quarter in range(4)
        ]
        left = low[...].reshape(512, 1024)
        if last:
            weight_grad(weights, KEY, left, grads.at[:, 0], 512)
            one.first(0, 1)
            weight_grad(weights, VALUE, left, grads.at[:, 1], 512)
            one.first(0, 2)
        heads.collect(2)
        head_sum[0] = head_sum[0] + jnp.sum(grads[layer, 2].astype(F32), 0, keepdims=True)
        join = new_join()
        for quarter in range(4):
            join.offer(
                quarter, early[quarter] + across(grads[layer, 2], quarter_of(weights, quarter, QUERY, 512))
            )
        if last:
            weight_grad(weights, QUERY, left, grads.at[:, 2], 512)
            one.first(0, 0)
            total_ref[1:2, 0:512] = head_sum[0]
            total_ref[1:2, 512:1024] = head_sum[1]
            count = sum(jnp.clip(lengths[s] - c * ROWS, 0, ROWS) for s in range(2)).astype(F32)
            total_ref[1:2, 1024:1152] = jnp.full((1, LANES), count, F32)
        else:
            join.wait()

    totals = Totals(total_ref, total_land, total_send, total_recv)
    totals.first(0)
    for third in each:
        two.settle(0, third)
        two.first(1, third)
    onward(three, 1)
    join.wait()
    for s in range(2):
        rows = pl.ds(s * ROWS, ROWS)
        stream_grad[:, s, :] = trunk[rows, :] + join.total(rows)
    onward(one, 0)
    totals.settle(0)
    totals.first(1)
    for third in each:
        three.settle(1, third)
        three.direct(2, third)
    onward(two, 1)
    result_ref[...] = jnp.stack([result[s * ROWS : s * ROWS + ROWS, :].astype(F32) for s in range(2)], 1).astype(BF16)
    for third in (1, 2, 0):
        one.settle(0, third)
        one.direct(1, third)
    totals.settle(1)
    totals.first(2)
    for third in each:
        two.settle(1, third)
        two.direct(2, third)
    for third in each:
        three.arrive(2, third)
    for third in (1, 2, 0):
        one.arrive(1, third)
        one.direct(2, third)

    def mine(start, width):
        return weights[x // 2, at["z"], x % 2, at["y"], :, start : start + width].astype(F32)

    outer_out[...] = mine(OUTER, 2048)
    for third in each:
        two.arrive(2, third)
    output_out[...] = mine(OUT, 512)
    inner_out[...] = mine(INNER, 2048)
    vector_out[...] = mine(EXTRA, LANES).T[0:8, :]
    totals.settle(2)
    scale = 1.0 / (total_ref[1:2, 1024:1025] * 1024.0)
    square = jnp.sum(total_ref[:, 0:1024], 1, keepdims=True)
    root_ref[...] = jnp.broadcast_to(jnp.sqrt(square * scale + 1e-06), root_ref.shape)
    for third in (1, 2, 0):
        one.arrive(2, third)
    query_out[...] = mine(QUERY, 512)
    key_out[...] = mine(KEY, 512)
    value_out[...] = mine(VALUE, 512)
    for item in closing + joined[-2:]:
        item.close()


def run_layers(*arguments):
    dma = pltpu.SemaphoreType.DMA
    out = lambda *shape: jax.ShapeDtypeStruct(shape, F32)
    vmem = lambda kind, *shape: pltpu.VMEM(shape, kind)
    return pl.pallas_call(
        layers_kernel,
        out_shape=(
            out(ROWS, 2, 1024), jax.ShapeDtypeStruct((ROWS, 2, 1024), BF16),
            out(16, 512), out(16, 512), out(16, 512), out(16, 512), out(16, 2048), out(16, 2048),
            out(8, 16), out(8, 2048), out(8, LANES),
        ),
        in_specs=[spec(pltpu.VMEM)] * 17 + [spec(pltpu.SMEM)],
        out_specs=(spec(pltpu.VMEM),) * 11,
        scratch_shapes=[
            vmem(BF16, *SHARDS, 16, WIDTH),
            vmem(F32, 1, 3072),
            vmem(F32, 8, 1024),
            vmem(BF16, 2, 256, 1024),
            vmem(BF16, 256, 1024),
            vmem(BF16, 256, 1024),
            vmem(F32, 256, 1024),
            vmem(BF16, 3, 256, 512),
            vmem(BF16, 2, 3, 1024, LANES),
            vmem(F32, 2, 1024, LANES),
            vmem(F32, 2, 8, 256),
            vmem(BF16, 2, 1024, LANES),
            vmem(BF16, 2, 256, 512),
            vmem(F32, 3, 256, 1024),
            vmem(F32, 3, 256, 1),
            vmem(BF16, 2, 256, 1024),
            vmem(BF16, 2, 256, 2048),
            vmem(BF16, 2, 256, 2048),
            vmem(BF16, 2, 256, 1024),
            vmem(BF16, 2, 256, 2048),
            vmem(BF16, 2, 256, 1024),
            vmem(BF16, 2, 3, 256, 512),
            vmem(BF16, 2, 256, 512),
            vmem(BF16, 2, 1024, LANES),
            vmem(BF16, 2048, LANES),
            vmem(F32, 2048, LANES),
            vmem(BF16, 2, 2, 1024, LANES),
            vmem(BF16, 2, 1024, LANES),
            vmem(BF16, 2, 2, 256, 512),
            vmem(BF16, 2, 2, 256, 512),
            vmem(F32, 3, 3, 8, 2048),
            dma((2, 4)),
            dma((3, 3, 3, 4)),
            dma((3, 3, 3, 4)),
            dma((2, 3, 7)),
            dma((2, 3, 7)),
            dma((2, 7)),
            dma((2, 7)),
            dma((8, 2)),
            dma((8, 2)),
            dma((2, 4)),
            dma((2, 7)),
            dma((2, 7)),
            dma((2, 3, 7)),
            dma((2, 3, 7)),
            dma((3, 3)),
            dma((3, 3)),
            dma((3, 3, 3, 6)),
            dma((3, 3, 3, 6)),
            *(shape for group in range(3) for shape in landing_shapes(group)),
        ],
        compiler_params=pltpu.CompilerParams(
            collective_id=3, has_side_effects=True, vmem_limit_bytes=LIMIT
        ),
        name="layers",
    )(*arguments)


def finish_kernel(
    stream_in, result_in, query_in, key_in, value_in, output_in, inner_in, outer_in, vectors, totals, roots,
    result, stream_grad, query, key, value, output, inner, outer, query_sum, value_sum, inner_sum, *rest,
):
    for source, target in (
        (result_in, result), (stream_in, stream_grad), (query_in, query), (key_in, key), (value_in, value),
        (output_in, output), (inner_in, inner), (outer_in, outer),
    ):
        target[...] = source[...]
    query_sum[...] = totals[1:2, 0:512].reshape(512)
    value_sum[...] = totals[1:2, 512:1024].reshape(512)
    inner_sum[...] = totals[0:1, :].reshape(2048)
    for j in range(6):
        rest[j][...] = vectors[j : j + 1, :].reshape(16)
    rest[6][...] = jnp.concatenate(
        [
            jnp.concatenate([roots[2 + 3 * layer + j : 3 + 3 * layer + j, 0:1] for j in range(3)], 1)
            for layer in range(LAYERS)
        ],
        0,
    )


def finish(partial):
    out = lambda *shape: jax.ShapeDtypeStruct(shape, F32)
    return pl.pallas_call(
        finish_kernel,
        out_shape=(
            jax.ShapeDtypeStruct((ROWS, 2, 1024), BF16), out(ROWS, 2, 1024),
            out(16, 512), out(16, 512), out(16, 512), out(16, 512), out(16, 2048), out(16, 2048),
            out(512), out(512), out(2048), *(out(16) for _ in range(6)), out(LAYERS, 3),
        ),
        in_specs=[spec(pltpu.VMEM)] * 11,
        out_specs=(spec(pltpu.VMEM),) * 18,
        name="finish",
    )(*partial)


def body(
    stream,
    lengths,
    query_weight,
    query_bias,
    key_weight,
    value_weight,
    value_bias,
    output_weight,
    output_bias,
    first_gain,
    first_shift,
    inner_weight,
    inner_bias,
    outer_weight,
    outer_bias,
    second_gain,
    second_shift,
    cotangent,
):
    partial = run_layers(
        stream, cotangent, query_weight, key_weight, value_weight, output_weight.T, inner_weight, outer_weight.T,
        output_bias, outer_bias, first_gain, first_shift, second_gain, second_shift,
        query_bias, value_bias, inner_bias, lengths,
    )
    (
        result, stream_grad, grad_query, grad_key, grad_value, grad_output, grad_inner, grad_outer,
        query_sum, value_sum, inner_sum, *vectors, roots,
    ) = finish(partial)
    return (
        result,
        stream_grad,
        grad_query,
        query_sum,
        grad_key,
        grad_value,
        value_sum,
        grad_output.T,
        vectors[0],
        vectors[2],
        vectors[3],
        grad_inner,
        inner_sum,
        grad_outer.T,
        vectors[1],
        vectors[4],
        vectors[5],
        roots,
    )


def solution(mesh):
    in_specs = (
        P("context", "fsdp", None),
        P("fsdp"),
        P(("fsdp", "context"), "tensor"),
        P("tensor"),
        P(("fsdp", "context"), "tensor"),
        P(("fsdp", "context"), "tensor"),
        P("tensor"),
        P("tensor", ("fsdp", "context")),
        P(("fsdp", "context")),
        P(("fsdp", "context")),
        P(("fsdp", "context")),
        P(("fsdp", "context"), "tensor"),
        P("tensor"),
        P("tensor", ("fsdp", "context")),
        P(("fsdp", "context")),
        P(("fsdp", "context")),
        P(("fsdp", "context")),
        P("context", "fsdp", None),
    )
    out_specs = (
        P("context", "fsdp", None),
        P("context", "fsdp", None),
        P(("fsdp", "context"), "tensor"),
        P("tensor"),
        P(("fsdp", "context"), "tensor"),
        P(("fsdp", "context"), "tensor"),
        P("tensor"),
        P("tensor", ("fsdp", "context")),
        P(("fsdp", "context")),
        P(("fsdp", "context")),
        P(("fsdp", "context")),
        P(("fsdp", "context"), "tensor"),
        P("tensor"),
        P("tensor", ("fsdp", "context")),
        P(("fsdp", "context")),
        P(("fsdp", "context")),
        P(("fsdp", "context")),
        P(),
    )
    return jax.shard_map(body, mesh=mesh, in_specs=in_specs, out_specs=out_specs, check_vma=False)
```

```python
import jax
import jax.numpy as jnp
from jax import lax
from jax.experimental import pallas as pl
from jax.experimental.pallas import tpu as pltpu
from jax.sharding import PartitionSpec as P

HEAD = 64
LAYERS = 2
LANES = 128
MESH = pl.DeviceIdType.MESH

F32 = jnp.float32
BF16 = jnp.bfloat16
ROWS = 128
LIMIT = 60 * 2**20
WIDTH = 6272
QUERY, KEY, VALUE, OUT, EXTRA, INNER, OUTER = 0, 512, 1024, 1536, 2048, 2176, 4224
GROUPS = ((QUERY, OUT), (OUT, OUTER), (OUTER, WIDTH))
TILES = (((2, 2), (2, 2), (2, 2)), ((3, 3), (4, 5), (3, 3)), ((2, 3), (3, 3), (2, 3)))
ORDERS = ("zyx", "yxz", "xzy")
SHARDS = (2, 4, 2, 4)


def spec(space):
    return pl.BlockSpec(memory_space=space)


def place():
    f = lax.axis_index("fsdp")
    c = lax.axis_index("context")
    t = lax.axis_index("tensor")
    return {"x": 2 * (f // 4) + c // 4, "y": c % 4, "z": f % 4, "t": t}


def device(at):
    x = at["x"]
    return ((x // 2) * 4 + at["z"], (x % 2) * 4 + at["y"], at["t"])


def shifted(at, axis, step):
    moved = dict(at)
    moved[axis] = lax.rem(at[axis] + step + 4, 4)
    return moved


def greet(devices):
    barrier = pltpu.get_barrier_semaphore()
    for device_id in devices:
        pl.semaphore_signal(barrier, inc=1, device_id=device_id, device_id_type=MESH)
    pl.semaphore_wait(barrier, len(devices))


def neighbours(at, steps):
    return [device(shifted(at, axis, step)) for axis in "xyz" for step in steps]


def context_peers():
    f = lax.axis_index("fsdp")
    c = lax.axis_index("context")
    t = lax.axis_index("tensor")
    return [(f, lax.rem(c + d, 8), t) for d in range(1, 8)]


def remote(src, dst, send_sem, recv_sem, device_id):
    return pltpu.make_async_remote_copy(
        src_ref=src,
        dst_ref=dst,
        send_sem=send_sem,
        recv_sem=recv_sem,
        device_id=device_id,
        device_id_type=MESH,
    )


def drain(ref, sem):
    pltpu.make_async_copy(ref, ref, sem).wait()


def bulk(ref, count, group):
    start, end = GROUPS[group]
    picks = {
        3: (0, 0, 0, slice(0, 3)),
        8: (0, slice(0, 2), 0),
        12: (0, slice(0, 3), 0),
        32: (0,),
        48: (slice(None), slice(0, 3)),
    }[count]
    picks = picks + (slice(None),) * (5 - len(picks))
    return ref.at[picks + (pl.ds(start, end - start),)]


def shards(ref, at, whole, cols):
    x = at["x"]
    xh = slice(None) if "x" in whole else x // 2
    xl = slice(None) if "x" in whole else x % 2
    z = slice(None) if "z" in whole else at["z"]
    y = slice(None) if "y" in whole else at["y"]
    return ref.at[xh, z, xl, y, :, pl.ds(cols[0], cols[1])]


def thirds(group):
    start = GROUPS[group][0]
    parts = []
    for pair in TILES[group]:
        halves = []
        for tiles in pair:
            halves.append((start, tiles * LANES))
            start += tiles * LANES
        parts.append(tuple(halves))
    return parts


def across(left, right):
    return lax.dot_general(left, right, (((1,), (1,)), ((), ())), preferred_element_type=F32)


def straight(left, right):
    return jnp.dot(left, right, preferred_element_type=F32)


def rows_of(block):
    return pl.ds(pl.multiple_of(block * ROWS, ROWS), ROWS)


def by_head(block):
    first = lax.broadcasted_iota(jnp.int32, block.shape, 1) < HEAD
    zero = jnp.zeros_like(block)
    return jnp.concatenate([jnp.where(first, block, zero), jnp.where(first, zero, block)], 0)


def key_mask(length, first, count):
    position = first + lax.broadcasted_iota(jnp.int32, (count, 1), 0)
    return jnp.where(position < length, 0.0, -1e30)


def columns_of(weights, start, width):
    return weights[:, :, :, :, :, pl.ds(start, width)].reshape(1024, width)


def quarter_of(weights, quarter, start, width):
    z = 2 * (quarter % 2)
    return weights[quarter // 2, z : z + 2, :, :, :, start : start + width].reshape(256, width)


def part(ref, peer):
    return ref.at[rows_of(peer // 4), rows_of(peer % 4)]


class Gather:
    def __init__(self, weights, group, send_sem, recv_sem):
        self.at = place()
        self.weights, self.group = weights, group
        self.send_sem, self.recv_sem = send_sem, recv_sem
        self.parts = thirds(group)
        self.sent = {}

    def send(self, third, phase, kind, origin, cols, step):
        order = ORDERS[third]
        block = shards(self.weights, origin, order[:phase], cols)
        if kind is None or kind > 1:
            slot = 6
        else:
            slot = 2 * third + kind
        copy = remote(
            block, block, self.send_sem.at[self.group, phase], self.recv_sem.at[self.group, phase, slot],
            device(shifted(self.at, order[phase], step)),
        )
        copy.start()
        self.sent[third, phase, kind] = copy

    def first(self, phase, thirds_now=range(3), pieces=(0, 1)):
        for piece in pieces:
            for third in thirds_now:
                low, high = self.parts[third]
                self.send(third, phase, 2 * piece, self.at, (low, high)[piece], 1)
                self.send(third, phase, 2 * piece + 1, self.at, (high, low)[piece], -1)

    def direct(self, phase):
        for third in range(3):
            low, high = self.parts[third]
            for step in (1, 2, 3):
                self.send(third, phase, None, self.at, (low[0], low[1] + high[1]), step)

    def arrive(self, phase):
        drain(bulk(self.weights, (3, 12)[phase], self.group), self.recv_sem.at[self.group, phase, 6])

    def onward(self, phase, thirds_now=range(3)):
        for third in thirds_now:
            axis = ORDERS[third][phase]
            low, high = self.parts[third]
            self.sent[third, phase, 0].wait_recv()
            self.send(third, phase, 4, shifted(self.at, axis, -1), low, 1)
            self.sent[third, phase, 1].wait_recv()
            self.send(third, phase, 5, shifted(self.at, axis, 1), high, -1)

    def settle(self, phase):
        drain(bulk(self.weights, (2, 8, 32)[phase], self.group), self.recv_sem.at[self.group, phase, 6])

    def close(self):
        for phase in range(3):
            drain(bulk(self.weights, (3, 12, 48)[phase], self.group), self.send_sem.at[self.group, phase])


def seven(ref):
    return ref.at[pl.ds(0, 7 * ROWS)]


class Heads:
    def __init__(self, own, unit, outcome, mixed, local_sem, send_sem, recv_sem, back_send, back_recv):
        self.f = lax.axis_index("fsdp")
        self.c = lax.axis_index("context")
        self.t = lax.axis_index("tensor")
        self.own, self.unit, self.outcome, self.mixed = own, unit, outcome, mixed
        self.local_sem, self.send_sem, self.recv_sem = local_sem, send_sem, recv_sem
        self.back_send, self.back_recv = back_send, back_recv

    def push(self, j, d):
        peer = lax.rem(self.c + d, 8)
        return remote(
            part(self.own.at[j], peer), self.unit.at[j, rows_of(self.c)],
            self.send_sem.at[j], self.recv_sem.at[j, d - 1 if j == 2 else 0], (self.f, peer, self.t),
        )

    def keep(self, j):
        return pltpu.make_async_copy(
            part(self.own.at[j], self.c), self.unit.at[j, rows_of(self.c)], self.local_sem.at[j]
        )

    def answer(self, d):
        peer = lax.rem(self.c + d, 8)
        return remote(
            self.outcome.at[rows_of(peer)], part(self.mixed, self.c),
            self.back_send.at[0], self.back_recv.at[0], (self.f, peer, self.t),
        )

    def keep_back(self):
        return pltpu.make_async_copy(
            self.outcome.at[rows_of(self.c)], part(self.mixed, self.c), self.local_sem.at[3]
        )

    def project(self, x, weights, bias):
        for j, column in enumerate((KEY, VALUE, QUERY)):
            product = straight(x, columns_of(weights, column, 512))
            if j == 1:
                product = product + bias[:, 512:1024]
            if j == 2:
                product = product + bias[:, 0:512]
            self.own[j] = product.astype(BF16)
            for d in (4, 1, 7, 5, 3, 2, 6):
                self.push(j, d).start()
            self.keep(j).start()

    def attend(self, length, exact, logs):
        c = self.c
        for j in range(2):
            self.keep(j).wait()
            drain(seven(self.outcome), self.recv_sem.at[j, 0])
        mask = key_mask(length, 0, 8 * ROWS)
        keys = self.unit[0]
        values_across = self.unit[1].T
        self.keep(2).wait()

        def step(d, carry):
            block = lax.rem(c + d, 8)

            @pl.when(d > 0)
            def _():
                self.push(2, 8 - d).wait_recv()

            queries = self.unit[2, rows_of(block), :] * jnp.asarray(0.125, BF16)
            scores = across(keys, by_head(queries)) + mask
            top = jnp.max(scores, 0, keepdims=True)
            exponent = jnp.exp(scores - top)
            total = jnp.sum(exponent, 0, keepdims=True)
            outcome = straight(values_across, exponent.astype(BF16)) / total
            both = jnp.concatenate([outcome[:HEAD, :ROWS], outcome[HEAD:, ROWS:]], 0).T
            exact[rows_of(block), :] = both
            self.outcome[rows_of(block), :] = both.astype(BF16)
            logs[pl.ds(block, 1), :] = top + jnp.log(total)

            @pl.when(d > 0)
            def _():
                self.answer(d).start()

            return carry

        lax.fori_loop(0, 8, step, 0)
        self.keep_back().start()

    def collect(self):
        self.keep_back().wait()
        drain(seven(self.outcome), self.back_recv.at[0])

    def close(self):
        drain(seven(self.outcome), self.back_send.at[0])
        for j in range(3):
            drain(seven(self.outcome), self.send_sem.at[j])


class Join:
    def __init__(self, number, before, sent, landed, send_sem, recv_sem):
        t = lax.axis_index("tensor")
        self.partner = (lax.axis_index("fsdp"), lax.axis_index("context"), 1 - t)
        self.sent, self.landed = sent.at[number % 2], landed.at[number % 2]
        self.send_sem, self.recv_sem = send_sem.at[number % 2], recv_sem.at[number % 2]
        self.before = before

    def copy(self, half):
        return remote(
            self.sent.at[half], self.landed.at[half], self.send_sem, self.recv_sem, self.partner,
        )

    def offer(self, quarter, term):
        half, side = quarter // 2, quarter % 2
        if quarter == 0 and self.before is not None:
            self.before.close()
        self.sent[half, :, side * 256 : side * 256 + 256] = term.astype(BF16)
        if side == 1:
            self.copy(half).start()

    def wait(self):
        drain(self.landed, self.recv_sem)

    def total(self, rows):
        return jnp.concatenate(
            [self.sent[half, rows, :].astype(F32) + self.landed[half, rows, :].astype(F32) for half in range(2)],
            1,
        )

    def close(self):
        drain(self.sent, self.send_sem)


def gelu_parts(argument):
    square = argument * argument
    inner = 0.7978845608028654 * argument * (1.0 + 0.044715 * square)
    bend = jnp.tanh(inner)
    half = 0.5 * (1.0 + bend)
    slope = half + 0.5 * argument * (1.0 - bend * bend) * 0.7978845608028654 * (
        1.0 + 3.0 * 0.044715 * square
    )
    return argument * half, slope


def norm_parts(hidden):
    centre = hidden - jnp.mean(hidden, -1, keepdims=True)
    inverse = lax.rsqrt(jnp.mean(centre * centre, -1, keepdims=True) + 1e-05)
    return centre * inverse, inverse


def live_rows(lengths, block, count):
    c = lax.axis_index("context")
    row = block * count + lax.broadcasted_iota(jnp.int32, (count, 1), 0)
    slot = c * ROWS + lax.rem(row, ROWS)
    return jnp.where(slot < jnp.where(row < ROWS, lengths[0], lengths[1]), 1.0, 0.0)


SLAB = 64


def slab_of(block):
    return pl.ds(pl.multiple_of(block * SLAB, SLAB), SLAB)


def pack(weights, own, query, key, value, output, inner, outer, vectors):
    xh, z, xl, y = own

    def put(start, block):
        weights[xh, z, xl, y, :, start : start + block.shape[1]] = block

    put(QUERY, query[...])
    put(KEY, key[...])
    put(VALUE, value[...])
    put(OUT, output[...])
    put(INNER, inner[...])
    put(OUTER, outer[...])
    eye = jnp.where(
        lax.broadcasted_iota(jnp.int32, (16, 16), 0) == lax.broadcasted_iota(jnp.int32, (16, 16), 1), 1.0, 0.0
    ).astype(BF16)
    rows = [vector[...].astype(F32).reshape(1, 16) for vector in vectors]
    table = jnp.concatenate(rows + [jnp.zeros((LANES - 6, 16), F32)], 0).astype(BF16)
    put(EXTRA, across(eye, table).astype(BF16))


def rows_by_sequence(source, target, keep):
    whole = source[...].astype(F32)
    for s in range(2):
        target[s * ROWS : s * ROWS + ROWS, :] = (whole[:, s, :] * keep(s)).astype(target.dtype)


def norm_back(grad_out, normed, inverse, gain):
    scaled = grad_out * gain
    return inverse * (
        scaled
        - jnp.mean(scaled, -1, keepdims=True)
        - normed * jnp.mean(scaled * normed, -1, keepdims=True)
    )


class Scatter:
    def __init__(self, work, group, landings, send_sem, recv_sem):
        self.at = place()
        self.work, self.group, self.landings = work, group, landings
        self.send_sem, self.recv_sem = send_sem, recv_sem
        self.parts = thirds(group)
        self.sent = {}

    def ring(self, third, phase):
        order = ORDERS[third][::-1]
        return order[phase], order[phase + 1 :]

    def send(self, third, phase, kind, away, cols, step):
        axis, whole = self.ring(third, phase)
        land = self.landings[third][phase].at[kind]
        if cols[1] != land.shape[-1]:
            land = land.at[..., pl.ds(0, cols[1])]
        slot = kind // 2 + 1 if kind > 1 else kind
        if phase in DIRECT[self.group]:
            slot = 0
        copy = remote(
            shards(self.work, shifted(self.at, axis, away), whole, cols), land,
            self.send_sem.at[self.group, phase], self.recv_sem.at[self.group, phase, third, slot],
            device(shifted(self.at, axis, step)),
        )
        copy.start()
        self.sent[third, phase, kind] = copy

    def add(self, third, phase, away, cols, kinds):
        axis, whole = self.ring(third, phase)
        origin = shifted(self.at, axis, away)
        land = self.landings[third][phase]
        x = origin["x"]
        wide = {name: name in whole for name in "xyz"}
        columns = pl.ds(cols[0], cols[1])

        def one(ix, iz):
            xh, xl = (ix // 2, ix % 2) if wide["x"] else (x // 2, x % 2)
            z = iz if wide["z"] else origin["z"]
            y = slice(None) if wide["y"] else origin["y"]
            index = (xh, z, xl, y, slice(None), columns)
            total = self.work[index].astype(F32)
            for kind in kinds:
                at = (kind,)
                at += (xh,) if wide["x"] else ()
                at += (z,) if wide["z"] else ()
                at += (xl,) if wide["x"] else ()
                at += (slice(None),) if wide["y"] else ()
                total = total + land[at + (slice(None), pl.ds(0, cols[1]))].astype(F32)
            self.work[index] = total.astype(BF16)

        count_z = 4 if wide["z"] else 1
        if not wide["x"]:
            for iz in range(count_z):
                one(0, iz)
        else:
            def turn(ix, carry):
                for iz in range(count_z):
                    one(ix, iz)
                return carry

            lax.fori_loop(0, 4, turn, 0)

    def first(self, phase, third, pieces=(0, 1)):
        low, high = self.parts[third]
        if 0 in pieces:
            self.send(third, phase, 0, 2, low, 1)
            self.send(third, phase, 1, 2, high, -1)
        if 1 in pieces:
            self.send(third, phase, 2, 1, high, 1)
            self.send(third, phase, 3, -1, low, -1)

    def direct(self, phase, third):
        low, high = self.parts[third]
        for step in (1, 2, 3):
            self.send(third, phase, step - 1, step, (low[0], low[1] + high[1]), step)

    def arrive(self, phase, third):
        low, high = self.parts[third]
        drain(self.landings[third][phase], self.recv_sem.at[self.group, phase, third, 0])
        self.add(third, phase, 0, (low[0], low[1] + high[1]), (0, 1, 2))

    def onward(self, phase, third):
        low, high = self.parts[third]
        self.sent[third, phase, 0].wait_recv()
        self.add(third, phase, 1, low, (0,))
        self.send(third, phase, 4, 1, low, 1)
        self.sent[third, phase, 1].wait_recv()
        self.add(third, phase, -1, high, (1,))
        self.send(third, phase, 5, -1, high, -1)

    def settle(self, phase, third):
        low, high = self.parts[third]
        axis, whole = self.ring(third, phase)
        block = shards(self.work, self.at, whole, (low[0], low[1] + high[1]))
        for slot in (2, 3):
            drain(block, self.recv_sem.at[self.group, phase, third, slot])
        self.add(third, phase, 0, high, (2, 5))
        self.add(third, phase, 0, low, (3, 4))

    def close(self):
        for phase in range(3):
            drain(bulk(self.work, (48, 12, 3)[phase], self.group), self.send_sem.at[self.group, phase])


DIRECT = ((1, 2), (2,), (2,))


def landing_shapes(group):
    shapes = []
    for third in range(3):
        order = ORDERS[third][::-1]
        low, high = thirds(group)[third]
        for phase in range(3):
            whole = order[phase + 1 :]
            direct = phase in DIRECT[group]
            shape = [3 if direct else 6]
            shape += [2] if "x" in whole else []
            shape += [4] if "z" in whole else []
            shape += [2] if "x" in whole else []
            shape += [4] if "y" in whole else []
            width = low[1] + high[1] if direct else max(low[1], high[1])
            shapes.append(pltpu.VMEM((*shape, 16, width), BF16))
    return shapes


class Totals:
    def __init__(self, total, landed, send_sem, recv_sem):
        self.at = place()
        self.total, self.landed, self.send_sem, self.recv_sem = total, landed, send_sem, recv_sem

    def copy(self, phase, step):
        return remote(
            self.total, self.landed.at[phase, step - 1], self.send_sem.at[phase], self.recv_sem.at[phase], device(shifted(self.at, "xyz"[phase], step)),
        )

    def first(self, phase):
        for step in (1, 2, 3):
            self.copy(phase, step).start()

    def settle(self, phase):
        drain(self.landed.at[phase], self.recv_sem.at[phase])
        drain(self.landed.at[phase], self.send_sem.at[phase])
        self.total[...] += self.landed[phase, 0] + self.landed[phase, 1] + self.landed[phase, 2]


class HeadsBack:
    def __init__(self, mixed_grad, taken, key_value, query, grads, local_sem, send_sem, recv_sem, back_send, back_recv):
        self.f = lax.axis_index("fsdp")
        self.c = lax.axis_index("context")
        self.t = lax.axis_index("tensor")
        self.mixed_grad, self.taken, self.grads = mixed_grad, taken, grads
        self.sources = (key_value.at[0], key_value.at[1], query)
        self.key_value, self.query = key_value, query
        self.local_sem, self.send_sem, self.recv_sem = local_sem, send_sem, recv_sem
        self.back_send, self.back_recv = back_send, back_recv

    def push(self, d):
        peer = lax.rem(self.c + d, 8)
        return remote(
            part(self.mixed_grad, peer), self.taken.at[rows_of(self.c)],
            self.send_sem.at[0], self.recv_sem.at[0], (self.f, peer, self.t),
        )

    def keep(self):
        return pltpu.make_async_copy(
            part(self.mixed_grad, self.c), self.taken.at[rows_of(self.c)], self.local_sem.at[3]
        )

    def answer(self, j, d):
        peer = lax.rem(self.c + d, 8)
        return remote(
            self.sources[j].at[rows_of(peer)], part(self.grads.at[j], self.c),
            self.back_send.at[j], self.back_recv.at[j, 0], (self.f, peer, self.t),
        )

    def keep_back(self, j):
        return pltpu.make_async_copy(
            self.sources[j].at[rows_of(self.c)], part(self.grads.at[j], self.c), self.local_sem.at[j]
        )

    def start(self):
        for d in (4, 1, 7, 5, 3, 2, 6):
            self.push(d).start()
        self.keep().start()

    def attend(self, length, unit, exact, logs_ref, grad_buf, query_sum, ahead, midway):
        c = self.c
        scale = jnp.asarray(0.125, BF16)
        queries = jnp.concatenate(
            [by_head(unit[2, pl.ds(block * ROWS, ROWS), :] * scale) for block in range(8)], 0
        )
        logs = jnp.concatenate([logs_ref[block : block + 1, :] for block in range(8)], 1)
        query_sum[...] = jnp.zeros_like(query_sum)
        ahead()
        self.keep().wait()
        drain(seven(self.taken), self.recv_sem.at[0])
        for block in range(8):
            grad_buf[pl.ds(block * 256, 256), :] = by_head(self.taken[pl.ds(block * ROWS, ROWS), :])
        head_row = lax.broadcasted_iota(jnp.int32, (8, LANES), 0)
        head_lane = lax.broadcasted_iota(jnp.int32, (8, LANES), 1) // HEAD
        chosen = jnp.where(head_row == head_lane, 1.0, 0.0)
        weighted = lax.dot_general(
            chosen, self.taken[...].astype(F32) * exact[...],
            (((1,), (1,)), ((), ())), precision=lax.Precision.HIGHEST, preferred_element_type=F32,
        )
        delta = jnp.concatenate(
            [
                weighted[head : head + 1, block * ROWS : (block + 1) * ROWS]
                for block in range(8)
                for head in range(2)
            ],
            1,
        )

        def step(turn, carry):
            pair = lax.rem(c // 2 + turn, 4)
            spot = pl.ds(pl.multiple_of(pair * 256, 256), 256)
            keys = unit[0, spot, :]
            values = unit[1, spot, :]
            scores = across(keys, queries) + key_mask(length, pair * 256, 256)
            soft = jnp.exp(scores - logs)
            self.key_value[1, spot, :] = straight(soft.astype(BF16), grad_buf[...]).astype(BF16)
            soft_grad = across(values, grad_buf[...])
            score_grad = (soft * (soft_grad - delta)).astype(BF16)
            self.key_value[0, spot, :] = straight(score_grad, queries).astype(BF16)
            query_sum[...] += lax.dot_general(
                score_grad, keys, (((0,), (0,)), ((), ())), preferred_element_type=F32
            )

            for side in range(2):
                d = lax.rem(pair * 2 + side - c + 8, 8)

                @pl.when(d > 0)
                def _():
                    for j in range(2):
                        self.answer(j, d).start()

            return carry

        lax.fori_loop(1, 3, step, 0)
        midway()
        lax.fori_loop(3, 5, step, 0)
        first_lane = lax.broadcasted_iota(jnp.int32, (ROWS, LANES), 1) < HEAD
        for block in range(8):
            start = block * 256
            total = jnp.where(
                first_lane, query_sum[pl.ds(start, ROWS), :], query_sum[pl.ds(start + ROWS, ROWS), :]
            )
            self.query[pl.ds(block * ROWS, ROWS), :] = (total * 0.125).astype(BF16)
        for d in (4, 1, 7, 5, 3, 2, 6):
            self.answer(2, d).start()
        for j in range(3):
            self.keep_back(j).start()

    def collect(self, j):
        self.keep_back(j).wait()
        drain(seven(self.taken), self.back_recv.at[j, 0])

    def close(self):
        drain(seven(self.taken), self.send_sem.at[0])
        for j in range(3):
            drain(seven(self.taken), self.back_send.at[j])


def put_quarter(work, quarter, start, value):
    z = 2 * (quarter % 2)
    work[quarter // 2, z : z + 2, :, :, :, pl.ds(start, value.shape[1])] = value.astype(BF16).reshape(
        2, 2, 4, 16, value.shape[1]
    )


def weight_grad(work, start, left, right, width):
    turned = left.T
    tile = 512

    def turn(i, carry):
        offset = pl.multiple_of(i * tile, tile)
        term = right[:, :, pl.ds(offset, tile)].reshape(512, tile)
        for quarter in range(4):
            put_quarter(work, quarter, start + offset, straight(turned[quarter * 256 : quarter * 256 + 256], term))
        return carry

    lax.fori_loop(0, width // tile, turn, 0)


def layers_kernel(
    stream, cotangent, query, key, value, output, inner, outer, bias0, bias1, gain1, shift1, gain2, shift2,
    query_bias, value_bias, inner_bias, lengths,
    stream_grad, result_ref, query_out, key_out, value_out, output_out, inner_out, outer_out, vector_out, total_ref,
    root_ref,
    weights, bias, rows_ref, low, grad_in, result, trunk,
    own, unit, exact, logs, outcome, mixed, normed, inverse, middle, act, slope,
    attn_grad, inner_grad, outer_grad, grads, mixed_grad, taken, grad_buf, query_sum, key_value, query_buf,
    sent, landed, total_land,
    local_sem, gather_send, gather_recv, send_sem, recv_sem, back_send, back_recv, pair_send, pair_recv,
    turn_send, turn_recv, total_send, total_recv,
    scatter_send, scatter_recv, *landings,
):
    at = place()
    c = lax.axis_index("context")
    t = lax.axis_index("tensor")
    partner = (lax.axis_index("fsdp"), c, 1 - t)
    x = at["x"]
    closing = []
    joined = []

    def new_join():
        before = joined[-2] if len(joined) > 1 else None
        joined.append(Join(len(joined), before, sent, landed, pair_send, pair_recv))
        return joined[-1]

    pack(
        weights, (x // 2, at["z"], x % 2, at["y"]), query, key, value, output, inner, outer,
        (bias0, bias1, gain1, shift1, gain2, shift2),
    )
    greet(neighbours(at, (1, 2, 3)) + context_peers() + [partner])
    one, two, three = (Gather(weights, group, gather_send, gather_recv) for group in range(3))
    gathers = (one, two, three)
    for group in gathers:
        group.direct(0)
    rows_by_sequence(stream, low.at[0], lambda s: 1.0)
    one.arrive(0)
    one.direct(1)
    two.arrive(0)
    two.first(1)
    three.arrive(0)
    three.first(1)
    bias[:, 0:512] = query_bias[...].astype(F32).reshape(1, 512)
    bias[:, 512:1024] = value_bias[...].astype(F32).reshape(1, 512)
    bias[:, 1024:3072] = inner_bias[...].astype(F32).reshape(1, 2048)
    position = c * ROWS + lax.broadcasted_iota(jnp.int32, (ROWS, 1), 0)
    rows_by_sequence(cotangent, grad_in, lambda s: jnp.where(position < lengths[s], 1.0, 0.0))
    trunk[...] = low[0].astype(F32)
    total_ref[...] = jnp.zeros_like(total_ref)
    one.arrive(1)
    one.first(2)
    two.onward(1)
    three.onward(1)
    one.onward(2)
    two.settle(1)
    two.first(2)
    three.settle(1)
    three.first(2, (1,))
    one.settle(2)
    length = lengths[c // 4]
    zero = jnp.zeros((1, 1024), F32)
    sums = [zero] * 6

    for layer in range(LAYERS):
        first = layer == 0
        heads = Heads(
            own, unit.at[layer], outcome.at[layer], mixed.at[layer], local_sem,
            send_sem, recv_sem, back_send, back_recv,
        )
        if not first:
            closing.pop().close()
        closing.append(heads)
        heads.project(low[layer], weights, bias)
        if first:
            two.onward(2, (0, 2))
            three.first(2, (0, 2))
            two.onward(2, (1,))
        heads.attend(length, exact.at[layer], logs.at[layer])
        if first:
            three.onward(2)
        heads.collect()
        if first:
            two.settle(2)
            pick = jnp.where(
                lax.broadcasted_iota(jnp.int32, (8, LANES), 0) == lax.broadcasted_iota(jnp.int32, (8, LANES), 1),
                1.0, 0.0,
            ).astype(BF16)
            rows_ref[...] = across(pick, columns_of(weights, EXTRA, LANES))
        join = new_join()
        for quarter in range(4):
            join.offer(quarter, across(mixed[layer], quarter_of(weights, quarter, OUT, 512)))
        join.wait()

        def after_attention(block, total):
            rows = slab_of(block)
            live = live_rows(lengths, block, SLAB)
            before = trunk[rows, :]
            branch = join.total(rows) + rows_ref[0:1, :]
            scaled, root = norm_parts(before + branch)
            after = scaled * rows_ref[2:3, :] + rows_ref[3:4, :]
            normed[2 * layer, rows, :] = scaled
            inverse[2 * layer, rows, :] = root
            trunk[rows, :] = after
            middle[layer, rows, :] = after.astype(BF16)
            return (
                total[0] + jnp.sum(live * before * before, 0, keepdims=True),
                total[1] + jnp.sum(live * branch * branch, 0, keepdims=True),
            )

        squares = lax.fori_loop(0, 256 // SLAB, after_attention, (zero, zero))
        total_ref[2 + 3 * layer : 3 + 3 * layer, 0:1024] = squares[0]
        total_ref[3 + 3 * layer : 4 + 3 * layer, 0:1024] = squares[1]

        def hidden(tile, carry):
            start = pl.multiple_of(tile * 512, 512)
            columns = pl.ds(start, 512)
            pre = straight(middle[layer], columns_of(weights, INNER + start, 512)) + bias[:, pl.ds(1024 + start, 512)]
            act_part, slope_part = gelu_parts(pre)
            act[layer, :, columns] = act_part.astype(BF16)
            slope[layer, :, columns] = slope_part.astype(BF16)
            return carry

        lax.fori_loop(0, 4, hidden, 0)
        if first:
            three.settle(2)
        join = new_join()
        for quarter in range(4):
            join.offer(quarter, across(act[layer], quarter_of(weights, quarter, OUTER, 2048)))
        join.wait()

        def after_hidden(block, total):
            rows = slab_of(block)
            live = live_rows(lengths, block, SLAB)
            branch = join.total(rows) + rows_ref[1:2, :]
            scaled, root = norm_parts(trunk[rows, :] + branch)
            after = scaled * rows_ref[4:5, :] + rows_ref[5:6, :]
            square = total[0] + jnp.sum(live * branch * branch, 0, keepdims=True)
            if first:
                normed[1, rows, :] = scaled
                inverse[1, rows, :] = root
                trunk[rows, :] = after
                low[1, rows, :] = after.astype(BF16)
                return (square,)
            result[rows, :] = (after * live).astype(BF16)
            grad = grad_in[rows, :].astype(F32)
            return (square, *from_output(rows, grad, scaled, root, total[1:]))

        def from_output(rows, grad, scaled, root, total, layer=layer):
            second = norm_back(grad, scaled, root, rows_ref[4:5, :])
            small = second.astype(BF16)
            trunk[rows, :] = second
            outer_grad[layer, rows, :] = small
            return (
                total[0] + jnp.sum(small.astype(F32), 0, keepdims=True),
                total[1] + jnp.sum(grad * scaled, 0, keepdims=True),
                total[2] + jnp.sum(grad, 0, keepdims=True),
            )

        initial = (zero,) if first else (zero,) * 4
        square, *back = lax.fori_loop(0, 256 // SLAB, after_hidden, initial)
        total_ref[4 + 3 * layer : 5 + 3 * layer, 0:1024] = square
        if not first:
            sums[1], sums[4], sums[5] = back

    for item in gathers:
        item.close()
    grouped = [landings[9 * group : 9 * group + 9] for group in range(3)]
    one, two, three = (
        Scatter(weights, group, [grouped[group][3 * i : 3 * i + 3] for i in range(3)], scatter_send, scatter_recv)
        for group in range(3)
    )
    closing = [one, two, three] + closing
    head_sum = [jnp.zeros((1, 512), F32)] * 2
    each = range(3)
    idle = lambda: None

    def onward(group, phase):
        for third in each:
            group.onward(phase, third)

    for layer in (1, 0):
        last = layer == 0
        heads = HeadsBack(
            mixed_grad.at[layer], taken.at[layer], key_value.at[layer], query_buf.at[layer], grads.at[layer],
            local_sem, turn_send, turn_recv, send_sem, recv_sem,
        )
        closing.pop().close()
        closing.append(heads)
        if last:

            def from_above(block, total):
                rows = slab_of(block)
                grad = trunk[rows, :] + join.total(rows)
                return from_output(rows, grad, normed[1, rows, :], inverse[1, rows, :], total, 0)

            sums[1], sums[4], sums[5] = lax.fori_loop(0, 256 // SLAB, from_above, (sums[1], sums[4], sums[5]))

        def hidden_back(tile, carry):
            start = pl.multiple_of(tile * 512, 512)
            columns = pl.ds(start, 512)
            grad = straight(outer_grad[layer], columns_of(weights, OUTER + start, 512))
            small = (grad * slope[layer, :, columns].astype(F32)).astype(BF16)
            inner_grad[layer, :, columns] = small
            total_ref[0:1, columns] += jnp.sum(small.astype(F32), 0, keepdims=True)
            return carry

        lax.fori_loop(0, 4, hidden_back, 0)
        join = new_join()
        for quarter in range(4):
            join.offer(quarter, across(inner_grad[layer], quarter_of(weights, quarter, INNER, 2048)))
        if last:
            weight_grad(weights, OUTER, outer_grad[...].reshape(512, 1024), act, 2048)
            for third in (1, 0, 2):
                three.first(0, third, (0,))
            three.first(0, 1, (1,))
            weight_grad(weights, INNER, middle[...].reshape(512, 1024), inner_grad, 2048)
            two.first(0, 1)
        join.wait()

        def from_middle(block, total):
            rows = slab_of(block)
            grad = trunk[rows, :] + join.total(rows)
            scaled = normed[2 * layer, rows, :]
            before = norm_back(grad, scaled, inverse[2 * layer, rows, :], rows_ref[2:3, :])
            small = before.astype(BF16)
            trunk[rows, :] = before
            attn_grad[layer, rows, :] = small
            return (
                total[0] + jnp.sum(small.astype(F32), 0, keepdims=True),
                total[1] + jnp.sum(grad * scaled, 0, keepdims=True),
                total[2] + jnp.sum(grad, 0, keepdims=True),
            )

        sums[0], sums[2], sums[3] = lax.fori_loop(0, 256 // SLAB, from_middle, (sums[0], sums[2], sums[3]))
        mixed_grad[layer] = straight(attn_grad[layer], columns_of(weights, OUT, 512)).astype(BF16)
        heads.start()
        if last:
            for third in (0, 2):
                three.first(0, third, (1,))
            weight_grad(weights, OUT, attn_grad[...].reshape(512, 1024), mixed, 512)
            columns = jnp.concatenate(sums + [jnp.zeros((LANES - 6, 1024), F32)], 0).T
            weights[:, :, :, :, :, EXTRA : EXTRA + LANES] = columns.astype(BF16).reshape(*SHARDS, 16, LANES)
            for third in (0, 2):
                two.first(0, third, (0,))
        heads.attend(
            length, unit.at[layer], exact.at[layer], logs.at[layer], grad_buf, query_sum,
            (lambda: onward(three, 0)) if last else idle, (lambda: two.onward(0, 1)) if last else idle,
        )
        if last:
            for third in (0, 2):
                two.first(0, third, (1,))
            for third in (0, 2):
                two.onward(0, third)
        heads.collect(0)
        heads.collect(1)
        head_sum[1] = head_sum[1] + jnp.sum(grads[layer, 1].astype(F32), 0, keepdims=True)
        early = [
            across(grads[layer, 0], quarter_of(weights, quarter, KEY, 512))
            + across(grads[layer, 1], quarter_of(weights, quarter, VALUE, 512))
            for quarter in range(4)
        ]
        left = low[...].reshape(512, 1024)
        if last:
            weight_grad(weights, KEY, left, grads.at[:, 0], 512)
            one.first(0, 1)
            weight_grad(weights, VALUE, left, grads.at[:, 1], 512)
            one.first(0, 2)
            for third in each:
                three.settle(0, third)
                three.first(1, third)
        heads.collect(2)
        head_sum[0] = head_sum[0] + jnp.sum(grads[layer, 2].astype(F32), 0, keepdims=True)
        join = new_join()
        for quarter in range(4):
            join.offer(
                quarter, early[quarter] + across(grads[layer, 2], quarter_of(weights, quarter, QUERY, 512))
            )
        if last:
            weight_grad(weights, QUERY, left, grads.at[:, 2], 512)
            one.first(0, 0)
            total_ref[1:2, 0:512] = head_sum[0]
            total_ref[1:2, 512:1024] = head_sum[1]
            count = sum(jnp.clip(lengths[s] - c * ROWS, 0, ROWS) for s in range(2)).astype(F32)
            total_ref[1:2, 1024:1152] = jnp.full((1, LANES), count, F32)
        else:
            join.wait()

    totals = Totals(total_ref, total_land, total_send, total_recv)
    totals.first(0)
    for third in each:
        two.settle(0, third)
        two.first(1, third)
    for third in (1, 2, 0):
        one.onward(0, third)
    onward(three, 1)
    join.wait()
    for s in range(2):
        rows = pl.ds(s * ROWS, ROWS)
        stream_grad[:, s, :] = trunk[rows, :] + join.total(rows)
    totals.settle(0)
    totals.first(1)
    for third in (1, 2, 0):
        one.settle(0, third)
        one.direct(1, third)
    onward(two, 1)
    for third in each:
        three.settle(1, third)
        three.direct(2, third)
    result_ref[...] = jnp.stack([result[s * ROWS : s * ROWS + ROWS, :].astype(F32) for s in range(2)], 1).astype(BF16)
    totals.settle(1)
    totals.first(2)
    for third in (1, 2, 0):
        one.arrive(1, third)
        one.direct(2, third)
    for third in each:
        two.settle(1, third)
        two.direct(2, third)
    for third in each:
        three.arrive(2, third)

    def mine(start, width):
        return weights[x // 2, at["z"], x % 2, at["y"], :, start : start + width].astype(F32)

    outer_out[...] = mine(OUTER, 2048)
    for third in each:
        two.arrive(2, third)
    output_out[...] = mine(OUT, 512)
    inner_out[...] = mine(INNER, 2048)
    vector_out[...] = mine(EXTRA, LANES).T[0:8, :]
    totals.settle(2)
    scale = 1.0 / (total_ref[1:2, 1024:1025] * 1024.0)
    square = jnp.sum(total_ref[:, 0:1024], 1, keepdims=True)
    root_ref[...] = jnp.broadcast_to(jnp.sqrt(square * scale + 1e-06), root_ref.shape)
    for third in (1, 2, 0):
        one.arrive(2, third)
    query_out[...] = mine(QUERY, 512)
    key_out[...] = mine(KEY, 512)
    value_out[...] = mine(VALUE, 512)
    for item in closing + joined[-2:]:
        item.close()


def run_layers(*arguments):
    dma = pltpu.SemaphoreType.DMA
    out = lambda *shape: jax.ShapeDtypeStruct(shape, F32)
    vmem = lambda kind, *shape: pltpu.VMEM(shape, kind)
    return pl.pallas_call(
        layers_kernel,
        out_shape=(
            out(ROWS, 2, 1024), jax.ShapeDtypeStruct((ROWS, 2, 1024), BF16),
            out(16, 512), out(16, 512), out(16, 512), out(16, 512), out(16, 2048), out(16, 2048),
            out(8, 16), out(8, 2048), out(8, LANES),
        ),
        in_specs=[spec(pltpu.VMEM)] * 17 + [spec(pltpu.SMEM)],
        out_specs=(spec(pltpu.VMEM),) * 11,
        scratch_shapes=[
            vmem(BF16, *SHARDS, 16, WIDTH),
            vmem(F32, 1, 3072),
            vmem(F32, 8, 1024),
            vmem(BF16, 2, 256, 1024),
            vmem(BF16, 256, 1024),
            vmem(BF16, 256, 1024),
            vmem(F32, 256, 1024),
            vmem(BF16, 3, 256, 512),
            vmem(BF16, 2, 3, 1024, LANES),
            vmem(F32, 2, 1024, LANES),
            vmem(F32, 2, 8, 256),
            vmem(BF16, 2, 1024, LANES),
            vmem(BF16, 2, 256, 512),
            vmem(F32, 3, 256, 1024),
            vmem(F32, 3, 256, 1),
            vmem(BF16, 2, 256, 1024),
            vmem(BF16, 2, 256, 2048),
            vmem(BF16, 2, 256, 2048),
            vmem(BF16, 2, 256, 1024),
            vmem(BF16, 2, 256, 2048),
            vmem(BF16, 2, 256, 1024),
            vmem(BF16, 2, 3, 256, 512),
            vmem(BF16, 2, 256, 512),
            vmem(BF16, 2, 1024, LANES),
            vmem(BF16, 2048, LANES),
            vmem(F32, 2048, LANES),
            vmem(BF16, 2, 2, 1024, LANES),
            vmem(BF16, 2, 1024, LANES),
            vmem(BF16, 2, 2, 256, 512),
            vmem(BF16, 2, 2, 256, 512),
            vmem(F32, 3, 3, 8, 2048),
            dma((4,)),
            dma((3, 3)),
            dma((3, 3, 7)),
            dma((3,)),
            dma((3, 7)),
            dma((1,)),
            dma((1,)),
            dma((2,)),
            dma((2,)),
            dma((1,)),
            dma((1,)),
            dma((3,)),
            dma((3,)),
            dma((3, 3)),
            dma((3, 3, 3, 4)),
            *(shape for group in range(3) for shape in landing_shapes(group)),
        ],
        compiler_params=pltpu.CompilerParams(
            collective_id=3, has_side_effects=True, vmem_limit_bytes=LIMIT
        ),
        name="layers",
    )(*arguments)


def finish_kernel(
    stream_in, result_in, query_in, key_in, value_in, output_in, inner_in, outer_in, vectors, totals, roots,
    result, stream_grad, query, key, value, output, inner, outer, query_sum, value_sum, inner_sum, *rest,
):
    for source, target in (
        (result_in, result), (stream_in, stream_grad), (query_in, query), (key_in, key), (value_in, value),
        (output_in, output), (inner_in, inner), (outer_in, outer),
    ):
        target[...] = source[...]
    query_sum[...] = totals[1:2, 0:512].reshape(512)
    value_sum[...] = totals[1:2, 512:1024].reshape(512)
    inner_sum[...] = totals[0:1, :].reshape(2048)
    for j in range(6):
        rest[j][...] = vectors[j : j + 1, :].reshape(16)
    rest[6][...] = jnp.concatenate(
        [
            jnp.concatenate([roots[2 + 3 * layer + j : 3 + 3 * layer + j, 0:1] for j in range(3)], 1)
            for layer in range(LAYERS)
        ],
        0,
    )


def finish(partial):
    out = lambda *shape: jax.ShapeDtypeStruct(shape, F32)
    return pl.pallas_call(
        finish_kernel,
        out_shape=(
            jax.ShapeDtypeStruct((ROWS, 2, 1024), BF16), out(ROWS, 2, 1024),
            out(16, 512), out(16, 512), out(16, 512), out(16, 512), out(16, 2048), out(16, 2048),
            out(512), out(512), out(2048), *(out(16) for _ in range(6)), out(LAYERS, 3),
        ),
        in_specs=[spec(pltpu.VMEM)] * 11,
        out_specs=(spec(pltpu.VMEM),) * 18,
        name="finish",
    )(*partial)


def body(
    stream,
    lengths,
    query_weight,
    query_bias,
    key_weight,
    value_weight,
    value_bias,
    output_weight,
    output_bias,
    first_gain,
    first_shift,
    inner_weight,
    inner_bias,
    outer_weight,
    outer_bias,
    second_gain,
    second_shift,
    cotangent,
):
    partial = run_layers(
        stream, cotangent, query_weight, key_weight, value_weight, output_weight.T, inner_weight, outer_weight.T,
        output_bias, outer_bias, first_gain, first_shift, second_gain, second_shift,
        query_bias, value_bias, inner_bias, lengths,
    )
    (
        result, stream_grad, grad_query, grad_key, grad_value, grad_output, grad_inner, grad_outer,
        query_sum, value_sum, inner_sum, *vectors, roots,
    ) = finish(partial)
    return (
        result,
        stream_grad,
        grad_query,
        query_sum,
        grad_key,
        grad_value,
        value_sum,
        grad_output.T,
        vectors[0],
        vectors[2],
        vectors[3],
        grad_inner,
        inner_sum,
        grad_outer.T,
        vectors[1],
        vectors[4],
        vectors[5],
        roots,
    )


def solution(mesh):
    in_specs = (
        P("context", "fsdp", None),
        P("fsdp"),
        P(("fsdp", "context"), "tensor"),
        P("tensor"),
        P(("fsdp", "context"), "tensor"),
        P(("fsdp", "context"), "tensor"),
        P("tensor"),
        P("tensor", ("fsdp", "context")),
        P(("fsdp", "context")),
        P(("fsdp", "context")),
        P(("fsdp", "context")),
        P(("fsdp", "context"), "tensor"),
        P("tensor"),
        P("tensor", ("fsdp", "context")),
        P(("fsdp", "context")),
        P(("fsdp", "context")),
        P(("fsdp", "context")),
        P("context", "fsdp", None),
    )
    out_specs = (
        P("context", "fsdp", None),
        P("context", "fsdp", None),
        P(("fsdp", "context"), "tensor"),
        P("tensor"),
        P(("fsdp", "context"), "tensor"),
        P(("fsdp", "context"), "tensor"),
        P("tensor"),
        P("tensor", ("fsdp", "context")),
        P(("fsdp", "context")),
        P(("fsdp", "context")),
        P(("fsdp", "context")),
        P(("fsdp", "context"), "tensor"),
        P("tensor"),
        P("tensor", ("fsdp", "context")),
        P(("fsdp", "context")),
        P(("fsdp", "context")),
        P(("fsdp", "context")),
        P(),
    )
    return jax.shard_map(body, mesh=mesh, in_specs=in_specs, out_specs=out_specs, check_vma=False)
```

```python
import jax
import jax.numpy as jnp
from jax import lax
from jax.experimental import pallas as pl
from jax.experimental.pallas import tpu as pltpu
from jax.sharding import PartitionSpec as P

HEAD = 64
LAYERS = 2
LANES = 128
MESH = pl.DeviceIdType.MESH

F32 = jnp.float32
BF16 = jnp.bfloat16
ROWS = 128
LIMIT = 60 * 2**20
WIDTH = 6272
QUERY, KEY, VALUE, OUT, EXTRA, INNER, OUTER = 0, 512, 1024, 1536, 2048, 2176, 4224
GROUPS = ((QUERY, OUT), (OUT, OUTER), (OUTER, WIDTH))
TILES = (((2, 2), (2, 2), (2, 2)), ((3, 3), (4, 5), (3, 3)), ((2, 3), (3, 3), (2, 3)))
ORDERS = ("zyx", "yxz", "xzy")
SHARDS = (2, 4, 2, 4)


def spec(space):
    return pl.BlockSpec(memory_space=space)


def place():
    f = lax.axis_index("fsdp")
    c = lax.axis_index("context")
    t = lax.axis_index("tensor")
    return {"x": 2 * (f // 4) + c // 4, "y": c % 4, "z": f % 4, "t": t}


def device(at):
    x = at["x"]
    return ((x // 2) * 4 + at["z"], (x % 2) * 4 + at["y"], at["t"])


def shifted(at, axis, step):
    moved = dict(at)
    moved[axis] = lax.rem(at[axis] + step + 4, 4)
    return moved


def greet(devices):
    barrier = pltpu.get_barrier_semaphore()
    for device_id in devices:
        pl.semaphore_signal(barrier, inc=1, device_id=device_id, device_id_type=MESH)
    pl.semaphore_wait(barrier, len(devices))


def neighbours(at, steps):
    return [device(shifted(at, axis, step)) for axis in "xyz" for step in steps]


def context_peers():
    f = lax.axis_index("fsdp")
    c = lax.axis_index("context")
    t = lax.axis_index("tensor")
    return [(f, lax.rem(c + d, 8), t) for d in range(1, 8)]


def remote(src, dst, send_sem, recv_sem, device_id):
    return pltpu.make_async_remote_copy(
        src_ref=src,
        dst_ref=dst,
        send_sem=send_sem,
        recv_sem=recv_sem,
        device_id=device_id,
        device_id_type=MESH,
    )


def drain(ref, sem):
    pltpu.make_async_copy(ref, ref, sem).wait()


def bulk(ref, count, group, groups=GROUPS):
    start, end = groups[group]
    picks = {
        3: (0, 0, 0, slice(0, 3)),
        8: (0, slice(0, 2), 0),
        12: (0, slice(0, 3), 0),
        32: (0,),
        48: (slice(None), slice(0, 3)),
    }[count]
    picks = picks + (slice(None),) * (5 - len(picks))
    return ref.at[picks + (pl.ds(start, end - start),)]


def shards(ref, at, whole, cols):
    x = at["x"]
    xh = slice(None) if "x" in whole else x // 2
    xl = slice(None) if "x" in whole else x % 2
    z = slice(None) if "z" in whole else at["z"]
    y = slice(None) if "y" in whole else at["y"]
    return ref.at[xh, z, xl, y, :, pl.ds(cols[0], cols[1])]


def thirds(group, groups=GROUPS, tiles_of=TILES):
    start = groups[group][0]
    parts = []
    for pair in tiles_of[group]:
        halves = []
        for tiles in pair:
            halves.append((start, tiles * LANES))
            start += tiles * LANES
        parts.append(tuple(halves))
    return parts


def across(left, right):
    return lax.dot_general(left, right, (((1,), (1,)), ((), ())), preferred_element_type=F32)


def straight(left, right):
    return jnp.dot(left, right, preferred_element_type=F32)


def rows_of(block):
    return pl.ds(pl.multiple_of(block * ROWS, ROWS), ROWS)


def by_head(block):
    first = lax.broadcasted_iota(jnp.int32, block.shape, 1) < HEAD
    zero = jnp.zeros_like(block)
    return jnp.concatenate([jnp.where(first, block, zero), jnp.where(first, zero, block)], 0)


def key_mask(length, first, count):
    position = first + lax.broadcasted_iota(jnp.int32, (count, 1), 0)
    return jnp.where(position < length, 0.0, -1e30)


def columns_of(weights, start, width):
    return weights[:, :, :, :, :, pl.ds(start, width)].reshape(1024, width)


def quarter_of(weights, quarter, start, width):
    z = 2 * (quarter % 2)
    return weights[quarter // 2, z : z + 2, :, :, :, start : start + width].reshape(256, width)


def part(ref, peer):
    return ref.at[rows_of(peer // 4), rows_of(peer % 4)]


GATHER_SLOTS = {(0, 0): 0, (0, 1): 1, (0, 2): 2, (1, 0): 9, (1, 1): 10, (1, 2): 17, (2, 0): 24, (2, 1): 25, (2, 2): 32}
GATHER_COUNT = 39


class Gather:
    def __init__(self, weights, group, send_sem, recv_sem):
        self.at = place()
        self.weights, self.group = weights, group
        self.send_sem, self.recv_sem = send_sem, recv_sem
        self.parts = thirds(group)
        self.sent = {}

    def send(self, third, phase, kind, origin, cols, step):
        order = ORDERS[third]
        block = shards(self.weights, origin, order[:phase], cols)
        slot = 0 if kind is None or kind > 1 else 1 + 2 * third + kind
        copy = remote(
            block, block, self.send_sem.at[self.group, phase], self.recv_sem.at[GATHER_SLOTS[self.group, phase] + slot],
            device(shifted(self.at, order[phase], step)),
        )
        copy.start()
        self.sent[third, phase, kind] = copy

    def first(self, phase, thirds_now=range(3), pieces=(0, 1)):
        for piece in pieces:
            for third in thirds_now:
                low, high = self.parts[third]
                self.send(third, phase, 2 * piece, self.at, (low, high)[piece], 1)
                self.send(third, phase, 2 * piece + 1, self.at, (high, low)[piece], -1)

    def direct(self, phase):
        for third in range(3):
            low, high = self.parts[third]
            for step in (1, 2, 3):
                self.send(third, phase, None, self.at, (low[0], low[1] + high[1]), step)

    def arrive(self, phase):
        drain(bulk(self.weights, (3, 12)[phase], self.group), self.recv_sem.at[GATHER_SLOTS[self.group, phase]])

    def onward(self, phase, thirds_now=range(3)):
        for third in thirds_now:
            axis = ORDERS[third][phase]
            low, high = self.parts[third]
            self.sent[third, phase, 0].wait_recv()
            self.send(third, phase, 4, shifted(self.at, axis, -1), low, 1)
            self.sent[third, phase, 1].wait_recv()
            self.send(third, phase, 5, shifted(self.at, axis, 1), high, -1)

    def settle(self, phase):
        drain(bulk(self.weights, (2, 8, 32)[phase], self.group), self.recv_sem.at[GATHER_SLOTS[self.group, phase]])

    def close(self):
        for phase in range(3):
            drain(bulk(self.weights, (3, 12, 48)[phase], self.group), self.send_sem.at[self.group, phase])


def seven(ref):
    return ref.at[pl.ds(0, 7 * ROWS)]


class Heads:
    def __init__(self, own, unit, outcome, mixed, local_sem, send_sem, recv_sem, back_send, back_recv):
        self.f = lax.axis_index("fsdp")
        self.c = lax.axis_index("context")
        self.t = lax.axis_index("tensor")
        self.own, self.unit, self.outcome, self.mixed = own, unit, outcome, mixed
        self.local_sem, self.send_sem, self.recv_sem = local_sem, send_sem, recv_sem
        self.back_send, self.back_recv = back_send, back_recv

    def push(self, j, d):
        peer = lax.rem(self.c + d, 8)
        return remote(
            part(self.own.at[j], peer), self.unit.at[j, rows_of(self.c)],
            self.send_sem.at[j], self.recv_sem.at[j + (d - 1 if j == 2 else 0)], (self.f, peer, self.t),
        )

    def keep(self, j):
        return pltpu.make_async_copy(
            part(self.own.at[j], self.c), self.unit.at[j, rows_of(self.c)], self.local_sem.at[j]
        )

    def answer(self, d):
        peer = lax.rem(self.c + d, 8)
        return remote(
            self.outcome.at[rows_of(peer)], part(self.mixed, self.c),
            self.back_send.at[0], self.back_recv.at[0], (self.f, peer, self.t),
        )

    def keep_back(self):
        return pltpu.make_async_copy(
            self.outcome.at[rows_of(self.c)], part(self.mixed, self.c), self.local_sem.at[3]
        )

    def project(self, x, weights, bias):
        for j, column in enumerate((KEY, VALUE, QUERY)):
            product = straight(x, columns_of(weights, column, 512))
            if j == 1:
                product = product + bias[:, 512:1024]
            if j == 2:
                product = product + bias[:, 0:512]
            self.own[j] = product.astype(BF16)
            for d in (4, 1, 7, 5, 3, 2, 6):
                self.push(j, d).start()
            self.keep(j).start()

    def attend(self, length, exact, logs):
        c = self.c
        for j in range(2):
            self.keep(j).wait()
            drain(seven(self.outcome), self.recv_sem.at[j])
        mask = key_mask(length, 0, 8 * ROWS)
        keys = self.unit[0]
        values_across = self.unit[1].T
        self.keep(2).wait()

        def step(d, carry):
            block = lax.rem(c + d, 8)

            @pl.when(d > 0)
            def _():
                self.push(2, 8 - d).wait_recv()

            queries = self.unit[2, rows_of(block), :] * jnp.asarray(0.125, BF16)
            scores = across(keys, by_head(queries)) + mask
            top = jnp.max(scores, 0, keepdims=True)
            exponent = jnp.exp(scores - top)
            total = jnp.sum(exponent, 0, keepdims=True)
            outcome = straight(values_across, exponent.astype(BF16)) / total
            both = jnp.concatenate([outcome[:HEAD, :ROWS], outcome[HEAD:, ROWS:]], 0).T
            exact[rows_of(block), :] = both
            self.outcome[rows_of(block), :] = both.astype(BF16)
            logs[pl.ds(block, 1), :] = top + jnp.log(total)

            @pl.when(d > 0)
            def _():
                self.answer(d).start()

            return carry

        lax.fori_loop(0, 8, step, 0)
        self.keep_back().start()

    def collect(self):
        self.keep_back().wait()
        drain(seven(self.outcome), self.back_recv.at[0])

    def close(self):
        drain(seven(self.outcome), self.back_send.at[0])
        for j in range(3):
            drain(seven(self.outcome), self.send_sem.at[j])


class Join:
    def __init__(self, number, before, sent, landed, send_sem, recv_sem):
        t = lax.axis_index("tensor")
        self.partner = (lax.axis_index("fsdp"), lax.axis_index("context"), 1 - t)
        self.sent, self.landed = sent.at[number % 2], landed.at[number % 2]
        self.send_sem, self.recv_sem = send_sem.at[number % 2], recv_sem.at[number % 2]
        self.before = before

    def copy(self, half):
        return remote(
            self.sent.at[half], self.landed.at[half], self.send_sem, self.recv_sem, self.partner,
        )

    def offer(self, quarter, term):
        half, side = quarter // 2, quarter % 2
        if quarter == 0 and self.before is not None:
            self.before.close()
        self.sent[half, :, side * 256 : side * 256 + 256] = term.astype(BF16)
        if side == 1:
            self.copy(half).start()

    def wait(self):
        drain(self.landed, self.recv_sem)

    def total(self, rows):
        return jnp.concatenate(
            [self.sent[half, rows, :].astype(F32) + self.landed[half, rows, :].astype(F32) for half in range(2)],
            1,
        )

    def close(self):
        drain(self.sent, self.send_sem)


def gelu_parts(argument):
    square = argument * argument
    inner = 0.7978845608028654 * argument * (1.0 + 0.044715 * square)
    bend = jnp.tanh(inner)
    half = 0.5 * (1.0 + bend)
    slope = half + 0.5 * argument * (1.0 - bend * bend) * 0.7978845608028654 * (
        1.0 + 3.0 * 0.044715 * square
    )
    return argument * half, slope


def norm_parts(hidden):
    centre = hidden - jnp.mean(hidden, -1, keepdims=True)
    inverse = lax.rsqrt(jnp.mean(centre * centre, -1, keepdims=True) + 1e-05)
    return centre * inverse, inverse


def live_rows(lengths, block, count):
    c = lax.axis_index("context")
    row = block * count + lax.broadcasted_iota(jnp.int32, (count, 1), 0)
    slot = c * ROWS + lax.rem(row, ROWS)
    return jnp.where(slot < jnp.where(row < ROWS, lengths[0], lengths[1]), 1.0, 0.0)


SLAB = 128


def slab_of(block):
    return pl.ds(pl.multiple_of(block * SLAB, SLAB), SLAB)


def pack(weights, own, query, key, value, output, inner, outer, vectors):
    xh, z, xl, y = own

    def put(start, block):
        weights[xh, z, xl, y, :, start : start + block.shape[1]] = block

    put(QUERY, query[...])
    put(KEY, key[...])
    put(VALUE, value[...])
    put(OUT, output[...])
    put(INNER, inner[...])
    put(OUTER, outer[...])
    eye = jnp.where(
        lax.broadcasted_iota(jnp.int32, (16, 16), 0) == lax.broadcasted_iota(jnp.int32, (16, 16), 1), 1.0, 0.0
    ).astype(BF16)
    rows = [vector[...].astype(F32).reshape(1, 16) for vector in vectors]
    table = jnp.concatenate(rows + [jnp.zeros((LANES - 6, 16), F32)], 0).astype(BF16)
    put(EXTRA, across(eye, table).astype(BF16))


def rows_by_sequence(source, target, keep):
    whole = source[...].astype(F32)
    for s in range(2):
        target[s * ROWS : s * ROWS + ROWS, :] = (whole[:, s, :] * keep(s)).astype(target.dtype)


def norm_back(grad_out, normed, inverse, gain):
    scaled = grad_out * gain
    return inverse * (
        scaled
        - jnp.mean(scaled, -1, keepdims=True)
        - normed * jnp.mean(scaled * normed, -1, keepdims=True)
    )


SCATTER_GROUPS = ((QUERY, KEY), (KEY, OUT), (OUT, OUTER), (OUTER, WIDTH))
SCATTER_TILES = (((1, 0), (1, 1), (1, 0)), ((1, 1), (2, 2), (1, 1)), *TILES[1:])
DIRECT = (((0, 1, 2), (1, 2), (0, 1, 2)), ((1, 2),) * 3, ((2,),) * 3, ((2,),) * 3)
SCATTER_SLOTS = {}
SCATTER_COUNT = 0
for _group in range(4):
    for _third in range(3):
        for _phase in range(3):
            SCATTER_SLOTS[_group, _third, _phase] = SCATTER_COUNT
            SCATTER_COUNT += 1 if _phase in DIRECT[_group][_third] else 4


class Scatter:
    def __init__(self, work, group, landings, send_sem, recv_sem):
        self.at = place()
        self.work, self.group, self.landings = work, group, landings
        self.send_sem, self.recv_sem = send_sem, recv_sem
        self.parts = thirds(group, SCATTER_GROUPS, SCATTER_TILES)
        self.sent = {}

    def slot(self, third, phase, number):
        return self.recv_sem.at[SCATTER_SLOTS[self.group, third, phase] + number]

    def ring(self, third, phase):
        order = ORDERS[third][::-1]
        return order[phase], order[phase + 1 :]

    def send(self, third, phase, kind, away, cols, step):
        axis, whole = self.ring(third, phase)
        land = self.landings[third][phase].at[kind]
        if cols[1] != land.shape[-1]:
            land = land.at[..., pl.ds(0, cols[1])]
        number = kind // 2 + 1 if kind > 1 else kind
        if phase in DIRECT[self.group][third]:
            number = 0
        copy = remote(
            shards(self.work, shifted(self.at, axis, away), whole, cols), land,
            self.send_sem.at[self.group, phase], self.slot(third, phase, number),
            device(shifted(self.at, axis, step)),
        )
        copy.start()
        self.sent[third, phase, kind] = copy

    def add(self, third, phase, away, cols, kinds):
        axis, whole = self.ring(third, phase)
        origin = shifted(self.at, axis, away)
        land = self.landings[third][phase]
        x = origin["x"]
        wide = {name: name in whole for name in "xyz"}
        columns = pl.ds(cols[0], cols[1])

        def one(ix, iz):
            xh, xl = (ix // 2, ix % 2) if wide["x"] else (x // 2, x % 2)
            z = iz if wide["z"] else origin["z"]
            y = slice(None) if wide["y"] else origin["y"]
            index = (xh, z, xl, y, slice(None), columns)
            total = self.work[index].astype(F32)
            for kind in kinds:
                at = (kind,)
                at += (xh,) if wide["x"] else ()
                at += (z,) if wide["z"] else ()
                at += (xl,) if wide["x"] else ()
                at += (slice(None),) if wide["y"] else ()
                total = total + land[at + (slice(None), pl.ds(0, cols[1]))].astype(F32)
            self.work[index] = total.astype(BF16)

        count_z = 4 if wide["z"] else 1
        if not wide["x"]:
            for iz in range(count_z):
                one(0, iz)
        else:
            def turn(ix, carry):
                for iz in range(count_z):
                    one(ix, iz)
                return carry

            lax.fori_loop(0, 4, turn, 0)

    def first(self, phase, third, pieces=(0, 1)):
        if phase in DIRECT[self.group][third]:
            self.direct(phase, third)
            return
        low, high = self.parts[third]
        if 0 in pieces:
            self.send(third, phase, 0, 2, low, 1)
            self.send(third, phase, 1, 2, high, -1)
        if 1 in pieces:
            self.send(third, phase, 2, 1, high, 1)
            self.send(third, phase, 3, -1, low, -1)

    def direct(self, phase, third):
        low, high = self.parts[third]
        for step in (1, 2, 3):
            self.send(third, phase, step - 1, step, (low[0], low[1] + high[1]), step)

    def arrive(self, phase, third):
        low, high = self.parts[third]
        drain(self.landings[third][phase], self.slot(third, phase, 0))
        self.add(third, phase, 0, (low[0], low[1] + high[1]), (0, 1, 2))

    def onward(self, phase, third):
        if phase in DIRECT[self.group][third]:
            return
        low, high = self.parts[third]
        self.sent[third, phase, 0].wait_recv()
        self.add(third, phase, 1, low, (0,))
        self.send(third, phase, 4, 1, low, 1)
        self.sent[third, phase, 1].wait_recv()
        self.add(third, phase, -1, high, (1,))
        self.send(third, phase, 5, -1, high, -1)

    def settle(self, phase, third):
        if phase in DIRECT[self.group][third]:
            self.arrive(phase, third)
            return
        low, high = self.parts[third]
        axis, whole = self.ring(third, phase)
        block = shards(self.work, self.at, whole, (low[0], low[1] + high[1]))
        for slot in (2, 3):
            drain(block, self.slot(third, phase, slot))
        self.add(third, phase, 0, high, (2, 5))
        self.add(third, phase, 0, low, (3, 4))

    def close(self):
        for phase in range(3):
            drain(bulk(self.work, (48, 12, 3)[phase], self.group, SCATTER_GROUPS), self.send_sem.at[self.group, phase])


def landing_shapes(group):
    shapes = []
    for third in range(3):
        order = ORDERS[third][::-1]
        low, high = thirds(group, SCATTER_GROUPS, SCATTER_TILES)[third]
        for phase in range(3):
            whole = order[phase + 1 :]
            direct = phase in DIRECT[group][third]
            shape = [3 if direct else 6]
            shape += [2] if "x" in whole else []
            shape += [4] if "z" in whole else []
            shape += [2] if "x" in whole else []
            shape += [4] if "y" in whole else []
            width = low[1] + high[1] if direct else max(low[1], high[1])
            shapes.append(pltpu.VMEM((*shape, 16, width), BF16))
    return shapes


class Totals:
    def __init__(self, total, landed, send_sem, recv_sem):
        self.at = place()
        self.total, self.landed, self.send_sem, self.recv_sem = total, landed, send_sem, recv_sem

    def copy(self, phase, step):
        return remote(
            self.total, self.landed.at[phase, step - 1], self.send_sem.at[phase], self.recv_sem.at[phase], device(shifted(self.at, "xyz"[phase], step)),
        )

    def first(self, phase):
        for step in (1, 2, 3):
            self.copy(phase, step).start()

    def settle(self, phase):
        drain(self.landed.at[phase], self.recv_sem.at[phase])
        drain(self.landed.at[phase], self.send_sem.at[phase])
        self.total[...] += self.landed[phase, 0] + self.landed[phase, 1] + self.landed[phase, 2]


class HeadsBack:
    def __init__(self, mixed_grad, taken, key_value, query, grads, local_sem, send_sem, recv_sem, back_send, back_recv):
        self.f = lax.axis_index("fsdp")
        self.c = lax.axis_index("context")
        self.t = lax.axis_index("tensor")
        self.mixed_grad, self.taken, self.grads = mixed_grad, taken, grads
        self.sources = (key_value.at[0], key_value.at[1], query)
        self.key_value, self.query = key_value, query
        self.local_sem, self.send_sem, self.recv_sem = local_sem, send_sem, recv_sem
        self.back_send, self.back_recv = back_send, back_recv

    def push(self, d):
        peer = lax.rem(self.c + d, 8)
        return remote(
            part(self.mixed_grad, peer), self.taken.at[rows_of(self.c)],
            self.send_sem.at[0], self.recv_sem.at[0], (self.f, peer, self.t),
        )

    def keep(self):
        return pltpu.make_async_copy(
            part(self.mixed_grad, self.c), self.taken.at[rows_of(self.c)], self.local_sem.at[3]
        )

    def answer(self, j, d):
        peer = lax.rem(self.c + d, 8)
        return remote(
            self.sources[j].at[rows_of(peer)], part(self.grads.at[j], self.c),
            self.back_send.at[j], self.back_recv.at[j], (self.f, peer, self.t),
        )

    def keep_back(self, j):
        return pltpu.make_async_copy(
            self.sources[j].at[rows_of(self.c)], part(self.grads.at[j], self.c), self.local_sem.at[j]
        )

    def start(self):
        for d in (4, 1, 7, 5, 3, 2, 6):
            self.push(d).start()
        self.keep().start()

    def attend(self, length, unit, exact, logs_ref, grad_buf, query_sum, ahead, midway):
        c = self.c
        scale = jnp.asarray(0.125, BF16)
        queries = jnp.concatenate(
            [by_head(unit[2, pl.ds(block * ROWS, ROWS), :] * scale) for block in range(8)], 0
        )
        logs = jnp.concatenate([logs_ref[block : block + 1, :] for block in range(8)], 1)
        query_sum[...] = jnp.zeros_like(query_sum)
        ahead()
        self.keep().wait()
        drain(seven(self.taken), self.recv_sem.at[0])
        for block in range(8):
            grad_buf[pl.ds(block * 256, 256), :] = by_head(self.taken[pl.ds(block * ROWS, ROWS), :])
        turned = (self.taken[...].astype(F32) * exact[...]).T
        weighted = [jnp.sum(turned[head * HEAD : head * HEAD + HEAD], 0, keepdims=True) for head in range(2)]
        delta = jnp.concatenate(
            [
                weighted[head][:, block * ROWS : (block + 1) * ROWS]
                for block in range(8)
                for head in range(2)
            ],
            1,
        )

        def step(turn, carry):
            pair = lax.rem(c // 2 + turn, 4)
            spot = pl.ds(pl.multiple_of(pair * 256, 256), 256)
            keys = unit[0, spot, :]
            values = unit[1, spot, :]
            scores = across(keys, queries) + key_mask(length, pair * 256, 256)
            soft = jnp.exp(scores - logs)
            self.key_value[1, spot, :] = straight(soft.astype(BF16), grad_buf[...]).astype(BF16)
            soft_grad = across(values, grad_buf[...])
            score_grad = (soft * (soft_grad - delta)).astype(BF16)
            self.key_value[0, spot, :] = straight(score_grad, queries).astype(BF16)
            query_sum[...] += lax.dot_general(
                score_grad, keys, (((0,), (0,)), ((), ())), preferred_element_type=F32
            )

            for side in range(2):
                d = lax.rem(pair * 2 + side - c + 8, 8)

                @pl.when(d > 0)
                def _():
                    for j in range(2):
                        self.answer(j, d).start()

            return carry

        lax.fori_loop(1, 3, step, 0)
        midway()
        lax.fori_loop(3, 5, step, 0)
        first_lane = lax.broadcasted_iota(jnp.int32, (ROWS, LANES), 1) < HEAD
        for block in range(8):
            start = block * 256
            total = jnp.where(
                first_lane, query_sum[pl.ds(start, ROWS), :], query_sum[pl.ds(start + ROWS, ROWS), :]
            )
            self.query[pl.ds(block * ROWS, ROWS), :] = (total * 0.125).astype(BF16)
        for d in (4, 1, 7, 5, 3, 2, 6):
            self.answer(2, d).start()
        for j in range(3):
            self.keep_back(j).start()

    def collect(self, j):
        self.keep_back(j).wait()
        drain(seven(self.taken), self.back_recv.at[j])

    def close(self):
        drain(seven(self.taken), self.send_sem.at[0])
        for j in range(3):
            drain(seven(self.taken), self.back_send.at[j])


def put_quarter(work, quarter, start, value):
    z = 2 * (quarter % 2)
    work[quarter // 2, z : z + 2, :, :, :, pl.ds(start, value.shape[1])] = value.astype(BF16).reshape(
        2, 2, 4, 16, value.shape[1]
    )


def weight_grad(work, start, left, right, width, first=0):
    turned = left.T
    tile = 512

    def turn(i, carry):
        offset = pl.multiple_of(i * tile, tile)
        term = right[:, :, pl.ds(offset, tile)].reshape(512, tile)
        for quarter in range(4):
            put_quarter(work, quarter, start + offset, straight(turned[quarter * 256 : quarter * 256 + 256], term))
        return carry

    lax.fori_loop(first // tile, (first + width) // tile, turn, 0)


def layers_kernel(
    stream, cotangent, query, key, value, output, inner, outer, bias0, bias1, gain1, shift1, gain2, shift2,
    query_bias, value_bias, inner_bias, lengths,
    stream_grad, result_ref, query_out, key_out, value_out, output_out, inner_out, outer_out, vector_out, total_ref,
    root_ref,
    weights, bias, rows_ref, low, grad_in, result, trunk,
    own, unit, exact, logs, outcome, mixed, normed, inverse, middle, act, slope,
    attn_grad, inner_grad, outer_grad, grads, mixed_grad, taken, grad_buf, query_sum, key_value, query_buf,
    sent, landed, total_land,
    local_sem, gather_send, gather_recv, send_sem, recv_sem, back_send, back_recv, pair_send, pair_recv,
    turn_send, turn_recv, total_send, total_recv,
    scatter_send, scatter_recv, *landings,
):
    at = place()
    c = lax.axis_index("context")
    t = lax.axis_index("tensor")
    partner = (lax.axis_index("fsdp"), c, 1 - t)
    x = at["x"]
    closing = []
    joined = []

    def new_join():
        before = joined[-2] if len(joined) > 1 else None
        joined.append(Join(len(joined), before, sent, landed, pair_send, pair_recv))
        return joined[-1]

    pack(
        weights, (x // 2, at["z"], x % 2, at["y"]), query, key, value, output, inner, outer,
        (bias0, bias1, gain1, shift1, gain2, shift2),
    )
    greet(neighbours(at, (1, 2, 3)) + context_peers() + [partner])
    one, two, three = (Gather(weights, group, gather_send, gather_recv) for group in range(3))
    gathers = (one, two, three)
    for group in gathers:
        group.direct(0)
    rows_by_sequence(stream, low.at[0], lambda s: 1.0)
    one.arrive(0)
    one.direct(1)
    two.arrive(0)
    two.first(1)
    three.arrive(0)
    three.first(1)
    bias[:, 0:512] = query_bias[...].astype(F32).reshape(1, 512)
    bias[:, 512:1024] = value_bias[...].astype(F32).reshape(1, 512)
    bias[:, 1024:3072] = inner_bias[...].astype(F32).reshape(1, 2048)
    position = c * ROWS + lax.broadcasted_iota(jnp.int32, (ROWS, 1), 0)
    rows_by_sequence(cotangent, grad_in, lambda s: jnp.where(position < lengths[s], 1.0, 0.0))
    trunk[...] = low[0].astype(F32)
    total_ref[...] = jnp.zeros_like(total_ref)
    one.arrive(1)
    one.first(2)
    two.onward(1)
    three.onward(1)
    one.onward(2)
    two.settle(1)
    two.first(2)
    three.settle(1)
    three.first(2, (1,))
    one.settle(2)
    length = lengths[c // 4]
    zero = jnp.zeros((1, 1024), F32)
    sums = [zero] * 6

    for layer in range(LAYERS):
        first = layer == 0
        heads = Heads(
            own, unit.at[layer], outcome.at[layer], mixed.at[layer], local_sem,
            send_sem, recv_sem, back_send, back_recv,
        )
        if not first:
            closing.pop().close()
        closing.append(heads)
        heads.project(low[layer], weights, bias)
        if first:
            two.onward(2, (0, 2))
            two.onward(2, (1,))
        heads.attend(length, exact.at[layer], logs.at[layer])
        if first:
            three.first(2, (0, 2))
            three.onward(2, (1,))
        heads.collect()
        if first:
            two.settle(2)
            pick = jnp.where(
                lax.broadcasted_iota(jnp.int32, (8, LANES), 0) == lax.broadcasted_iota(jnp.int32, (8, LANES), 1),
                1.0, 0.0,
            ).astype(BF16)
            rows_ref[...] = across(pick, columns_of(weights, EXTRA, LANES))
        join = new_join()
        for quarter in range(4):
            join.offer(quarter, across(mixed[layer], quarter_of(weights, quarter, OUT, 512)))
        if first:
            three.onward(2, (0, 2))
        join.wait()

        def after_attention(block, total):
            rows = slab_of(block)
            live = live_rows(lengths, block, SLAB)
            before = trunk[rows, :]
            branch = join.total(rows) + rows_ref[0:1, :]
            scaled, root = norm_parts(before + branch)
            after = scaled * rows_ref[2:3, :] + rows_ref[3:4, :]
            normed[2 * layer, rows, :] = scaled
            inverse[2 * layer, rows, :] = root
            trunk[rows, :] = after
            middle[layer, rows, :] = after.astype(BF16)
            return (
                total[0] + jnp.sum(live * before * before, 0, keepdims=True),
                total[1] + jnp.sum(live * branch * branch, 0, keepdims=True),
            )

        squares = lax.fori_loop(0, 256 // SLAB, after_attention, (zero, zero))
        total_ref[2 + 3 * layer : 3 + 3 * layer, 0:1024] = squares[0]
        total_ref[3 + 3 * layer : 4 + 3 * layer, 0:1024] = squares[1]

        def hidden(tile, carry):
            start = pl.multiple_of(tile * 512, 512)
            columns = pl.ds(start, 512)
            pre = straight(middle[layer], columns_of(weights, INNER + start, 512)) + bias[:, pl.ds(1024 + start, 512)]
            act_part, slope_part = gelu_parts(pre)
            act[layer, :, columns] = act_part.astype(BF16)
            slope[layer, :, columns] = slope_part.astype(BF16)
            return carry

        lax.fori_loop(0, 4, hidden, 0)
        if first:
            three.settle(2)
        join = new_join()
        for quarter in range(4):
            join.offer(quarter, across(act[layer], quarter_of(weights, quarter, OUTER, 2048)))
        join.wait()

        def after_hidden(block, total):
            rows = slab_of(block)
            live = live_rows(lengths, block, SLAB)
            branch = join.total(rows) + rows_ref[1:2, :]
            scaled, root = norm_parts(trunk[rows, :] + branch)
            after = scaled * rows_ref[4:5, :] + rows_ref[5:6, :]
            square = total[0] + jnp.sum(live * branch * branch, 0, keepdims=True)
            if first:
                normed[1, rows, :] = scaled
                inverse[1, rows, :] = root
                trunk[rows, :] = after
                low[1, rows, :] = after.astype(BF16)
                return (square,)
            result[rows, :] = (after * live).astype(BF16)
            grad = grad_in[rows, :].astype(F32)
            return (square, *from_output(rows, grad, scaled, root, total[1:]))

        def from_output(rows, grad, scaled, root, total, layer=layer):
            second = norm_back(grad, scaled, root, rows_ref[4:5, :])
            small = second.astype(BF16)
            trunk[rows, :] = second
            outer_grad[layer, rows, :] = small
            return (
                total[0] + jnp.sum(small.astype(F32), 0, keepdims=True),
                total[1] + jnp.sum(grad * scaled, 0, keepdims=True),
                total[2] + jnp.sum(grad, 0, keepdims=True),
            )

        initial = (zero,) if first else (zero,) * 4
        square, *back = lax.fori_loop(0, 256 // SLAB, after_hidden, initial)
        total_ref[4 + 3 * layer : 5 + 3 * layer, 0:1024] = square
        if not first:
            sums[1], sums[4], sums[5] = back

    for item in gathers:
        item.close()
    grouped = [landings[9 * group : 9 * group + 9] for group in range(4)]
    last_one, one, two, three = (
        Scatter(weights, group, [grouped[group][3 * i : 3 * i + 3] for i in range(3)], scatter_send, scatter_recv)
        for group in range(4)
    )
    closing = [last_one, one, two, three] + closing
    head_sum = [jnp.zeros((1, 512), F32)] * 2
    each = range(3)
    idle = lambda: None

    def onward(group, phase):
        for third in each:
            group.onward(phase, third)

    for layer in (1, 0):
        last = layer == 0
        heads = HeadsBack(
            mixed_grad.at[layer], taken.at[layer], key_value.at[layer], query_buf.at[layer], grads.at[layer],
            local_sem, turn_send, turn_recv, send_sem, recv_sem,
        )
        closing.pop().close()
        closing.append(heads)
        if last:

            def from_above(block, total):
                rows = slab_of(block)
                grad = trunk[rows, :] + join.total(rows)
                return from_output(rows, grad, normed[1, rows, :], inverse[1, rows, :], total, 0)

            sums[1], sums[4], sums[5] = lax.fori_loop(0, 256 // SLAB, from_above, (sums[1], sums[4], sums[5]))

        def hidden_back(tile, carry):
            start = pl.multiple_of(tile * 512, 512)
            columns = pl.ds(start, 512)
            grad = straight(outer_grad[layer], columns_of(weights, OUTER + start, 512))
            small = (grad * slope[layer, :, columns].astype(F32)).astype(BF16)
            inner_grad[layer, :, columns] = small
            total_ref[0:1, columns] += jnp.sum(small.astype(F32), 0, keepdims=True)
            return carry

        lax.fori_loop(0, 4, hidden_back, 0)
        join = new_join()
        for quarter in range(4):
            join.offer(quarter, across(inner_grad[layer], quarter_of(weights, quarter, INNER, 2048)))
        if last:
            left = outer_grad[...].reshape(512, 1024)
            weight_grad(weights, OUTER, left, act, 1536)
            three.first(0, 1)
            three.first(0, 0, (0,))
            weight_grad(weights, OUTER, left, act, 512, 1536)
            three.first(0, 2, (0,))
            weight_grad(weights, INNER, middle[...].reshape(512, 1024), inner_grad, 2048)
            two.first(0, 1)
        join.wait()

        def from_middle(block, total):
            rows = slab_of(block)
            grad = trunk[rows, :] + join.total(rows)
            scaled = normed[2 * layer, rows, :]
            before = norm_back(grad, scaled, inverse[2 * layer, rows, :], rows_ref[2:3, :])
            small = before.astype(BF16)
            trunk[rows, :] = before
            attn_grad[layer, rows, :] = small
            return (
                total[0] + jnp.sum(small.astype(F32), 0, keepdims=True),
                total[1] + jnp.sum(grad * scaled, 0, keepdims=True),
                total[2] + jnp.sum(grad, 0, keepdims=True),
            )

        sums[0], sums[2], sums[3] = lax.fori_loop(0, 256 // SLAB, from_middle, (sums[0], sums[2], sums[3]))
        mixed_grad[layer] = straight(attn_grad[layer], columns_of(weights, OUT, 512)).astype(BF16)
        heads.start()
        if last:
            for third in (0, 2):
                three.first(0, third, (1,))
            weight_grad(weights, OUT, attn_grad[...].reshape(512, 1024), mixed, 512)
            columns = jnp.concatenate(sums + [jnp.zeros((LANES - 6, 1024), F32)], 0).T
            weights[:, :, :, :, :, EXTRA : EXTRA + LANES] = columns.astype(BF16).reshape(*SHARDS, 16, LANES)
            for third in (0, 2):
                two.first(0, third, (0,))
        heads.attend(
            length, unit.at[layer], exact.at[layer], logs.at[layer], grad_buf, query_sum,
            (lambda: onward(three, 0)) if last else idle, (lambda: two.onward(0, 1)) if last else idle,
        )
        if last:
            for third in (0, 2):
                two.first(0, third, (1,))
            for third in (0, 2):
                two.onward(0, third)
        heads.collect(0)
        heads.collect(1)
        head_sum[1] = head_sum[1] + jnp.sum(grads[layer, 1].astype(F32), 0, keepdims=True)
        early = [
            across(grads[layer, 0], quarter_of(weights, quarter, KEY, 512))
            + across(grads[layer, 1], quarter_of(weights, quarter, VALUE, 512))
            for quarter in range(4)
        ]
        left = low[...].reshape(512, 1024)
        if last:
            weight_grad(weights, KEY, left, grads.at[:, 0], 512)
            weight_grad(weights, VALUE, left, grads.at[:, 1], 512)
            for third in (1, 0, 2):
                one.first(0, third)
            for third in each:
                three.settle(0, third)
                three.first(1, third)
        heads.collect(2)
        head_sum[0] = head_sum[0] + jnp.sum(grads[layer, 2].astype(F32), 0, keepdims=True)
        join = new_join()
        for quarter in range(4):
            join.offer(
                quarter, early[quarter] + across(grads[layer, 2], quarter_of(weights, quarter, QUERY, 512))
            )
        if last:
            weight_grad(weights, QUERY, left, grads.at[:, 2], 512)
            for third in (1, 0, 2):
                last_one.first(0, third)
            total_ref[1:2, 0:512] = head_sum[0]
            total_ref[1:2, 512:1024] = head_sum[1]
            count = sum(jnp.clip(lengths[s] - c * ROWS, 0, ROWS) for s in range(2)).astype(F32)
            total_ref[1:2, 1024:1152] = jnp.full((1, LANES), count, F32)
        else:
            join.wait()

    totals = Totals(total_ref, total_land, total_send, total_recv)
    totals.first(0)

    def settle(group, phase):
        for third in (1, 0, 2):
            group.settle(phase, third)
            if phase < 2:
                group.first(phase + 1, third)

    settle(two, 0)
    onward(one, 0)
    onward(last_one, 0)
    onward(three, 1)
    join.wait()
    for s in range(2):
        rows = pl.ds(s * ROWS, ROWS)
        stream_grad[:, s, :] = trunk[rows, :] + join.total(rows)
    totals.settle(0)
    totals.first(1)
    settle(one, 0)
    settle(last_one, 0)
    onward(two, 1)
    settle(three, 1)
    result_ref[...] = jnp.stack([result[s * ROWS : s * ROWS + ROWS, :].astype(F32) for s in range(2)], 1).astype(BF16)
    totals.settle(1)
    totals.first(2)
    settle(one, 1)
    settle(last_one, 1)
    settle(two, 1)
    settle(three, 2)

    def mine(start, width):
        return weights[x // 2, at["z"], x % 2, at["y"], :, start : start + width].astype(F32)

    outer_out[...] = mine(OUTER, 2048)
    settle(two, 2)
    output_out[...] = mine(OUT, 512)
    inner_out[...] = mine(INNER, 2048)
    vector_out[...] = mine(EXTRA, LANES).T[0:8, :]
    totals.settle(2)
    scale = 1.0 / (total_ref[1:2, 1024:1025] * 1024.0)
    square = jnp.sum(total_ref[:, 0:1024], 1, keepdims=True)
    root_ref[...] = jnp.broadcast_to(jnp.sqrt(square * scale + 1e-06), root_ref.shape)
    settle(one, 2)
    settle(last_one, 2)
    query_out[...] = mine(QUERY, 512)
    key_out[...] = mine(KEY, 512)
    value_out[...] = mine(VALUE, 512)
    for item in closing + joined[-2:]:
        item.close()


def run_layers(*arguments):
    dma = pltpu.SemaphoreType.DMA
    out = lambda *shape: jax.ShapeDtypeStruct(shape, F32)
    vmem = lambda kind, *shape: pltpu.VMEM(shape, kind)
    return pl.pallas_call(
        layers_kernel,
        out_shape=(
            out(ROWS, 2, 1024), jax.ShapeDtypeStruct((ROWS, 2, 1024), BF16),
            out(16, 512), out(16, 512), out(16, 512), out(16, 512), out(16, 2048), out(16, 2048),
            out(8, 16), out(8, 2048), out(8, LANES),
        ),
        in_specs=[spec(pltpu.VMEM)] * 17 + [spec(pltpu.SMEM)],
        out_specs=(spec(pltpu.VMEM),) * 11,
        scratch_shapes=[
            vmem(BF16, *SHARDS, 16, WIDTH),
            vmem(F32, 1, 3072),
            vmem(F32, 8, 1024),
            vmem(BF16, 2, 256, 1024),
            vmem(BF16, 256, 1024),
            vmem(BF16, 256, 1024),
            vmem(F32, 256, 1024),
            vmem(BF16, 3, 256, 512),
            vmem(BF16, 2, 3, 1024, LANES),
            vmem(F32, 2, 1024, LANES),
            vmem(F32, 2, 8, 256),
            vmem(BF16, 2, 1024, LANES),
            vmem(BF16, 2, 256, 512),
            vmem(F32, 3, 256, 1024),
            vmem(F32, 3, 256, 1),
            vmem(BF16, 2, 256, 1024),
            vmem(BF16, 2, 256, 2048),
            vmem(BF16, 2, 256, 2048),
            vmem(BF16, 2, 256, 1024),
            vmem(BF16, 2, 256, 2048),
            vmem(BF16, 2, 256, 1024),
            vmem(BF16, 2, 3, 256, 512),
            vmem(BF16, 2, 256, 512),
            vmem(BF16, 2, 1024, LANES),
            vmem(BF16, 2048, LANES),
            vmem(F32, 2048, LANES),
            vmem(BF16, 2, 2, 1024, LANES),
            vmem(BF16, 2, 1024, LANES),
            vmem(BF16, 2, 2, 256, 512),
            vmem(BF16, 2, 2, 256, 512),
            vmem(F32, 3, 3, 8, 2048),
            dma((4,)),
            dma((3, 3)),
            dma((GATHER_COUNT,)),
            dma((3,)),
            dma((9,)),
            dma((1,)),
            dma((1,)),
            dma((2,)),
            dma((2,)),
            dma((1,)),
            dma((1,)),
            dma((3,)),
            dma((3,)),
            dma((4, 3)),
            dma((SCATTER_COUNT,)),
            *(shape for group in range(4) for shape in landing_shapes(group)),
        ],
        compiler_params=pltpu.CompilerParams(
            collective_id=3, has_side_effects=True, vmem_limit_bytes=LIMIT
        ),
        name="layers",
    )(*arguments)


def finish_kernel(
    stream_in, result_in, query_in, key_in, value_in, output_in, inner_in, outer_in, vectors, totals, roots,
    result, stream_grad, query, key, value, output, inner, outer, query_sum, value_sum, inner_sum, *rest,
):
    for source, target in (
        (result_in, result), (stream_in, stream_grad), (query_in, query), (key_in, key), (value_in, value),
        (output_in, output), (inner_in, inner), (outer_in, outer),
    ):
        target[...] = source[...]
    query_sum[...] = totals[1:2, 0:512].reshape(512)
    value_sum[...] = totals[1:2, 512:1024].reshape(512)
    inner_sum[...] = totals[0:1, :].reshape(2048)
    for j in range(6):
        rest[j][...] = vectors[j : j + 1, :].reshape(16)
    rest[6][...] = jnp.concatenate(
        [
            jnp.concatenate([roots[2 + 3 * layer + j : 3 + 3 * layer + j, 0:1] for j in range(3)], 1)
            for layer in range(LAYERS)
        ],
        0,
    )


def finish(partial):
    out = lambda *shape: jax.ShapeDtypeStruct(shape, F32)
    return pl.pallas_call(
        finish_kernel,
        out_shape=(
            jax.ShapeDtypeStruct((ROWS, 2, 1024), BF16), out(ROWS, 2, 1024),
            out(16, 512), out(16, 512), out(16, 512), out(16, 512), out(16, 2048), out(16, 2048),
            out(512), out(512), out(2048), *(out(16) for _ in range(6)), out(LAYERS, 3),
        ),
        in_specs=[spec(pltpu.VMEM)] * 11,
        out_specs=(spec(pltpu.VMEM),) * 18,
        name="finish",
    )(*partial)


def body(
    stream,
    lengths,
    query_weight,
    query_bias,
    key_weight,
    value_weight,
    value_bias,
    output_weight,
    output_bias,
    first_gain,
    first_shift,
    inner_weight,
    inner_bias,
    outer_weight,
    outer_bias,
    second_gain,
    second_shift,
    cotangent,
):
    partial = run_layers(
        stream, cotangent, query_weight, key_weight, value_weight, output_weight.T, inner_weight, outer_weight.T,
        output_bias, outer_bias, first_gain, first_shift, second_gain, second_shift,
        query_bias, value_bias, inner_bias, lengths,
    )
    (
        result, stream_grad, grad_query, grad_key, grad_value, grad_output, grad_inner, grad_outer,
        query_sum, value_sum, inner_sum, *vectors, roots,
    ) = finish(partial)
    return (
        result,
        stream_grad,
        grad_query,
        query_sum,
        grad_key,
        grad_value,
        value_sum,
        grad_output.T,
        vectors[0],
        vectors[2],
        vectors[3],
        grad_inner,
        inner_sum,
        grad_outer.T,
        vectors[1],
        vectors[4],
        vectors[5],
        roots,
    )


def solution(mesh):
    in_specs = (
        P("context", "fsdp", None),
        P("fsdp"),
        P(("fsdp", "context"), "tensor"),
        P("tensor"),
        P(("fsdp", "context"), "tensor"),
        P(("fsdp", "context"), "tensor"),
        P("tensor"),
        P("tensor", ("fsdp", "context")),
        P(("fsdp", "context")),
        P(("fsdp", "context")),
        P(("fsdp", "context")),
        P(("fsdp", "context"), "tensor"),
        P("tensor"),
        P("tensor", ("fsdp", "context")),
        P(("fsdp", "context")),
        P(("fsdp", "context")),
        P(("fsdp", "context")),
        P("context", "fsdp", None),
    )
    out_specs = (
        P("context", "fsdp", None),
        P("context", "fsdp", None),
        P(("fsdp", "context"), "tensor"),
        P("tensor"),
        P(("fsdp", "context"), "tensor"),
        P(("fsdp", "context"), "tensor"),
        P("tensor"),
        P("tensor", ("fsdp", "context")),
        P(("fsdp", "context")),
        P(("fsdp", "context")),
        P(("fsdp", "context")),
        P(("fsdp", "context"), "tensor"),
        P("tensor"),
        P("tensor", ("fsdp", "context")),
        P(("fsdp", "context")),
        P(("fsdp", "context")),
        P(("fsdp", "context")),
        P(),
    )
    return jax.shard_map(body, mesh=mesh, in_specs=in_specs, out_specs=out_specs, check_vma=False)
```

```python
import jax
import jax.numpy as jnp
from jax import lax
from jax.experimental import pallas as pl
from jax.experimental.pallas import tpu as pltpu
from jax.sharding import PartitionSpec as P

HEAD = 64
LAYERS = 2
LANES = 128
MESH = pl.DeviceIdType.MESH

F32 = jnp.float32
BF16 = jnp.bfloat16
ROWS = 128
LIMIT = 60 * 2**20
WIDTH = 6272
QUERY, KEY, VALUE, OUT, EXTRA, INNER, OUTER = 0, 512, 1024, 1536, 2048, 2176, 4224
GROUPS = ((QUERY, OUT), (OUT, OUTER), (OUTER, WIDTH))
TILES = (((2, 2), (2, 2), (2, 2)), ((3, 3), (4, 5), (3, 3)), ((2, 3), (3, 3), (2, 3)))
ORDERS = ("zyx", "yxz", "xzy")
SHARDS = (2, 4, 2, 4)


def spec(space):
    return pl.BlockSpec(memory_space=space)


def place():
    f = lax.axis_index("fsdp")
    c = lax.axis_index("context")
    t = lax.axis_index("tensor")
    return {"x": 2 * (f // 4) + c // 4, "y": c % 4, "z": f % 4, "t": t}


def device(at):
    x = at["x"]
    return ((x // 2) * 4 + at["z"], (x % 2) * 4 + at["y"], at["t"])


def shifted(at, axis, step):
    moved = dict(at)
    moved[axis] = lax.rem(at[axis] + step + 4, 4)
    return moved


def greet(devices):
    barrier = pltpu.get_barrier_semaphore()
    for device_id in devices:
        pl.semaphore_signal(barrier, inc=1, device_id=device_id, device_id_type=MESH)
    pl.semaphore_wait(barrier, len(devices))


def neighbours(at, steps):
    return [device(shifted(at, axis, step)) for axis in "xyz" for step in steps]


def far_peers():
    f = lax.axis_index("fsdp")
    c = lax.axis_index("context")
    t = lax.axis_index("tensor")
    return [(f, (1 - c // 4) * 4 + y, t) for y in range(4)]


def remote(src, dst, send_sem, recv_sem, device_id):
    return pltpu.make_async_remote_copy(
        src_ref=src,
        dst_ref=dst,
        send_sem=send_sem,
        recv_sem=recv_sem,
        device_id=device_id,
        device_id_type=MESH,
    )


def drain(ref, sem):
    pltpu.make_async_copy(ref, ref, sem).wait()


def bulk(ref, count, group, groups=GROUPS):
    start, end = groups[group]
    picks = {
        3: (0, 0, 0, slice(0, 3)),
        8: (0, slice(0, 2), 0),
        12: (0, slice(0, 3), 0),
        32: (0,),
        48: (slice(None), slice(0, 3)),
    }[count]
    picks = picks + (slice(None),) * (5 - len(picks))
    return ref.at[picks + (pl.ds(start, end - start),)]


def shards(ref, at, whole, cols):
    x = at["x"]
    xh = slice(None) if "x" in whole else x // 2
    xl = slice(None) if "x" in whole else x % 2
    z = slice(None) if "z" in whole else at["z"]
    y = slice(None) if "y" in whole else at["y"]
    return ref.at[xh, z, xl, y, :, pl.ds(cols[0], cols[1])]


def thirds(group, groups=GROUPS, tiles_of=TILES):
    start = groups[group][0]
    parts = []
    for pair in tiles_of[group]:
        halves = []
        for tiles in pair:
            halves.append((start, tiles * LANES))
            start += tiles * LANES
        parts.append(tuple(halves))
    return parts


def across(left, right):
    return lax.dot_general(left, right, (((1,), (1,)), ((), ())), preferred_element_type=F32)


def straight(left, right):
    return jnp.dot(left, right, preferred_element_type=F32)


def rows_of(block):
    return pl.ds(pl.multiple_of(block * ROWS, ROWS), ROWS)


def by_head(block):
    first = lax.broadcasted_iota(jnp.int32, block.shape, 1) < HEAD
    zero = jnp.zeros_like(block)
    return jnp.concatenate([jnp.where(first, block, zero), jnp.where(first, zero, block)], 0)


def key_mask(length, first, count):
    position = first + lax.broadcasted_iota(jnp.int32, (count, 1), 0)
    return jnp.where(position < length, 0.0, -1e30)


def columns_of(weights, start, width):
    return weights[:, :, :, :, :, pl.ds(start, width)].reshape(1024, width)


def quarter_of(weights, quarter, start, width):
    z = 2 * (quarter % 2)
    return weights[quarter // 2, z : z + 2, :, :, :, start : start + width].reshape(256, width)


def part(ref, peer):
    return ref.at[rows_of(peer // 4), rows_of(peer % 4)]


GATHER_SLOTS = {(0, 0): 0, (0, 1): 1, (0, 2): 2, (1, 0): 9, (1, 1): 10, (1, 2): 17, (2, 0): 24, (2, 1): 25, (2, 2): 32}
GATHER_COUNT = 39


class Gather:
    def __init__(self, weights, group, send_sem, recv_sem):
        self.at = place()
        self.weights, self.group = weights, group
        self.send_sem, self.recv_sem = send_sem, recv_sem
        self.parts = thirds(group)
        self.sent = {}

    def send(self, third, phase, kind, origin, cols, step):
        order = ORDERS[third]
        block = shards(self.weights, origin, order[:phase], cols)
        slot = 0 if kind is None or kind > 1 else 1 + 2 * third + kind
        copy = remote(
            block, block, self.send_sem.at[self.group, phase], self.recv_sem.at[GATHER_SLOTS[self.group, phase] + slot],
            device(shifted(self.at, order[phase], step)),
        )
        copy.start()
        self.sent[third, phase, kind] = copy

    def first(self, phase, thirds_now=range(3), pieces=(0, 1)):
        for piece in pieces:
            for third in thirds_now:
                low, high = self.parts[third]
                self.send(third, phase, 2 * piece, self.at, (low, high)[piece], 1)
                self.send(third, phase, 2 * piece + 1, self.at, (high, low)[piece], -1)

    def direct(self, phase):
        for third in range(3):
            low, high = self.parts[third]
            for step in (1, 2, 3):
                self.send(third, phase, None, self.at, (low[0], low[1] + high[1]), step)

    def arrive(self, phase):
        drain(bulk(self.weights, (3, 12)[phase], self.group), self.recv_sem.at[GATHER_SLOTS[self.group, phase]])

    def onward(self, phase, thirds_now=range(3)):
        for third in thirds_now:
            axis = ORDERS[third][phase]
            low, high = self.parts[third]
            self.sent[third, phase, 0].wait_recv()
            self.send(third, phase, 4, shifted(self.at, axis, -1), low, 1)
            self.sent[third, phase, 1].wait_recv()
            self.send(third, phase, 5, shifted(self.at, axis, 1), high, -1)

    def settle(self, phase):
        drain(bulk(self.weights, (2, 8, 32)[phase], self.group), self.recv_sem.at[GATHER_SLOTS[self.group, phase]])

    def close(self):
        for phase in range(3):
            drain(bulk(self.weights, (3, 12, 48)[phase], self.group), self.send_sem.at[self.group, phase])


def seven(ref):
    return ref.at[pl.ds(0, 7 * ROWS)]


class Heads:
    def __init__(self, own, unit, outcome, mixed, local_sem, send_sem, recv_sem, back_send, back_recv):
        self.f = lax.axis_index("fsdp")
        self.c = lax.axis_index("context")
        self.t = lax.axis_index("tensor")
        self.own, self.unit, self.outcome, self.mixed = own, unit, outcome, mixed
        self.local_sem, self.send_sem, self.recv_sem = local_sem, send_sem, recv_sem
        self.back_send, self.back_recv = back_send, back_recv

    def push(self, j, d):
        peer = lax.rem(self.c + d, 8)
        return remote(
            part(self.own.at[j], peer), self.unit.at[j, rows_of(self.c)],
            self.send_sem.at[j], self.recv_sem.at[j + (d - 1 if j == 2 else 0)], (self.f, peer, self.t),
        )

    def keep(self, j):
        return pltpu.make_async_copy(
            part(self.own.at[j], self.c), self.unit.at[j, rows_of(self.c)], self.local_sem.at[j]
        )

    def answer(self, d):
        peer = lax.rem(self.c + d, 8)
        return remote(
            self.outcome.at[rows_of(peer)], part(self.mixed, self.c),
            self.back_send.at[0], self.back_recv.at[0], (self.f, peer, self.t),
        )

    def keep_back(self):
        return pltpu.make_async_copy(
            self.outcome.at[rows_of(self.c)], part(self.mixed, self.c), self.local_sem.at[3]
        )

    def project(self, x, weights, bias):
        for j, column in enumerate((KEY, VALUE, QUERY)):
            product = straight(x, columns_of(weights, column, 512))
            if j == 1:
                product = product + bias[:, 512:1024]
            if j == 2:
                product = product + bias[:, 0:512]
            self.own[j] = product.astype(BF16)
            for d in (4, 1, 7, 5, 3, 2, 6):
                self.push(j, d).start()
            self.keep(j).start()

    def attend(self, length, exact, logs):
        c = self.c
        for j in range(2):
            self.keep(j).wait()
            drain(seven(self.outcome), self.recv_sem.at[j])
        mask = key_mask(length, 0, 8 * ROWS)
        keys = self.unit[0]
        values_across = self.unit[1].T
        self.keep(2).wait()

        def step(d, carry):
            block = lax.rem(c + d, 8)

            @pl.when(d > 0)
            def _():
                self.push(2, 8 - d).wait_recv()

            queries = self.unit[2, rows_of(block), :] * jnp.asarray(0.125, BF16)
            scores = across(keys, by_head(queries)) + mask
            top = jnp.max(scores, 0, keepdims=True)
            exponent = jnp.exp(scores - top)
            total = jnp.sum(exponent, 0, keepdims=True)
            outcome = straight(values_across, exponent.astype(BF16)) / total
            both = jnp.concatenate([outcome[:HEAD, :ROWS], outcome[HEAD:, ROWS:]], 0).T
            exact[rows_of(block), :] = both
            self.outcome[rows_of(block), :] = both.astype(BF16)
            logs[pl.ds(block, 1), :] = top + jnp.log(total)

            @pl.when(d > 0)
            def _():
                self.answer(d).start()

            return carry

        lax.fori_loop(0, 8, step, 0, unroll=2)
        self.keep_back().start()

    def collect(self):
        self.keep_back().wait()
        drain(seven(self.outcome), self.back_recv.at[0])

    def close(self):
        drain(seven(self.outcome), self.back_send.at[0])
        for j in range(3):
            drain(seven(self.outcome), self.send_sem.at[j])


class Join:
    def __init__(self, number, before, sent, landed, send_sem, recv_sem):
        t = lax.axis_index("tensor")
        self.partner = (lax.axis_index("fsdp"), lax.axis_index("context"), 1 - t)
        self.sent, self.landed = sent.at[number % 2], landed.at[number % 2]
        self.send_sem, self.recv_sem = send_sem.at[number % 2], recv_sem.at[number % 2]
        self.before = before

    def copy(self, half):
        return remote(
            self.sent.at[half], self.landed.at[half], self.send_sem, self.recv_sem, self.partner,
        )

    def offer(self, quarter, term):
        half, side = quarter // 2, quarter % 2
        if quarter == 0 and self.before is not None:
            self.before.close()
        self.sent[half, :, side * 256 : side * 256 + 256] = term.astype(BF16)
        if side == 1:
            self.copy(half).start()

    def wait(self):
        drain(self.landed, self.recv_sem)

    def total(self, rows):
        return jnp.concatenate(
            [self.sent[half, rows, :].astype(F32) + self.landed[half, rows, :].astype(F32) for half in range(2)],
            1,
        )

    def close(self):
        drain(self.sent, self.send_sem)


def gelu_parts(argument):
    square = argument * argument
    inner = 0.7978845608028654 * argument * (1.0 + 0.044715 * square)
    bend = jnp.tanh(inner)
    half = 0.5 * (1.0 + bend)
    slope = half + 0.5 * argument * (1.0 - bend * bend) * 0.7978845608028654 * (
        1.0 + 3.0 * 0.044715 * square
    )
    return argument * half, slope


def norm_parts(hidden):
    centre = hidden - jnp.mean(hidden, -1, keepdims=True)
    inverse = lax.rsqrt(jnp.mean(centre * centre, -1, keepdims=True) + 1e-05)
    return centre * inverse, inverse


def live_rows(lengths, block, count):
    c = lax.axis_index("context")
    row = block * count + lax.broadcasted_iota(jnp.int32, (count, 1), 0)
    slot = c * ROWS + lax.rem(row, ROWS)
    return jnp.where(slot < jnp.where(row < ROWS, lengths[0], lengths[1]), 1.0, 0.0)


SLAB = 128


def slab_of(block):
    return pl.ds(pl.multiple_of(block * SLAB, SLAB), SLAB)


def pack(weights, own, query, key, value, output, inner, outer, vectors):
    xh, z, xl, y = own

    def put(start, block):
        weights[xh, z, xl, y, :, start : start + block.shape[1]] = block

    put(QUERY, query[...])
    put(KEY, key[...])
    put(VALUE, value[...])
    put(OUT, output[...])
    put(INNER, inner[...])
    put(OUTER, outer[...])
    eye = jnp.where(
        lax.broadcasted_iota(jnp.int32, (16, 16), 0) == lax.broadcasted_iota(jnp.int32, (16, 16), 1), 1.0, 0.0
    ).astype(BF16)
    rows = [vector[...].astype(F32).reshape(1, 16) for vector in vectors]
    table = jnp.concatenate(rows + [jnp.zeros((LANES - 6, 16), F32)], 0).astype(BF16)
    put(EXTRA, across(eye, table).astype(BF16))


def rows_by_sequence(source, target, keep):
    whole = source[...].astype(F32)
    for s in range(2):
        target[s * ROWS : s * ROWS + ROWS, :] = (whole[:, s, :] * keep(s)).astype(target.dtype)


def norm_back(grad_out, normed, inverse, gain):
    scaled = grad_out * gain
    return inverse * (
        scaled
        - jnp.mean(scaled, -1, keepdims=True)
        - normed * jnp.mean(scaled * normed, -1, keepdims=True)
    )


SCATTER_GROUPS = ((QUERY, KEY), (KEY, OUT), (OUT, OUTER), (OUTER, WIDTH))
SCATTER_TILES = (((1, 0), (1, 1), (1, 0)), ((1, 1), (2, 2), (1, 1)), *TILES[1:])
DIRECT = (((0, 1, 2), (1, 2), (0, 1, 2)), ((1, 2),) * 3, ((2,),) * 3, ((2,),) * 3)
SCATTER_SLOTS = {}
SCATTER_COUNT = 0
for _group in range(4):
    for _third in range(3):
        for _phase in range(3):
            SCATTER_SLOTS[_group, _third, _phase] = SCATTER_COUNT
            SCATTER_COUNT += 1 if _phase in DIRECT[_group][_third] else 4


class Scatter:
    def __init__(self, work, group, landings, send_sem, recv_sem):
        self.at = place()
        self.work, self.group, self.landings = work, group, landings
        self.send_sem, self.recv_sem = send_sem, recv_sem
        self.parts = thirds(group, SCATTER_GROUPS, SCATTER_TILES)
        self.sent = {}

    def slot(self, third, phase, number):
        return self.recv_sem.at[SCATTER_SLOTS[self.group, third, phase] + number]

    def ring(self, third, phase):
        order = ORDERS[third][::-1]
        return order[phase], order[phase + 1 :]

    def send(self, third, phase, kind, away, cols, step):
        axis, whole = self.ring(third, phase)
        land = self.landings[third][phase].at[kind]
        if cols[1] != land.shape[-1]:
            land = land.at[..., pl.ds(0, cols[1])]
        number = kind // 2 + 1 if kind > 1 else kind
        if phase in DIRECT[self.group][third]:
            number = 0
        copy = remote(
            shards(self.work, shifted(self.at, axis, away), whole, cols), land,
            self.send_sem.at[self.group, phase], self.slot(third, phase, number),
            device(shifted(self.at, axis, step)),
        )
        copy.start()
        self.sent[third, phase, kind] = copy

    def add(self, third, phase, away, cols, kinds):
        axis, whole = self.ring(third, phase)
        origin = shifted(self.at, axis, away)
        land = self.landings[third][phase]
        x = origin["x"]
        wide = {name: name in whole for name in "xyz"}
        columns = pl.ds(cols[0], cols[1])

        def one(ix, iz):
            xh, xl = (ix // 2, ix % 2) if wide["x"] else (x // 2, x % 2)
            z = iz if wide["z"] else origin["z"]
            y = slice(None) if wide["y"] else origin["y"]
            index = (xh, z, xl, y, slice(None), columns)
            total = self.work[index].astype(F32)
            for kind in kinds:
                at = (kind,)
                at += (xh,) if wide["x"] else ()
                at += (z,) if wide["z"] else ()
                at += (xl,) if wide["x"] else ()
                at += (slice(None),) if wide["y"] else ()
                total = total + land[at + (slice(None), pl.ds(0, cols[1]))].astype(F32)
            self.work[index] = total.astype(BF16)

        count_z = 4 if wide["z"] else 1
        if not wide["x"]:
            for iz in range(count_z):
                one(0, iz)
        else:
            def turn(ix, carry):
                for iz in range(count_z):
                    one(ix, iz)
                return carry

            lax.fori_loop(0, 4, turn, 0)

    def first(self, phase, third, pieces=(0, 1)):
        if phase in DIRECT[self.group][third]:
            self.direct(phase, third)
            return
        low, high = self.parts[third]
        if 0 in pieces:
            self.send(third, phase, 0, 2, low, 1)
            self.send(third, phase, 1, 2, high, -1)
        if 1 in pieces:
            self.send(third, phase, 2, 1, high, 1)
            self.send(third, phase, 3, -1, low, -1)

    def direct(self, phase, third):
        low, high = self.parts[third]
        for step in (1, 2, 3):
            self.send(third, phase, step - 1, step, (low[0], low[1] + high[1]), step)

    def arrive(self, phase, third):
        low, high = self.parts[third]
        drain(self.landings[third][phase], self.slot(third, phase, 0))
        self.add(third, phase, 0, (low[0], low[1] + high[1]), (0, 1, 2))

    def onward(self, phase, third):
        if phase in DIRECT[self.group][third]:
            return
        low, high = self.parts[third]
        self.sent[third, phase, 0].wait_recv()
        self.add(third, phase, 1, low, (0,))
        self.send(third, phase, 4, 1, low, 1)
        self.sent[third, phase, 1].wait_recv()
        self.add(third, phase, -1, high, (1,))
        self.send(third, phase, 5, -1, high, -1)

    def settle(self, phase, third):
        if phase in DIRECT[self.group][third]:
            self.arrive(phase, third)
            return
        low, high = self.parts[third]
        axis, whole = self.ring(third, phase)
        block = shards(self.work, self.at, whole, (low[0], low[1] + high[1]))
        for slot in (2, 3):
            drain(block, self.slot(third, phase, slot))
        self.add(third, phase, 0, high, (2, 5))
        self.add(third, phase, 0, low, (3, 4))

    def close(self):
        for phase in range(3):
            drain(bulk(self.work, (48, 12, 3)[phase], self.group, SCATTER_GROUPS), self.send_sem.at[self.group, phase])


def landing_shapes(group):
    shapes = []
    for third in range(3):
        order = ORDERS[third][::-1]
        low, high = thirds(group, SCATTER_GROUPS, SCATTER_TILES)[third]
        for phase in range(3):
            whole = order[phase + 1 :]
            direct = phase in DIRECT[group][third]
            shape = [3 if direct else 6]
            shape += [2] if "x" in whole else []
            shape += [4] if "z" in whole else []
            shape += [2] if "x" in whole else []
            shape += [4] if "y" in whole else []
            width = low[1] + high[1] if direct else max(low[1], high[1])
            shapes.append(pltpu.VMEM((*shape, 16, width), BF16))
    return shapes


class Totals:
    def __init__(self, total, landed, send_sem, recv_sem):
        self.at = place()
        self.total, self.landed, self.send_sem, self.recv_sem = total, landed, send_sem, recv_sem

    def copy(self, phase, step):
        return remote(
            self.total, self.landed.at[phase, step - 1], self.send_sem.at[phase], self.recv_sem.at[phase], device(shifted(self.at, "xyz"[phase], step)),
        )

    def first(self, phase):
        for step in (1, 2, 3):
            self.copy(phase, step).start()

    def settle(self, phase):
        drain(self.landed.at[phase], self.recv_sem.at[phase])
        drain(self.landed.at[phase], self.send_sem.at[phase])
        self.total[...] += self.landed[phase, 0] + self.landed[phase, 1] + self.landed[phase, 2]


class HeadsBack:
    def __init__(self, mixed_grad, taken, key_value, query, grads, local_sem, send_sem, recv_sem, back_send, back_recv):
        self.f = lax.axis_index("fsdp")
        self.c = lax.axis_index("context")
        self.t = lax.axis_index("tensor")
        self.mixed_grad, self.taken, self.grads = mixed_grad, taken, grads
        self.sources = (key_value.at[0], key_value.at[1], query)
        self.key_value, self.query = key_value, query
        self.local_sem, self.send_sem, self.recv_sem = local_sem, send_sem, recv_sem
        self.back_send, self.back_recv = back_send, back_recv

    def push(self, d):
        peer = lax.rem(self.c + d, 8)
        return remote(
            part(self.mixed_grad, peer), self.taken.at[rows_of(self.c)],
            self.send_sem.at[0], self.recv_sem.at[0], (self.f, peer, self.t),
        )

    def keep(self):
        return pltpu.make_async_copy(
            part(self.mixed_grad, self.c), self.taken.at[rows_of(self.c)], self.local_sem.at[3]
        )

    def answer(self, j, d):
        peer = lax.rem(self.c + d, 8)
        return remote(
            self.sources[j].at[rows_of(peer)], part(self.grads.at[j], self.c),
            self.back_send.at[j], self.back_recv.at[j], (self.f, peer, self.t),
        )

    def keep_back(self, j):
        return pltpu.make_async_copy(
            self.sources[j].at[rows_of(self.c)], part(self.grads.at[j], self.c), self.local_sem.at[j]
        )

    def start(self):
        for d in (4, 1, 7, 5, 3, 2, 6):
            self.push(d).start()
        self.keep().start()

    def attend(self, length, unit, exact, logs_ref, grad_buf, query_sum, ahead, midway):
        c = self.c
        scale = jnp.asarray(0.125, BF16)
        queries = jnp.concatenate(
            [by_head(unit[2, pl.ds(block * ROWS, ROWS), :] * scale) for block in range(8)], 0
        )
        logs = jnp.concatenate([logs_ref[block : block + 1, :] for block in range(8)], 1)
        query_sum[...] = jnp.zeros_like(query_sum)
        ahead()
        self.keep().wait()
        drain(seven(self.taken), self.recv_sem.at[0])
        for block in range(8):
            grad_buf[pl.ds(block * 256, 256), :] = by_head(self.taken[pl.ds(block * ROWS, ROWS), :])
        turned = (self.taken[...].astype(F32) * exact[...]).T
        weighted = [jnp.sum(turned[head * HEAD : head * HEAD + HEAD], 0, keepdims=True) for head in range(2)]
        delta = jnp.concatenate(
            [
                weighted[head][:, block * ROWS : (block + 1) * ROWS]
                for block in range(8)
                for head in range(2)
            ],
            1,
        )

        def step(turn, carry):
            pair = lax.rem(c // 2 + turn, 4)
            spot = pl.ds(pl.multiple_of(pair * 256, 256), 256)
            keys = unit[0, spot, :]
            values = unit[1, spot, :]
            scores = across(keys, queries) + key_mask(length, pair * 256, 256)
            soft = jnp.exp(scores - logs)
            self.key_value[1, spot, :] = straight(soft.astype(BF16), grad_buf[...]).astype(BF16)
            soft_grad = across(values, grad_buf[...])
            score_grad = (soft * (soft_grad - delta)).astype(BF16)
            self.key_value[0, spot, :] = straight(score_grad, queries).astype(BF16)
            query_sum[...] += lax.dot_general(
                score_grad, keys, (((0,), (0,)), ((), ())), preferred_element_type=F32
            )

            for side in range(2):
                d = lax.rem(pair * 2 + side - c + 8, 8)

                @pl.when(d > 0)
                def _():
                    for j in range(2):
                        self.answer(j, d).start()

            return carry

        lax.fori_loop(1, 3, step, 0)
        midway()
        lax.fori_loop(3, 5, step, 0)
        first_lane = lax.broadcasted_iota(jnp.int32, (ROWS, LANES), 1) < HEAD
        for block in range(8):
            start = block * 256
            total = jnp.where(
                first_lane, query_sum[pl.ds(start, ROWS), :], query_sum[pl.ds(start + ROWS, ROWS), :]
            )
            self.query[pl.ds(block * ROWS, ROWS), :] = (total * 0.125).astype(BF16)
        for d in (4, 1, 7, 5, 3, 2, 6):
            self.answer(2, d).start()
        for j in range(3):
            self.keep_back(j).start()

    def collect(self, j):
        self.keep_back(j).wait()
        drain(seven(self.taken), self.back_recv.at[j])

    def close(self):
        drain(seven(self.taken), self.send_sem.at[0])
        for j in range(3):
            drain(seven(self.taken), self.back_send.at[j])


def put_quarter(work, quarter, start, value):
    z = 2 * (quarter % 2)
    work[quarter // 2, z : z + 2, :, :, :, pl.ds(start, value.shape[1])] = value.astype(BF16).reshape(
        2, 2, 4, 16, value.shape[1]
    )


def weight_grad(work, start, left, right, width, first=0):
    turned = left.T
    tile = 512

    def turn(i, carry):
        offset = pl.multiple_of(i * tile, tile)
        term = right[:, :, pl.ds(offset, tile)].reshape(512, tile)
        for quarter in range(4):
            put_quarter(work, quarter, start + offset, straight(turned[quarter * 256 : quarter * 256 + 256], term))
        return carry

    lax.fori_loop(first // tile, (first + width) // tile, turn, 0)


def layers_kernel(
    stream, cotangent, query, key, value, output, inner, outer, bias0, bias1, gain1, shift1, gain2, shift2,
    query_bias, value_bias, inner_bias, lengths,
    stream_grad, result_ref, query_out, key_out, value_out, output_out, inner_out, outer_out, vector_out, total_ref,
    root_ref,
    weights, bias, rows_ref, low, grad_in, result, trunk,
    own, unit, exact, logs, outcome, mixed, normed, inverse, middle, act, slope,
    attn_grad, inner_grad, outer_grad, grads, mixed_grad, taken, grad_buf, query_sum, key_value, query_buf,
    sent, landed, total_land,
    local_sem, gather_send, gather_recv, send_sem, recv_sem, back_send, back_recv, pair_send, pair_recv,
    turn_send, turn_recv, total_send, total_recv,
    scatter_send, scatter_recv, *landings,
):
    at = place()
    c = lax.axis_index("context")
    t = lax.axis_index("tensor")
    partner = (lax.axis_index("fsdp"), c, 1 - t)
    x = at["x"]
    closing = []
    joined = []

    def new_join():
        before = joined[-2] if len(joined) > 1 else None
        joined.append(Join(len(joined), before, sent, landed, pair_send, pair_recv))
        return joined[-1]

    pack(
        weights, (x // 2, at["z"], x % 2, at["y"]), query, key, value, output, inner, outer,
        (bias0, bias1, gain1, shift1, gain2, shift2),
    )
    greet(neighbours(at, (1, 2, 3)) + far_peers() + [partner])
    one, two, three = (Gather(weights, group, gather_send, gather_recv) for group in range(3))
    gathers = (one, two, three)
    for group in gathers:
        group.direct(0)
    rows_by_sequence(stream, low.at[0], lambda s: 1.0)
    one.arrive(0)
    one.direct(1)
    two.arrive(0)
    two.first(1)
    three.arrive(0)
    three.first(1)
    bias[:, 0:512] = query_bias[...].astype(F32).reshape(1, 512)
    bias[:, 512:1024] = value_bias[...].astype(F32).reshape(1, 512)
    bias[:, 1024:3072] = inner_bias[...].astype(F32).reshape(1, 2048)
    position = c * ROWS + lax.broadcasted_iota(jnp.int32, (ROWS, 1), 0)
    rows_by_sequence(cotangent, grad_in, lambda s: jnp.where(position < lengths[s], 1.0, 0.0))
    trunk[...] = low[0].astype(F32)
    total_ref[...] = jnp.zeros_like(total_ref)
    one.arrive(1)
    one.first(2)
    two.onward(1)
    three.onward(1)
    one.onward(2)
    two.settle(1)
    two.first(2)
    three.settle(1)
    three.first(2, (1,))
    one.settle(2)
    length = lengths[c // 4]
    zero = jnp.zeros((1, 1024), F32)
    sums = [zero] * 6

    for layer in range(LAYERS):
        first = layer == 0
        heads = Heads(
            own, unit.at[layer], outcome.at[layer], mixed.at[layer], local_sem,
            send_sem, recv_sem, back_send, back_recv,
        )
        if not first:
            closing.pop().close()
        closing.append(heads)
        heads.project(low[layer], weights, bias)
        if first:
            two.onward(2, (0, 2))
            two.onward(2, (1,))
        heads.attend(length, exact.at[layer], logs.at[layer])
        if first:
            three.first(2, (0, 2))
            three.onward(2, (1,))
        heads.collect()
        if first:
            two.settle(2)
            pick = jnp.where(
                lax.broadcasted_iota(jnp.int32, (8, LANES), 0) == lax.broadcasted_iota(jnp.int32, (8, LANES), 1),
                1.0, 0.0,
            ).astype(BF16)
            rows_ref[...] = across(pick, columns_of(weights, EXTRA, LANES))
        join = new_join()
        for quarter in range(4):
            join.offer(quarter, across(mixed[layer], quarter_of(weights, quarter, OUT, 512)))
        if first:
            three.onward(2, (0, 2))
        join.wait()

        def after_attention(block, total):
            rows = slab_of(block)
            live = live_rows(lengths, block, SLAB)
            before = trunk[rows, :]
            branch = join.total(rows) + rows_ref[0:1, :]
            scaled, root = norm_parts(before + branch)
            after = scaled * rows_ref[2:3, :] + rows_ref[3:4, :]
            normed[2 * layer, rows, :] = scaled
            inverse[2 * layer, rows, :] = root
            trunk[rows, :] = after
            middle[layer, rows, :] = after.astype(BF16)
            return (
                total[0] + jnp.sum(live * before * before, 0, keepdims=True),
                total[1] + jnp.sum(live * branch * branch, 0, keepdims=True),
            )

        squares = lax.fori_loop(0, 256 // SLAB, after_attention, (zero, zero))
        total_ref[2 + 3 * layer : 3 + 3 * layer, 0:1024] = squares[0]
        total_ref[3 + 3 * layer : 4 + 3 * layer, 0:1024] = squares[1]

        def hidden(tile, carry):
            start = pl.multiple_of(tile * 512, 512)
            columns = pl.ds(start, 512)
            pre = straight(middle[layer], columns_of(weights, INNER + start, 512)) + bias[:, pl.ds(1024 + start, 512)]
            act_part, slope_part = gelu_parts(pre)
            act[layer, :, columns] = act_part.astype(BF16)
            slope[layer, :, columns] = slope_part.astype(BF16)
            return carry

        lax.fori_loop(0, 4, hidden, 0)
        if first:
            three.settle(2)
        join = new_join()
        for quarter in range(4):
            join.offer(quarter, across(act[layer], quarter_of(weights, quarter, OUTER, 2048)))
        join.wait()

        def after_hidden(block, total):
            rows = slab_of(block)
            live = live_rows(lengths, block, SLAB)
            branch = join.total(rows) + rows_ref[1:2, :]
            scaled, root = norm_parts(trunk[rows, :] + branch)
            after = scaled * rows_ref[4:5, :] + rows_ref[5:6, :]
            square = total[0] + jnp.sum(live * branch * branch, 0, keepdims=True)
            if first:
                normed[1, rows, :] = scaled
                inverse[1, rows, :] = root
                trunk[rows, :] = after
                low[1, rows, :] = after.astype(BF16)
                return (square,)
            result[rows, :] = (after * live).astype(BF16)
            grad = grad_in[rows, :].astype(F32)
            return (square, *from_output(rows, grad, scaled, root, total[1:]))

        def from_output(rows, grad, scaled, root, total, layer=layer):
            second = norm_back(grad, scaled, root, rows_ref[4:5, :])
            small = second.astype(BF16)
            trunk[rows, :] = second
            outer_grad[layer, rows, :] = small
            return (
                total[0] + jnp.sum(small.astype(F32), 0, keepdims=True),
                total[1] + jnp.sum(grad * scaled, 0, keepdims=True),
                total[2] + jnp.sum(grad, 0, keepdims=True),
            )

        initial = (zero,) if first else (zero,) * 4
        square, *back = lax.fori_loop(0, 256 // SLAB, after_hidden, initial)
        total_ref[4 + 3 * layer : 5 + 3 * layer, 0:1024] = square
        if not first:
            sums[1], sums[4], sums[5] = back

    for item in gathers:
        item.close()
    grouped = [landings[9 * group : 9 * group + 9] for group in range(4)]
    last_one, one, two, three = (
        Scatter(weights, group, [grouped[group][3 * i : 3 * i + 3] for i in range(3)], scatter_send, scatter_recv)
        for group in range(4)
    )
    closing = [last_one, one, two, three] + closing
    head_sum = [jnp.zeros((1, 512), F32)] * 2
    each = range(3)
    idle = lambda: None

    def onward(group, phase):
        for third in each:
            group.onward(phase, third)

    for layer in (1, 0):
        last = layer == 0
        heads = HeadsBack(
            mixed_grad.at[layer], taken.at[layer], key_value.at[layer], query_buf.at[layer], grads.at[layer],
            local_sem, turn_send, turn_recv, send_sem, recv_sem,
        )
        closing.pop().close()
        closing.append(heads)
        if last:

            def from_above(block, total):
                rows = slab_of(block)
                grad = trunk[rows, :] + join.total(rows)
                return from_output(rows, grad, normed[1, rows, :], inverse[1, rows, :], total, 0)

            sums[1], sums[4], sums[5] = lax.fori_loop(0, 256 // SLAB, from_above, (sums[1], sums[4], sums[5]))

        def hidden_back(tile, carry):
            start = pl.multiple_of(tile * 512, 512)
            columns = pl.ds(start, 512)
            grad = straight(outer_grad[layer], columns_of(weights, OUTER + start, 512))
            small = (grad * slope[layer, :, columns].astype(F32)).astype(BF16)
            inner_grad[layer, :, columns] = small
            total_ref[0:1, columns] += jnp.sum(small.astype(F32), 0, keepdims=True)
            return carry

        lax.fori_loop(0, 4, hidden_back, 0)
        join = new_join()
        for quarter in range(4):
            join.offer(quarter, across(inner_grad[layer], quarter_of(weights, quarter, INNER, 2048)))
        if last:
            left = outer_grad[...].reshape(512, 1024)
            weight_grad(weights, OUTER, left, act, 1536)
            three.first(0, 1)
            three.first(0, 0, (0,))
            weight_grad(weights, OUTER, left, act, 512, 1536)
            three.first(0, 2, (0,))
            weight_grad(weights, INNER, middle[...].reshape(512, 1024), inner_grad, 2048)
            two.first(0, 1)
        join.wait()

        def from_middle(block, total):
            rows = slab_of(block)
            grad = trunk[rows, :] + join.total(rows)
            scaled = normed[2 * layer, rows, :]
            before = norm_back(grad, scaled, inverse[2 * layer, rows, :], rows_ref[2:3, :])
            small = before.astype(BF16)
            trunk[rows, :] = before
            attn_grad[layer, rows, :] = small
            return (
                total[0] + jnp.sum(small.astype(F32), 0, keepdims=True),
                total[1] + jnp.sum(grad * scaled, 0, keepdims=True),
                total[2] + jnp.sum(grad, 0, keepdims=True),
            )

        sums[0], sums[2], sums[3] = lax.fori_loop(0, 256 // SLAB, from_middle, (sums[0], sums[2], sums[3]))
        mixed_grad[layer] = straight(attn_grad[layer], columns_of(weights, OUT, 512)).astype(BF16)
        heads.start()
        if last:
            for third in (0, 2):
                three.first(0, third, (1,))
            weight_grad(weights, OUT, attn_grad[...].reshape(512, 1024), mixed, 512)
            columns = jnp.concatenate(sums + [jnp.zeros((LANES - 6, 1024), F32)], 0).T
            weights[:, :, :, :, :, EXTRA : EXTRA + LANES] = columns.astype(BF16).reshape(*SHARDS, 16, LANES)
            for third in (0, 2):
                two.first(0, third, (0,))
        heads.attend(
            length, unit.at[layer], exact.at[layer], logs.at[layer], grad_buf, query_sum,
            (lambda: onward(three, 0)) if last else idle, (lambda: two.onward(0, 1)) if last else idle,
        )
        if last:
            for third in (0, 2):
                two.first(0, third, (1,))
            for third in (0, 2):
                two.onward(0, third)
        heads.collect(0)
        heads.collect(1)
        head_sum[1] = head_sum[1] + jnp.sum(grads[layer, 1].astype(F32), 0, keepdims=True)
        early = [
            across(grads[layer, 0], quarter_of(weights, quarter, KEY, 512))
            + across(grads[layer, 1], quarter_of(weights, quarter, VALUE, 512))
            for quarter in range(4)
        ]
        left = low[...].reshape(512, 1024)
        if last:
            weight_grad(weights, KEY, left, grads.at[:, 0], 512)
            weight_grad(weights, VALUE, left, grads.at[:, 1], 512)
            for third in (1, 0, 2):
                one.first(0, third)
            for third in each:
                three.settle(0, third)
                three.first(1, third)
        heads.collect(2)
        head_sum[0] = head_sum[0] + jnp.sum(grads[layer, 2].astype(F32), 0, keepdims=True)
        join = new_join()
        for quarter in range(4):
            join.offer(
                quarter, early[quarter] + across(grads[layer, 2], quarter_of(weights, quarter, QUERY, 512))
            )
        if last:
            weight_grad(weights, QUERY, left, grads.at[:, 2], 512)
            for third in (1, 0, 2):
                last_one.first(0, third)
            total_ref[1:2, 0:512] = head_sum[0]
            total_ref[1:2, 512:1024] = head_sum[1]
            count = sum(jnp.clip(lengths[s] - c * ROWS, 0, ROWS) for s in range(2)).astype(F32)
            total_ref[1:2, 1024:1152] = jnp.full((1, LANES), count, F32)
        else:
            join.wait()

    totals = Totals(total_ref, total_land, total_send, total_recv)
    totals.first(0)

    def settle(group, phase):
        for third in (1, 0, 2):
            group.settle(phase, third)
            if phase < 2:
                group.first(phase + 1, third)

    settle(two, 0)
    onward(one, 0)
    onward(last_one, 0)
    onward(three, 1)
    join.wait()
    for s in range(2):
        rows = pl.ds(s * ROWS, ROWS)
        stream_grad[:, s, :] = trunk[rows, :] + join.total(rows)
    totals.settle(0)
    totals.first(1)
    settle(one, 0)
    settle(last_one, 0)
    onward(two, 1)
    settle(three, 1)
    result_ref[...] = jnp.stack([result[s * ROWS : s * ROWS + ROWS, :].astype(F32) for s in range(2)], 1).astype(BF16)
    totals.settle(1)
    totals.first(2)
    settle(one, 1)
    settle(last_one, 1)
    settle(two, 1)
    settle(three, 2)

    def mine(start, width):
        return weights[x // 2, at["z"], x % 2, at["y"], :, start : start + width].astype(F32)

    outer_out[...] = mine(OUTER, 2048)
    settle(two, 2)
    output_out[...] = mine(OUT, 512)
    inner_out[...] = mine(INNER, 2048)
    vector_out[...] = mine(EXTRA, LANES).T[0:8, :]
    totals.settle(2)
    scale = 1.0 / (total_ref[1:2, 1024:1025] * 1024.0)
    square = jnp.sum(total_ref[:, 0:1024], 1, keepdims=True)
    root_ref[...] = jnp.broadcast_to(jnp.sqrt(square * scale + 1e-06), root_ref.shape)
    settle(one, 2)
    settle(last_one, 2)
    query_out[...] = mine(QUERY, 512)
    key_out[...] = mine(KEY, 512)
    value_out[...] = mine(VALUE, 512)
    for item in closing + joined[-2:]:
        item.close()


def run_layers(*arguments):
    dma = pltpu.SemaphoreType.DMA
    out = lambda *shape: jax.ShapeDtypeStruct(shape, F32)
    vmem = lambda kind, *shape: pltpu.VMEM(shape, kind)
    return pl.pallas_call(
        layers_kernel,
        out_shape=(
            out(ROWS, 2, 1024), jax.ShapeDtypeStruct((ROWS, 2, 1024), BF16),
            out(16, 512), out(16, 512), out(16, 512), out(16, 512), out(16, 2048), out(16, 2048),
            out(8, 16), out(8, 2048), out(8, LANES),
        ),
        in_specs=[spec(pltpu.VMEM)] * 17 + [spec(pltpu.SMEM)],
        out_specs=(spec(pltpu.VMEM),) * 11,
        scratch_shapes=[
            vmem(BF16, *SHARDS, 16, WIDTH),
            vmem(F32, 1, 3072),
            vmem(F32, 8, 1024),
            vmem(BF16, 2, 256, 1024),
            vmem(BF16, 256, 1024),
            vmem(BF16, 256, 1024),
            vmem(F32, 256, 1024),
            vmem(BF16, 3, 256, 512),
            vmem(BF16, 2, 3, 1024, LANES),
            vmem(F32, 2, 1024, LANES),
            vmem(F32, 2, 8, 256),
            vmem(BF16, 2, 1024, LANES),
            vmem(BF16, 2, 256, 512),
            vmem(F32, 3, 256, 1024),
            vmem(F32, 3, 256, 1),
            vmem(BF16, 2, 256, 1024),
            vmem(BF16, 2, 256, 2048),
            vmem(BF16, 2, 256, 2048),
            vmem(BF16, 2, 256, 1024),
            vmem(BF16, 2, 256, 2048),
            vmem(BF16, 2, 256, 1024),
            vmem(BF16, 2, 3, 256, 512),
            vmem(BF16, 2, 256, 512),
            vmem(BF16, 2, 1024, LANES),
            vmem(BF16, 2048, LANES),
            vmem(F32, 2048, LANES),
            vmem(BF16, 2, 2, 1024, LANES),
            vmem(BF16, 2, 1024, LANES),
            vmem(BF16, 2, 2, 256, 512),
            vmem(BF16, 2, 2, 256, 512),
            vmem(F32, 3, 3, 8, 2048),
            dma((4,)),
            dma((3, 3)),
            dma((GATHER_COUNT,)),
            dma((3,)),
            dma((9,)),
            dma((1,)),
            dma((1,)),
            dma((2,)),
            dma((2,)),
            dma((1,)),
            dma((1,)),
            dma((3,)),
            dma((3,)),
            dma((4, 3)),
            dma((SCATTER_COUNT,)),
            *(shape for group in range(4) for shape in landing_shapes(group)),
        ],
        compiler_params=pltpu.CompilerParams(
            collective_id=3, has_side_effects=True, vmem_limit_bytes=LIMIT
        ),
        name="layers",
    )(*arguments)


def finish_kernel(
    stream_in, result_in, query_in, key_in, value_in, output_in, inner_in, outer_in, vectors, totals, roots,
    result, stream_grad, query, key, value, output, inner, outer, query_sum, value_sum, inner_sum, *rest,
):
    for source, target in (
        (result_in, result), (stream_in, stream_grad), (query_in, query), (key_in, key), (value_in, value),
        (output_in, output), (inner_in, inner), (outer_in, outer),
    ):
        target[...] = source[...]
    query_sum[...] = totals[1:2, 0:512].reshape(512)
    value_sum[...] = totals[1:2, 512:1024].reshape(512)
    inner_sum[...] = totals[0:1, :].reshape(2048)
    for j in range(6):
        rest[j][...] = vectors[j : j + 1, :].reshape(16)
    rest[6][...] = jnp.concatenate(
        [
            jnp.concatenate([roots[2 + 3 * layer + j : 3 + 3 * layer + j, 0:1] for j in range(3)], 1)
            for layer in range(LAYERS)
        ],
        0,
    )


def finish(partial):
    out = lambda *shape: jax.ShapeDtypeStruct(shape, F32)
    return pl.pallas_call(
        finish_kernel,
        out_shape=(
            jax.ShapeDtypeStruct((ROWS, 2, 1024), BF16), out(ROWS, 2, 1024),
            out(16, 512), out(16, 512), out(16, 512), out(16, 512), out(16, 2048), out(16, 2048),
            out(512), out(512), out(2048), *(out(16) for _ in range(6)), out(LAYERS, 3),
        ),
        in_specs=[spec(pltpu.VMEM)] * 11,
        out_specs=(spec(pltpu.VMEM),) * 18,
        name="finish",
    )(*partial)


def body(
    stream,
    lengths,
    query_weight,
    query_bias,
    key_weight,
    value_weight,
    value_bias,
    output_weight,
    output_bias,
    first_gain,
    first_shift,
    inner_weight,
    inner_bias,
    outer_weight,
    outer_bias,
    second_gain,
    second_shift,
    cotangent,
):
    partial = run_layers(
        stream, cotangent, query_weight, key_weight, value_weight, output_weight.T, inner_weight, outer_weight.T,
        output_bias, outer_bias, first_gain, first_shift, second_gain, second_shift,
        query_bias, value_bias, inner_bias, lengths,
    )
    (
        result, stream_grad, grad_query, grad_key, grad_value, grad_output, grad_inner, grad_outer,
        query_sum, value_sum, inner_sum, *vectors, roots,
    ) = finish(partial)
    return (
        result,
        stream_grad,
        grad_query,
        query_sum,
        grad_key,
        grad_value,
        value_sum,
        grad_output.T,
        vectors[0],
        vectors[2],
        vectors[3],
        grad_inner,
        inner_sum,
        grad_outer.T,
        vectors[1],
        vectors[4],
        vectors[5],
        roots,
    )


def solution(mesh):
    in_specs = (
        P("context", "fsdp", None),
        P("fsdp"),
        P(("fsdp", "context"), "tensor"),
        P("tensor"),
        P(("fsdp", "context"), "tensor"),
        P(("fsdp", "context"), "tensor"),
        P("tensor"),
        P("tensor", ("fsdp", "context")),
        P(("fsdp", "context")),
        P(("fsdp", "context")),
        P(("fsdp", "context")),
        P(("fsdp", "context"), "tensor"),
        P("tensor"),
        P("tensor", ("fsdp", "context")),
        P(("fsdp", "context")),
        P(("fsdp", "context")),
        P(("fsdp", "context")),
        P("context", "fsdp", None),
    )
    out_specs = (
        P("context", "fsdp", None),
        P("context", "fsdp", None),
        P(("fsdp", "context"), "tensor"),
        P("tensor"),
        P(("fsdp", "context"), "tensor"),
        P(("fsdp", "context"), "tensor"),
        P("tensor"),
        P("tensor", ("fsdp", "context")),
        P(("fsdp", "context")),
        P(("fsdp", "context")),
        P(("fsdp", "context")),
        P(("fsdp", "context"), "tensor"),
        P("tensor"),
        P("tensor", ("fsdp", "context")),
        P(("fsdp", "context")),
        P(("fsdp", "context")),
        P(("fsdp", "context")),
        P(),
    )
    return jax.shard_map(body, mesh=mesh, in_specs=in_specs, out_specs=out_specs, check_vma=False)
```
